32 devices in a mesh: row: 16 (over z, y, x), head: 2 (over core).
Axes of the slice: x: 2, y: 2, z: 4, core: 2. Of those that a mesh axis runs over, the one named last changes fastest.
Arguments:
- query_single: bfloat16 [16, 384], P('row'), may hold values from -6 to 6
- key_single: bfloat16 [1024, 384], P('row'), may hold values from -6 to 6
- pair: bfloat16 [16, 1024, 128], P('row'), may hold values from -6 to 32
- query_frames: float32 [12, 16], P(None, 'row'), may hold values from -2.5 to 2.5, as said below
- key_frames: float32 [12, 1024], P(None, 'row'), may hold values from -2.5 to 2.5, as said below
- w_query: bfloat16 [384, 96], P(None, 'head'), may hold values from -0.3125 to 0.3125
- w_key: bfloat16 [384, 96], P(None, 'head'), may hold values from -0.3125 to 0.3125
- w_value: bfloat16 [384, 96], P(None, 'head'), may hold values from -0.3125 to 0.3125
- w_query_points: bfloat16 [384, 72], P(None, 'head'), may hold values from -0.3125 to 0.3125
- w_key_points: bfloat16 [384, 72], P(None, 'head'), may hold values from -0.3125 to 0.3125
- w_value_points: bfloat16 [384, 144], P(None, 'head'), may hold values from -0.3125 to 0.3125
- head_weight: float32 [6], P('head'), may hold values from -2.5 to 0.5
- bias_weight: bfloat16 [6, 128], P('head'), as said below
- w_out: bfloat16 [1056, 384], P('head'), may hold values from -0.1875 to 0.1875
- d_out: bfloat16 [16, 384], P('row'), may hold values from -24 to 24
Outputs:
- output: bfloat16 [16, 384], P('row')
- grad_query: float32 [16, 384], P('row')
- grad_keys: float32 [1024, 384], P('row')
The draws below stay inside these ranges and needn't reach their ends.
Inputs may be any that keep to these rules, and one draw needn't show every extreme that they name: `bias_weight`: entries within -2.5 and 2.5 over the square root of 128. `query_frames`: rows 0 to 8 of each column form a rotation matrix. `key_frames`: rows 0 to 8 of each column form a rotation matrix.
All inputs are finite; a program needn't handle non-finite values.
Results may differ from the reference program's by a relative error of at most 0.012.
The reference program's roundings to bfloat16 on the way count: a program that leaves them out, or rounds other values in their place, can miss the bound.
Values may be sent and summed in bfloat16 or wider, within the bound.
No kernel may reach another device: no remote copies, remote signals or barrier semaphores. Data moves between devices by JAX's collectives and lax.ppermute only.
A program may use at most 64 MiB of HBM per device.

```python
import math
import jax
import jax.numpy as jnp
from jax import lax

CS = 384
H = 6
C = 16
PQ = 4
PV = 8
CZ = 128
Q = 16
K = 1024


def frame_table(key, count):
    key_rot, key_move = jax.random.split(key)
    along = jax.random.normal(key_rot, (3, count), jnp.float32)
    scale_inv = 1.0 / jnp.sqrt(1.0 + jnp.sum(along * along, axis=0))
    scalar_part = scale_inv
    vector_one = along[0] * scale_inv
    vector_two = along[1] * scale_inv
    vector_three = along[2] * scale_inv
    entries = [scalar_part * scalar_part + vector_one * vector_one - vector_two * vector_two - vector_three * vector_three, 2.0 * (vector_one * vector_two - scalar_part * vector_three), 2.0 * (vector_one * vector_three + scalar_part * vector_two), 2.0 * (vector_one * vector_two + scalar_part * vector_three), scalar_part * scalar_part - vector_one * vector_one + vector_two * vector_two - vector_three * vector_three, 2.0 * (vector_two * vector_three - scalar_part * vector_one), 2.0 * (vector_one * vector_three - scalar_part * vector_two), 2.0 * (vector_two * vector_three + scalar_part * vector_one), scalar_part * scalar_part - vector_one * vector_one - vector_two * vector_two + vector_three * vector_three]
    moves = jnp.clip(0.5 * jax.random.normal(key_move, (3, count), jnp.float32), -2.5, 2.5)
    return jnp.concatenate([jnp.stack(entries, axis=0), moves], axis=0)


def draw_query_frames(key, part):
    return frame_table(jax.random.fold_in(key, 17), Q)


def draw_key_frames(key, part):
    return frame_table(jax.random.fold_in(key, 29), K)


def draw_pair(key, part):
    return jnp.clip(jax.random.normal(key, (Q, K, CZ), jnp.float32), -6.0, 6.0).astype(jnp.bfloat16)


def draw_bias_weight(key, part):
    return (jnp.clip(jax.random.normal(key, (H, CZ), jnp.float32), -2.5, 2.5) / math.sqrt(CZ)).astype(jnp.bfloat16)


def shard_levels(stream_key, shape, shards, least, largest):
    def one(axis_at, parts):
        draws = jax.random.uniform(jax.random.fold_in(jax.random.fold_in(stream_key, 6), axis_at), (parts,), jnp.float32, least / len(shards), largest / len(shards))
        return jnp.repeat(jnp.exp(draws), shape[axis_at] // parts).reshape((-1,) + (1,) * (len(shape) - axis_at - 1))

    loudness = one(*shards[0])
    for cut in shards[1:]:
        loudness = loudness * one(*cut)
    return loudness


def noise(key, dims, deviation, reach, shards=(), kind=jnp.bfloat16):
    array = deviation * jax.random.normal(key, dims, jnp.float32)
    if shards:
        array = array * shard_levels(key, dims, shards, -0.22, 0.18)
    return jnp.clip(array, -reach, reach).astype(kind)


def setup_inputs(seed: int = 0) -> dict:
    seeds = jax.random.split(jax.random.key(seed), 16)
    return {
        "query_single": noise(seeds[0], (Q, CS), 1.0, 6.0, ((0, 16),)),
        "key_single": noise(seeds[1], (K, CS), 1.0, 6.0, ((0, 16),)),
        "pair": draw_pair(jax.random.fold_in(seeds[15], 71), 0),
        "query_frames": draw_query_frames(jax.random.fold_in(seeds[15], 71), 0),
        "key_frames": draw_key_frames(jax.random.fold_in(seeds[15], 71), 0),
        "w_query": noise(seeds[5], (CS, H * C), CS ** -0.5, 0.3125, ((1, 2),)),
        "w_key": noise(seeds[6], (CS, H * C), CS ** -0.5, 0.3125, ((1, 2),)),
        "w_value": noise(seeds[7], (CS, H * C), CS ** -0.5, 0.3125, ((1, 2),)),
        "w_query_points": noise(seeds[8], (CS, H * PQ * 3), CS ** -0.5, 0.3125, ((1, 2),)),
        "w_key_points": noise(seeds[9], (CS, H * PQ * 3), CS ** -0.5, 0.3125, ((1, 2),)),
        "w_value_points": noise(seeds[10], (CS, H * PV * 3), CS ** -0.5, 0.3125, ((1, 2),)),
        "head_weight": jnp.clip(-2.5 + 3.0 * jax.random.uniform(seeds[11], (H,), jnp.float32) ** shard_levels(seeds[11], (H,), ((0, 2),), -0.2, 0.2), -2.5, 0.5),
        "bias_weight": draw_bias_weight(jax.random.fold_in(seeds[15], 71), 0),
        "w_out": noise(seeds[13], (H * (C + 4 * PV + CZ), CS), (H * (C + 4 * PV + CZ)) ** -0.5, 0.1875, ((0, 2),)),
        "d_out": jnp.clip(jax.random.uniform(seeds[14], (Q, CS), jnp.float32, -24.0, 24.0) * shard_levels(seeds[14], (Q, CS), ((0, 16),), -0.4, 0.0), -24.0, 24.0).astype(jnp.bfloat16),
    }


LOGIT_SCALE = math.sqrt(1.0 / 3.0)

def point_scale(points):
    return math.sqrt(2.0 / (9.0 * points))

def product(form, former, latter):
    return jnp.einsum(form, former.astype(jnp.float32), latter.astype(jnp.float32))

def frame_parts(frames):
    columns = frames.shape[1]
    return (frames[:9].reshape(3, 3, columns), frames[9:12])

def rotate(vectors, rotation):
    return jnp.einsum('xyn,nhpy->nhpx', rotation, vectors, precision=lax.Precision.HIGHEST)

def unrotate(vectors, rotation):
    return jnp.einsum('xyn,nhpx->nhpy', rotation, vectors, precision=lax.Precision.HIGHEST)

def split_columns(packed, extents, axis_index):
    pieces = []
    cursor = 0
    for extent in extents:
        pieces.append(lax.slice_in_dim(packed, cursor, cursor + extent, axis=axis_index))
        cursor = cursor + extent
    return pieces

def key_side(key_single, key_frames, w_key, w_value, w_key_points, w_value_points, head_count):
    rows_k = key_single.shape[0]
    rotation, offset = frame_parts(key_frames)
    offset_rows = jnp.transpose(offset)[:, None, None, :]
    keys_b = jnp.dot(key_single, w_key, preferred_element_type=jnp.float32).astype(jnp.bfloat16)
    values_b = jnp.dot(key_single, w_value, preferred_element_type=jnp.float32).astype(jnp.bfloat16)
    local_k = jnp.dot(key_single, w_key_points, preferred_element_type=jnp.float32).reshape(rows_k, head_count, PQ, 3)
    key_pts = (rotate(local_k, rotation) + offset_rows).astype(jnp.bfloat16).reshape(rows_k, -1)
    local_v = jnp.dot(key_single, w_value_points, preferred_element_type=jnp.float32).reshape(rows_k, head_count, PV, 3)
    value_pts = (rotate(local_v, rotation) + offset_rows).astype(jnp.bfloat16).reshape(rows_k, -1)
    return (keys_b, values_b, key_pts, value_pts)

def query_pass(query_single, pair, query_frames, w_query, w_query_points, head_weight, bias_weight, w_out, d_out, keys_all, values_all, kp_all, vp_all):
    rows_q = query_single.shape[0]
    head_count = head_weight.shape[0]
    rotation, offset = frame_parts(query_frames)
    offset_rows = jnp.transpose(offset)[:, None, None, :]
    point_gain = (jax.nn.softplus(head_weight) * point_scale(PQ))[None, :, None]
    query_b = jnp.dot(query_single, w_query, preferred_element_type=jnp.float32).astype(jnp.bfloat16).reshape(rows_q, head_count, C)
    local_q = jnp.dot(query_single, w_query_points, preferred_element_type=jnp.float32).reshape(rows_q, head_count, PQ, 3)
    query_pts = (rotate(local_q, rotation) + offset_rows).astype(jnp.bfloat16).reshape(rows_q, head_count, 3 * PQ)
    query_sq = lax.optimization_barrier(jnp.sum(jnp.square(query_pts.astype(jnp.float32)), axis=-1))
    key_sq = lax.optimization_barrier(jnp.sum(jnp.square(kp_all.astype(jnp.float32)), axis=-1))
    pair_bias = product('hc,qkc->qhk', bias_weight, pair)
    distance = query_sq[:, :, None] + jnp.transpose(key_sq)[None, :, :] - 2.0 * product('qhe,khe->qhk', query_pts, kp_all)
    logits = LOGIT_SCALE * (product('qhc,khc->qhk', query_b, keys_all) / math.sqrt(C) + pair_bias - 0.5 * point_gain * distance)
    attention = jax.nn.softmax(logits, axis=-1)
    attention_b = attention.astype(jnp.bfloat16)
    attended = product('qhk,khc->qhc', attention_b, values_all)
    point_sum = product('qhk,khe->qhe', attention_b, vp_all).reshape(rows_q, head_count, PV, 3)
    pair_out = product('qhk,qkc->qhc', attention_b, pair)
    local_pts = unrotate(point_sum - offset_rows, rotation)
    lengths = jnp.sqrt(1.0 + lax.optimization_barrier(jnp.sum(jnp.square(local_pts), axis=-1)))
    features = jnp.concatenate([attended, local_pts.reshape(rows_q, head_count, 3 * PV), lengths, pair_out], axis=-1)
    features = features.astype(jnp.bfloat16).reshape(rows_q, -1)
    output_part = jnp.dot(features, w_out, preferred_element_type=jnp.float32)
    d_features = jnp.dot(d_out, jnp.transpose(w_out), preferred_element_type=jnp.float32).reshape(rows_q, head_count, -1)
    d_attended = d_features[:, :, :C].astype(jnp.bfloat16)
    d_local = d_features[:, :, C:C + 3 * PV].reshape(rows_q, head_count, PV, 3)
    d_lengths = d_features[:, :, C + 3 * PV:C + 4 * PV]
    d_pair = d_features[:, :, C + 4 * PV:].astype(jnp.bfloat16)
    d_local = d_local + (d_lengths / lengths)[..., None] * local_pts
    d_points = rotate(d_local, rotation).astype(jnp.bfloat16).reshape(rows_q, head_count, 3 * PV)
    d_attention = product('qhc,khc->qhk', d_attended, values_all) + product('qhe,khe->qhk', d_points, vp_all) + product('qhc,qkc->qhk', d_pair, pair)
    row_total = lax.optimization_barrier(jnp.sum(attention * d_attention, axis=-1, keepdims=True))
    score_b = (LOGIT_SCALE * attention * (d_attention - row_total)).astype(jnp.bfloat16)
    d_query = product('qhk,khc->qhc', score_b, keys_all) / math.sqrt(C)
    score_rows = lax.optimization_barrier(jnp.sum(score_b.astype(jnp.float32), axis=-1))[:, :, None]
    d_qpts = point_gain * (product('qhk,khe->qhe', score_b, kp_all) - score_rows * query_pts.astype(jnp.float32))
    d_qlocal = unrotate(d_qpts.reshape(rows_q, head_count, PQ, 3), rotation).astype(jnp.bfloat16).reshape(rows_q, -1)
    grad_part = jnp.dot(d_query.astype(jnp.bfloat16).reshape(rows_q, -1), jnp.transpose(w_query), preferred_element_type=jnp.float32)
    grad_part = grad_part + jnp.dot(d_qlocal, jnp.transpose(w_query_points), preferred_element_type=jnp.float32)
    query_side = jnp.concatenate([query_b.reshape(rows_q, -1), query_pts.reshape(rows_q, -1), d_attended.reshape(rows_q, -1), d_points.reshape(rows_q, -1)], axis=1)
    return (output_part, grad_part, query_side, attention_b, score_b)

def key_terms(attention_b, score_b, query_side, key_points, point_gain, head_count):
    count_q = query_side.shape[0]
    count_k = key_points.shape[0]
    side_parts = split_columns(query_side, [head_count * C, head_count * 3 * PQ, head_count * C, head_count * 3 * PV], 1)
    query_b = side_parts[0].reshape(count_q, head_count, C)
    query_pts = side_parts[1].reshape(count_q, head_count, 3 * PQ)
    grad_att = side_parts[2].reshape(count_q, head_count, C)
    grad_pts = side_parts[3].reshape(count_q, head_count, 3 * PV)
    d_key = product('qhk,qhc->khc', score_b, query_b) / math.sqrt(C)
    score_sum = lax.optimization_barrier(jnp.sum(score_b.astype(jnp.float32), axis=0))
    d_kpts = point_gain * (product('qhk,qhe->khe', score_b, query_pts) - jnp.transpose(score_sum)[:, :, None] * key_points.astype(jnp.float32))
    d_value = product('qhk,qhc->khc', attention_b, grad_att)
    d_vpts = product('qhk,qhe->khe', attention_b, grad_pts)
    return jnp.concatenate([d_key.reshape(count_k, -1), d_value.reshape(count_k, -1), d_kpts.reshape(count_k, -1), d_vpts.reshape(count_k, -1)], axis=1)

def key_finish(key_rows, key_frames, w_key, w_value, w_key_points, w_value_points, head_count):
    rows_k = key_rows.shape[0]
    rotation, offset = frame_parts(key_frames)
    pieces = split_columns(key_rows, [head_count * C, head_count * C, head_count * 3 * PQ, head_count * 3 * PV], 1)
    kp_local = unrotate(pieces[2].reshape(rows_k, head_count, PQ, 3), rotation).astype(jnp.bfloat16).reshape(rows_k, -1)
    vp_local = unrotate(pieces[3].reshape(rows_k, head_count, PV, 3), rotation).astype(jnp.bfloat16).reshape(rows_k, -1)
    result = jnp.dot(pieces[0].astype(jnp.bfloat16), jnp.transpose(w_key), preferred_element_type=jnp.float32)
    result = result + jnp.dot(pieces[1].astype(jnp.bfloat16), jnp.transpose(w_value), preferred_element_type=jnp.float32)
    result = result + jnp.dot(kp_local, jnp.transpose(w_key_points), preferred_element_type=jnp.float32)
    return result + jnp.dot(vp_local, jnp.transpose(w_value_points), preferred_element_type=jnp.float32)

def reference(query_single, key_single, pair, query_frames, key_frames, w_query, w_key, w_value, w_query_points, w_key_points, w_value_points, head_weight, bias_weight, w_out, d_out):
    head_count = head_weight.shape[0]
    total_q = query_single.shape[0]
    total_keys = key_single.shape[0]
    keys_b, values_b, key_pts, value_pts = key_side(key_single, key_frames, w_key, w_value, w_key_points, w_value_points, head_count)
    keys_all = keys_b.reshape(total_keys, head_count, C)
    values_all = values_b.reshape(total_keys, head_count, C)
    kp_all = key_pts.reshape(total_keys, head_count, 3 * PQ)
    vp_all = value_pts.reshape(total_keys, head_count, 3 * PV)
    point_gain = (jax.nn.softplus(head_weight) * point_scale(PQ))[None, :, None]
    block_rows = math.gcd(total_q, 32)
    block_count = total_q // block_rows
    blocks_in = (query_single.reshape(block_count, block_rows, -1), pair.reshape(block_count, block_rows, total_keys, -1), jnp.transpose(query_frames.reshape(12, block_count, block_rows), (1, 0, 2)), d_out.reshape(block_count, block_rows, -1))

    def one_block(carry, blocks):
        single_blk, pair_blk, frames_blk, cotangent_blk = blocks
        output_part, grad_part, query_side, attention_b, score_b = query_pass(single_blk, pair_blk, frames_blk, w_query, w_query_points, head_weight, bias_weight, w_out, cotangent_blk, keys_all, values_all, kp_all, vp_all)
        terms = key_terms(attention_b, score_b, query_side, kp_all, point_gain, head_count)
        return (carry + terms, (output_part.astype(jnp.bfloat16), grad_part))
    width_all = head_count * (2 * C + 3 * PQ + 3 * PV)
    key_rows, results = lax.scan(one_block, jnp.zeros((total_keys, width_all), jnp.float32), blocks_in)
    outputs, grads = results
    grad_keys = key_finish(key_rows, key_frames, w_key, w_value, w_key_points, w_value_points, head_count)
    return (outputs.reshape(total_q, -1), grads.reshape(total_q, -1), grad_keys)
```

```python
import math

import jax
import jax.numpy as jnp
from jax import lax
from jax.sharding import PartitionSpec as P

C = 16
PQ = 4
PV = 8


LOGIT_SCALE = math.sqrt(1.0 / 3.0)


def point_scale(points):
    return math.sqrt(2.0 / (9.0 * points))


def product(form, former, latter):
    return jnp.einsum(form, former, latter, preferred_element_type=jnp.float32)


def frame_parts(frames):
    columns = frames.shape[1]
    return (frames[:9].reshape(3, 3, columns), frames[9:12])


def rotate(vectors, rotation):
    return jnp.einsum("xyn,nhpy->nhpx", rotation, vectors, precision=lax.Precision.HIGHEST)


def unrotate(vectors, rotation):
    return jnp.einsum("xyn,nhpx->nhpy", rotation, vectors, precision=lax.Precision.HIGHEST)


def split_columns(packed, extents, axis_index):
    pieces = []
    cursor = 0
    for extent in extents:
        pieces.append(lax.slice_in_dim(packed, cursor, cursor + extent, axis=axis_index))
        cursor = cursor + extent
    return pieces


def key_side(key_single, key_frames, w_key, w_value, w_key_points, w_value_points, head_count):
    rows_k = key_single.shape[0]
    rotation, offset = frame_parts(key_frames)
    offset_rows = jnp.transpose(offset)[:, None, None, :]
    keys_b = jnp.dot(key_single, w_key, preferred_element_type=jnp.float32).astype(jnp.bfloat16)
    values_b = jnp.dot(key_single, w_value, preferred_element_type=jnp.float32).astype(jnp.bfloat16)
    local_k = jnp.dot(key_single, w_key_points, preferred_element_type=jnp.float32).reshape(
        rows_k, head_count, PQ, 3
    )
    key_pts = (rotate(local_k, rotation) + offset_rows).astype(jnp.bfloat16).reshape(rows_k, -1)
    local_v = jnp.dot(key_single, w_value_points, preferred_element_type=jnp.float32).reshape(
        rows_k, head_count, PV, 3
    )
    value_pts = (rotate(local_v, rotation) + offset_rows).astype(jnp.bfloat16).reshape(rows_k, -1)
    return (keys_b, values_b, key_pts, value_pts)


def query_pass(
    query_single,
    pair,
    query_frames,
    w_query,
    w_query_points,
    head_weight,
    bias_weight,
    w_out,
    d_out,
    keys_all,
    values_all,
    kp_all,
    vp_all,
):
    rows_q = query_single.shape[0]
    head_count = head_weight.shape[0]
    rotation, offset = frame_parts(query_frames)
    offset_rows = jnp.transpose(offset)[:, None, None, :]
    point_gain = (jax.nn.softplus(head_weight) * point_scale(PQ))[None, :, None]
    query_b = (
        jnp.dot(query_single, w_query, preferred_element_type=jnp.float32)
        .astype(jnp.bfloat16)
        .reshape(rows_q, head_count, C)
    )
    local_q = jnp.dot(query_single, w_query_points, preferred_element_type=jnp.float32).reshape(
        rows_q, head_count, PQ, 3
    )
    query_pts = (
        (rotate(local_q, rotation) + offset_rows)
        .astype(jnp.bfloat16)
        .reshape(rows_q, head_count, 3 * PQ)
    )
    query_sq = jnp.sum(jnp.square(query_pts.astype(jnp.float32)), axis=-1)
    key_sq = jnp.sum(jnp.square(kp_all.astype(jnp.float32)), axis=-1)
    pair_bias = product("hc,qkc->qhk", bias_weight, pair)
    distance = (
        query_sq[:, :, None]
        + jnp.transpose(key_sq)[None, :, :]
        - 2.0 * product("qhe,khe->qhk", query_pts, kp_all)
    )
    logits = LOGIT_SCALE * (
        product("qhc,khc->qhk", query_b, keys_all) / math.sqrt(C)
        + pair_bias
        - 0.5 * point_gain * distance
    )
    attention = jax.nn.softmax(logits, axis=-1)
    attention_b = attention.astype(jnp.bfloat16)
    attended = product("qhk,khc->qhc", attention_b, values_all)
    point_sum = product("qhk,khe->qhe", attention_b, vp_all).reshape(rows_q, head_count, PV, 3)
    pair_out = product("qhk,qkc->qhc", attention_b, pair)
    local_pts = unrotate(point_sum - offset_rows, rotation)
    lengths = jnp.sqrt(1.0 + jnp.sum(jnp.square(local_pts), axis=-1))
    features = jnp.concatenate(
        [attended, local_pts.reshape(rows_q, head_count, 3 * PV), lengths, pair_out], axis=-1
    )
    features = features.astype(jnp.bfloat16).reshape(rows_q, -1)
    output_part = jnp.dot(features, w_out, preferred_element_type=jnp.float32)
    d_features = jnp.dot(d_out, jnp.transpose(w_out), preferred_element_type=jnp.float32).reshape(
        rows_q, head_count, -1
    )
    d_attended = d_features[:, :, :C].astype(jnp.bfloat16)
    d_local = d_features[:, :, C : C + 3 * PV].reshape(rows_q, head_count, PV, 3)
    d_lengths = d_features[:, :, C + 3 * PV : C + 4 * PV]
    d_pair = d_features[:, :, C + 4 * PV :].astype(jnp.bfloat16)
    d_local = d_local + (d_lengths / lengths)[..., None] * local_pts
    d_points = rotate(d_local, rotation).astype(jnp.bfloat16).reshape(rows_q, head_count, 3 * PV)
    d_attention = (
        product("qhc,khc->qhk", d_attended, values_all)
        + product("qhe,khe->qhk", d_points, vp_all)
        + product("qhc,qkc->qhk", d_pair, pair)
    )
    row_total = jnp.sum(attention * d_attention, axis=-1, keepdims=True)
    score_b = (LOGIT_SCALE * attention * (d_attention - row_total)).astype(jnp.bfloat16)
    d_query = product("qhk,khc->qhc", score_b, keys_all) / math.sqrt(C)
    score_rows = jnp.sum(score_b.astype(jnp.float32), axis=-1)[:, :, None]
    d_qpts = point_gain * (
        product("qhk,khe->qhe", score_b, kp_all) - score_rows * query_pts.astype(jnp.float32)
    )
    d_qlocal = (
        unrotate(d_qpts.reshape(rows_q, head_count, PQ, 3), rotation)
        .astype(jnp.bfloat16)
        .reshape(rows_q, -1)
    )
    grad_part = jnp.dot(
        d_query.astype(jnp.bfloat16).reshape(rows_q, -1),
        jnp.transpose(w_query),
        preferred_element_type=jnp.float32,
    )
    grad_part = grad_part + jnp.dot(
        d_qlocal, jnp.transpose(w_query_points), preferred_element_type=jnp.float32
    )
    query_side = jnp.concatenate(
        [
            query_b.reshape(rows_q, -1),
            query_pts.reshape(rows_q, -1),
            d_attended.reshape(rows_q, -1),
            d_points.reshape(rows_q, -1),
        ],
        axis=1,
    )
    return (output_part, grad_part, query_side, attention_b, score_b)


def key_terms(attention_b, score_b, query_side, key_points, point_gain, head_count):
    count_q = query_side.shape[0]
    count_k = key_points.shape[0]
    side_parts = split_columns(
        query_side, [head_count * C, head_count * 3 * PQ, head_count * C, head_count * 3 * PV], 1
    )
    query_b = side_parts[0].reshape(count_q, head_count, C)
    query_pts = side_parts[1].reshape(count_q, head_count, 3 * PQ)
    grad_att = side_parts[2].reshape(count_q, head_count, C)
    grad_pts = side_parts[3].reshape(count_q, head_count, 3 * PV)
    d_key = product("qhk,qhc->khc", score_b, query_b) / math.sqrt(C)
    score_sum = jnp.sum(score_b.astype(jnp.float32), axis=0)
    d_kpts = point_gain * (
        product("qhk,qhe->khe", score_b, query_pts)
        - jnp.transpose(score_sum)[:, :, None] * key_points.astype(jnp.float32)
    )
    d_value = product("qhk,qhc->khc", attention_b, grad_att)
    d_vpts = product("qhk,qhe->khe", attention_b, grad_pts)
    return jnp.concatenate(
        [
            d_key.reshape(count_k, -1),
            d_value.reshape(count_k, -1),
            d_kpts.reshape(count_k, -1),
            d_vpts.reshape(count_k, -1),
        ],
        axis=1,
    )


def key_finish(key_rows, key_frames, w_key, w_value, w_key_points, w_value_points, head_count):
    rows_k = key_rows.shape[0]
    rotation, offset = frame_parts(key_frames)
    pieces = split_columns(
        key_rows, [head_count * C, head_count * C, head_count * 3 * PQ, head_count * 3 * PV], 1
    )
    kp_local = (
        unrotate(pieces[2].reshape(rows_k, head_count, PQ, 3), rotation)
        .astype(jnp.bfloat16)
        .reshape(rows_k, -1)
    )
    vp_local = (
        unrotate(pieces[3].reshape(rows_k, head_count, PV, 3), rotation)
        .astype(jnp.bfloat16)
        .reshape(rows_k, -1)
    )
    result = jnp.dot(
        pieces[0].astype(jnp.bfloat16), jnp.transpose(w_key), preferred_element_type=jnp.float32
    )
    result = result + jnp.dot(
        pieces[1].astype(jnp.bfloat16), jnp.transpose(w_value), preferred_element_type=jnp.float32
    )
    result = result + jnp.dot(
        kp_local, jnp.transpose(w_key_points), preferred_element_type=jnp.float32
    )
    return result + jnp.dot(
        vp_local, jnp.transpose(w_value_points), preferred_element_type=jnp.float32
    )


def shards(
    query_single,
    key_single,
    pair,
    query_frames,
    key_frames,
    w_query,
    w_key,
    w_value,
    w_query_points,
    w_key_points,
    w_value_points,
    head_weight,
    bias_weight,
    w_out,
    d_out,
):
    head_count = head_weight.shape[0]
    rows_k = key_single.shape[0]
    keys_b, values_b, key_pts, value_pts = key_side(
        key_single, key_frames, w_key, w_value, w_key_points, w_value_points, head_count
    )
    packed = jnp.concatenate([keys_b, values_b, key_pts, value_pts], axis=1)
    row_count = lax.axis_size("row")
    gathered = lax.all_to_all(
        jnp.broadcast_to(packed[None], (row_count,) + packed.shape),
        "row", split_axis=0, concat_axis=0, tiled=True,
    ).reshape(row_count * rows_k, packed.shape[1])
    total_keys = gathered.shape[0]
    pieces = split_columns(
        gathered, [head_count * C, head_count * C, head_count * 3 * PQ, head_count * 3 * PV], 1
    )
    keys_all = pieces[0].reshape(total_keys, head_count, C)
    values_all = pieces[1].reshape(total_keys, head_count, C)
    kp_all = pieces[2].reshape(total_keys, head_count, 3 * PQ)
    vp_all = pieces[3].reshape(total_keys, head_count, 3 * PV)
    output_part, grad_part, query_side, attention_b, score_b = query_pass(
        query_single,
        pair,
        query_frames,
        w_query,
        w_query_points,
        head_weight,
        bias_weight,
        w_out,
        d_out,
        keys_all,
        values_all,
        kp_all,
        vp_all,
    )
    point_gain = (jax.nn.softplus(head_weight) * point_scale(PQ))[None, :, None]
    rows_q = query_single.shape[0]
    block = rows_q * head_count * rows_k
    message = jnp.concatenate(
        [
            jnp.moveaxis(attention_b.reshape(-1, row_count, rows_k), 1, 0).reshape(row_count, block),
            jnp.moveaxis(score_b.reshape(-1, row_count, rows_k), 1, 0).reshape(row_count, block),
            jnp.broadcast_to(query_side.reshape(1, -1), (row_count, query_side.size)),
        ],
        axis=1,
    )
    message = jnp.pad(message, ((0, 0), (0, -message.shape[1] % 1024))).reshape(row_count, -1, 128)
    arrived = lax.all_to_all(message, "row", split_axis=0, concat_axis=0, tiled=True)
    arrived = arrived.reshape(row_count, -1)
    attention_to = arrived[:, :block].reshape(row_count * rows_q, head_count, rows_k)
    score_to = arrived[:, block : 2 * block].reshape(row_count * rows_q, head_count, rows_k)
    every_query = arrived[:, 2 * block : 2 * block + query_side.size].reshape(row_count * rows_q, -1)
    swap = [(i, (i + 1) % 2) for i in range(2)]
    rows_part = jnp.concatenate([output_part, grad_part], axis=1)
    rows_sum = rows_part + lax.ppermute(rows_part, "head", swap)
    output = rows_sum[:, : output_part.shape[1]].astype(jnp.bfloat16)
    grad_query = rows_sum[:, output_part.shape[1] :]
    own_points = key_pts.reshape(rows_k, head_count, 3 * PQ)
    key_rows = key_terms(attention_to, score_to, every_query, own_points, point_gain, head_count)
    grad_keys_part = key_finish(
        key_rows, key_frames, w_key, w_value, w_key_points, w_value_points, head_count
    )
    grad_keys = grad_keys_part + lax.ppermute(grad_keys_part, "head", swap)
    return (output, grad_query, grad_keys)


def solution(mesh):
    return jax.shard_map(
        shards,
        mesh=mesh,
        in_specs=(
            P("row", None),
            P("row", None),
            P("row", None, None),
            P(None, "row"),
            P(None, "row"),
            P(None, "head"),
            P(None, "head"),
            P(None, "head"),
            P(None, "head"),
            P(None, "head"),
            P(None, "head"),
            P("head"),
            P("head", None),
            P("head", None),
            P("row", None),
        ),
        out_specs=(P("row", None), P("row", None), P("row", None)),
        check_vma=False,
    )
```

```python
import functools
import math

import jax
import jax.numpy as jnp
from jax import lax
from jax.experimental import pallas as pl
from jax.experimental.pallas import tpu as pltpu
from jax.sharding import PartitionSpec as P

C = 16
PQ = 4
PV = 8
LANES = 128
SUBLANES = 8
ROWS16 = 16
LOGIT_SCALE = math.sqrt(1.0 / 3.0)
POINT_SCALE = math.sqrt(2.0 / (9.0 * PQ))
F32 = jnp.float32
B16 = jnp.bfloat16


class Layout:
    def __init__(self, heads):
        self.heads = heads
        self.keys = heads * C
        self.square = 2 * heads * C
        self.kp = heads * PQ
        self.seg = heads * (PQ + PV)
        assert self.square + 3 * heads <= LANES and 3 * self.seg <= LANES and heads <= SUBLANES


def nn(a, b, precision=None):
    return lax.dot_general(a, b, (((1,), (0,)), ((), ())), precision=precision, preferred_element_type=F32)


def nt(a, b):
    return lax.dot_general(a, b, (((1,), (1,)), ((), ())), preferred_element_type=F32)


def iota(shape, dim):
    return lax.broadcasted_iota(jnp.int32, shape, dim)


def pick(condition):
    return jnp.where(condition, 1.0, 0.0).astype(B16)


def to_lane(rows, offset, count):
    i, j = iota((rows, LANES), 0), iota((rows, LANES), 1)
    return pick((j == i + offset) & (i < count))


def to_components(rows, offset, points, seg):
    i, j = iota((rows, LANES), 0), iota((rows, LANES), 1)
    found = j < 0
    for c in range(3):
        m = j - (c * seg + offset)
        found = found | ((m >= 0) & (m < points) & (i == 3 * m + c))
    return pick(found)


def unpack(tile, seg):
    return tile, pltpu.roll(tile, LANES - seg, 1), pltpu.roll(tile, LANES - 2 * seg, 1)


def pack(x, y, z, seg, low, high):
    lane = iota(x.shape, 1)
    keep = (lane >= low) & (lane < high)
    x, y, z = (jnp.where(keep, v, 0.0) for v in (x, y, z))
    return x + pltpu.roll(y, seg, 1) + pltpu.roll(z, 2 * seg, 1)


def head_of(shape, lay):
    lane = iota(shape, 1)
    zero = jnp.full(shape, -1, jnp.int32)
    one = jnp.full(shape, -1, jnp.int32)
    for h in range(lay.heads):
        for base in (0, lay.keys):
            zero = jnp.where((lane >= base + h * C) & (lane < base + (h + 1) * C), h, zero)
        for c in range(3):
            k = c * lay.seg + h * PQ
            v = c * lay.seg + lay.kp + h * PV
            one = jnp.where((lane >= k) & (lane < k + PQ), h, one)
            one = jnp.where((lane >= v) & (lane < v + PV), h, one)
    return zero, one


def in_segments(shape, lay, low, high):
    lane = iota(shape, 1)
    found = lane < 0
    for c in range(3):
        found = found | ((lane >= c * lay.seg + low) & (lane < c * lay.seg + high))
    return found


def key_kernel(lay, key_single, frames, w_key, w_value, w_kp, w_vp, packed, weights):
    seg = lay.seg
    zero = nn(w_key[...], to_lane(lay.keys, 0, lay.keys)) + nn(w_value[...], to_lane(lay.keys, lay.keys, lay.keys))
    one = nn(w_kp[...], to_components(3 * lay.kp, 0, lay.kp, seg)) + nn(
        w_vp[...], to_components(3 * (seg - lay.kp), lay.kp, seg - lay.kp, seg)
    )
    w_all = jnp.concatenate([zero, one], axis=1).astype(B16)
    weights[...] = w_all
    rows = nn(key_single[...], w_all)
    turn = jnp.transpose(frames[...])
    x, y, z = unpack(rows[:, LANES:], seg)
    out = []
    for c in range(3):
        r = [turn[:, 3 * c + d : 3 * c + d + 1] for d in range(3)]
        out.append((r[0] * x + r[1] * y + r[2] * z + turn[:, 9 + c : 10 + c]).astype(B16).astype(F32))
    points = pack(*out, seg, 0, seg)
    square = out[0] * out[0] + out[1] * out[1] + out[2] * out[2]
    square = jnp.where(iota(square.shape, 1) < lay.kp, square, 0.0)
    i, j = iota((LANES, LANES), 0), iota((LANES, LANES), 1)
    chosen = j < 0
    for h in range(lay.heads):
        for piece in range(3):
            lane = lay.square + piece * lay.heads + h
            chosen = chosen | ((j == lane) & (i >= h * PQ) & (i < (h + 1) * PQ))
    total = nn(square, jnp.where(chosen, 1.0, 0.0), lax.Precision.HIGHEST)
    first = total.astype(B16).astype(F32)
    second = (total - first).astype(B16).astype(F32)
    third = total - first - second
    lane = iota(total.shape, 1)
    piece = jnp.where(
        lane < lay.square + lay.heads, first, jnp.where(lane < lay.square + 2 * lay.heads, second, third)
    )
    tile0 = jnp.where(lane < lay.square, rows[:, :LANES], piece).astype(B16)
    tile1 = points.astype(B16)
    for copy in range(packed.shape[0]):
        packed[copy, :, :LANES] = tile0
        packed[copy, :, LANES:] = tile1


def natural_blocks(pair, block, order):
    return jnp.concatenate([pair[0, j * block : (j + 1) * block, :] for j in order], axis=0)


def gain_rows(head_weight, lay):
    row = iota((SUBLANES, LANES), 0)
    raw = jnp.zeros((SUBLANES, LANES), F32)
    for h in range(lay.heads):
        raw = jnp.where(row == h, head_weight[h], raw)
    gain = (jnp.maximum(raw, 0.0) + jnp.log1p(jnp.exp(-jnp.abs(raw)))) * POINT_SCALE
    return jnp.where(row < lay.heads, gain, 0.0)


def gain_lanes(gain, lay):
    _, one = head_of(gain.shape, lay)
    return jnp.sum(jnp.where(one == iota(gain.shape, 0), gain, 0.0), axis=0, keepdims=True)


def early_kernel(
    lay, block, order, head_weight, frames, query_single, w_query, w_qp, bias_weight, w_out, d_out, pair,
    left, base, d_base, d_row, w_out_rows, w_query_rows, scratch,
):
    heads, seg = lay.heads, lay.seg
    width = C + 4 * PV + LANES
    shape = (SUBLANES, LANES)
    row, lane = iota(shape, 0), iota(shape, 1)
    zero_head, one_head = head_of(shape, lay)
    zero = nn(w_query[...], to_lane(lay.keys, 0, lay.keys))
    one = nn(w_qp[...], to_components(3 * lay.kp, 0, lay.kp, seg))
    w_q = jnp.concatenate([zero, one], axis=1).astype(B16)
    w_query_rows[...] = w_q
    near = C + 4 * PV
    w_o = jnp.zeros((2 * LANES, w_out.shape[1]), F32)
    for h in range(heads):
        i, j = iota((2 * LANES, near), 0), iota((2 * LANES, near), 1)
        m = i - (lay.keys + h * C)
        found = (m >= 0) & (m < C) & (j == m)
        m = i - h * PV
        found = found | ((m >= 0) & (m < PV) & (j == C + 3 * PV + m))
        for c in range(3):
            m = i - (LANES + c * seg + lay.kp + h * PV)
            found = found | ((m >= 0) & (m < PV) & (j == C + 3 * m + c))
        w_o = w_o + nn(pick(found), w_out[h * width : h * width + near, :])
    w_o = w_o.astype(B16)
    w_out_rows[...] = w_o
    single = jnp.broadcast_to(query_single[...], (SUBLANES, query_single.shape[1]))
    rows = nn(single, w_q)
    x, y, z = unpack(rows[:, LANES:], seg)
    out = []
    for c in range(3):
        value = frames[3 * c, 0] * x + frames[3 * c + 1, 0] * y + frames[3 * c + 2, 0] * z + frames[9 + c, 0]
        out.append(value.astype(B16).astype(F32))
    points = pack(*out, seg, 0, lay.kp)
    query = rows[:, :LANES].astype(B16).astype(F32)
    is_key = lane < lay.keys
    left[:SUBLANES, :LANES] = jnp.where(is_key & (zero_head == row), query, 0.0)
    left[:SUBLANES, LANES:] = jnp.zeros(shape, F32)
    minus = lane < 0
    for piece in range(3):
        minus = minus | (lane == lay.square + piece * heads + row)
    left[SUBLANES:, :LANES] = jnp.where(minus & (row < heads), -0.5, 0.0)
    mine = jnp.where(one_head == row, points, 0.0)
    left[SUBLANES:, LANES:] = mine
    gain = gain_rows(head_weight, lay)
    cotangent = jnp.broadcast_to(d_out[...], (SUBLANES, d_out.shape[1]))
    d_row[...] = nt(cotangent, w_o)
    scratch[...] = jnp.zeros_like(scratch)
    scratch[:heads, :] = bias_weight[...].astype(F32)
    for h in range(heads):
        d_pair = nt(cotangent, w_out[h * width + near : (h + 1) * width, :])
        scratch[SUBLANES + h : SUBLANES + h + 1, :] = d_pair[:1, :]
    both = nt(scratch[...].astype(B16), natural_blocks(pair, block, order))
    square = jnp.sum(mine * mine, axis=1, keepdims=True)
    base[...] = both[:SUBLANES] - 0.5 * gain[:, :1] * square
    d_base[...] = both[SUBLANES:]


def attention_kernel(
    lay, block, order, head_weight, frames, gathered, pair, left, base, d_base, d_row, message, features, pair_sum,
    scores,
):
    heads, seg = lay.heads, lay.seg
    shape = (SUBLANES, LANES)
    row, lane = iota(shape, 0), iota(shape, 1)
    zero_head, one_head = head_of(shape, lay)
    gain = gain_rows(head_weight, lay)
    keys = gathered[...].reshape(-1, 2 * LANES)
    first = nt(left[...].astype(B16), keys)
    logits = LOGIT_SCALE * (first[:SUBLANES] * (1.0 / math.sqrt(C)) + base[...] + gain[:, :1] * first[SUBLANES:])
    weight = jnp.exp(logits - jnp.max(logits, axis=1, keepdims=True))
    attention = weight / jnp.sum(weight, axis=1, keepdims=True)
    attention = jnp.where(iota(attention.shape, 0) < heads, attention, 0.0)
    attention_b = attention.astype(B16)
    sums = nn(attention_b, keys)
    pair_sum[...] = nn(attention_b, natural_blocks(pair, block, order))
    attended = jnp.sum(jnp.where(zero_head == row, sums[:, :LANES], 0.0), axis=0, keepdims=True)
    points = jnp.sum(jnp.where(one_head == row, sums[:, LANES:], 0.0), axis=0, keepdims=True)
    attended = jnp.broadcast_to(attended, shape)
    points = jnp.broadcast_to(points, shape)
    moved = [v - frames[9 + c, 0] for c, v in enumerate(unpack(points, seg))]
    local = [
        frames[d, 0] * moved[0] + frames[3 + d, 0] * moved[1] + frames[6 + d, 0] * moved[2] for d in range(3)
    ]
    lengths = jnp.sqrt(1.0 + (local[0] * local[0] + local[1] * local[1] + local[2] * local[2]))
    value_points = heads * PV
    is_value = (lane >= lay.keys) & (lane < lay.square)
    features[:, :LANES] = jnp.where(
        is_value, attended, jnp.where(lane < value_points, pltpu.roll(lengths, LANES - lay.kp, 1), 0.0)
    )
    features[:, LANES:] = pack(*local, seg, lay.kp, seg)
    d_zero = d_row[:, :LANES]
    share = pltpu.roll(d_zero, lay.kp, 1) / lengths
    d_local = [v + share * u for v, u in zip(unpack(d_row[:, LANES:], seg), local)]
    d_points = [
        frames[3 * c, 0] * d_local[0] + frames[3 * c + 1, 0] * d_local[1] + frames[3 * c + 2, 0] * d_local[2]
        for c in range(3)
    ]
    d_points = pack(*d_points, seg, lay.kp, seg)
    d_attended = jnp.where(is_value, d_zero, 0.0)
    right = jnp.concatenate(
        [jnp.where(zero_head == row, d_attended, 0.0), jnp.where(one_head == row, d_points, 0.0)], axis=1
    )
    d_attention = nt(right.astype(B16), keys) + d_base[...]
    total = jnp.sum(attention * d_attention, axis=1, keepdims=True)
    score_b = (LOGIT_SCALE * attention * (d_attention - total)).astype(B16)
    scores[...] = score_b.astype(F32)
    query0 = jnp.sum(left[:SUBLANES, :LANES], axis=0, keepdims=True)
    query1 = jnp.sum(left[SUBLANES:, LANES:], axis=0, keepdims=True)
    side = jnp.where(row == 0, jnp.broadcast_to(query0, shape) + d_attended, 0.0)
    side = side + jnp.where(row == 1, jnp.broadcast_to(query1, shape) + d_points, 0.0)
    side = side.astype(B16)
    high = attention_b.astype(F32)
    low = score_b.astype(F32)
    half = lane < block
    for place, j in enumerate(order):
        at = place * block // LANES * LANES
        a, s = high[:, at : at + LANES], low[:, at : at + LANES]
        if place * block % LANES:
            a = pltpu.roll(a, LANES - block, 1)
        else:
            s = pltpu.roll(s, block, 1)
        message[j, :, :] = jnp.concatenate([jnp.where(half, a, s).astype(B16), side], axis=0)


def rows_kernel(
    lay, head_weight, frames, gathered, left, scores, features, pair_sum, w_out, w_out_rows, w_query_rows, sums
):
    heads, seg = lay.heads, lay.seg
    width = C + 4 * PV + LANES
    near = C + 4 * PV
    shape = (SUBLANES, LANES)
    row, lane = iota(shape, 0), iota(shape, 1)
    zero_head, one_head = head_of(shape, lay)
    keys = gathered[...].reshape(-1, 2 * LANES)
    result = nn(features[...].astype(B16), w_out_rows[...])
    for h in range(heads):
        part = jnp.broadcast_to(pair_sum[h : h + 1, :], shape).astype(B16)
        result = result + nn(part, w_out[h * width + near : (h + 1) * width, :])
    gain = gain_rows(head_weight, lay)
    score = scores[...]
    d_rows = nn(score.astype(B16), keys)
    d_query = jnp.sum(
        jnp.where((lane < lay.keys) & (zero_head == row), d_rows[:, :LANES], 0.0), axis=0, keepdims=True
    ) * (1.0 / math.sqrt(C))
    score_sum = jnp.sum(score, axis=1, keepdims=True)
    d_points = gain * (d_rows[:, LANES:] - score_sum * left[SUBLANES:, LANES:])
    d_points = jnp.sum(jnp.where(one_head == row, d_points, 0.0), axis=0, keepdims=True)
    x, y, z = unpack(jnp.broadcast_to(d_points, shape), seg)
    local = [frames[d, 0] * x + frames[3 + d, 0] * y + frames[6 + d, 0] * z for d in range(3)]
    local = pack(*local, seg, 0, lay.kp)
    both = jnp.concatenate([jnp.broadcast_to(d_query, shape), local], axis=1).astype(B16)
    grad = nt(both, w_query_rows[...])
    sums[...] = jnp.concatenate([result, grad], axis=1)


def owner_kernel(lay, head_weight, arrived, frames, packed, weights, result):
    heads, seg = lay.heads, lay.seg
    count = arrived.shape[0]
    block = packed.shape[1]
    took = arrived[...].astype(F32)
    shape = (ROWS16, LANES)
    row = iota(shape, 0)
    zero_head, one_head = head_of(shape, lay)
    keep0 = (zero_head == row)[None]
    keep1 = (one_head == row)[None]
    whole = (count, ROWS16, LANES)
    side0 = jnp.where(keep0, jnp.broadcast_to(took[:, SUBLANES : SUBLANES + 1, :], whole), 0.0)
    side1 = jnp.where(keep1, jnp.broadcast_to(took[:, SUBLANES + 1 : SUBLANES + 2, :], whole), 0.0)
    ones = jnp.where(jnp.broadcast_to(keep1, whole), 1.0, 0.0)
    right = jnp.concatenate([side0, side1, ones], axis=2).reshape(count * ROWS16, 3 * LANES).astype(B16)
    turned = jnp.transpose(took.reshape(count * ROWS16, LANES)).astype(B16)
    both = nn(turned, right)
    high, low = both[:block], both[block:]
    small = (block, LANES)
    lane = iota(small, 1)
    tile0 = jnp.where(lane < lay.keys, low[:, :LANES] * (1.0 / math.sqrt(C)), high[:, :LANES])
    gain = gain_lanes(gain_rows(head_weight, lay), lay)
    own = packed[0, :, LANES:].astype(F32)
    kp_part = gain * (low[:, LANES : 2 * LANES] - low[:, 2 * LANES :] * own)
    tile1 = jnp.where(in_segments(small, lay, 0, lay.kp), kp_part, high[:, LANES : 2 * LANES])
    turn = jnp.transpose(frames[...])
    x, y, z = unpack(tile1, seg)
    local = []
    for d in range(3):
        r = [turn[:, 3 * c + d : 3 * c + d + 1] for c in range(3)]
        local.append(r[0] * x + r[1] * y + r[2] * z)
    tile1 = pack(*local, seg, 0, seg)
    rows = jnp.concatenate([tile0, tile1], axis=1).astype(B16)
    result[...] = nt(rows, weights[...])


VMEM = pl.BlockSpec(memory_space=pltpu.VMEM)
SMEM = pl.BlockSpec(memory_space=pltpu.SMEM)


def call(body, outs, args, scalars=(), scratch=(), flops=1000000):
    size = sum(math.prod(v.shape) * v.dtype.itemsize for v in list(args) + list(outs))
    return pl.pallas_call(
        body,
        out_shape=tuple(outs),
        in_specs=[SMEM] * len(scalars) + [VMEM] * len(args),
        out_specs=tuple([VMEM] * len(outs)),
        scratch_shapes=list(scratch),
        compiler_params=pltpu.CompilerParams(vmem_limit_bytes=(16 << 20) + 6 * size),
        cost_estimate=pl.CostEstimate(flops=flops, bytes_accessed=size, transcendentals=0),
    )(*scalars, *args)


def shape_of(*dims, dtype=F32):
    return jax.ShapeDtypeStruct(dims, dtype)


def shards(
    query_single, key_single, pair, query_frames, key_frames, w_query, w_key, w_value, w_query_points, w_key_points,
    w_value_points, head_weight, bias_weight, w_out, d_out,
):
    lay = Layout(head_weight.shape[0])
    count = lax.axis_size("row")
    block, width = key_single.shape
    total = count * block
    near = 1
    while 4 * near * near <= count:
        near *= 2
    far = count // near
    order = [(place % far) * near + place // far for place in range(count)]
    lines = [[z * near + y for z in range(far)] for y in range(near)]
    planes = [[z * near + y for y in range(near)] for z in range(far)]

    packed, weights = call(
        functools.partial(key_kernel, lay),
        [shape_of(far, block, 2 * LANES, dtype=B16), shape_of(width, 2 * LANES, dtype=B16)],
        [key_single, key_frames, w_key, w_value, w_key_points, w_value_points],
    )
    line = lax.all_to_all(packed, "row", 0, 0, axis_index_groups=lines, tiled=True)
    copies = jnp.broadcast_to(line[None], (near,) + line.shape)
    gathered = lax.all_to_all(copies, "row", 0, 0, axis_index_groups=planes, tiled=True)
    left, base, d_base, d_row, w_out_rows, w_query_rows = call(
        functools.partial(early_kernel, lay, block, order),
        [
            shape_of(ROWS16, 2 * LANES), shape_of(SUBLANES, total), shape_of(SUBLANES, total),
            shape_of(SUBLANES, 2 * LANES), shape_of(2 * LANES, width, dtype=B16),
            shape_of(width, 2 * LANES, dtype=B16),
        ],
        [query_single, w_query, w_query_points, bias_weight, w_out, d_out, pair],
        [head_weight, query_frames],
        [pltpu.VMEM((ROWS16, LANES), F32)],
    )
    message, features, pair_sum, scores = call(
        functools.partial(attention_kernel, lay, block, order),
        [
            shape_of(count, ROWS16, LANES, dtype=B16), shape_of(SUBLANES, 2 * LANES), shape_of(SUBLANES, LANES),
            shape_of(SUBLANES, total),
        ],
        [gathered, pair, left, base, d_base, d_row],
        [head_weight, query_frames],
    )
    arrived = lax.all_to_all(message, "row", 0, 0, tiled=True)
    (sums,) = call(
        functools.partial(rows_kernel, lay),
        [shape_of(SUBLANES, 2 * width)],
        [gathered, left, scores, features, pair_sum, w_out, w_out_rows, w_query_rows],
        [head_weight, query_frames],
    )
    swap = [(i, (i + 1) % 2) for i in range(2)]
    sums = sums[:1]
    sums = sums + lax.ppermute(sums, "head", swap)
    output = sums[:, :width].astype(B16)
    grad_query = sums[:, width:]
    (part,) = call(
        functools.partial(owner_kernel, lay),
        [shape_of(block, width)],
        [arrived, key_frames, packed, weights],
        [head_weight],
    )
    grad_keys = part + lax.ppermute(part, "head", swap)
    return (output, grad_query, grad_keys)


def solution(mesh):
    return jax.shard_map(
        shards,
        mesh=mesh,
        in_specs=(
            P("row", None),
            P("row", None),
            P("row", None, None),
            P(None, "row"),
            P(None, "row"),
            P(None, "head"),
            P(None, "head"),
            P(None, "head"),
            P(None, "head"),
            P(None, "head"),
            P(None, "head"),
            P("head"),
            P("head", None),
            P("head", None),
            P("row", None),
        ),
        out_specs=(P("row", None), P("row", None), P("row", None)),
        check_vma=False,
    )
```

```python
import functools
import math

import jax
import jax.numpy as jnp
from jax import lax
from jax.experimental import pallas as pl
from jax.experimental.pallas import tpu as pltpu
from jax.sharding import PartitionSpec as P

C = 16
PQ = 4
PV = 8
LANES = 128
SUBLANES = 8
ROWS16 = 16
LOGIT_SCALE = math.sqrt(1.0 / 3.0)
POINT_SCALE = math.sqrt(2.0 / (9.0 * PQ))
F32 = jnp.float32
B16 = jnp.bfloat16


class Layout:
    def __init__(self, heads):
        self.heads = heads
        self.keys = heads * C
        self.square = 2 * heads * C
        self.kp = heads * PQ
        self.seg = heads * (PQ + PV)
        assert self.square + 3 * heads <= LANES and 3 * self.seg <= LANES and heads + 2 <= SUBLANES


def nn(a, b, precision=None):
    return lax.dot_general(a, b, (((1,), (0,)), ((), ())), precision=precision, preferred_element_type=F32)


def nt(a, b):
    return lax.dot_general(a, b, (((1,), (1,)), ((), ())), preferred_element_type=F32)


def iota(shape, dim):
    return lax.broadcasted_iota(jnp.int32, shape, dim)


def pick(condition):
    return jnp.where(condition, 1.0, 0.0).astype(B16)


def to_lane(rows, offset):
    j, i = iota((LANES, rows), 0), iota((LANES, rows), 1)
    return pick(j == i + offset)


def to_components(rows, offset, points, seg):
    j, i = iota((LANES, rows), 0), iota((LANES, rows), 1)
    found = j < 0
    for c in range(3):
        m = j - (c * seg + offset)
        found = found | ((m >= 0) & (m < points) & (i == 3 * m + c))
    return pick(found)


def unpack(tile, seg):
    return tile, pltpu.roll(tile, LANES - seg, 1), pltpu.roll(tile, LANES - 2 * seg, 1)


def pack(x, y, z, seg, low, high):
    lane = iota(x.shape, 1)
    keep = (lane >= low) & (lane < high)
    x, y, z = (jnp.where(keep, v, 0.0) for v in (x, y, z))
    return x + pltpu.roll(y, seg, 1) + pltpu.roll(z, 2 * seg, 1)


def head_of(shape, lay):
    lane = iota(shape, 1)
    zero = jnp.full(shape, -1, jnp.int32)
    one = jnp.full(shape, -1, jnp.int32)
    for h in range(lay.heads):
        for base in (0, lay.keys):
            zero = jnp.where((lane >= base + h * C) & (lane < base + (h + 1) * C), h, zero)
        for c in range(3):
            k = c * lay.seg + h * PQ
            v = c * lay.seg + lay.kp + h * PV
            one = jnp.where((lane >= k) & (lane < k + PQ), h, one)
            one = jnp.where((lane >= v) & (lane < v + PV), h, one)
    return zero, one


def in_segments(shape, lay, low, high):
    lane = iota(shape, 1)
    found = lane < 0
    for c in range(3):
        found = found | ((lane >= c * lay.seg + low) & (lane < c * lay.seg + high))
    return found


def key_kernel(lay, key_single, frames, w_key, w_value, w_kp, w_vp, packed, weights):
    seg = lay.seg
    zero = nn(to_lane(lay.keys, 0), w_key[...]) + nn(to_lane(lay.keys, lay.keys), w_value[...])
    one = nn(to_components(3 * lay.kp, 0, lay.kp, seg), w_kp[...]) + nn(
        to_components(3 * (seg - lay.kp), lay.kp, seg - lay.kp, seg), w_vp[...]
    )
    w_all = jnp.concatenate([zero, one], axis=0).astype(B16)
    weights[...] = w_all
    rows = nt(key_single[...], w_all)
    turn = jnp.transpose(frames[...])
    x, y, z = unpack(rows[:, LANES:], seg)
    out = []
    for c in range(3):
        r = [turn[:, 3 * c + d : 3 * c + d + 1] for d in range(3)]
        out.append((r[0] * x + r[1] * y + r[2] * z + turn[:, 9 + c : 10 + c]).astype(B16).astype(F32))
    points = pack(*out, seg, 0, seg)
    square = out[0] * out[0] + out[1] * out[1] + out[2] * out[2]
    square = jnp.where(iota(square.shape, 1) < lay.kp, square, 0.0)
    i, j = iota((LANES, LANES), 0), iota((LANES, LANES), 1)
    chosen = j < 0
    for h in range(lay.heads):
        for piece in range(3):
            lane = lay.square + piece * lay.heads + h
            chosen = chosen | ((j == lane) & (i >= h * PQ) & (i < (h + 1) * PQ))
    total = nn(square, jnp.where(chosen, 1.0, 0.0), lax.Precision.HIGHEST)
    first = total.astype(B16).astype(F32)
    second = (total - first).astype(B16).astype(F32)
    third = total - first - second
    lane = iota(total.shape, 1)
    piece = jnp.where(
        lane < lay.square + lay.heads, first, jnp.where(lane < lay.square + 2 * lay.heads, second, third)
    )
    tile0 = jnp.where(lane < lay.square, rows[:, :LANES], piece).astype(B16)
    tile1 = points.astype(B16)
    packed[:, :LANES] = tile0
    packed[:, LANES:] = tile1


def natural_blocks(pair, block, order):
    return jnp.concatenate([pair[0, j * block : (j + 1) * block, :] for j in order], axis=0)


def gain_rows(head_weight, lay):
    row = iota((SUBLANES, LANES), 0)
    raw = jnp.zeros((SUBLANES, LANES), F32)
    for h in range(lay.heads):
        raw = jnp.where(row == h, head_weight[h], raw)
    gain = (jnp.maximum(raw, 0.0) + jnp.log1p(jnp.exp(-jnp.abs(raw)))) * POINT_SCALE
    return jnp.where(row < lay.heads, gain, 0.0)


def gain_lanes(gain, lay):
    _, one = head_of(gain.shape, lay)
    return jnp.sum(jnp.where(one == iota(gain.shape, 0), gain, 0.0), axis=0, keepdims=True)


def early_kernel(
    lay, block, order, head_weight, frames, query_single, w_query, w_qp, bias_weight, w_out, d_out, pair,
    left, base, d_base, d_row, w_out_rows, w_query_rows, scratch,
):
    heads, seg = lay.heads, lay.seg
    width = C + 4 * PV + LANES
    shape = (SUBLANES, LANES)
    row, lane = iota(shape, 0), iota(shape, 1)
    zero_head, one_head = head_of(shape, lay)
    zero = nn(to_lane(lay.keys, 0), w_query[...])
    one = nn(to_components(3 * lay.kp, 0, lay.kp, seg), w_qp[...])
    w_q = jnp.concatenate([zero, one], axis=0).astype(B16)
    w_query_rows[...] = w_q
    near = C + 4 * PV
    w_o = jnp.zeros((2 * LANES, w_out.shape[1]), F32)
    for h in range(heads):
        i, j = iota((2 * LANES, near), 0), iota((2 * LANES, near), 1)
        m = i - (lay.keys + h * C)
        found = (m >= 0) & (m < C) & (j == m)
        m = i - h * PV
        found = found | ((m >= 0) & (m < PV) & (j == C + 3 * PV + m))
        for c in range(3):
            m = i - (LANES + c * seg + lay.kp + h * PV)
            found = found | ((m >= 0) & (m < PV) & (j == C + 3 * m + c))
        w_o = w_o + nn(pick(found), w_out[h * width : h * width + near, :])
    w_o = w_o.astype(B16)
    w_out_rows[...] = w_o
    single = jnp.broadcast_to(query_single[...], (SUBLANES, query_single.shape[1]))
    rows = nt(single, w_q)
    x, y, z = unpack(rows[:, LANES:], seg)
    out = []
    for c in range(3):
        value = frames[0, 3 * c] * x + frames[0, 3 * c + 1] * y + frames[0, 3 * c + 2] * z + frames[0, 9 + c]
        out.append(value.astype(B16).astype(F32))
    points = pack(*out, seg, 0, lay.kp)
    query = rows[:, :LANES].astype(B16).astype(F32)
    is_key = lane < lay.keys
    left[:SUBLANES, :LANES] = jnp.where(is_key & (zero_head == row), query, 0.0)
    left[:SUBLANES, LANES:] = jnp.zeros(shape, F32)
    minus = lane < 0
    for piece in range(3):
        minus = minus | (lane == lay.square + piece * heads + row)
    left[SUBLANES:, :LANES] = jnp.where(minus & (row < heads), -0.5, 0.0)
    mine = jnp.where(one_head == row, points, 0.0)
    left[SUBLANES:, LANES:] = mine
    gain = gain_rows(head_weight, lay)
    cotangent = jnp.broadcast_to(d_out[...], (SUBLANES, d_out.shape[1]))
    d_row[...] = nt(cotangent, w_o)
    scratch[...] = jnp.zeros_like(scratch)
    scratch[:heads, :] = bias_weight[...].astype(F32)
    for h in range(heads):
        d_pair = nt(cotangent, w_out[h * width + near : (h + 1) * width, :])
        scratch[SUBLANES + h : SUBLANES + h + 1, :] = d_pair[:1, :]
    both = nt(scratch[...].astype(B16), natural_blocks(pair, block, order))
    square = jnp.sum(mine * mine, axis=1, keepdims=True)
    base[...] = both[:SUBLANES] - 0.5 * gain[:, :1] * square
    d_base[...] = both[SUBLANES:]


def attention_kernel(
    lay, block, order, head_weight, frames, gathered, pair, left, base, d_base, d_row, message, features, pair_sum,
    scores,
):
    heads, seg = lay.heads, lay.seg
    shape = (SUBLANES, LANES)
    row, lane = iota(shape, 0), iota(shape, 1)
    zero_head, one_head = head_of(shape, lay)
    gain = gain_rows(head_weight, lay)
    keys = gathered[...].reshape(-1, 2 * LANES)
    first = nt(left[...].astype(B16), keys)
    logits = LOGIT_SCALE * (first[:SUBLANES] * (1.0 / math.sqrt(C)) + base[...] + gain[:, :1] * first[SUBLANES:])
    weight = jnp.exp(logits - jnp.max(logits, axis=1, keepdims=True))
    attention = weight / jnp.sum(weight, axis=1, keepdims=True)
    attention = jnp.where(iota(attention.shape, 0) < heads, attention, 0.0)
    attention_b = attention.astype(B16)
    sums = nn(attention_b, keys)
    pair_sum[...] = nn(attention_b, natural_blocks(pair, block, order))
    attended = jnp.sum(jnp.where(zero_head == row, sums[:, :LANES], 0.0), axis=0, keepdims=True)
    points = jnp.sum(jnp.where(one_head == row, sums[:, LANES:], 0.0), axis=0, keepdims=True)
    attended = jnp.broadcast_to(attended, shape)
    points = jnp.broadcast_to(points, shape)
    moved = [v - frames[0, 9 + c] for c, v in enumerate(unpack(points, seg))]
    local = [
        frames[0, d] * moved[0] + frames[0, 3 + d] * moved[1] + frames[0, 6 + d] * moved[2] for d in range(3)
    ]
    lengths = jnp.sqrt(1.0 + (local[0] * local[0] + local[1] * local[1] + local[2] * local[2]))
    value_points = heads * PV
    is_value = (lane >= lay.keys) & (lane < lay.square)
    features[:, :LANES] = jnp.where(
        is_value, attended, jnp.where(lane < value_points, pltpu.roll(lengths, LANES - lay.kp, 1), 0.0)
    )
    features[:, LANES:] = pack(*local, seg, lay.kp, seg)
    d_zero = d_row[:, :LANES]
    share = pltpu.roll(d_zero, lay.kp, 1) / lengths
    d_local = [v + share * u for v, u in zip(unpack(d_row[:, LANES:], seg), local)]
    d_points = [
        frames[0, 3 * c] * d_local[0] + frames[0, 3 * c + 1] * d_local[1] + frames[0, 3 * c + 2] * d_local[2]
        for c in range(3)
    ]
    d_points = pack(*d_points, seg, lay.kp, seg)
    d_attended = jnp.where(is_value, d_zero, 0.0)
    right = jnp.concatenate(
        [jnp.where(zero_head == row, d_attended, 0.0), jnp.where(one_head == row, d_points, 0.0)], axis=1
    )
    d_attention = nt(right.astype(B16), keys) + d_base[...]
    total = jnp.sum(attention * d_attention, axis=1, keepdims=True)
    score_b = (LOGIT_SCALE * attention * (d_attention - total)).astype(B16)
    scores[...] = score_b.astype(F32)
    query0 = jnp.sum(left[:SUBLANES, :LANES], axis=0, keepdims=True)
    query1 = jnp.sum(left[SUBLANES:, LANES:], axis=0, keepdims=True)
    side = jnp.where(row == heads, jnp.broadcast_to(query0, shape) + d_attended, 0.0)
    side = side + jnp.where(row == heads + 1, jnp.broadcast_to(query1, shape) + d_points, 0.0)
    high = attention_b.astype(F32)
    low = score_b.astype(F32)
    half = lane < block
    for place, j in enumerate(order):
        at = place * block // LANES * LANES
        a, s = high[:, at : at + LANES], low[:, at : at + LANES]
        if place * block % LANES:
            a = pltpu.roll(a, LANES - block, 1)
        else:
            s = pltpu.roll(s, block, 1)
        message[j, :, :] = jnp.where(row < heads, jnp.where(half, a, s), side).astype(B16)


def rows_kernel(
    lay, head_weight, frames, gathered, left, scores, features, pair_sum, w_out, w_out_rows, w_query_rows, sums
):
    heads, seg = lay.heads, lay.seg
    width = C + 4 * PV + LANES
    near = C + 4 * PV
    shape = (SUBLANES, LANES)
    row, lane = iota(shape, 0), iota(shape, 1)
    zero_head, one_head = head_of(shape, lay)
    keys = gathered[...].reshape(-1, 2 * LANES)
    result = nn(features[...].astype(B16), w_out_rows[...])
    for h in range(heads):
        part = jnp.broadcast_to(pair_sum[h : h + 1, :], shape).astype(B16)
        result = result + nn(part, w_out[h * width + near : (h + 1) * width, :])
    gain = gain_rows(head_weight, lay)
    score = scores[...]
    d_rows = nn(score.astype(B16), keys)
    d_query = jnp.sum(
        jnp.where((lane < lay.keys) & (zero_head == row), d_rows[:, :LANES], 0.0), axis=0, keepdims=True
    ) * (1.0 / math.sqrt(C))
    score_sum = jnp.sum(score, axis=1, keepdims=True)
    d_points = gain * (d_rows[:, LANES:] - score_sum * left[SUBLANES:, LANES:])
    d_points = jnp.sum(jnp.where(one_head == row, d_points, 0.0), axis=0, keepdims=True)
    x, y, z = unpack(jnp.broadcast_to(d_points, shape), seg)
    local = [frames[0, d] * x + frames[0, 3 + d] * y + frames[0, 6 + d] * z for d in range(3)]
    local = pack(*local, seg, 0, lay.kp)
    both = jnp.concatenate([jnp.broadcast_to(d_query, shape), local], axis=1).astype(B16)
    grad = nn(both, w_query_rows[...])
    sums[...] = jnp.concatenate([result, grad], axis=1)


def owner_kernel(lay, head_weight, arrived, frames, packed, weights, result):
    heads, seg = lay.heads, lay.seg
    count = arrived.shape[0]
    block = packed.shape[0]
    took = arrived[...].astype(F32)
    shape = (SUBLANES, LANES)
    row = iota(shape, 0)
    zero_head, one_head = head_of(shape, lay)
    keep0 = (zero_head == row)[None]
    keep1 = (one_head == row)[None]
    whole = (count, SUBLANES, LANES)
    side0 = jnp.where(keep0, jnp.broadcast_to(took[:, heads : heads + 1, :], whole), 0.0)
    side1 = jnp.where(keep1, jnp.broadcast_to(took[:, heads + 1 : heads + 2, :], whole), 0.0)
    ones = jnp.where(jnp.broadcast_to(keep1, whole), 1.0, 0.0)
    right = jnp.concatenate([side0, side1, ones], axis=2).reshape(count * SUBLANES, 3 * LANES).astype(B16)
    turned = jnp.transpose(took.reshape(count * SUBLANES, LANES)).astype(B16)
    both = nn(turned, right)
    high, low = both[:block], both[block:]
    small = (block, LANES)
    lane = iota(small, 1)
    tile0 = jnp.where(lane < lay.keys, low[:, :LANES] * (1.0 / math.sqrt(C)), high[:, :LANES])
    gain = gain_lanes(gain_rows(head_weight, lay), lay)
    own = packed[:, LANES:].astype(F32)
    kp_part = gain * (low[:, LANES : 2 * LANES] - low[:, 2 * LANES :] * own)
    tile1 = jnp.where(in_segments(small, lay, 0, lay.kp), kp_part, high[:, LANES : 2 * LANES])
    turn = jnp.transpose(frames[...])
    x, y, z = unpack(tile1, seg)
    local = []
    for d in range(3):
        r = [turn[:, 3 * c + d : 3 * c + d + 1] for c in range(3)]
        local.append(r[0] * x + r[1] * y + r[2] * z)
    tile1 = pack(*local, seg, 0, seg)
    rows = jnp.concatenate([tile0, tile1], axis=1).astype(B16)
    result[...] = nn(rows, weights[...])


VMEM = pl.BlockSpec(memory_space=pltpu.VMEM)
SMEM = pl.BlockSpec(memory_space=pltpu.SMEM)


def call(body, outs, args, scalars=(), scratch=(), flops=1000000):
    size = sum(math.prod(v.shape) * v.dtype.itemsize for v in list(args) + list(outs))
    return pl.pallas_call(
        body,
        out_shape=tuple(outs),
        in_specs=[SMEM] * len(scalars) + [VMEM] * len(args),
        out_specs=tuple([VMEM] * len(outs)),
        scratch_shapes=list(scratch),
        compiler_params=pltpu.CompilerParams(vmem_limit_bytes=(16 << 20) + 6 * size),
        cost_estimate=pl.CostEstimate(flops=flops, bytes_accessed=size, transcendentals=0),
    )(*scalars, *args)


def shape_of(*dims, dtype=F32):
    return jax.ShapeDtypeStruct(dims, dtype)


def shards(
    query_single, key_single, pair, query_frames, key_frames, w_query, w_key, w_value, w_query_points, w_key_points,
    w_value_points, head_weight, bias_weight, w_out, d_out,
):
    lay = Layout(head_weight.shape[0])
    count = lax.axis_size("row")
    block, width = key_single.shape
    total = count * block
    near = 1
    while 4 * near * near <= count:
        near *= 2
    far = count // near
    order = [(place % far) * near + place // far for place in range(count)]
    lines = [[z * near + y for z in range(far)] for y in range(near)]
    planes = [[z * near + y for y in range(near)] for z in range(far)]

    packed, weights = call(
        functools.partial(key_kernel, lay),
        [shape_of(block, 2 * LANES, dtype=B16), shape_of(2 * LANES, width, dtype=B16)],
        [key_single, key_frames, w_key.T, w_value.T, w_key_points.T, w_value_points.T],
    )
    line = lax.all_gather(packed, "row", axis_index_groups=lines)
    gathered = lax.all_gather(line, "row", axis_index_groups=planes)
    left, base, d_base, d_row, w_out_rows, w_query_rows = call(
        functools.partial(early_kernel, lay, block, order),
        [
            shape_of(ROWS16, 2 * LANES), shape_of(SUBLANES, total), shape_of(SUBLANES, total),
            shape_of(SUBLANES, 2 * LANES), shape_of(2 * LANES, width, dtype=B16),
            shape_of(2 * LANES, width, dtype=B16),
        ],
        [query_single, w_query.T, w_query_points.T, bias_weight, w_out, d_out, pair],
        [head_weight, query_frames.T],
        [pltpu.VMEM((ROWS16, LANES), F32)],
    )
    message, features, pair_sum, scores = call(
        functools.partial(attention_kernel, lay, block, order),
        [
            shape_of(count, SUBLANES, LANES, dtype=B16), shape_of(SUBLANES, 2 * LANES), shape_of(SUBLANES, LANES),
            shape_of(SUBLANES, total),
        ],
        [gathered, pair, left, base, d_base, d_row],
        [head_weight, query_frames.T],
    )
    arrived = lax.all_to_all(message, "row", 0, 0, tiled=True)
    (sums,) = call(
        functools.partial(rows_kernel, lay),
        [shape_of(SUBLANES, 2 * width)],
        [gathered, left, scores, features, pair_sum, w_out, w_out_rows, w_query_rows],
        [head_weight, query_frames.T],
    )
    swap = [(i, (i + 1) % 2) for i in range(2)]
    sums = sums[:1]
    sums = sums + lax.ppermute(sums, "head", swap)
    output = sums[:, :width].astype(B16)
    grad_query = sums[:, width:]
    (part,) = call(
        functools.partial(owner_kernel, lay),
        [shape_of(block, width)],
        [arrived, key_frames, packed, weights],
        [head_weight],
    )
    grad_keys = part + lax.ppermute(part, "head", swap)
    return (output, grad_query, grad_keys)


def solution(mesh):
    return jax.shard_map(
        shards,
        mesh=mesh,
        in_specs=(
            P("row", None),
            P("row", None),
            P("row", None, None),
            P(None, "row"),
            P(None, "row"),
            P(None, "head"),
            P(None, "head"),
            P(None, "head"),
            P(None, "head"),
            P(None, "head"),
            P(None, "head"),
            P("head"),
            P("head", None),
            P("head", None),
            P("row", None),
        ),
        out_specs=(P("row", None), P("row", None), P("row", None)),
        check_vma=False,
    )
```

```python
import functools
import math

import jax
import jax.numpy as jnp
from jax import lax
from jax.experimental import pallas as pl
from jax.experimental.pallas import tpu as pltpu
from jax.sharding import PartitionSpec as P

C = 16
PQ = 4
PV = 8
LANES = 128
SUBLANES = 8
ROWS16 = 16
LOGIT_SCALE = math.sqrt(1.0 / 3.0)
POINT_SCALE = math.sqrt(2.0 / (9.0 * PQ))
F32 = jnp.float32
B16 = jnp.bfloat16


class Layout:
    def __init__(self, heads):
        self.heads = heads
        self.keys = heads * C
        self.square = 2 * heads * C
        self.kp = heads * PQ
        self.seg = heads * (PQ + PV)
        assert self.square + 3 * heads <= LANES and 3 * self.seg <= LANES and heads + 2 <= SUBLANES


def nn(a, b, precision=None):
    return lax.dot_general(a, b, (((1,), (0,)), ((), ())), precision=precision, preferred_element_type=F32)


def nt(a, b):
    return lax.dot_general(a, b, (((1,), (1,)), ((), ())), preferred_element_type=F32)


def iota(shape, dim):
    return lax.broadcasted_iota(jnp.int32, shape, dim)


def pick(condition):
    return jnp.where(condition, 1.0, 0.0).astype(B16)


def to_lane(rows, offset):
    j, i = iota((LANES, rows), 0), iota((LANES, rows), 1)
    return pick(j == i + offset)


def to_components(rows, offset, points, seg):
    j, i = iota((LANES, rows), 0), iota((LANES, rows), 1)
    found = j < 0
    for c in range(3):
        m = j - (c * seg + offset)
        found = found | ((m >= 0) & (m < points) & (i == 3 * m + c))
    return pick(found)


def unpack(tile, seg):
    return tile, pltpu.roll(tile, LANES - seg, 1), pltpu.roll(tile, LANES - 2 * seg, 1)


def pack(x, y, z, seg, low, high):
    lane = iota(x.shape, 1)
    keep = (lane >= low) & (lane < high)
    x, y, z = (jnp.where(keep, v, 0.0) for v in (x, y, z))
    return x + pltpu.roll(y, seg, 1) + pltpu.roll(z, 2 * seg, 1)


def head_of(shape, lay):
    lane = iota(shape, 1)
    zero = jnp.full(shape, -1, jnp.int32)
    one = jnp.full(shape, -1, jnp.int32)
    for h in range(lay.heads):
        for base in (0, lay.keys):
            zero = jnp.where((lane >= base + h * C) & (lane < base + (h + 1) * C), h, zero)
        for c in range(3):
            k = c * lay.seg + h * PQ
            v = c * lay.seg + lay.kp + h * PV
            one = jnp.where((lane >= k) & (lane < k + PQ), h, one)
            one = jnp.where((lane >= v) & (lane < v + PV), h, one)
    return zero, one


def in_segments(shape, lay, low, high):
    lane = iota(shape, 1)
    found = lane < 0
    for c in range(3):
        found = found | ((lane >= c * lay.seg + low) & (lane < c * lay.seg + high))
    return found


def key_kernel(lay, key_single, frames, w_key, w_value, w_kp, w_vp, packed, weights, turned):
    seg = lay.seg
    zero = nn(to_lane(lay.keys, 0), w_key[...]) + nn(to_lane(lay.keys, lay.keys), w_value[...])
    one = nn(to_components(3 * lay.kp, 0, lay.kp, seg), w_kp[...]) + nn(
        to_components(3 * (seg - lay.kp), lay.kp, seg - lay.kp, seg), w_vp[...]
    )
    w_all = jnp.concatenate([zero, one], axis=0).astype(B16)
    weights[...] = w_all
    rows = nt(key_single[...], w_all)
    turn = jnp.transpose(frames[...])
    turned[:, : turn.shape[1]] = turn
    x, y, z = unpack(rows[:, LANES:], seg)
    out = []
    for c in range(3):
        r = [turn[:, 3 * c + d : 3 * c + d + 1] for d in range(3)]
        out.append((r[0] * x + r[1] * y + r[2] * z + turn[:, 9 + c : 10 + c]).astype(B16).astype(F32))
    points = pack(*out, seg, 0, seg)
    square = out[0] * out[0] + out[1] * out[1] + out[2] * out[2]
    square = jnp.where(iota(square.shape, 1) < lay.kp, square, 0.0)
    i, j = iota((LANES, LANES), 0), iota((LANES, LANES), 1)
    chosen = j < 0
    for h in range(lay.heads):
        for piece in range(3):
            lane = lay.square + piece * lay.heads + h
            chosen = chosen | ((j == lane) & (i >= h * PQ) & (i < (h + 1) * PQ))
    total = nn(square, jnp.where(chosen, 1.0, 0.0), lax.Precision.HIGHEST)
    first = total.astype(B16).astype(F32)
    second = (total - first).astype(B16).astype(F32)
    third = total - first - second
    lane = iota(total.shape, 1)
    piece = jnp.where(
        lane < lay.square + lay.heads, first, jnp.where(lane < lay.square + 2 * lay.heads, second, third)
    )
    tile0 = jnp.where(lane < lay.square, rows[:, :LANES], piece).astype(B16)
    tile1 = points.astype(B16)
    packed[:, :LANES] = tile0
    packed[:, LANES:] = tile1


def gain_rows(head_weight, lay):
    row = iota((SUBLANES, LANES), 0)
    raw = jnp.zeros((SUBLANES, LANES), F32)
    for h in range(lay.heads):
        raw = jnp.where(row == h, jnp.broadcast_to(head_weight[:, h : h + 1], raw.shape), raw)
    gain = (jnp.maximum(raw, 0.0) + jnp.log1p(jnp.exp(-jnp.abs(raw)))) * POINT_SCALE
    return jnp.where(row < lay.heads, gain, 0.0)


def gain_lanes(gain, lay):
    _, one = head_of(gain.shape, lay)
    return jnp.sum(jnp.where(one == iota(gain.shape, 0), gain, 0.0), axis=0, keepdims=True)


def early_kernel(
    lay, block, order, head_weight, frames, query_single, w_query, w_qp, bias_weight, w_out, d_out, pair,
    left, base, d_base, d_row, w_out_rows, w_query_rows, gains, table, pair_rows, scratch,
):
    me = lax.axis_index("row")
    for place, offset in enumerate(order):
        j = pl.multiple_of((me ^ offset) * block, block)
        pair_rows[place * block : (place + 1) * block, :] = pair[0, pl.ds(j, block), :]
    turn = [jnp.broadcast_to(frames[:, i : i + 1], (1, LANES)) for i in range(12)]
    for i in range(12):
        table[i : i + 1, :] = turn[i]
    heads, seg = lay.heads, lay.seg
    width = C + 4 * PV + LANES
    shape = (SUBLANES, LANES)
    row, lane = iota(shape, 0), iota(shape, 1)
    zero_head, one_head = head_of(shape, lay)
    zero = nn(to_lane(lay.keys, 0), w_query[...])
    one = nn(to_components(3 * lay.kp, 0, lay.kp, seg), w_qp[...])
    w_q = jnp.concatenate([zero, one], axis=0).astype(B16)
    w_query_rows[...] = w_q
    near = C + 4 * PV
    w_o = jnp.zeros((2 * LANES, w_out.shape[1]), F32)
    for h in range(heads):
        i, j = iota((2 * LANES, near), 0), iota((2 * LANES, near), 1)
        m = i - (lay.keys + h * C)
        found = (m >= 0) & (m < C) & (j == m)
        m = i - h * PV
        found = found | ((m >= 0) & (m < PV) & (j == C + 3 * PV + m))
        for c in range(3):
            m = i - (LANES + c * seg + lay.kp + h * PV)
            found = found | ((m >= 0) & (m < PV) & (j == C + 3 * m + c))
        w_o = w_o + nn(pick(found), w_out[h * width : h * width + near, :])
    w_o = w_o.astype(B16)
    w_out_rows[: 2 * LANES, :] = w_o
    for h in range(heads):
        w_out_rows[(2 + h) * LANES : (3 + h) * LANES, :] = w_out[h * width + near : (h + 1) * width, :]
    single = jnp.broadcast_to(query_single[...], (SUBLANES, query_single.shape[1]))
    rows = nt(single, w_q)
    x, y, z = unpack(rows[:, LANES:], seg)
    out = []
    for c in range(3):
        value = turn[3 * c] * x + turn[3 * c + 1] * y + turn[3 * c + 2] * z + turn[9 + c]
        out.append(value.astype(B16).astype(F32))
    points = pack(*out, seg, 0, lay.kp)
    query = rows[:, :LANES].astype(B16).astype(F32)
    is_key = lane < lay.keys
    left[:SUBLANES, :LANES] = jnp.where(is_key & (zero_head == row), query, 0.0)
    left[:SUBLANES, LANES:] = jnp.zeros(shape, F32)
    minus = lane < 0
    for piece in range(3):
        minus = minus | (lane == lay.square + piece * heads + row)
    left[SUBLANES:, :LANES] = jnp.where(minus & (row < heads), -0.5, 0.0)
    mine = jnp.where(one_head == row, points, 0.0)
    left[SUBLANES:, LANES:] = mine
    gain = gain_rows(head_weight, lay)
    gains[...] = gain
    cotangent = jnp.broadcast_to(d_out[...], (SUBLANES, d_out.shape[1]))
    d_row[...] = nt(cotangent, w_o)
    scratch[...] = jnp.zeros_like(scratch)
    scratch[:heads, :] = bias_weight[...].astype(F32)
    for h in range(heads):
        d_pair = nt(cotangent, w_out[h * width + near : (h + 1) * width, :])
        scratch[SUBLANES + h : SUBLANES + h + 1, :] = d_pair[:1, :]
    both = nt(scratch[...].astype(B16), pair_rows[...])
    square = jnp.sum(mine * mine, axis=1, keepdims=True)
    base[...] = both[:SUBLANES] - 0.5 * gain[:, :1] * square
    d_base[...] = both[SUBLANES:]


def attention_kernel(
    lay, block, order, *refs
):
    *parts, pair, left, base, d_base, d_row, gains, table, message, features, pair_sum, scores = refs
    frames = [table[i : i + 1, :] for i in range(12)]
    me = lax.axis_index("row")
    heads, seg = lay.heads, lay.seg
    shape = (SUBLANES, LANES)
    row, lane = iota(shape, 0), iota(shape, 1)
    zero_head, one_head = head_of(shape, lay)
    gain = gains[...]
    keys = jnp.concatenate([part[...].reshape(-1, 2 * LANES) for part in parts], axis=0)
    first = nt(left[...].astype(B16), keys)
    logits = LOGIT_SCALE * (first[:SUBLANES] * (1.0 / math.sqrt(C)) + base[...] + gain[:, :1] * first[SUBLANES:])
    weight = jnp.exp(logits - jnp.max(logits, axis=1, keepdims=True))
    attention = weight / jnp.sum(weight, axis=1, keepdims=True)
    attention = jnp.where(iota(attention.shape, 0) < heads, attention, 0.0)
    attention_b = attention.astype(B16)
    sums = nn(attention_b, keys)
    pair_sum[...] = nn(attention_b, pair[...])
    attended = jnp.sum(jnp.where(zero_head == row, sums[:, :LANES], 0.0), axis=0, keepdims=True)
    points = jnp.sum(jnp.where(one_head == row, sums[:, LANES:], 0.0), axis=0, keepdims=True)
    attended = jnp.broadcast_to(attended, shape)
    points = jnp.broadcast_to(points, shape)
    moved = [v - frames[9 + c] for c, v in enumerate(unpack(points, seg))]
    local = [
        frames[d] * moved[0] + frames[3 + d] * moved[1] + frames[6 + d] * moved[2] for d in range(3)
    ]
    lengths = jnp.sqrt(1.0 + (local[0] * local[0] + local[1] * local[1] + local[2] * local[2]))
    value_points = heads * PV
    is_value = (lane >= lay.keys) & (lane < lay.square)
    features[:, :LANES] = jnp.where(
        is_value, attended, jnp.where(lane < value_points, pltpu.roll(lengths, LANES - lay.kp, 1), 0.0)
    )
    features[:, LANES:] = pack(*local, seg, lay.kp, seg)
    d_zero = d_row[:, :LANES]
    share = pltpu.roll(d_zero, lay.kp, 1) / lengths
    d_local = [v + share * u for v, u in zip(unpack(d_row[:, LANES:], seg), local)]
    d_points = [
        frames[3 * c] * d_local[0] + frames[3 * c + 1] * d_local[1] + frames[3 * c + 2] * d_local[2]
        for c in range(3)
    ]
    d_points = pack(*d_points, seg, lay.kp, seg)
    d_attended = jnp.where(is_value, d_zero, 0.0)
    right = jnp.concatenate(
        [jnp.where(zero_head == row, d_attended, 0.0), jnp.where(one_head == row, d_points, 0.0)], axis=1
    )
    d_attention = nt(right.astype(B16), keys) + d_base[...]
    total = jnp.sum(attention * d_attention, axis=1, keepdims=True)
    score_b = (LOGIT_SCALE * attention * (d_attention - total)).astype(B16)
    scores[...] = score_b.astype(F32)
    query0 = jnp.sum(left[:SUBLANES, :LANES], axis=0, keepdims=True)
    query1 = jnp.sum(left[SUBLANES:, LANES:], axis=0, keepdims=True)
    side = jnp.where(row == heads, jnp.broadcast_to(query0, shape) + d_attended, 0.0)
    side = side + jnp.where(row == heads + 1, jnp.broadcast_to(query1, shape) + d_points, 0.0)
    high = attention_b.astype(F32)
    low = score_b.astype(F32)
    half = lane < block
    for place, j in enumerate(order):
        at = place * block // LANES * LANES
        a, s = high[:, at : at + LANES], low[:, at : at + LANES]
        if place * block % LANES:
            a = pltpu.roll(a, LANES - block, 1)
        else:
            s = pltpu.roll(s, block, 1)
        message[me ^ j, :, :] = jnp.where(row < heads, jnp.where(half, a, s), side).astype(B16)


def rows_kernel(
    lay, *refs
):
    *parts, left, scores, features, pair_sum, w_out_rows, w_query_rows, gains, table, sums = refs
    frames = [table[i : i + 1, :] for i in range(12)]
    heads, seg = lay.heads, lay.seg
    shape = (SUBLANES, LANES)
    row, lane = iota(shape, 0), iota(shape, 1)
    zero_head, one_head = head_of(shape, lay)
    keys = jnp.concatenate([part[...].reshape(-1, 2 * LANES) for part in parts], axis=0)
    pairs = [jnp.broadcast_to(pair_sum[h : h + 1, :], shape) for h in range(heads)]
    result = nn(jnp.concatenate([features[...]] + pairs, axis=1).astype(B16), w_out_rows[...])
    gain = gains[...]
    score = scores[...]
    d_rows = nn(score.astype(B16), keys)
    d_query = jnp.sum(
        jnp.where((lane < lay.keys) & (zero_head == row), d_rows[:, :LANES], 0.0), axis=0, keepdims=True
    ) * (1.0 / math.sqrt(C))
    score_sum = jnp.sum(score, axis=1, keepdims=True)
    d_points = gain * (d_rows[:, LANES:] - score_sum * left[SUBLANES:, LANES:])
    d_points = jnp.sum(jnp.where(one_head == row, d_points, 0.0), axis=0, keepdims=True)
    x, y, z = unpack(jnp.broadcast_to(d_points, shape), seg)
    local = [frames[d] * x + frames[3 + d] * y + frames[6 + d] * z for d in range(3)]
    local = pack(*local, seg, 0, lay.kp)
    both = jnp.concatenate([jnp.broadcast_to(d_query, shape), local], axis=1).astype(B16)
    grad = nn(both, w_query_rows[...])
    sums[...] = jnp.concatenate([result, grad], axis=1)


def owner_kernel(lay, arrived, turned, packed, weights, gains, result):
    heads, seg = lay.heads, lay.seg
    count = arrived.shape[0]
    block = packed.shape[0]
    took = arrived[...].astype(F32)
    shape = (SUBLANES, LANES)
    row = iota(shape, 0)
    zero_head, one_head = head_of(shape, lay)
    keep0 = (zero_head == row)[None]
    keep1 = (one_head == row)[None]
    whole = (count, SUBLANES, LANES)
    side0 = jnp.where(keep0, jnp.broadcast_to(took[:, heads : heads + 1, :], whole), 0.0)
    side1 = jnp.where(keep1, jnp.broadcast_to(took[:, heads + 1 : heads + 2, :], whole), 0.0)
    ones = jnp.where(jnp.broadcast_to(keep1, whole), 1.0, 0.0)
    right = jnp.concatenate([side0, side1, ones], axis=2).reshape(count * SUBLANES, 3 * LANES).astype(B16)
    moved = jnp.transpose(took.reshape(count * SUBLANES, LANES)).astype(B16)
    both = nn(moved, right)
    high, low = both[:block], both[block:]
    small = (block, LANES)
    lane = iota(small, 1)
    tile0 = jnp.where(lane < lay.keys, low[:, :LANES] * (1.0 / math.sqrt(C)), high[:, :LANES])
    gain = gain_lanes(gains[...], lay)
    own = packed[:, LANES:].astype(F32)
    kp_part = gain * (low[:, LANES : 2 * LANES] - low[:, 2 * LANES :] * own)
    tile1 = jnp.where(in_segments(small, lay, 0, lay.kp), kp_part, high[:, LANES : 2 * LANES])
    turn = turned[...]
    x, y, z = unpack(tile1, seg)
    local = []
    for d in range(3):
        r = [turn[:, 3 * c + d : 3 * c + d + 1] for c in range(3)]
        local.append(r[0] * x + r[1] * y + r[2] * z)
    tile1 = pack(*local, seg, 0, seg)
    rows = jnp.concatenate([tile0, tile1], axis=1).astype(B16)
    result[...] = nn(rows, weights[...])


VMEM = pl.BlockSpec(memory_space=pltpu.VMEM)
HBM = pl.BlockSpec(memory_space=pltpu.HBM)


def call(body, outs, args, fresh=0, scratch=(), flops=1000000):
    size = sum(math.prod(v.shape) * v.dtype.itemsize for v in list(args) + list(outs))

    def kernel(*refs):
        if fresh:
            *refs, sems = refs
            held = refs[len(refs) - fresh :]
            copies = [pltpu.make_async_copy(refs[i], held[i], sems.at[i]) for i in range(fresh)]
            for copy in copies:
                copy.start()
            for copy in copies:
                copy.wait()
            refs = list(held) + list(refs[fresh : len(refs) - fresh])
        body(*refs)

    own = [pltpu.VMEM(v.shape, v.dtype) for v in args[:fresh]]
    return pl.pallas_call(
        kernel,
        out_shape=tuple(outs),
        in_specs=[HBM] * fresh + [VMEM] * (len(args) - fresh),
        out_specs=tuple([VMEM] * len(outs)),
        scratch_shapes=list(scratch) + own + ([pltpu.SemaphoreType.DMA((fresh,))] if fresh else []),
        compiler_params=pltpu.CompilerParams(vmem_limit_bytes=(16 << 20) + 6 * size),
        cost_estimate=pl.CostEstimate(flops=flops, bytes_accessed=size, transcendentals=0),
    )(*[pltpu.with_memory_space_constraint(v, pltpu.HBM) for v in args[:fresh]], *args[fresh:])


def shape_of(*dims, dtype=F32):
    return jax.ShapeDtypeStruct(dims, dtype)


def shards(
    query_single, key_single, pair, query_frames, key_frames, w_query, w_key, w_value, w_query_points, w_key_points,
    w_value_points, head_weight, bias_weight, w_out, d_out,
):
    lay = Layout(head_weight.shape[0])
    count = lax.axis_size("row")
    block, width = key_single.shape
    total = count * block
    near = 1
    while 4 * near * near <= count:
        near *= 2
    assert count & (count - 1) == 0

    def exchange(value, mask):
        return lax.ppermute(value, "row", [(i, i ^ mask) for i in range(count)])

    packed, weights, turned = call(
        functools.partial(key_kernel, lay),
        [shape_of(block, 2 * LANES, dtype=B16), shape_of(2 * LANES, width, dtype=B16), shape_of(block, LANES)],
        [key_single, key_frames, w_key.T, w_value.T, w_key_points.T, w_value_points.T],
        6,
    )
    line, offsets, mask = packed, [0], count // 2
    while mask >= near:
        line = jnp.concatenate([line, exchange(line, mask)], axis=0)
        offsets = offsets + [o ^ mask for o in offsets]
        mask //= 2
    parts = [line] + [exchange(line, m) for m in range(1, near)]
    order = [m ^ o for m in range(near) for o in offsets]

    left, base, d_base, d_row, w_out_rows, w_query_rows, gains, table, pair_rows = call(
        functools.partial(early_kernel, lay, block, order),
        [
            shape_of(ROWS16, 2 * LANES), shape_of(SUBLANES, total), shape_of(SUBLANES, total),
            shape_of(SUBLANES, 2 * LANES), shape_of((2 + lay.heads) * LANES, width, dtype=B16),
            shape_of(2 * LANES, width, dtype=B16), shape_of(SUBLANES, LANES), shape_of(ROWS16, LANES),
            shape_of(total, LANES, dtype=B16),
        ],
        [
            head_weight.reshape(1, -1), query_frames.T, query_single, w_query.T, w_query_points.T, bias_weight, w_out,
            d_out, pair,
        ],
        9,
        [pltpu.VMEM((ROWS16, LANES), F32)],
    )
    message, features, pair_sum, scores = call(
        functools.partial(attention_kernel, lay, block, order),
        [
            shape_of(count, SUBLANES, LANES, dtype=B16), shape_of(SUBLANES, 2 * LANES), shape_of(SUBLANES, LANES),
            shape_of(SUBLANES, total),
        ],
        parts + [pair_rows, left, base, d_base, d_row, gains, table],
    )
    arrived = lax.all_to_all(message, "row", 0, 0, tiled=True)
    (sums,) = call(
        functools.partial(rows_kernel, lay),
        [shape_of(SUBLANES, 2 * width)],
        parts + [left, scores, features, pair_sum, w_out_rows, w_query_rows, gains, table],
    )
    swap = [(i, (i + 1) % 2) for i in range(2)]
    sums = sums[:1]
    sums = sums + lax.ppermute(sums, "head", swap)
    output = sums[:, :width].astype(B16)
    grad_query = sums[:, width:]
    (part,) = call(
        functools.partial(owner_kernel, lay),
        [shape_of(block, width)],
        [arrived, turned, packed, weights, gains],
    )
    grad_keys = part + lax.ppermute(part, "head", swap)
    return (output, grad_query, grad_keys)


def solution(mesh):
    return jax.shard_map(
        shards,
        mesh=mesh,
        in_specs=(
            P("row", None),
            P("row", None),
            P("row", None, None),
            P(None, "row"),
            P(None, "row"),
            P(None, "head"),
            P(None, "head"),
            P(None, "head"),
            P(None, "head"),
            P(None, "head"),
            P(None, "head"),
            P("head"),
            P("head", None),
            P("head", None),
            P("row", None),
        ),
        out_specs=(P("row", None), P("row", None), P("row", None)),
        check_vma=False,
    )
```

```python
import functools
import math

import jax
import jax.numpy as jnp
from jax import lax
from jax.experimental import pallas as pl
from jax.experimental.pallas import tpu as pltpu
from jax.sharding import PartitionSpec as P

C = 16
PQ = 4
PV = 8
LANES = 128
SUBLANES = 8
ROWS16 = 16
LOGIT_SCALE = math.sqrt(1.0 / 3.0)
POINT_SCALE = math.sqrt(2.0 / (9.0 * PQ))
F32 = jnp.float32
B16 = jnp.bfloat16


class Layout:
    def __init__(self, heads):
        self.heads = heads
        self.keys = heads * C
        self.square = 2 * heads * C
        self.kp = heads * PQ
        self.seg = heads * (PQ + PV)
        assert self.square + 3 * heads <= LANES and 3 * self.seg <= LANES and 2 * heads + 2 <= SUBLANES


def nn(a, b, precision=None):
    return lax.dot_general(a, b, (((1,), (0,)), ((), ())), precision=precision, preferred_element_type=F32)


def nt(a, b):
    return lax.dot_general(a, b, (((1,), (1,)), ((), ())), preferred_element_type=F32)


def iota(shape, dim):
    return lax.broadcasted_iota(jnp.int32, shape, dim)


def pick(condition):
    return jnp.where(condition, 1.0, 0.0).astype(B16)


def to_lane(rows, offset):
    j, i = iota((LANES, rows), 0), iota((LANES, rows), 1)
    return pick(j == i + offset)


def to_components(rows, offset, points, seg):
    j, i = iota((LANES, rows), 0), iota((LANES, rows), 1)
    found = j < 0
    for c in range(3):
        m = j - (c * seg + offset)
        found = found | ((m >= 0) & (m < points) & (i == 3 * m + c))
    return pick(found)


def unpack(tile, seg):
    return tile, pltpu.roll(tile, LANES - seg, 1), pltpu.roll(tile, LANES - 2 * seg, 1)


def pack(x, y, z, seg, low, high):
    lane = iota(x.shape, 1)
    keep = (lane >= low) & (lane < high)
    x, y, z = (jnp.where(keep, v, 0.0) for v in (x, y, z))
    return x + pltpu.roll(y, seg, 1) + pltpu.roll(z, 2 * seg, 1)


def head_of(shape, lay):
    lane = iota(shape, 1)
    zero = jnp.full(shape, -1, jnp.int32)
    one = jnp.full(shape, -1, jnp.int32)
    for h in range(lay.heads):
        for base in (0, lay.keys):
            zero = jnp.where((lane >= base + h * C) & (lane < base + (h + 1) * C), h, zero)
        for c in range(3):
            k = c * lay.seg + h * PQ
            v = c * lay.seg + lay.kp + h * PV
            one = jnp.where((lane >= k) & (lane < k + PQ), h, one)
            one = jnp.where((lane >= v) & (lane < v + PV), h, one)
    return zero, one


def in_segments(shape, lay, low, high):
    lane = iota(shape, 1)
    found = lane < 0
    for c in range(3):
        found = found | ((lane >= c * lay.seg + low) & (lane < c * lay.seg + high))
    return found


def key_kernel(lay, key_single, frames, w_key, w_value, w_kp, w_vp, packed, weights, turned):
    seg = lay.seg
    zero = nn(to_lane(lay.keys, 0), w_key[...]) + nn(to_lane(lay.keys, lay.keys), w_value[...])
    one = nn(to_components(3 * lay.kp, 0, lay.kp, seg), w_kp[...]) + nn(
        to_components(3 * (seg - lay.kp), lay.kp, seg - lay.kp, seg), w_vp[...]
    )
    w_all = jnp.concatenate([zero, one], axis=0).astype(B16)
    weights[...] = w_all
    rows = nt(key_single[...], w_all)
    turn = jnp.transpose(frames[...])
    turned[:, : turn.shape[1]] = turn
    x, y, z = unpack(rows[:, LANES:], seg)
    out = []
    for c in range(3):
        r = [turn[:, 3 * c + d : 3 * c + d + 1] for d in range(3)]
        out.append((r[0] * x + r[1] * y + r[2] * z + turn[:, 9 + c : 10 + c]).astype(B16).astype(F32))
    points = pack(*out, seg, 0, seg)
    square = out[0] * out[0] + out[1] * out[1] + out[2] * out[2]
    square = jnp.where(iota(square.shape, 1) < lay.kp, square, 0.0)
    i, j = iota((LANES, LANES), 0), iota((LANES, LANES), 1)
    chosen = j < 0
    for h in range(lay.heads):
        for piece in range(3):
            lane = lay.square + piece * lay.heads + h
            chosen = chosen | ((j == lane) & (i >= h * PQ) & (i < (h + 1) * PQ))
    total = nn(square, jnp.where(chosen, 1.0, 0.0), lax.Precision.HIGHEST)
    first = total.astype(B16).astype(F32)
    second = (total - first).astype(B16).astype(F32)
    third = total - first - second
    lane = iota(total.shape, 1)
    piece = jnp.where(
        lane < lay.square + lay.heads, first, jnp.where(lane < lay.square + 2 * lay.heads, second, third)
    )
    tile0 = jnp.where(lane < lay.square, rows[:, :LANES], piece).astype(B16)
    tile1 = points.astype(B16)
    packed[:, :LANES] = tile0
    packed[:, LANES:] = tile1


def gain_rows(head_weight, lay):
    row = iota((SUBLANES, LANES), 0)
    raw = jnp.zeros((SUBLANES, LANES), F32)
    for h in range(lay.heads):
        raw = jnp.where(row == h, jnp.broadcast_to(head_weight[:, h : h + 1], raw.shape), raw)
    gain = (jnp.maximum(raw, 0.0) + jnp.log1p(jnp.exp(-jnp.abs(raw)))) * POINT_SCALE
    return jnp.where(row < lay.heads, gain, 0.0)


def gain_lanes(gain, lay):
    _, one = head_of(gain.shape, lay)
    return jnp.sum(jnp.where(one == iota(gain.shape, 0), gain, 0.0), axis=0, keepdims=True)


def early_kernel(
    lay, block, order, head_weight, frames, query_single, w_query, w_qp, bias_weight, w_out, d_out, pair,
    left, base, d_base, d_row, w_out_rows, w_query_rows, gains, table, pair_rows, scratch,
):
    me = lax.axis_index("row")
    for place, offset in enumerate(order):
        j = pl.multiple_of((me ^ offset) * block, block)
        pair_rows[place * block : (place + 1) * block, :] = pair[0, pl.ds(j, block), :]
    turn = [jnp.broadcast_to(frames[:, i : i + 1], (1, LANES)) for i in range(12)]
    for i in range(12):
        table[i : i + 1, :] = turn[i]
    heads, seg = lay.heads, lay.seg
    width = C + 4 * PV + LANES
    shape = (SUBLANES, LANES)
    row, lane = iota(shape, 0), iota(shape, 1)
    zero_head, one_head = head_of(shape, lay)
    zero = nn(to_lane(lay.keys, 0), w_query[...])
    one = nn(to_components(3 * lay.kp, 0, lay.kp, seg), w_qp[...])
    w_q = jnp.concatenate([zero, one], axis=0).astype(B16)
    w_query_rows[...] = w_q
    near = C + 4 * PV
    w_o = jnp.zeros((2 * LANES, w_out.shape[1]), F32)
    for h in range(heads):
        i, j = iota((2 * LANES, near), 0), iota((2 * LANES, near), 1)
        m = i - (lay.keys + h * C)
        found = (m >= 0) & (m < C) & (j == m)
        m = i - h * PV
        found = found | ((m >= 0) & (m < PV) & (j == C + 3 * PV + m))
        for c in range(3):
            m = i - (LANES + c * seg + lay.kp + h * PV)
            found = found | ((m >= 0) & (m < PV) & (j == C + 3 * m + c))
        w_o = w_o + nn(pick(found), w_out[h * width : h * width + near, :])
    w_o = w_o.astype(B16)
    w_out_rows[: 2 * LANES, :] = w_o
    for h in range(heads):
        w_out_rows[(2 + h) * LANES : (3 + h) * LANES, :] = w_out[h * width + near : (h + 1) * width, :]
    single = jnp.broadcast_to(query_single[...], (SUBLANES, query_single.shape[1]))
    rows = nt(single, w_q)
    x, y, z = unpack(rows[:, LANES:], seg)
    out = []
    for c in range(3):
        value = turn[3 * c] * x + turn[3 * c + 1] * y + turn[3 * c + 2] * z + turn[9 + c]
        out.append(value.astype(B16).astype(F32))
    points = pack(*out, seg, 0, lay.kp)
    query = rows[:, :LANES].astype(B16).astype(F32)
    is_key = lane < lay.keys
    left[:SUBLANES, :LANES] = jnp.where(is_key & (zero_head == row), query, 0.0)
    left[:SUBLANES, LANES:] = jnp.zeros(shape, F32)
    minus = lane < 0
    for piece in range(3):
        minus = minus | (lane == lay.square + piece * heads + row)
    left[SUBLANES:, :LANES] = jnp.where(minus & (row < heads), -0.5, 0.0)
    mine = jnp.where(one_head == row, points, 0.0)
    left[SUBLANES:, LANES:] = mine
    gain = gain_rows(head_weight, lay)
    gains[...] = gain
    cotangent = jnp.broadcast_to(d_out[...], (SUBLANES, d_out.shape[1]))
    d_row[...] = nt(cotangent, w_o)
    scratch[...] = jnp.zeros_like(scratch)
    scratch[:heads, :] = bias_weight[...].astype(F32)
    for h in range(heads):
        d_pair = nt(cotangent, w_out[h * width + near : (h + 1) * width, :])
        scratch[SUBLANES + h : SUBLANES + h + 1, :] = d_pair[:1, :]
    both = nt(scratch[...].astype(B16), pair_rows[...])
    square = jnp.sum(mine * mine, axis=1, keepdims=True)
    base[...] = both[:SUBLANES] - 0.5 * gain[:, :1] * square
    d_base[...] = both[SUBLANES:]


def spread(weights, parts):
    total, at = 0.0, 0
    for part in parts:
        total = total + nn(weights[:, at : at + part.shape[0]], part[...])
        at += part.shape[0]
    return total


def attention_kernel(
    lay, block, order, *refs
):
    *parts, left, base, d_base, d_row, gains, table, message, features, weights, scores = refs
    frames = [table[i : i + 1, :] for i in range(12)]
    me = lax.axis_index("row")
    heads, seg = lay.heads, lay.seg
    shape = (SUBLANES, LANES)
    row, lane = iota(shape, 0), iota(shape, 1)
    zero_head, one_head = head_of(shape, lay)
    gain = gains[...]
    queries = left[...].astype(B16)
    first = jnp.concatenate([nt(queries, part[...]) for part in parts], axis=1)
    logits = LOGIT_SCALE * (first[:SUBLANES] * (1.0 / math.sqrt(C)) + base[...] + gain[:, :1] * first[SUBLANES:])
    weight = jnp.exp(logits - jnp.max(logits, axis=1, keepdims=True))
    attention = weight / jnp.sum(weight, axis=1, keepdims=True)
    attention = jnp.where(iota(attention.shape, 0) < heads, attention, 0.0)
    attention_b = attention.astype(B16)
    sums = spread(attention_b, parts)
    weights[...] = attention_b
    attended = jnp.sum(jnp.where(zero_head == row, sums[:, :LANES], 0.0), axis=0, keepdims=True)
    points = jnp.sum(jnp.where(one_head == row, sums[:, LANES:], 0.0), axis=0, keepdims=True)
    attended = jnp.broadcast_to(attended, shape)
    points = jnp.broadcast_to(points, shape)
    moved = [v - frames[9 + c] for c, v in enumerate(unpack(points, seg))]
    local = [
        frames[d] * moved[0] + frames[3 + d] * moved[1] + frames[6 + d] * moved[2] for d in range(3)
    ]
    lengths = jnp.sqrt(1.0 + (local[0] * local[0] + local[1] * local[1] + local[2] * local[2]))
    value_points = heads * PV
    is_value = (lane >= lay.keys) & (lane < lay.square)
    features[:, :LANES] = jnp.where(
        is_value, attended, jnp.where(lane < value_points, pltpu.roll(lengths, LANES - lay.kp, 1), 0.0)
    )
    features[:, LANES:] = pack(*local, seg, lay.kp, seg)
    d_zero = d_row[:, :LANES]
    share = pltpu.roll(d_zero, lay.kp, 1) / lengths
    d_local = [v + share * u for v, u in zip(unpack(d_row[:, LANES:], seg), local)]
    d_points = [
        frames[3 * c] * d_local[0] + frames[3 * c + 1] * d_local[1] + frames[3 * c + 2] * d_local[2]
        for c in range(3)
    ]
    d_points = pack(*d_points, seg, lay.kp, seg)
    d_attended = jnp.where(is_value, d_zero, 0.0)
    right = jnp.concatenate(
        [jnp.where(zero_head == row, d_attended, 0.0), jnp.where(one_head == row, d_points, 0.0)], axis=1
    )
    right = right.astype(B16)
    d_attention = jnp.concatenate([nt(right, part[...]) for part in parts], axis=1) + d_base[...]
    total = jnp.sum(attention * d_attention, axis=1, keepdims=True)
    score_b = (LOGIT_SCALE * attention * (d_attention - total)).astype(B16)
    scores[...] = score_b
    query0 = jnp.sum(left[:SUBLANES, :LANES], axis=0, keepdims=True)
    query1 = jnp.sum(left[SUBLANES:, LANES:], axis=0, keepdims=True)
    side = jnp.where(row == 2 * heads, jnp.broadcast_to(query0, shape) + d_attended, 0.0)
    side = side + jnp.where(row == 2 * heads + 1, jnp.broadcast_to(query1, shape) + d_points, 0.0)
    both = attention_b.astype(F32) + pltpu.roll(score_b.astype(F32), heads, 0)
    for at in range(0, both.shape[1], LANES):
        tile = jnp.where(row < 2 * heads, both[:, at : at + LANES], side).astype(B16)
        for place in range(at // block, (at + LANES) // block):
            message[me ^ order[place], :, :] = tile


def rows_kernel(
    lay, *refs
):
    *parts, pair, left, scores, features, weights, w_out_rows, w_query_rows, gains, table, sums = refs
    frames = [table[i : i + 1, :] for i in range(12)]
    heads, seg = lay.heads, lay.seg
    shape = (SUBLANES, LANES)
    row, lane = iota(shape, 0), iota(shape, 1)
    zero_head, one_head = head_of(shape, lay)
    pair_sum = nn(weights[...], pair[...])
    pairs = [jnp.broadcast_to(pair_sum[h : h + 1, :], shape) for h in range(heads)]
    result = nn(jnp.concatenate([features[...]] + pairs, axis=1).astype(B16), w_out_rows[...])
    gain = gains[...]
    score = scores[...].astype(F32)
    d_rows = spread(scores[...], parts)
    d_query = jnp.sum(
        jnp.where((lane < lay.keys) & (zero_head == row), d_rows[:, :LANES], 0.0), axis=0, keepdims=True
    ) * (1.0 / math.sqrt(C))
    score_sum = jnp.sum(score, axis=1, keepdims=True)
    d_points = gain * (d_rows[:, LANES:] - score_sum * left[SUBLANES:, LANES:])
    d_points = jnp.sum(jnp.where(one_head == row, d_points, 0.0), axis=0, keepdims=True)
    x, y, z = unpack(jnp.broadcast_to(d_points, shape), seg)
    local = [frames[d] * x + frames[3 + d] * y + frames[6 + d] * z for d in range(3)]
    local = pack(*local, seg, 0, lay.kp)
    both = jnp.concatenate([jnp.broadcast_to(d_query, shape), local], axis=1).astype(B16)
    grad = nn(both, w_query_rows[...])
    sums[...] = jnp.concatenate([result, grad], axis=1)


def owner_kernel(lay, near, arrived, turned, packed, weights, gains, result):
    heads, seg = lay.heads, lay.seg
    count = arrived.shape[0]
    block = packed.shape[0]
    took = arrived[...].astype(F32)
    shape = (SUBLANES, LANES)
    whole = (count, SUBLANES, LANES)
    per = LANES // block
    place = ((iota(whole, 0) ^ lax.axis_index("row")) // near) % per
    mine = took
    for part in range(1, per):
        mine = jnp.where(place == part, pltpu.roll(took, LANES - part * block, 2), mine)
    row = iota(shape, 0)
    zero_head, one_head = head_of(shape, lay)
    lane = iota(shape, 1)
    from_score0 = lane < lay.keys
    from_score1 = in_segments(shape, lay, 0, lay.kp)
    keep0 = (zero_head >= 0) & (jnp.where(from_score0, zero_head + heads, zero_head) == row)
    keep1 = (one_head >= 0) & (jnp.where(from_score1, one_head + heads, one_head) == row)
    side0 = jnp.where(keep0[None], jnp.broadcast_to(took[:, 2 * heads : 2 * heads + 1, :], whole), 0.0)
    side1 = jnp.where(keep1[None], jnp.broadcast_to(took[:, 2 * heads + 1 : 2 * heads + 2, :], whole), 0.0)
    ones = jnp.broadcast_to(jnp.where(keep1 & from_score1, 1.0, 0.0)[None], whole)
    right = jnp.concatenate([side0, side1, ones], axis=2).reshape(count * SUBLANES, 3 * LANES).astype(B16)
    moved = jnp.transpose(mine.reshape(count * SUBLANES, LANES)).astype(B16)
    both = nn(moved, right)[:block]
    small = (block, LANES)
    lane = iota(small, 1)
    tile0 = jnp.where(lane < lay.keys, both[:, :LANES] * (1.0 / math.sqrt(C)), both[:, :LANES])
    gain = gain_lanes(gains[...], lay)
    own = packed[:, LANES:].astype(F32)
    tile1 = both[:, LANES : 2 * LANES]
    kp_part = gain * (tile1 - both[:, 2 * LANES :] * own)
    tile1 = jnp.where(in_segments(small, lay, 0, lay.kp), kp_part, tile1)
    turn = turned[...]
    x, y, z = unpack(tile1, seg)
    local = []
    for d in range(3):
        r = [turn[:, 3 * c + d : 3 * c + d + 1] for c in range(3)]
        local.append(r[0] * x + r[1] * y + r[2] * z)
    tile1 = pack(*local, seg, 0, seg)
    rows = jnp.concatenate([tile0, tile1], axis=1).astype(B16)
    result[...] = nn(rows, weights[...])


VMEM = pl.BlockSpec(memory_space=pltpu.VMEM)
HBM = pl.BlockSpec(memory_space=pltpu.HBM)


def call(body, outs, args, fresh=0, scratch=(), flops=1000000):
    size = sum(math.prod(v.shape) * v.dtype.itemsize for v in list(args) + list(outs))

    def kernel(*refs):
        if fresh:
            *refs, sems = refs
            held = refs[len(refs) - fresh :]
            copies = [pltpu.make_async_copy(refs[i], held[i], sems.at[i]) for i in range(fresh)]
            for copy in copies:
                copy.start()
            for copy in copies:
                copy.wait()
            refs = list(held) + list(refs[fresh : len(refs) - fresh])
        body(*refs)

    own = [pltpu.VMEM(v.shape, v.dtype) for v in args[:fresh]]
    return pl.pallas_call(
        kernel,
        out_shape=tuple(outs),
        in_specs=[HBM] * fresh + [VMEM] * (len(args) - fresh),
        out_specs=tuple([VMEM] * len(outs)),
        scratch_shapes=list(scratch) + own + ([pltpu.SemaphoreType.DMA((fresh,))] if fresh else []),
        compiler_params=pltpu.CompilerParams(vmem_limit_bytes=(16 << 20) + 6 * size),
        cost_estimate=pl.CostEstimate(flops=flops, bytes_accessed=size, transcendentals=0),
    )(*[pltpu.with_memory_space_constraint(v, pltpu.HBM) for v in args[:fresh]], *args[fresh:])


def shape_of(*dims, dtype=F32):
    return jax.ShapeDtypeStruct(dims, dtype)


def shards(
    query_single, key_single, pair, query_frames, key_frames, w_query, w_key, w_value, w_query_points, w_key_points,
    w_value_points, head_weight, bias_weight, w_out, d_out,
):
    lay = Layout(head_weight.shape[0])
    count = lax.axis_size("row")
    block, width = key_single.shape
    total = count * block
    near = 1
    while 4 * near * near <= count:
        near *= 2
    assert count & (count - 1) == 0

    def exchange(value, mask):
        return lax.ppermute(value, "row", [(i, i ^ mask) for i in range(count)])

    packed, weights, turned = call(
        functools.partial(key_kernel, lay),
        [shape_of(block, 2 * LANES, dtype=B16), shape_of(2 * LANES, width, dtype=B16), shape_of(block, LANES)],
        [key_single, key_frames, w_key.T, w_value.T, w_key_points.T, w_value_points.T],
        6,
    )
    offsets = list(range(0, count, near))
    line = jnp.concatenate([packed] + [exchange(packed, mask) for mask in offsets[1:]], axis=0)
    parts = [line] + [exchange(line, m) for m in range(1, near)]
    order = [m ^ o for m in range(near) for o in offsets]

    left, base, d_base, d_row, w_out_rows, w_query_rows, gains, table, pair_rows = call(
        functools.partial(early_kernel, lay, block, order),
        [
            shape_of(ROWS16, 2 * LANES), shape_of(SUBLANES, total), shape_of(SUBLANES, total),
            shape_of(SUBLANES, 2 * LANES), shape_of((2 + lay.heads) * LANES, width, dtype=B16),
            shape_of(2 * LANES, width, dtype=B16), shape_of(SUBLANES, LANES), shape_of(ROWS16, LANES),
            shape_of(total, LANES, dtype=B16),
        ],
        [
            head_weight.reshape(1, -1), query_frames.T, query_single, w_query.T, w_query_points.T, bias_weight, w_out,
            d_out, pair,
        ],
        9,
        [pltpu.VMEM((ROWS16, LANES), F32)],
    )
    message, features, weight_rows, scores = call(
        functools.partial(attention_kernel, lay, block, order),
        [
            shape_of(count, SUBLANES, LANES, dtype=B16), shape_of(SUBLANES, 2 * LANES),
            shape_of(SUBLANES, total, dtype=B16), shape_of(SUBLANES, total, dtype=B16),
        ],
        parts + [left, base, d_base, d_row, gains, table],
    )
    arrived = lax.all_to_all(message, "row", 0, 0, tiled=True)
    (sums,) = call(
        functools.partial(rows_kernel, lay),
        [shape_of(SUBLANES, 2 * width)],
        parts + [pair_rows, left, scores, features, weight_rows, w_out_rows, w_query_rows, gains, table],
    )
    swap = [(i, (i + 1) % 2) for i in range(2)]
    sums = sums[:1]
    sums = sums + lax.ppermute(sums, "head", swap)
    output = sums[:, :width].astype(B16)
    grad_query = sums[:, width:]
    (part,) = call(
        functools.partial(owner_kernel, lay, near),
        [shape_of(block, width)],
        [arrived, turned, packed, weights, gains],
    )
    grad_keys = part + lax.ppermute(part, "head", swap)
    return (output, grad_query, grad_keys)


def solution(mesh):
    return jax.shard_map(
        shards,
        mesh=mesh,
        in_specs=(
            P("row", None),
            P("row", None),
            P("row", None, None),
            P(None, "row"),
            P(None, "row"),
            P(None, "head"),
            P(None, "head"),
            P(None, "head"),
            P(None, "head"),
            P(None, "head"),
            P(None, "head"),
            P("head"),
            P("head", None),
            P("head", None),
            P("row", None),
        ),
        out_specs=(P("row", None), P("row", None), P("row", None)),
        check_vma=False,
    )
```

```python
import functools
import math

import jax
import jax.numpy as jnp
from jax import lax
from jax.experimental import pallas as pl
from jax.experimental.pallas import tpu as pltpu
from jax.sharding import PartitionSpec as P

C = 16
PQ = 4
PV = 8
LANES = 128
SUBLANES = 8
ROWS16 = 16
LOGIT_SCALE = math.sqrt(1.0 / 3.0)
POINT_SCALE = math.sqrt(2.0 / (9.0 * PQ))
F32 = jnp.float32
B16 = jnp.bfloat16


class Layout:
    def __init__(self, heads):
        self.heads = heads
        self.keys = heads * C
        self.square = 2 * heads * C
        self.kp = heads * PQ
        self.seg = heads * (PQ + PV)
        assert self.square + 3 * heads <= LANES and 3 * self.seg <= LANES and 2 * heads + 2 <= SUBLANES


def nn(a, b, precision=None):
    return lax.dot_general(a, b, (((1,), (0,)), ((), ())), precision=precision, preferred_element_type=F32)


def nt(a, b):
    return lax.dot_general(a, b, (((1,), (1,)), ((), ())), preferred_element_type=F32)


def iota(shape, dim):
    return lax.broadcasted_iota(jnp.int32, shape, dim)


def pick(condition):
    return jnp.where(condition, 1.0, 0.0).astype(B16)


def to_lane(rows, offset):
    j, i = iota((LANES, rows), 0), iota((LANES, rows), 1)
    return pick(j == i + offset)


def to_components(rows, offset, points, seg):
    j, i = iota((LANES, rows), 0), iota((LANES, rows), 1)
    found = j < 0
    for c in range(3):
        m = j - (c * seg + offset)
        found = found | ((m >= 0) & (m < points) & (i == 3 * m + c))
    return pick(found)


def unpack(tile, seg):
    return tile, pltpu.roll(tile, LANES - seg, 1), pltpu.roll(tile, LANES - 2 * seg, 1)


def pack(x, y, z, seg, low, high):
    lane = iota(x.shape, 1)
    keep = (lane >= low) & (lane < high)
    x, y, z = (jnp.where(keep, v, 0.0) for v in (x, y, z))
    return x + pltpu.roll(y, seg, 1) + pltpu.roll(z, 2 * seg, 1)


def head_of(shape, lay):
    lane = iota(shape, 1)
    zero = jnp.full(shape, -1, jnp.int32)
    one = jnp.full(shape, -1, jnp.int32)
    for h in range(lay.heads):
        for base in (0, lay.keys):
            zero = jnp.where((lane >= base + h * C) & (lane < base + (h + 1) * C), h, zero)
        for c in range(3):
            k = c * lay.seg + h * PQ
            v = c * lay.seg + lay.kp + h * PV
            one = jnp.where((lane >= k) & (lane < k + PQ), h, one)
            one = jnp.where((lane >= v) & (lane < v + PV), h, one)
    return zero, one


def in_segments(shape, lay, low, high):
    lane = iota(shape, 1)
    found = lane < 0
    for c in range(3):
        found = found | ((lane >= c * lay.seg + low) & (lane < c * lay.seg + high))
    return found


def key_kernel(lay, key_single, frames, w_key, w_value, w_kp, w_vp, packed, weights, turned):
    seg = lay.seg
    zero = nn(to_lane(lay.keys, 0), w_key[...]) + nn(to_lane(lay.keys, lay.keys), w_value[...])
    one = nn(to_components(3 * lay.kp, 0, lay.kp, seg), w_kp[...]) + nn(
        to_components(3 * (seg - lay.kp), lay.kp, seg - lay.kp, seg), w_vp[...]
    )
    w_all = jnp.concatenate([zero, one], axis=0).astype(B16)
    weights[...] = w_all
    rows = nt(key_single[...], w_all)
    turn = jnp.transpose(frames[...])
    turned[:, : turn.shape[1]] = turn
    x, y, z = unpack(rows[:, LANES:], seg)
    out = []
    for c in range(3):
        r = [turn[:, 3 * c + d : 3 * c + d + 1] for d in range(3)]
        out.append((r[0] * x + r[1] * y + r[2] * z + turn[:, 9 + c : 10 + c]).astype(B16).astype(F32))
    points = pack(*out, seg, 0, seg)
    square = out[0] * out[0] + out[1] * out[1] + out[2] * out[2]
    square = jnp.where(iota(square.shape, 1) < lay.kp, square, 0.0)
    i, j = iota((LANES, LANES), 0), iota((LANES, LANES), 1)
    chosen = j < 0
    for h in range(lay.heads):
        for piece in range(3):
            lane = lay.square + piece * lay.heads + h
            chosen = chosen | ((j == lane) & (i >= h * PQ) & (i < (h + 1) * PQ))
    total = nn(square, jnp.where(chosen, 1.0, 0.0), lax.Precision.HIGHEST)
    first = total.astype(B16).astype(F32)
    second = (total - first).astype(B16).astype(F32)
    third = total - first - second
    lane = iota(total.shape, 1)
    piece = jnp.where(
        lane < lay.square + lay.heads, first, jnp.where(lane < lay.square + 2 * lay.heads, second, third)
    )
    tile0 = jnp.where(lane < lay.square, rows[:, :LANES], piece).astype(B16)
    tile1 = points.astype(B16)
    packed[:, :LANES] = tile0
    packed[:, LANES:] = tile1


def gain_rows(head_weight, lay):
    row = iota((SUBLANES, LANES), 0)
    raw = jnp.zeros((SUBLANES, LANES), F32)
    for h in range(lay.heads):
        raw = jnp.where(row == h, jnp.broadcast_to(head_weight[:, h : h + 1], raw.shape), raw)
    gain = (jnp.maximum(raw, 0.0) + jnp.log1p(jnp.exp(-jnp.abs(raw)))) * POINT_SCALE
    return jnp.where(row < lay.heads, gain, 0.0)


def gain_lanes(gain, lay):
    _, one = head_of(gain.shape, lay)
    return jnp.sum(jnp.where(one == iota(gain.shape, 0), gain, 0.0), axis=0, keepdims=True)


def early_kernel(
    lay, block, order, head_weight, frames, query_single, w_query, w_qp, bias_weight, w_out, d_out, pair,
    left, base, d_base, d_row, w_out_rows, w_query_rows, gains, table, pair_rows, scratch,
):
    me = lax.axis_index("row")
    for place, offset in enumerate(order):
        j = pl.multiple_of((me ^ offset) * block, block)
        pair_rows[place * block : (place + 1) * block, :] = pair[0, pl.ds(j, block), :]
    turn = [jnp.broadcast_to(frames[:, i : i + 1], (1, LANES)) for i in range(12)]
    for i in range(12):
        table[i : i + 1, :] = turn[i]
    heads, seg = lay.heads, lay.seg
    width = C + 4 * PV + LANES
    shape = (SUBLANES, LANES)
    row, lane = iota(shape, 0), iota(shape, 1)
    zero_head, one_head = head_of(shape, lay)
    zero = nn(to_lane(lay.keys, 0), w_query[...])
    one = nn(to_components(3 * lay.kp, 0, lay.kp, seg), w_qp[...])
    w_q = jnp.concatenate([zero, one], axis=0).astype(B16)
    w_query_rows[...] = w_q
    near = C + 4 * PV
    w_o = jnp.zeros((2 * LANES, w_out.shape[1]), F32)
    for h in range(heads):
        i, j = iota((2 * LANES, near), 0), iota((2 * LANES, near), 1)
        m = i - (lay.keys + h * C)
        found = (m >= 0) & (m < C) & (j == m)
        m = i - h * PV
        found = found | ((m >= 0) & (m < PV) & (j == C + 3 * PV + m))
        for c in range(3):
            m = i - (LANES + c * seg + lay.kp + h * PV)
            found = found | ((m >= 0) & (m < PV) & (j == C + 3 * m + c))
        w_o = w_o + nn(pick(found), w_out[h * width : h * width + near, :])
    w_o = w_o.astype(B16)
    w_out_rows[: 2 * LANES, :] = w_o
    for h in range(heads):
        w_out_rows[(2 + h) * LANES : (3 + h) * LANES, :] = w_out[h * width + near : (h + 1) * width, :]
    single = jnp.broadcast_to(query_single[...], (SUBLANES, query_single.shape[1]))
    rows = nt(single, w_q)
    x, y, z = unpack(rows[:, LANES:], seg)
    out = []
    for c in range(3):
        value = turn[3 * c] * x + turn[3 * c + 1] * y + turn[3 * c + 2] * z + turn[9 + c]
        out.append(value.astype(B16).astype(F32))
    points = pack(*out, seg, 0, lay.kp)
    query = rows[:, :LANES].astype(B16).astype(F32)
    is_key = lane < lay.keys
    left[:SUBLANES, :LANES] = jnp.where(is_key & (zero_head == row), query, 0.0)
    left[:SUBLANES, LANES:] = jnp.zeros(shape, F32)
    minus = lane < 0
    for piece in range(3):
        minus = minus | (lane == lay.square + piece * heads + row)
    left[SUBLANES:, :LANES] = jnp.where(minus & (row < heads), -0.5, 0.0)
    mine = jnp.where(one_head == row, points, 0.0)
    left[SUBLANES:, LANES:] = mine
    gain = gain_rows(head_weight, lay)
    gains[...] = gain
    cotangent = jnp.broadcast_to(d_out[...], (SUBLANES, d_out.shape[1]))
    d_row[...] = nt(cotangent, w_o)
    scratch[...] = jnp.zeros_like(scratch)
    scratch[:heads, :] = bias_weight[...].astype(F32)
    for h in range(heads):
        d_pair = nt(cotangent, w_out[h * width + near : (h + 1) * width, :])
        scratch[SUBLANES + h : SUBLANES + h + 1, :] = d_pair[:1, :]
    both = nt(scratch[...].astype(B16), pair_rows[...])
    square = jnp.sum(mine * mine, axis=1, keepdims=True)
    base[...] = both[:SUBLANES] - 0.5 * gain[:, :1] * square
    d_base[...] = both[SUBLANES:]


def spread(weights, parts):
    total, at = 0.0, 0
    for part in parts:
        total = total + nn(weights[:, at : at + part.shape[0]], part[...])
        at += part.shape[0]
    return total


def attention_kernel(
    lay, block, order, *refs
):
    *parts, left, base, d_base, d_row, gains, table, message, features, weights, scores = refs
    frames = [table[i : i + 1, :] for i in range(12)]
    me = lax.axis_index("row")
    heads, seg = lay.heads, lay.seg
    shape = (SUBLANES, LANES)
    row, lane = iota(shape, 0), iota(shape, 1)
    zero_head, one_head = head_of(shape, lay)
    gain = gains[...]
    queries = left[...].astype(B16)
    first = jnp.concatenate([nt(queries, part[...]) for part in parts], axis=1)
    logits = LOGIT_SCALE * (first[:SUBLANES] * (1.0 / math.sqrt(C)) + base[...] + gain[:, :1] * first[SUBLANES:])
    weight = jnp.exp(logits - jnp.max(logits, axis=1, keepdims=True))
    attention = weight / jnp.sum(weight, axis=1, keepdims=True)
    attention = jnp.where(iota(attention.shape, 0) < heads, attention, 0.0)
    attention_b = attention.astype(B16)
    sums = spread(attention_b, parts)
    weights[...] = attention_b
    attended = jnp.sum(jnp.where(zero_head == row, sums[:, :LANES], 0.0), axis=0, keepdims=True)
    points = jnp.sum(jnp.where(one_head == row, sums[:, LANES:], 0.0), axis=0, keepdims=True)
    attended = jnp.broadcast_to(attended, shape)
    points = jnp.broadcast_to(points, shape)
    moved = [v - frames[9 + c] for c, v in enumerate(unpack(points, seg))]
    local = [
        frames[d] * moved[0] + frames[3 + d] * moved[1] + frames[6 + d] * moved[2] for d in range(3)
    ]
    lengths = jnp.sqrt(1.0 + (local[0] * local[0] + local[1] * local[1] + local[2] * local[2]))
    value_points = heads * PV
    is_value = (lane >= lay.keys) & (lane < lay.square)
    features[:, :LANES] = jnp.where(
        is_value, attended, jnp.where(lane < value_points, pltpu.roll(lengths, LANES - lay.kp, 1), 0.0)
    )
    features[:, LANES:] = pack(*local, seg, lay.kp, seg)
    d_zero = d_row[:, :LANES]
    share = pltpu.roll(d_zero, lay.kp, 1) / lengths
    d_local = [v + share * u for v, u in zip(unpack(d_row[:, LANES:], seg), local)]
    d_points = [
        frames[3 * c] * d_local[0] + frames[3 * c + 1] * d_local[1] + frames[3 * c + 2] * d_local[2]
        for c in range(3)
    ]
    d_points = pack(*d_points, seg, lay.kp, seg)
    d_attended = jnp.where(is_value, d_zero, 0.0)
    right = jnp.concatenate(
        [jnp.where(zero_head == row, d_attended, 0.0), jnp.where(one_head == row, d_points, 0.0)], axis=1
    )
    right = right.astype(B16)
    d_attention = jnp.concatenate([nt(right, part[...]) for part in parts], axis=1) + d_base[...]
    total = jnp.sum(attention * d_attention, axis=1, keepdims=True)
    score_b = (LOGIT_SCALE * attention * (d_attention - total)).astype(B16)
    scores[...] = score_b
    query0 = jnp.sum(left[:SUBLANES, :LANES], axis=0, keepdims=True)
    query1 = jnp.sum(left[SUBLANES:, LANES:], axis=0, keepdims=True)
    side = jnp.where(row == 2 * heads, jnp.broadcast_to(query0, shape) + d_attended, 0.0)
    side = side + jnp.where(row == 2 * heads + 1, jnp.broadcast_to(query1, shape) + d_points, 0.0)
    both = attention_b.astype(F32) + pltpu.roll(score_b.astype(F32), heads, 0)
    for at in range(0, both.shape[1], LANES):
        tile = jnp.where(row < 2 * heads, both[:, at : at + LANES], side).astype(B16)
        for place in range(at // block, (at + LANES) // block):
            message[me ^ order[place], :, :] = tile


def rows_kernel(
    lay, *refs
):
    *parts, pair, left, scores, features, weights, w_out_rows, w_query_rows, gains, table, sums = refs
    frames = [table[i : i + 1, :] for i in range(12)]
    heads, seg = lay.heads, lay.seg
    shape = (SUBLANES, LANES)
    row, lane = iota(shape, 0), iota(shape, 1)
    zero_head, one_head = head_of(shape, lay)
    pair_sum = nn(weights[...], pair[...])
    pairs = [jnp.broadcast_to(pair_sum[h : h + 1, :], shape) for h in range(heads)]
    result = nn(jnp.concatenate([features[...]] + pairs, axis=1).astype(B16), w_out_rows[...])
    gain = gains[...]
    score = scores[...].astype(F32)
    d_rows = spread(scores[...], parts)
    d_query = jnp.sum(
        jnp.where((lane < lay.keys) & (zero_head == row), d_rows[:, :LANES], 0.0), axis=0, keepdims=True
    ) * (1.0 / math.sqrt(C))
    score_sum = jnp.sum(score, axis=1, keepdims=True)
    d_points = gain * (d_rows[:, LANES:] - score_sum * left[SUBLANES:, LANES:])
    d_points = jnp.sum(jnp.where(one_head == row, d_points, 0.0), axis=0, keepdims=True)
    x, y, z = unpack(jnp.broadcast_to(d_points, shape), seg)
    local = [frames[d] * x + frames[3 + d] * y + frames[6 + d] * z for d in range(3)]
    local = pack(*local, seg, 0, lay.kp)
    both = jnp.concatenate([jnp.broadcast_to(d_query, shape), local], axis=1).astype(B16)
    grad = nn(both, w_query_rows[...])
    sums[...] = jnp.concatenate([result, grad], axis=1)


def owner_kernel(lay, near, arrived, turned, packed, weights, gains, result):
    heads, seg = lay.heads, lay.seg
    count = arrived.shape[0]
    block = packed.shape[0]
    took = arrived[...].astype(F32)
    shape = (SUBLANES, LANES)
    whole = (count, SUBLANES, LANES)
    per = LANES // block
    place = ((iota(whole, 0) ^ lax.axis_index("row")) // near) % per
    mine = took
    for part in range(1, per):
        mine = jnp.where(place == part, pltpu.roll(took, LANES - part * block, 2), mine)
    row = iota(shape, 0)
    zero_head, one_head = head_of(shape, lay)
    lane = iota(shape, 1)
    from_score0 = lane < lay.keys
    from_score1 = in_segments(shape, lay, 0, lay.kp)
    keep0 = (zero_head >= 0) & (jnp.where(from_score0, zero_head + heads, zero_head) == row)
    keep1 = (one_head >= 0) & (jnp.where(from_score1, one_head + heads, one_head) == row)
    side0 = jnp.where(keep0[None], jnp.broadcast_to(took[:, 2 * heads : 2 * heads + 1, :], whole), 0.0)
    side1 = jnp.where(keep1[None], jnp.broadcast_to(took[:, 2 * heads + 1 : 2 * heads + 2, :], whole), 0.0)
    ones = jnp.broadcast_to(jnp.where(keep1 & from_score1, 1.0, 0.0)[None], whole)
    right = jnp.concatenate([side0, side1, ones], axis=2).reshape(count * SUBLANES, 3 * LANES).astype(B16)
    moved = jnp.transpose(mine.reshape(count * SUBLANES, LANES)).astype(B16)
    both = nn(moved, right)[:block]
    small = (block, LANES)
    lane = iota(small, 1)
    tile0 = jnp.where(lane < lay.keys, both[:, :LANES] * (1.0 / math.sqrt(C)), both[:, :LANES])
    gain = gain_lanes(gains[...], lay)
    own = packed[:, LANES:].astype(F32)
    tile1 = both[:, LANES : 2 * LANES]
    kp_part = gain * (tile1 - both[:, 2 * LANES :] * own)
    tile1 = jnp.where(in_segments(small, lay, 0, lay.kp), kp_part, tile1)
    turn = turned[...]
    x, y, z = unpack(tile1, seg)
    local = []
    for d in range(3):
        r = [turn[:, 3 * c + d : 3 * c + d + 1] for c in range(3)]
        local.append(r[0] * x + r[1] * y + r[2] * z)
    tile1 = pack(*local, seg, 0, seg)
    rows = jnp.concatenate([tile0, tile1], axis=1).astype(B16)
    result[...] = nn(rows, weights[...])


VMEM = pl.BlockSpec(memory_space=pltpu.VMEM)
HBM = pl.BlockSpec(memory_space=pltpu.HBM)


def call(body, outs, args, fresh=0, scratch=(), flops=1000000):
    size = sum(math.prod(v.shape) * v.dtype.itemsize for v in list(args) + list(outs))

    def kernel(*refs):
        if fresh:
            *refs, sems = refs
            held = refs[len(refs) - fresh :]
            copies = [pltpu.make_async_copy(refs[i], held[i], sems.at[i]) for i in range(fresh)]
            for copy in copies:
                copy.start()
            for copy in copies:
                copy.wait()
            refs = list(held) + list(refs[fresh : len(refs) - fresh])
        body(*refs)

    own = [pltpu.VMEM(v.shape, v.dtype) for v in args[:fresh]]
    return pl.pallas_call(
        kernel,
        out_shape=tuple(outs),
        in_specs=[HBM] * fresh + [VMEM] * (len(args) - fresh),
        out_specs=tuple([VMEM] * len(outs)),
        scratch_shapes=list(scratch) + own + ([pltpu.SemaphoreType.DMA((fresh,))] if fresh else []),
        compiler_params=pltpu.CompilerParams(vmem_limit_bytes=(16 << 20) + 6 * size),
        cost_estimate=pl.CostEstimate(flops=flops, bytes_accessed=size, transcendentals=0),
    )(*[pltpu.with_memory_space_constraint(v, pltpu.HBM) for v in args[:fresh]], *args[fresh:])


def shape_of(*dims, dtype=F32):
    return jax.ShapeDtypeStruct(dims, dtype)


def shards(
    query_single, key_single, pair, query_frames, key_frames, w_query, w_key, w_value, w_query_points, w_key_points,
    w_value_points, head_weight, bias_weight, w_out, d_out,
):
    lay = Layout(head_weight.shape[0])
    count = lax.axis_size("row")
    block, width = key_single.shape
    total = count * block
    near = 1
    while 4 * near * near <= count:
        near *= 2
    assert count & (count - 1) == 0

    def exchange(value, mask):
        return lax.ppermute(value, "row", [(i, i ^ mask) for i in range(count)])

    packed, weights, turned = call(
        functools.partial(key_kernel, lay),
        [shape_of(block, 2 * LANES, dtype=B16), shape_of(2 * LANES, width, dtype=B16), shape_of(block, LANES)],
        [key_single, key_frames, w_key.T, w_value.T, w_key_points.T, w_value_points.T],
        6,
    )
    offsets = [0] + list(range(count - near, 0, -near))
    line = jnp.concatenate([packed] + [exchange(packed, mask) for mask in offsets[1:]], axis=0)
    planes = [0] + list(range(near - 1, 0, -1))
    parts = [line] + [exchange(line, m) for m in planes[1:]]
    order = [m ^ o for m in planes for o in offsets]

    left, base, d_base, d_row, w_out_rows, w_query_rows, gains, table, pair_rows = call(
        functools.partial(early_kernel, lay, block, order),
        [
            shape_of(ROWS16, 2 * LANES), shape_of(SUBLANES, total), shape_of(SUBLANES, total),
            shape_of(SUBLANES, 2 * LANES), shape_of((2 + lay.heads) * LANES, width, dtype=B16),
            shape_of(2 * LANES, width, dtype=B16), shape_of(SUBLANES, LANES), shape_of(ROWS16, LANES),
            shape_of(total, LANES, dtype=B16),
        ],
        [
            head_weight.reshape(1, -1), query_frames.T, query_single, w_query.T, w_query_points.T, bias_weight, w_out,
            d_out, pair,
        ],
        9,
        [pltpu.VMEM((ROWS16, LANES), F32)],
    )
    message, features, weight_rows, scores = call(
        functools.partial(attention_kernel, lay, block, order),
        [
            shape_of(count, SUBLANES, LANES, dtype=B16), shape_of(SUBLANES, 2 * LANES),
            shape_of(SUBLANES, total, dtype=B16), shape_of(SUBLANES, total, dtype=B16),
        ],
        parts + [left, base, d_base, d_row, gains, table],
    )
    arrived = lax.all_to_all(message, "row", 0, 0, tiled=True)
    (sums,) = call(
        functools.partial(rows_kernel, lay),
        [shape_of(SUBLANES, 2 * width)],
        parts + [pair_rows, left, scores, features, weight_rows, w_out_rows, w_query_rows, gains, table],
    )
    swap = [(i, (i + 1) % 2) for i in range(2)]
    sums = sums[:1]
    sums = sums + lax.ppermute(sums, "head", swap)
    output = sums[:, :width].astype(B16)
    grad_query = sums[:, width:]
    (part,) = call(
        functools.partial(owner_kernel, lay, near),
        [shape_of(block, width)],
        [arrived, turned, packed, weights, gains],
    )
    grad_keys = part + lax.ppermute(part, "head", swap)
    return (output, grad_query, grad_keys)


def solution(mesh):
    return jax.shard_map(
        shards,
        mesh=mesh,
        in_specs=(
            P("row", None),
            P("row", None),
            P("row", None, None),
            P(None, "row"),
            P(None, "row"),
            P(None, "head"),
            P(None, "head"),
            P(None, "head"),
            P(None, "head"),
            P(None, "head"),
            P(None, "head"),
            P("head"),
            P("head", None),
            P("head", None),
            P("row", None),
        ),
        out_specs=(P("row", None), P("row", None), P("row", None)),
        check_vma=False,
    )
```

```python
import functools
import math

import jax
import jax.numpy as jnp
from jax import lax
from jax.experimental import pallas as pl
from jax.experimental.pallas import tpu as pltpu
from jax.sharding import PartitionSpec as P

C = 16
PQ = 4
PV = 8
LANES = 128
SUBLANES = 8
ROWS16 = 16
LOGIT_SCALE = math.sqrt(1.0 / 3.0)
POINT_SCALE = math.sqrt(2.0 / (9.0 * PQ))
F32 = jnp.float32
B16 = jnp.bfloat16


class Layout:
    def __init__(self, heads):
        self.heads = heads
        self.keys = heads * C
        self.square = 2 * heads * C
        self.kp = heads * PQ
        self.seg = heads * (PQ + PV)
        assert self.square + 3 * heads <= LANES and 3 * self.seg <= LANES and 2 * heads + 2 <= SUBLANES


def nn(a, b, precision=None):
    return lax.dot_general(a, b, (((1,), (0,)), ((), ())), precision=precision, preferred_element_type=F32)


def nt(a, b):
    return lax.dot_general(a, b, (((1,), (1,)), ((), ())), preferred_element_type=F32)


def iota(shape, dim):
    return lax.broadcasted_iota(jnp.int32, shape, dim)


def pick(condition):
    return jnp.where(condition, 1.0, 0.0).astype(B16)


def to_lane(rows, offset):
    j, i = iota((LANES, rows), 0), iota((LANES, rows), 1)
    return pick(j == i + offset)


def to_components(rows, offset, points, seg):
    j, i = iota((LANES, rows), 0), iota((LANES, rows), 1)
    found = j < 0
    for c in range(3):
        m = j - (c * seg + offset)
        found = found | ((m >= 0) & (m < points) & (i == 3 * m + c))
    return pick(found)


def unpack(tile, seg):
    return tile, pltpu.roll(tile, LANES - seg, 1), pltpu.roll(tile, LANES - 2 * seg, 1)


def pack(x, y, z, seg, low, high):
    lane = iota(x.shape, 1)
    keep = (lane >= low) & (lane < high)
    x, y, z = (jnp.where(keep, v, 0.0) for v in (x, y, z))
    return x + pltpu.roll(y, seg, 1) + pltpu.roll(z, 2 * seg, 1)


def head_of(shape, lay):
    lane = iota(shape, 1)
    zero = jnp.full(shape, -1, jnp.int32)
    one = jnp.full(shape, -1, jnp.int32)
    for h in range(lay.heads):
        for base in (0, lay.keys):
            zero = jnp.where((lane >= base + h * C) & (lane < base + (h + 1) * C), h, zero)
        for c in range(3):
            k = c * lay.seg + h * PQ
            v = c * lay.seg + lay.kp + h * PV
            one = jnp.where((lane >= k) & (lane < k + PQ), h, one)
            one = jnp.where((lane >= v) & (lane < v + PV), h, one)
    return zero, one


def in_segments(shape, lay, low, high):
    lane = iota(shape, 1)
    found = lane < 0
    for c in range(3):
        found = found | ((lane >= c * lay.seg + low) & (lane < c * lay.seg + high))
    return found


def key_kernel(lay, key_single, frames, w_key, w_value, w_kp, w_vp, packed, weights, turned):
    seg = lay.seg
    zero = nn(to_lane(lay.keys, 0), w_key[...]) + nn(to_lane(lay.keys, lay.keys), w_value[...])
    one = nn(to_components(3 * lay.kp, 0, lay.kp, seg), w_kp[...]) + nn(
        to_components(3 * (seg - lay.kp), lay.kp, seg - lay.kp, seg), w_vp[...]
    )
    w_all = jnp.concatenate([zero, one], axis=0).astype(B16)
    weights[...] = w_all
    rows = nt(key_single[...], w_all)
    turn = jnp.transpose(frames[...])
    turned[:, : turn.shape[1]] = turn
    x, y, z = unpack(rows[:, LANES:], seg)
    out = []
    for c in range(3):
        r = [turn[:, 3 * c + d : 3 * c + d + 1] for d in range(3)]
        out.append((r[0] * x + r[1] * y + r[2] * z + turn[:, 9 + c : 10 + c]).astype(B16).astype(F32))
    points = pack(*out, seg, 0, seg)
    square = out[0] * out[0] + out[1] * out[1] + out[2] * out[2]
    square = jnp.where(iota(square.shape, 1) < lay.kp, square, 0.0)
    i, j = iota((LANES, LANES), 0), iota((LANES, LANES), 1)
    chosen = j < 0
    for h in range(lay.heads):
        for piece in range(3):
            lane = lay.square + piece * lay.heads + h
            chosen = chosen | ((j == lane) & (i >= h * PQ) & (i < (h + 1) * PQ))
    total = nn(square, jnp.where(chosen, 1.0, 0.0), lax.Precision.HIGHEST)
    first = total.astype(B16).astype(F32)
    second = (total - first).astype(B16).astype(F32)
    third = total - first - second
    lane = iota(total.shape, 1)
    piece = jnp.where(
        lane < lay.square + lay.heads, first, jnp.where(lane < lay.square + 2 * lay.heads, second, third)
    )
    tile0 = jnp.where(lane < lay.square, rows[:, :LANES], piece).astype(B16)
    tile1 = points.astype(B16)
    packed[:, :LANES] = tile0
    packed[:, LANES:] = tile1


def gain_rows(head_weight, lay):
    row = iota((SUBLANES, LANES), 0)
    raw = jnp.zeros((SUBLANES, LANES), F32)
    for h in range(lay.heads):
        raw = jnp.where(row == h, jnp.broadcast_to(head_weight[:, h : h + 1], raw.shape), raw)
    gain = (jnp.maximum(raw, 0.0) + jnp.log1p(jnp.exp(-jnp.abs(raw)))) * POINT_SCALE
    return jnp.where(row < lay.heads, gain, 0.0)


def gain_lanes(gain, lay):
    _, one = head_of(gain.shape, lay)
    return jnp.sum(jnp.where(one == iota(gain.shape, 0), gain, 0.0), axis=0, keepdims=True)


def early_kernel(
    lay, block, order, head_weight, frames, query_single, w_query, w_qp, bias_weight, w_out, d_out, pair,
    w_out_rows, w_query_rows, gains, table, pair_rows, *rest
):
    *sides, scratch = rest
    me = lax.axis_index("row")
    for place, offset in enumerate(order):
        j = pl.multiple_of((me ^ offset) * block, block)
        pair_rows[place * block : (place + 1) * block, :] = pair[0, pl.ds(j, block), :]
    turn = [jnp.broadcast_to(frames[:, i : i + 1], (1, LANES)) for i in range(12)]
    for i in range(12):
        table[i : i + 1, :] = turn[i]
    heads, seg = lay.heads, lay.seg
    width = C + 4 * PV + LANES
    shape = (SUBLANES, LANES)
    row, lane = iota(shape, 0), iota(shape, 1)
    zero_head, one_head = head_of(shape, lay)
    zero = nn(to_lane(lay.keys, 0), w_query[...])
    one = nn(to_components(3 * lay.kp, 0, lay.kp, seg), w_qp[...])
    w_q = jnp.concatenate([zero, one], axis=0).astype(B16)
    w_query_rows[...] = w_q
    near = C + 4 * PV
    w_o = jnp.zeros((2 * LANES, w_out.shape[1]), F32)
    for h in range(heads):
        i, j = iota((2 * LANES, near), 0), iota((2 * LANES, near), 1)
        m = i - (lay.keys + h * C)
        found = (m >= 0) & (m < C) & (j == m)
        m = i - h * PV
        found = found | ((m >= 0) & (m < PV) & (j == C + 3 * PV + m))
        for c in range(3):
            m = i - (LANES + c * seg + lay.kp + h * PV)
            found = found | ((m >= 0) & (m < PV) & (j == C + 3 * m + c))
        w_o = w_o + nn(pick(found), w_out[h * width : h * width + near, :])
    w_o = w_o.astype(B16)
    w_out_rows[: 2 * LANES, :] = w_o
    for h in range(heads):
        w_out_rows[(2 + h) * LANES : (3 + h) * LANES, :] = w_out[h * width + near : (h + 1) * width, :]
    single = jnp.broadcast_to(query_single[...], (SUBLANES, query_single.shape[1]))
    rows = nt(single, w_q)
    x, y, z = unpack(rows[:, LANES:], seg)
    out = []
    for c in range(3):
        value = turn[3 * c] * x + turn[3 * c + 1] * y + turn[3 * c + 2] * z + turn[9 + c]
        out.append(value.astype(B16).astype(F32))
    points = pack(*out, seg, 0, lay.kp)
    query = jnp.where(lane < lay.keys, rows[:, :LANES], 0.0).astype(B16).astype(F32)
    mine = jnp.where(one_head == row, points, 0.0)
    gain = gain_rows(head_weight, lay)
    gains[...] = gain
    cotangent = jnp.broadcast_to(d_out[...], (SUBLANES, d_out.shape[1]))
    d_row = nt(cotangent, w_o)
    d_zero = d_row[:, :LANES]
    for i in range(12):
        d_zero = jnp.where(lane == lay.square + i, turn[i], d_zero)
    scratch[...] = jnp.zeros_like(scratch)
    scratch[:heads, :] = bias_weight[...].astype(F32)
    for h in range(heads):
        d_pair = nt(cotangent, w_out[h * width + near : (h + 1) * width, :])
        scratch[SUBLANES + h : SUBLANES + h + 1, :] = d_pair[:1, :]
    both = nt(scratch[...].astype(B16), pair_rows[...])
    square = jnp.sum(mine * mine, axis=1, keepdims=True)
    base = both[:SUBLANES] - 0.5 * gain[:, :1] * square
    d_base = pltpu.roll(both[SUBLANES:], heads, 0)
    for m, side in enumerate(sides):
        width = side.shape[1]
        at = m * width
        side[...] = jnp.where(
            iota((SUBLANES, width), 0) < heads, base[:, at : at + width], d_base[:, at : at + width]
        )
        side[2 * heads : 2 * heads + 1, :LANES] = query[:1]
        side[2 * heads : 2 * heads + 1, LANES : 2 * LANES] = points[:1]
        side[2 * heads + 1 : 2 * heads + 2, :LANES] = d_zero[:1]
        side[2 * heads + 1 : 2 * heads + 2, LANES : 2 * LANES] = d_row[:1, LANES:]


def spread(weights, parts):
    total, at = 0.0, 0
    for part in parts:
        total = total + nn(weights[:, at : at + part.shape[0]], part[...])
        at += part.shape[0]
    return total


def by_head(shape, lay, head, values):
    total = jnp.zeros(shape, F32)
    for h in range(lay.heads):
        total = jnp.where(head == h, values[h], total)
    return total


def flip(rows, mask):
    row = iota(rows.shape, 0)
    for bit in (1, 2, 4):
        if mask & bit:
            rows = jnp.where((row & bit) > 0, pltpu.roll(rows, bit, 0), pltpu.roll(rows, SUBLANES - bit, 0))
    return rows


def group(h):
    return slice(h * SUBLANES, (h + 1) * SUBLANES)


def partial_kernel(lay, near, *refs):
    heads = lay.heads
    parts, sides = refs[:-6 - near], refs[-6 - near : -6]
    gains, weights, d_base, stats, base, rows = refs[-6:]
    shape = (SUBLANES, LANES)
    row, lane = iota(shape, 0), iota(shape, 1)
    zero_head, one_head = head_of(shape, lay)
    base[...] = jnp.zeros_like(base)
    d_base[...] = jnp.zeros_like(d_base)
    rows[...] = jnp.zeros_like(rows)
    for i, side in enumerate(sides):
        for h in range(heads):
            at = h * SUBLANES + i
            base[at : at + 1, :] = side[h : h + 1, :]
            d_base[at : at + 1, :] = side[heads + h : heads + h + 1, :]
        rows[i : i + 1, :] = side[2 * heads : 2 * heads + 1, : 2 * LANES]
    query, points = rows[:, :LANES], rows[:, LANES:]
    nothing = jnp.zeros(shape, F32)
    tops, lows = [], []
    for h in range(heads):
        tops.append(jnp.concatenate([jnp.where(zero_head == h, query, 0.0), nothing], axis=1))
        minus = lane < 0
        for piece in range(3):
            minus = minus | (lane == lay.square + piece * heads + h)
        lows.append(
            jnp.concatenate([jnp.where(minus, -0.5, 0.0), jnp.where(one_head == h, points, 0.0)], axis=1)
        )
    left = jnp.concatenate(tops + lows, axis=0).astype(B16)
    first = jnp.concatenate([nt(left, part[...]) for part in parts], axis=1)
    high, low, extra = [], [], nothing
    for h in range(heads):
        gain = gains[h : h + 1, :1]
        logits = LOGIT_SCALE * (
            first[group(h)] * (1.0 / math.sqrt(C)) + base[group(h), :] + gain * first[group(heads + h)]
        )
        most = jnp.max(logits, axis=1, keepdims=True)
        weight = jnp.exp(logits - most)
        weights[group(h), :] = weight
        total = jnp.sum(weight, axis=1, keepdims=True)
        d_total = jnp.sum(weight * d_base[group(h), :], axis=1, keepdims=True)
        extra = jnp.where(lane == h, most, extra)
        extra = jnp.where(lane == SUBLANES + h, total, extra)
        extra = jnp.where(lane == 2 * SUBLANES + h, d_total, extra)
        rounded = weight.astype(B16).astype(F32)
        high.append(rounded)
        low.append(weight - rounded)
    both = jnp.concatenate(high + low, axis=0).astype(B16)
    sums = spread(both, parts)
    sums = sums[: heads * SUBLANES] + sums[heads * SUBLANES :]
    is_value = (lane >= lay.keys) & (lane < lay.square)
    attended = by_head(shape, lay, zero_head, [sums[group(h), :LANES] for h in range(heads)])
    stats[:, :LANES] = jnp.where(is_value, attended, extra)
    stats[:, LANES:] = by_head(shape, lay, one_head, [sums[group(h), LANES:] for h in range(heads)])


def score_kernel(lay, near, block, *refs):
    heads, seg = lay.heads, lay.seg
    rows = refs[-1]
    refs = refs[:-1]
    far = refs[0].shape[1] // block
    weights, d_base = refs[:2]
    stats = refs[2 : 2 + near]
    sides = refs[2 + near : 2 + 2 * near]
    parts = refs[2 + 2 * near : 2 + 2 * near + far]
    features, attention_out, scores, *messages = refs[2 + 2 * near + far :]
    shape = (SUBLANES, LANES)
    row, lane = iota(shape, 0), iota(shape, 1)
    zero_head, one_head = head_of(shape, lay)
    rows[...] = jnp.zeros_like(rows)
    for i, side in enumerate(sides):
        rows[i : i + 1, :] = side[2 * heads : 2 * heads + 1, : 2 * LANES]
        rows[SUBLANES + i : SUBLANES + i + 1, :] = side[2 * heads + 1 : 2 * heads + 2, : 2 * LANES]
    query, points = rows[:SUBLANES, :LANES], rows[:SUBLANES, LANES:]
    d_zero, d_one = rows[SUBLANES:, :LANES], rows[SUBLANES:, LANES:]
    told = [flip(stat[...], m) for m, stat in enumerate(stats)]
    most = told[0][:, :LANES]
    for stat in told[1:]:
        most = jnp.maximum(most, stat[:, :LANES])
    shares = [jnp.exp(jnp.where(lane < heads, stat[:, :LANES] - most, 0.0)) for stat in told]
    total, d_total, attended, point_sum = 0.0, 0.0, 0.0, 0.0
    for share, stat in zip(shares, told):
        total = total + share * pltpu.roll(stat[:, :LANES], LANES - SUBLANES, 1)
        d_total = d_total + share * pltpu.roll(stat[:, :LANES], LANES - 2 * SUBLANES, 1)
        columns = [share[:, h : h + 1] for h in range(heads)]
        attended = attended + by_head(shape, lay, zero_head, columns) * stat[:, :LANES]
        point_sum = point_sum + by_head(shape, lay, one_head, columns) * stat[:, LANES:]
    inverse = 1.0 / jnp.where(lane < heads, total, 1.0)
    columns = [inverse[:, h : h + 1] for h in range(heads)]
    is_value = (lane >= lay.keys) & (lane < lay.square)
    attended = jnp.where(is_value, attended * by_head(shape, lay, zero_head, columns), 0.0)
    point_sum = point_sum * by_head(shape, lay, one_head, columns)
    d_total = d_total * inverse
    own = shares[0] * inverse
    turn = [d_zero[:, lay.square + i : lay.square + i + 1] for i in range(12)]
    moved = [v - turn[9 + c] for c, v in enumerate(unpack(point_sum, seg))]
    local = [turn[d] * moved[0] + turn[3 + d] * moved[1] + turn[6 + d] * moved[2] for d in range(3)]
    lengths = jnp.sqrt(1.0 + (local[0] * local[0] + local[1] * local[1] + local[2] * local[2]))
    features[:, :LANES] = jnp.where(
        is_value, attended, jnp.where(lane < heads * PV, pltpu.roll(lengths, LANES - lay.kp, 1), 0.0)
    )
    features[:, LANES:] = pack(*local, seg, lay.kp, seg)
    share = pltpu.roll(d_zero, lay.kp, 1) / lengths
    d_local = [v + share * u for v, u in zip(unpack(d_one, seg), local)]
    d_points = [
        turn[3 * c] * d_local[0] + turn[3 * c + 1] * d_local[1] + turn[3 * c + 2] * d_local[2] for c in range(3)
    ]
    d_points = pack(*d_points, seg, lay.kp, seg).astype(B16).astype(F32)
    d_attended = jnp.where(is_value, d_zero, 0.0).astype(B16).astype(F32)
    right = jnp.concatenate(
        [
            jnp.concatenate(
                [jnp.where(zero_head == h, d_attended, 0.0), jnp.where(one_head == h, d_points, 0.0)], axis=1
            )
            for h in range(heads)
        ],
        axis=0,
    ).astype(B16)
    d_attention = jnp.concatenate([nt(right, part[...]) for part in parts], axis=1) + d_base[...]
    inner0, inner1 = d_attended * attended, d_points * point_sum
    high, low = [], []
    for h in range(heads):
        inner = jnp.where(zero_head == h, inner0, 0.0) + jnp.where(one_head == h, inner1, 0.0)
        inner = jnp.sum(inner, axis=1, keepdims=True) + d_total[:, h : h + 1]
        attention = weights[group(h), :] * own[:, h : h + 1]
        high.append(attention.astype(B16).astype(F32))
        score = LOGIT_SCALE * attention * (d_attention[group(h)] - inner)
        low.append(score.astype(B16).astype(F32))
    high, low = jnp.concatenate(high, axis=0), jnp.concatenate(low, axis=0)
    attention_out[...] = high
    scores[...] = low.astype(B16)
    tail = [query + d_attended, points + d_points]
    half = iota((heads * SUBLANES, LANES), 1) < block
    for place, message in enumerate(messages):
        at = place * block // LANES * LANES
        a, b = high[:, at : at + LANES], low[:, at : at + LANES]
        if place * block % LANES:
            a = pltpu.roll(a, LANES - block, 1)
        else:
            b = pltpu.roll(b, block, 1)
        message[...] = jnp.concatenate([jnp.where(half, a, b)] + tail, axis=0).astype(B16)


def return_kernel(lay, *refs):
    heads = lay.heads
    attention, scores, *rest = refs
    far = sum(1 for ref in rest if ref.dtype == B16)
    parts, returns = rest[:far], rest[far:]
    shape = (SUBLANES, LANES)
    lane = iota(shape, 1)
    zero_head, one_head = head_of(shape, lay)
    d_rows = spread(scores[...], parts)
    zero = by_head(shape, lay, zero_head, [d_rows[group(h), :LANES] for h in range(heads)])
    one = by_head(shape, lay, one_head, [d_rows[group(h), LANES:] for h in range(heads)])
    zero = jnp.where(lane < lay.keys, zero, 0.0)
    for h in range(heads):
        total = jnp.sum(scores[group(h), :].astype(F32), axis=1, keepdims=True)
        zero = jnp.where(lane == lay.square + h, total, zero)
    for i, back in enumerate(returns):
        for h in range(heads):
            back[h : h + 1, :] = attention[h * SUBLANES + i : h * SUBLANES + i + 1, :]
        back[heads:, :] = jnp.zeros((SUBLANES - heads, back.shape[1]), F32)
        back[heads : heads + 1, :LANES] = zero[i : i + 1, :]
        back[heads : heads + 1, LANES : 2 * LANES] = one[i : i + 1, :]


def rows_kernel(lay, near, *refs):
    heads, seg = lay.heads, lay.seg
    backs = refs[:near]
    pair, side, features, w_out_rows, w_query_rows, gains, table, sums = refs[near:]
    frames = [table[i : i + 1, :] for i in range(12)]
    shape = (SUBLANES, LANES)
    row, lane = iota(shape, 0), iota(shape, 1)
    zero_head, one_head = head_of(shape, lay)
    width = backs[0].shape[1]
    pair_sum = 0.0
    d_zero, d_one = 0.0, 0.0
    for m, back in enumerate(backs):
        weight = jnp.where(iota((SUBLANES, width), 0) < heads, back[...], 0.0).astype(B16)
        pair_sum = pair_sum + nn(weight, pair[m * width : (m + 1) * width, :])
        d_zero = d_zero + back[heads : heads + 1, :LANES]
        d_one = d_one + back[heads : heads + 1, LANES : 2 * LANES]
    pairs = [jnp.broadcast_to(pair_sum[h : h + 1, :], shape) for h in range(heads)]
    mine = [jnp.broadcast_to(features[:1, :], (SUBLANES, 2 * LANES))]
    result = nn(jnp.concatenate(mine + pairs, axis=1).astype(B16), w_out_rows[...])
    d_zero, d_one = jnp.broadcast_to(d_zero, shape), jnp.broadcast_to(d_one, shape)
    score_sum = by_head(shape, lay, one_head, [d_zero[:, lay.square + h : lay.square + h + 1] for h in range(heads)])
    points = jnp.broadcast_to(side[2 * heads : 2 * heads + 1, LANES : 2 * LANES], shape)
    d_query = jnp.where(lane < lay.keys, d_zero, 0.0) * (1.0 / math.sqrt(C))
    d_points = gain_lanes(gains[...], lay) * (d_one - score_sum * points)
    x, y, z = unpack(d_points, seg)
    local = [frames[d] * x + frames[3 + d] * y + frames[6 + d] * z for d in range(3)]
    local = pack(*local, seg, 0, lay.kp)
    both = jnp.concatenate([d_query, local], axis=1).astype(B16)
    grad = nn(both, w_query_rows[...])
    sums[...] = jnp.concatenate([result, grad], axis=1)


def owner_kernel(lay, *refs):
    heads, seg = lay.heads, lay.seg
    *arrived, turned, packed, weights, gains, result = refs
    block = packed.shape[0]
    shape = (SUBLANES, LANES)
    lane = iota(shape, 1)
    zero_head, one_head = head_of(shape, lay)
    is_kp = in_segments(shape, lay, 0, lay.kp)
    tops, rights = [], []
    for message in arrived:
        took = message[...].astype(F32)
        tops.append(took[: heads * SUBLANES])
        side0 = took[heads * SUBLANES : (heads + 1) * SUBLANES]
        side1 = took[(heads + 1) * SUBLANES :]
        for h in range(heads):
            rights.append(
                jnp.concatenate(
                    [
                        jnp.where(zero_head == h, side0, 0.0),
                        jnp.where(one_head == h, side1, 0.0),
                        jnp.where((one_head == h) & is_kp, 1.0, 0.0),
                    ],
                    axis=1,
                )
            )
    right = jnp.concatenate(rights, axis=0).astype(B16)
    moved = jnp.transpose(jnp.concatenate(tops, axis=0)).astype(B16)
    both = nn(moved, right)
    high, low = both[:block], both[block : 2 * block]
    small = (block, LANES)
    lane = iota(small, 1)
    tile0 = jnp.where(lane < lay.keys, low[:, :LANES] * (1.0 / math.sqrt(C)), high[:, :LANES])
    gain = gain_lanes(gains[...], lay)
    own = packed[:, LANES:].astype(F32)
    kp_part = gain * (low[:, LANES : 2 * LANES] - low[:, 2 * LANES :] * own)
    tile1 = jnp.where(in_segments(small, lay, 0, lay.kp), kp_part, high[:, LANES : 2 * LANES])
    turn = turned[...]
    x, y, z = unpack(tile1, seg)
    local = []
    for d in range(3):
        r = [turn[:, 3 * c + d : 3 * c + d + 1] for c in range(3)]
        local.append(r[0] * x + r[1] * y + r[2] * z)
    tile1 = pack(*local, seg, 0, seg)
    rows = jnp.concatenate([tile0, tile1], axis=1).astype(B16)
    result[...] = nn(rows, weights[...])


VMEM = pl.BlockSpec(memory_space=pltpu.VMEM)
HBM = pl.BlockSpec(memory_space=pltpu.HBM)


def call(body, outs, args, fresh=0, scratch=(), flops=1000000):
    size = sum(math.prod(v.shape) * v.dtype.itemsize for v in list(args) + list(outs))

    def kernel(*refs):
        if fresh:
            *refs, sems = refs
            held = refs[len(refs) - fresh :]
            copies = [pltpu.make_async_copy(refs[i], held[i], sems.at[i]) for i in range(fresh)]
            for copy in copies:
                copy.start()
            for copy in copies:
                copy.wait()
            refs = list(held) + list(refs[fresh : len(refs) - fresh])
        body(*refs)

    own = [pltpu.VMEM(v.shape, v.dtype) for v in args[:fresh]]
    return pl.pallas_call(
        kernel,
        out_shape=tuple(outs),
        in_specs=[HBM] * fresh + [VMEM] * (len(args) - fresh),
        out_specs=tuple([VMEM] * len(outs)),
        scratch_shapes=list(scratch) + own + ([pltpu.SemaphoreType.DMA((fresh,))] if fresh else []),
        compiler_params=pltpu.CompilerParams(vmem_limit_bytes=(16 << 20) + 6 * size),
        cost_estimate=pl.CostEstimate(flops=flops, bytes_accessed=size, transcendentals=0),
    )(*[pltpu.with_memory_space_constraint(v, pltpu.HBM) for v in args[:fresh]], *args[fresh:])


def shape_of(*dims, dtype=F32):
    return jax.ShapeDtypeStruct(dims, dtype)


def shards(
    query_single, key_single, pair, query_frames, key_frames, w_query, w_key, w_value, w_query_points, w_key_points,
    w_value_points, head_weight, bias_weight, w_out, d_out,
):
    lay = Layout(head_weight.shape[0])
    count = lax.axis_size("row")
    block, width = key_single.shape
    total = count * block
    near = 1
    while 4 * near * near <= count:
        near *= 2
    far = count // near
    assert count & (count - 1) == 0 and near <= SUBLANES and 2 * block == LANES and far * block >= 2 * LANES

    def exchange(value, mask):
        return lax.ppermute(value, "row", [(i, i ^ mask) for i in range(count)])

    packed, weights, turned = call(
        functools.partial(key_kernel, lay),
        [shape_of(block, 2 * LANES, dtype=B16), shape_of(2 * LANES, width, dtype=B16), shape_of(block, LANES)],
        [key_single, key_frames, w_key.T, w_value.T, w_key_points.T, w_value_points.T],
        6,
    )
    offsets = list(range(0, count, near))
    planes = list(range(near))
    order = [m ^ o for m in planes for o in offsets]
    keys = far * block

    def gather(values, masks):
        return [values[0]] + [exchange(value, mask) for value, mask in zip(values[1:], masks[1:])]

    parts = gather([packed] * far, offsets)
    w_out_rows, w_query_rows, gains, table, pair_rows, *sides = call(
        functools.partial(early_kernel, lay, block, order),
        [
            shape_of((2 + lay.heads) * LANES, width, dtype=B16), shape_of(2 * LANES, width, dtype=B16),
            shape_of(SUBLANES, LANES), shape_of(ROWS16, LANES), shape_of(total, LANES, dtype=B16),
        ]
        + [shape_of(SUBLANES, keys)] * near,
        [
            head_weight.reshape(1, -1), query_frames.T, query_single, w_query.T, w_query_points.T, bias_weight, w_out,
            d_out, pair,
        ],
        9,
        [pltpu.VMEM((ROWS16, LANES), F32)],
    )
    sides = gather(sides, planes)
    tall = lay.heads * SUBLANES
    weight_rows, d_base, stats = call(
        functools.partial(partial_kernel, lay, near),
        [shape_of(tall, keys), shape_of(tall, keys), shape_of(SUBLANES, 2 * LANES)],
        parts + sides + [gains],
        scratch=[pltpu.VMEM((tall, keys), F32), pltpu.VMEM((SUBLANES, 2 * LANES), F32)],
    )
    stats = gather([stats] * near, planes)
    features, attention, scores, *messages = call(
        functools.partial(score_kernel, lay, near, block),
        [shape_of(SUBLANES, 2 * LANES), shape_of(tall, keys), shape_of(tall, keys, dtype=B16)]
        + [shape_of(tall + 2 * SUBLANES, LANES, dtype=B16)] * far,
        [weight_rows, d_base] + stats + sides + parts,
        scratch=[pltpu.VMEM((ROWS16, 2 * LANES), F32)],
    )
    arrived = gather(messages, offsets)
    backs = call(
        functools.partial(return_kernel, lay), [shape_of(SUBLANES, keys)] * near, [attention, scores] + parts
    )
    backs = gather(backs, planes)
    (sums,) = call(
        functools.partial(rows_kernel, lay, near),
        [shape_of(SUBLANES, 2 * width)],
        backs + [pair_rows, sides[0], features, w_out_rows, w_query_rows, gains, table],
    )
    swap = [(i, (i + 1) % 2) for i in range(2)]
    sums = sums[:1]
    sums = sums + lax.ppermute(sums, "head", swap)
    output = sums[:, :width].astype(B16)
    grad_query = sums[:, width:]
    (part,) = call(
        functools.partial(owner_kernel, lay),
        [shape_of(block, width)],
        arrived + [turned, packed, weights, gains],
    )
    grad_keys = part + lax.ppermute(part, "head", swap)
    return (output, grad_query, grad_keys)


def solution(mesh):
    return jax.shard_map(
        shards,
        mesh=mesh,
        in_specs=(
            P("row", None),
            P("row", None),
            P("row", None, None),
            P(None, "row"),
            P(None, "row"),
            P(None, "head"),
            P(None, "head"),
            P(None, "head"),
            P(None, "head"),
            P(None, "head"),
            P(None, "head"),
            P("head"),
            P("head", None),
            P("head", None),
            P("row", None),
        ),
        out_specs=(P("row", None), P("row", None), P("row", None)),
        check_vma=False,
    )
```

```python
import functools
import math

import jax
import jax.numpy as jnp
from jax import lax
from jax.experimental import pallas as pl
from jax.experimental.pallas import tpu as pltpu
from jax.sharding import PartitionSpec as P

C = 16
PQ = 4
PV = 8
LANES = 128
SUBLANES = 8
ROWS16 = 16
LOGIT_SCALE = math.sqrt(1.0 / 3.0)
POINT_SCALE = math.sqrt(2.0 / (9.0 * PQ))
F32 = jnp.float32
B16 = jnp.bfloat16


class Layout:
    def __init__(self, heads):
        self.heads = heads
        self.keys = heads * C
        self.square = 2 * heads * C
        self.half = LANES // 2
        self.kp = heads * PQ
        self.seg = heads * (PQ + PV)
        self.end = LANES - self.square
        self.mid = 3 * self.seg - self.half - self.end
        assert 3 * self.seg <= LANES and 2 * heads + 2 <= SUBLANES and self.mid > 0

    def rows(self, block):
        assert block // SUBLANES * self.mid <= LANES
        return block + block // 2 + SUBLANES

    def squeeze(self, zero, one):
        block = one.shape[0]
        lane = iota((SUBLANES, LANES), 1)
        last = self.half + self.mid
        wide = iota(one.shape, 1)
        tail = pltpu.roll(jnp.where((wide >= last) & (wide < 3 * self.seg), one, 0.0), self.square - last, 1)
        both = iota((block // 2, LANES), 1) < self.half
        sides = jnp.where(both, one[: block // 2], pltpu.roll(one[block // 2 :], self.half, 1))
        middle = jnp.zeros((SUBLANES, LANES), F32)
        for g in range(block // SUBLANES):
            piece = one[g * SUBLANES : (g + 1) * SUBLANES]
            piece = pltpu.roll(piece, (g * self.mid - self.half) % LANES, 1)
            middle = jnp.where((lane >= g * self.mid) & (lane < (g + 1) * self.mid), piece, middle)
        return jnp.concatenate([jnp.where(wide < self.square, zero, tail), sides, middle], axis=0)

    def restore(self, rows, block):
        lane = iota((block, LANES), 1)
        last = self.half + self.mid
        tail = pltpu.roll(rows[:block], (last - self.square) % LANES, 1)
        sides = rows[block : block + block // 2]
        sides = jnp.concatenate([sides, pltpu.roll(sides, self.half, 1)], axis=0)
        middle = rows[block + block // 2 :]
        middle = jnp.concatenate(
            [pltpu.roll(middle, (self.half - g * self.mid) % LANES, 1) for g in range(block // SUBLANES)], axis=0
        )
        tile = jnp.where(lane < self.half, sides, jnp.where(lane < last, middle, tail))
        return jnp.where(lane < 3 * self.seg, tile, 0.0)


def nn(a, b, precision=None):
    return lax.dot_general(a, b, (((1,), (0,)), ((), ())), precision=precision, preferred_element_type=F32)


def nt(a, b):
    return lax.dot_general(a, b, (((1,), (1,)), ((), ())), preferred_element_type=F32)


def iota(shape, dim):
    return lax.broadcasted_iota(jnp.int32, shape, dim)


def pick(condition):
    return jnp.where(condition, 1.0, 0.0).astype(B16)


def to_lane(rows, offset):
    j, i = iota((LANES, rows), 0), iota((LANES, rows), 1)
    return pick(j == i + offset)


def to_components(rows, offset, points, seg):
    j, i = iota((LANES, rows), 0), iota((LANES, rows), 1)
    found = j < 0
    for c in range(3):
        m = j - (c * seg + offset)
        found = found | ((m >= 0) & (m < points) & (i == 3 * m + c))
    return pick(found)


def unpack(tile, seg):
    return tile, pltpu.roll(tile, LANES - seg, 1), pltpu.roll(tile, LANES - 2 * seg, 1)


def pack(x, y, z, seg, low, high):
    lane = iota(x.shape, 1)
    keep = (lane >= low) & (lane < high)
    x, y, z = (jnp.where(keep, v, 0.0) for v in (x, y, z))
    return x + pltpu.roll(y, seg, 1) + pltpu.roll(z, 2 * seg, 1)


def head_of(shape, lay):
    lane = iota(shape, 1)
    zero = jnp.full(shape, -1, jnp.int32)
    one = jnp.full(shape, -1, jnp.int32)
    for h in range(lay.heads):
        for base in (0, lay.keys):
            zero = jnp.where((lane >= base + h * C) & (lane < base + (h + 1) * C), h, zero)
        for c in range(3):
            k = c * lay.seg + h * PQ
            v = c * lay.seg + lay.kp + h * PV
            one = jnp.where((lane >= k) & (lane < k + PQ), h, one)
            one = jnp.where((lane >= v) & (lane < v + PV), h, one)
    return zero, one


def in_segments(shape, lay, low, high):
    lane = iota(shape, 1)
    found = lane < 0
    for c in range(3):
        found = found | ((lane >= c * lay.seg + low) & (lane < c * lay.seg + high))
    return found


def key_kernel(lay, key_single, frames, w_key, w_value, w_kp, w_vp, packed, own, weights, turned):
    seg = lay.seg
    zero = nn(to_lane(lay.keys, 0), w_key[...]) + nn(to_lane(lay.keys, lay.keys), w_value[...])
    one = nn(to_components(3 * lay.kp, 0, lay.kp, seg), w_kp[...]) + nn(
        to_components(3 * (seg - lay.kp), lay.kp, seg - lay.kp, seg), w_vp[...]
    )
    w_all = jnp.concatenate([zero, one], axis=0).astype(B16)
    weights[...] = w_all
    rows = nt(key_single[...], w_all)
    turn = jnp.transpose(frames[...])
    turned[:, : turn.shape[1]] = turn
    x, y, z = unpack(rows[:, LANES:], seg)
    out = []
    for c in range(3):
        r = [turn[:, 3 * c + d : 3 * c + d + 1] for d in range(3)]
        out.append((r[0] * x + r[1] * y + r[2] * z + turn[:, 9 + c : 10 + c]).astype(B16).astype(F32))
    points = pack(*out, seg, 0, seg)
    packed[...] = lay.squeeze(rows[:, :LANES], points).astype(B16)
    own[...] = points


def is_own(shape, lay):
    return in_segments(shape, lay, 0, lay.kp)


def gain_rows(head_weight, lay):
    row = iota((SUBLANES, LANES), 0)
    raw = jnp.zeros((SUBLANES, LANES), F32)
    for h in range(lay.heads):
        raw = jnp.where(row == h, jnp.broadcast_to(head_weight[:, h : h + 1], raw.shape), raw)
    gain = (jnp.maximum(raw, 0.0) + jnp.log1p(jnp.exp(-jnp.abs(raw)))) * POINT_SCALE
    return jnp.where(row < lay.heads, gain, 0.0)


def gain_lanes(gain, lay):
    _, one = head_of(gain.shape, lay)
    return jnp.sum(jnp.where(one == iota(gain.shape, 0), gain, 0.0), axis=0, keepdims=True)


def early_kernel(
    lay, block, order, head_weight, frames, query_single, w_query, w_qp, bias_weight, w_out, d_out, pair,
    left, base, d_base, d_row, w_out_rows, w_query_rows, gains, table, pair_rows, scratch,
):
    me = lax.axis_index("row")
    for place, offset in enumerate(order):
        j = pl.multiple_of((me ^ offset) * block, block)
        pair_rows[place * block : (place + 1) * block, :] = pair[0, pl.ds(j, block), :]
    turn = [jnp.broadcast_to(frames[:, i : i + 1], (1, LANES)) for i in range(12)]
    for i in range(12):
        table[i : i + 1, :] = turn[i]
    heads, seg = lay.heads, lay.seg
    width = C + 4 * PV + LANES
    shape = (SUBLANES, LANES)
    row, lane = iota(shape, 0), iota(shape, 1)
    zero_head, one_head = head_of(shape, lay)
    zero = nn(to_lane(lay.keys, 0), w_query[...])
    one = nn(to_components(3 * lay.kp, 0, lay.kp, seg), w_qp[...])
    w_q = jnp.concatenate([zero, one], axis=0).astype(B16)
    w_query_rows[...] = w_q
    near = C + 4 * PV
    w_o = jnp.zeros((2 * LANES, w_out.shape[1]), F32)
    for h in range(heads):
        i, j = iota((2 * LANES, near), 0), iota((2 * LANES, near), 1)
        m = i - (lay.keys + h * C)
        found = (m >= 0) & (m < C) & (j == m)
        m = i - h * PV
        found = found | ((m >= 0) & (m < PV) & (j == C + 3 * PV + m))
        for c in range(3):
            m = i - (LANES + c * seg + lay.kp + h * PV)
            found = found | ((m >= 0) & (m < PV) & (j == C + 3 * m + c))
        w_o = w_o + nn(pick(found), w_out[h * width : h * width + near, :])
    w_o = w_o.astype(B16)
    w_out_rows[: 2 * LANES, :] = w_o
    for h in range(heads):
        w_out_rows[(2 + h) * LANES : (3 + h) * LANES, :] = w_out[h * width + near : (h + 1) * width, :]
    single = jnp.broadcast_to(query_single[...], (SUBLANES, query_single.shape[1]))
    rows = nt(single, w_q)
    x, y, z = unpack(rows[:, LANES:], seg)
    out = []
    for c in range(3):
        value = turn[3 * c] * x + turn[3 * c + 1] * y + turn[3 * c + 2] * z + turn[9 + c]
        out.append(value.astype(B16).astype(F32))
    points = pack(*out, seg, 0, lay.kp)
    query = rows[:, :LANES].astype(B16).astype(F32)
    is_key = lane < lay.keys
    left[:SUBLANES, :LANES] = jnp.where(is_key & (zero_head == row), query, 0.0)
    left[:SUBLANES, LANES:] = jnp.zeros(shape, F32)
    left[SUBLANES:, :LANES] = jnp.zeros(shape, F32)
    mine = jnp.where(one_head == row, points, 0.0)
    left[SUBLANES:, LANES:] = mine
    gain = gain_rows(head_weight, lay)
    gains[...] = gain
    cotangent = jnp.broadcast_to(d_out[...], (SUBLANES, d_out.shape[1]))
    d_row[...] = nt(cotangent, w_o)
    scratch[...] = jnp.zeros_like(scratch)
    scratch[:heads, :] = bias_weight[...].astype(F32)
    for h in range(heads):
        d_pair = nt(cotangent, w_out[h * width + near : (h + 1) * width, :])
        scratch[SUBLANES + h : SUBLANES + h + 1, :] = d_pair[:1, :]
    both = nt(scratch[...].astype(B16), pair_rows[...])
    square = jnp.sum(mine * mine, axis=1, keepdims=True)
    base[...] = both[:SUBLANES] - 0.5 * gain[:, :1] * square
    d_base[...] = both[SUBLANES:]


def attention_kernel(
    lay, block, order, *refs
):
    *parts, left, base, d_base, d_row, gains, table, message, features, weights, scores, gathered, squares = refs
    height = lay.rows(block)
    is_kp = in_segments((block, LANES), lay, 0, lay.kp)
    at = 0
    for part in parts:
        rows = part[...].astype(F32)
        for start in range(0, rows.shape[0], height):
            piece = rows[start : start + height]
            tile = lay.restore(piece, block)
            square = jnp.where(is_kp, tile * tile, 0.0)
            whole = square.astype(B16).astype(F32)
            gathered[at : at + block, :LANES] = piece[:block].astype(B16)
            gathered[at : at + block, LANES:] = tile.astype(B16)
            squares[at : at + block, :LANES] = whole.astype(B16)
            squares[at : at + block, LANES:] = (square - whole).astype(B16)
            at += block
    frames = [table[i : i + 1, :] for i in range(12)]
    me = lax.axis_index("row")
    heads, seg = lay.heads, lay.seg
    shape = (SUBLANES, LANES)
    row, lane = iota(shape, 0), iota(shape, 1)
    zero_head, one_head = head_of(shape, lay)
    gain = gains[...]
    queries = left[...].astype(B16)
    minus = jnp.where(is_own(shape, lay) & (one_head == row), -0.5, 0.0)
    minus = jnp.concatenate([jnp.zeros(shape, F32), minus], axis=0)
    minus = jnp.concatenate([minus, minus], axis=1).astype(B16)
    first = nt(queries, gathered[...]) + nt(minus, squares[...])
    logits = LOGIT_SCALE * (first[:SUBLANES] * (1.0 / math.sqrt(C)) + base[...] + gain[:, :1] * first[SUBLANES:])
    weight = jnp.exp(logits - jnp.max(logits, axis=1, keepdims=True))
    attention = weight / jnp.sum(weight, axis=1, keepdims=True)
    attention = jnp.where(iota(attention.shape, 0) < heads, attention, 0.0)
    attention_b = attention.astype(B16)
    sums = nn(attention_b, gathered[...])
    weights[...] = attention_b
    attended = jnp.sum(jnp.where(zero_head == row, sums[:, :LANES], 0.0), axis=0, keepdims=True)
    points = jnp.sum(jnp.where(one_head == row, sums[:, LANES:], 0.0), axis=0, keepdims=True)
    attended = jnp.broadcast_to(attended, shape)
    points = jnp.broadcast_to(points, shape)
    moved = [v - frames[9 + c] for c, v in enumerate(unpack(points, seg))]
    local = [
        frames[d] * moved[0] + frames[3 + d] * moved[1] + frames[6 + d] * moved[2] for d in range(3)
    ]
    lengths = jnp.sqrt(1.0 + (local[0] * local[0] + local[1] * local[1] + local[2] * local[2]))
    value_points = heads * PV
    is_value = (lane >= lay.keys) & (lane < lay.square)
    features[:, :LANES] = jnp.where(
        is_value, attended, jnp.where(lane < value_points, pltpu.roll(lengths, LANES - lay.kp, 1), 0.0)
    )
    features[:, LANES:] = pack(*local, seg, lay.kp, seg)
    d_zero = d_row[:, :LANES]
    share = pltpu.roll(d_zero, lay.kp, 1) / lengths
    d_local = [v + share * u for v, u in zip(unpack(d_row[:, LANES:], seg), local)]
    d_points = [
        frames[3 * c] * d_local[0] + frames[3 * c + 1] * d_local[1] + frames[3 * c + 2] * d_local[2]
        for c in range(3)
    ]
    d_points = pack(*d_points, seg, lay.kp, seg)
    d_attended = jnp.where(is_value, d_zero, 0.0)
    right = jnp.concatenate(
        [jnp.where(zero_head == row, d_attended, 0.0), jnp.where(one_head == row, d_points, 0.0)], axis=1
    )
    right = right.astype(B16)
    d_attention = nt(right, gathered[...]) + d_base[...]
    total = jnp.sum(attention * d_attention, axis=1, keepdims=True)
    score_b = (LOGIT_SCALE * attention * (d_attention - total)).astype(B16)
    scores[...] = score_b
    query0 = jnp.sum(left[:SUBLANES, :LANES], axis=0, keepdims=True)
    query1 = jnp.sum(left[SUBLANES:, LANES:], axis=0, keepdims=True)
    side = jnp.where(row == 2 * heads, jnp.broadcast_to(query0, shape) + d_attended, 0.0)
    side = side + jnp.where(row == 2 * heads + 1, jnp.broadcast_to(query1, shape) + d_points, 0.0)
    both = attention_b.astype(F32) + pltpu.roll(score_b.astype(F32), heads, 0)
    for at in range(0, both.shape[1], LANES):
        tile = jnp.where(row < 2 * heads, both[:, at : at + LANES], side).astype(B16)
        for place in range(at // block, (at + LANES) // block):
            message[me ^ order[place], :, :] = tile


def rows_kernel(
    lay, *refs
):
    gathered, pair, left, scores, features, weights, w_out_rows, w_query_rows, gains, table, sums = refs
    frames = [table[i : i + 1, :] for i in range(12)]
    heads, seg = lay.heads, lay.seg
    shape = (SUBLANES, LANES)
    row, lane = iota(shape, 0), iota(shape, 1)
    zero_head, one_head = head_of(shape, lay)
    pair_sum = nn(weights[...], pair[...])
    pairs = [jnp.broadcast_to(pair_sum[h : h + 1, :], shape) for h in range(heads)]
    result = nn(jnp.concatenate([features[...]] + pairs, axis=1).astype(B16), w_out_rows[...])
    gain = gains[...]
    score = scores[...].astype(F32)
    d_rows = nn(scores[...], gathered[...])
    d_query = jnp.sum(
        jnp.where((lane < lay.keys) & (zero_head == row), d_rows[:, :LANES], 0.0), axis=0, keepdims=True
    ) * (1.0 / math.sqrt(C))
    score_sum = jnp.sum(score, axis=1, keepdims=True)
    d_points = gain * (d_rows[:, LANES:] - score_sum * left[SUBLANES:, LANES:])
    d_points = jnp.sum(jnp.where(one_head == row, d_points, 0.0), axis=0, keepdims=True)
    x, y, z = unpack(jnp.broadcast_to(d_points, shape), seg)
    local = [frames[d] * x + frames[3 + d] * y + frames[6 + d] * z for d in range(3)]
    local = pack(*local, seg, 0, lay.kp)
    both = jnp.concatenate([jnp.broadcast_to(d_query, shape), local], axis=1).astype(B16)
    grad = nn(both, w_query_rows[...])
    sums[...] = jnp.concatenate([result, grad], axis=1)


def owner_kernel(lay, near, arrived, turned, points, weights, gains, result):
    heads, seg = lay.heads, lay.seg
    count = arrived.shape[0]
    block = points.shape[0]
    took = arrived[...].astype(F32)
    shape = (SUBLANES, LANES)
    whole = (count, SUBLANES, LANES)
    per = LANES // block
    place = ((iota(whole, 0) ^ lax.axis_index("row")) // near) % per
    mine = took
    for part in range(1, per):
        mine = jnp.where(place == part, pltpu.roll(took, LANES - part * block, 2), mine)
    row = iota(shape, 0)
    zero_head, one_head = head_of(shape, lay)
    lane = iota(shape, 1)
    from_score0 = lane < lay.keys
    from_score1 = in_segments(shape, lay, 0, lay.kp)
    keep0 = (zero_head >= 0) & (jnp.where(from_score0, zero_head + heads, zero_head) == row)
    keep1 = (one_head >= 0) & (jnp.where(from_score1, one_head + heads, one_head) == row)
    side0 = jnp.where(keep0[None], jnp.broadcast_to(took[:, 2 * heads : 2 * heads + 1, :], whole), 0.0)
    side1 = jnp.where(keep1[None], jnp.broadcast_to(took[:, 2 * heads + 1 : 2 * heads + 2, :], whole), 0.0)
    ones = jnp.broadcast_to(jnp.where(keep1 & from_score1, 1.0, 0.0)[None], whole)
    right = jnp.concatenate([side0, side1, ones], axis=2).reshape(count * SUBLANES, 3 * LANES).astype(B16)
    moved = jnp.transpose(mine.reshape(count * SUBLANES, LANES)).astype(B16)
    both = nn(moved, right)[:block]
    small = (block, LANES)
    lane = iota(small, 1)
    tile0 = jnp.where(lane < lay.keys, both[:, :LANES] * (1.0 / math.sqrt(C)), both[:, :LANES])
    gain = gain_lanes(gains[...], lay)
    own = points[...]
    tile1 = both[:, LANES : 2 * LANES]
    kp_part = gain * (tile1 - both[:, 2 * LANES :] * own)
    tile1 = jnp.where(in_segments(small, lay, 0, lay.kp), kp_part, tile1)
    turn = turned[...]
    x, y, z = unpack(tile1, seg)
    local = []
    for d in range(3):
        r = [turn[:, 3 * c + d : 3 * c + d + 1] for c in range(3)]
        local.append(r[0] * x + r[1] * y + r[2] * z)
    tile1 = pack(*local, seg, 0, seg)
    rows = jnp.concatenate([tile0, tile1], axis=1).astype(B16)
    result[...] = nn(rows, weights[...])


VMEM = pl.BlockSpec(memory_space=pltpu.VMEM)
HBM = pl.BlockSpec(memory_space=pltpu.HBM)


def call(body, outs, args, fresh=0, scratch=(), flops=1000000):
    size = sum(math.prod(v.shape) * v.dtype.itemsize for v in list(args) + list(outs))

    def kernel(*refs):
        if fresh:
            *refs, sems = refs
            held = refs[len(refs) - fresh :]
            copies = [pltpu.make_async_copy(refs[i], held[i], sems.at[i]) for i in range(fresh)]
            for copy in copies:
                copy.start()
            for copy in copies:
                copy.wait()
            refs = list(held) + list(refs[fresh : len(refs) - fresh])
        body(*refs)

    own = [pltpu.VMEM(v.shape, v.dtype) for v in args[:fresh]]
    return pl.pallas_call(
        kernel,
        out_shape=tuple(outs),
        in_specs=[HBM] * fresh + [VMEM] * (len(args) - fresh),
        out_specs=tuple([VMEM] * len(outs)),
        scratch_shapes=list(scratch) + own + ([pltpu.SemaphoreType.DMA((fresh,))] if fresh else []),
        compiler_params=pltpu.CompilerParams(vmem_limit_bytes=(16 << 20) + 6 * size),
        cost_estimate=pl.CostEstimate(flops=flops, bytes_accessed=size, transcendentals=0),
    )(*[pltpu.with_memory_space_constraint(v, pltpu.HBM) for v in args[:fresh]], *args[fresh:])


def shape_of(*dims, dtype=F32):
    return jax.ShapeDtypeStruct(dims, dtype)


def shards(
    query_single, key_single, pair, query_frames, key_frames, w_query, w_key, w_value, w_query_points, w_key_points,
    w_value_points, head_weight, bias_weight, w_out, d_out,
):
    lay = Layout(head_weight.shape[0])
    count = lax.axis_size("row")
    block, width = key_single.shape
    total = count * block
    near = 1
    while 4 * near * near <= count:
        near *= 2
    assert count & (count - 1) == 0

    def exchange(value, mask):
        return lax.ppermute(value, "row", [(i, i ^ mask) for i in range(count)])

    packed, own, weights, turned = call(
        functools.partial(key_kernel, lay),
        [
            shape_of(lay.rows(block), LANES, dtype=B16), shape_of(block, LANES),
            shape_of(2 * LANES, width, dtype=B16), shape_of(block, LANES),
        ],
        [key_single, key_frames, w_key.T, w_value.T, w_key_points.T, w_value_points.T],
        6,
    )
    offsets = list(range(0, count, near))
    line = jnp.concatenate([packed] + [exchange(packed, mask) for mask in offsets[1:]], axis=0)
    parts = [line] + [exchange(line, m) for m in range(1, near)]
    order = [m ^ o for m in range(near) for o in offsets]

    left, base, d_base, d_row, w_out_rows, w_query_rows, gains, table, pair_rows = call(
        functools.partial(early_kernel, lay, block, order),
        [
            shape_of(ROWS16, 2 * LANES), shape_of(SUBLANES, total), shape_of(SUBLANES, total),
            shape_of(SUBLANES, 2 * LANES), shape_of((2 + lay.heads) * LANES, width, dtype=B16),
            shape_of(2 * LANES, width, dtype=B16), shape_of(SUBLANES, LANES), shape_of(ROWS16, LANES),
            shape_of(total, LANES, dtype=B16),
        ],
        [
            head_weight.reshape(1, -1), query_frames.T, query_single, w_query.T, w_query_points.T, bias_weight, w_out,
            d_out, pair,
        ],
        9,
        [pltpu.VMEM((ROWS16, LANES), F32)],
    )
    message, features, weight_rows, scores, gathered = call(
        functools.partial(attention_kernel, lay, block, order),
        [
            shape_of(count, SUBLANES, LANES, dtype=B16), shape_of(SUBLANES, 2 * LANES),
            shape_of(SUBLANES, total, dtype=B16), shape_of(SUBLANES, total, dtype=B16),
            shape_of(total, 2 * LANES, dtype=B16),
        ],
        parts + [left, base, d_base, d_row, gains, table],
        scratch=[pltpu.VMEM((total, 2 * LANES), B16)],
    )
    arrived = lax.all_to_all(message, "row", 0, 0, tiled=True)
    (sums,) = call(
        functools.partial(rows_kernel, lay),
        [shape_of(SUBLANES, 2 * width)],
        [gathered, pair_rows, left, scores, features, weight_rows, w_out_rows, w_query_rows, gains, table],
    )
    swap = [(i, (i + 1) % 2) for i in range(2)]
    sums = sums[:1]
    sums = sums + lax.ppermute(sums, "head", swap)
    output = sums[:, :width].astype(B16)
    grad_query = sums[:, width:]
    (part,) = call(
        functools.partial(owner_kernel, lay, near),
        [shape_of(block, width)],
        [arrived, turned, own, weights, gains],
    )
    grad_keys = part + lax.ppermute(part, "head", swap)
    return (output, grad_query, grad_keys)


def solution(mesh):
    return jax.shard_map(
        shards,
        mesh=mesh,
        in_specs=(
            P("row", None),
            P("row", None),
            P("row", None, None),
            P(None, "row"),
            P(None, "row"),
            P(None, "head"),
            P(None, "head"),
            P(None, "head"),
            P(None, "head"),
            P(None, "head"),
            P(None, "head"),
            P("head"),
            P("head", None),
            P("head", None),
            P("row", None),
        ),
        out_specs=(P("row", None), P("row", None), P("row", None)),
        check_vma=False,
    )
```

```python
import functools
import math

import jax
import jax.numpy as jnp
from jax import lax
from jax.experimental import pallas as pl
from jax.experimental.pallas import tpu as pltpu
from jax.sharding import PartitionSpec as P

C = 16
PQ = 4
PV = 8
LANES = 128
SUBLANES = 8
ROWS16 = 16
LOGIT_SCALE = math.sqrt(1.0 / 3.0)
POINT_SCALE = math.sqrt(2.0 / (9.0 * PQ))
F32 = jnp.float32
B16 = jnp.bfloat16


class Layout:
    def __init__(self, heads):
        self.heads = heads
        self.keys = heads * C
        self.square = 2 * heads * C
        self.kp = heads * PQ
        self.seg = heads * (PQ + PV)
        assert self.square + 3 * heads <= LANES and 3 * self.seg <= LANES and 2 * heads + 2 <= SUBLANES


def nn(a, b, precision=None):
    return lax.dot_general(a, b, (((1,), (0,)), ((), ())), precision=precision, preferred_element_type=F32)


def nt(a, b):
    return lax.dot_general(a, b, (((1,), (1,)), ((), ())), preferred_element_type=F32)


def iota(shape, dim):
    return lax.broadcasted_iota(jnp.int32, shape, dim)


def pick(condition):
    return jnp.where(condition, 1.0, 0.0).astype(B16)


def to_lane(rows, offset):
    j, i = iota((LANES, rows), 0), iota((LANES, rows), 1)
    return pick(j == i + offset)


def to_components(rows, offset, points, seg):
    j, i = iota((LANES, rows), 0), iota((LANES, rows), 1)
    found = j < 0
    for c in range(3):
        m = j - (c * seg + offset)
        found = found | ((m >= 0) & (m < points) & (i == 3 * m + c))
    return pick(found)


def unpack(tile, seg):
    return tile, pltpu.roll(tile, LANES - seg, 1), pltpu.roll(tile, LANES - 2 * seg, 1)


def pack(x, y, z, seg, low, high):
    lane = iota(x.shape, 1)
    keep = (lane >= low) & (lane < high)
    x, y, z = (jnp.where(keep, v, 0.0) for v in (x, y, z))
    return x + pltpu.roll(y, seg, 1) + pltpu.roll(z, 2 * seg, 1)


def head_of(shape, lay):
    lane = iota(shape, 1)
    zero = jnp.full(shape, -1, jnp.int32)
    one = jnp.full(shape, -1, jnp.int32)
    for h in range(lay.heads):
        for base in (0, lay.keys):
            zero = jnp.where((lane >= base + h * C) & (lane < base + (h + 1) * C), h, zero)
        for c in range(3):
            k = c * lay.seg + h * PQ
            v = c * lay.seg + lay.kp + h * PV
            one = jnp.where((lane >= k) & (lane < k + PQ), h, one)
            one = jnp.where((lane >= v) & (lane < v + PV), h, one)
    return zero, one


def in_segments(shape, lay, low, high):
    lane = iota(shape, 1)
    found = lane < 0
    for c in range(3):
        found = found | ((lane >= c * lay.seg + low) & (lane < c * lay.seg + high))
    return found


def key_kernel(lay, head_weight, key_single, frames, w_key, w_value, w_kp, w_vp, packed, parcel, turned, gains):
    seg = lay.seg
    zero = nn(to_lane(lay.keys, 0), w_key[...]) + nn(to_lane(lay.keys, lay.keys), w_value[...])
    one = nn(to_components(3 * lay.kp, 0, lay.kp, seg), w_kp[...]) + nn(
        to_components(3 * (seg - lay.kp), lay.kp, seg - lay.kp, seg), w_vp[...]
    )
    w_all = jnp.concatenate([zero, one], axis=0).astype(B16)
    parcel[: 2 * LANES, :] = w_all
    rows = nt(key_single[...], w_all)
    turn = jnp.transpose(frames[...])
    turned[:, : turn.shape[1]] = turn
    x, y, z = unpack(rows[:, LANES:], seg)
    out = []
    for c in range(3):
        r = [turn[:, 3 * c + d : 3 * c + d + 1] for d in range(3)]
        out.append((r[0] * x + r[1] * y + r[2] * z + turn[:, 9 + c : 10 + c]).astype(B16).astype(F32))
    points = pack(*out, seg, 0, seg)
    square = out[0] * out[0] + out[1] * out[1] + out[2] * out[2]
    square = jnp.where(iota(square.shape, 1) < lay.kp, square, 0.0)
    i, j = iota((LANES, LANES), 0), iota((LANES, LANES), 1)
    chosen = j < 0
    for h in range(lay.heads):
        for piece in range(3):
            lane = lay.square + piece * lay.heads + h
            chosen = chosen | ((j == lane) & (i >= h * PQ) & (i < (h + 1) * PQ))
    total = nn(square, jnp.where(chosen, 1.0, 0.0), lax.Precision.HIGHEST)
    first = total.astype(B16).astype(F32)
    second = (total - first).astype(B16).astype(F32)
    third = total - first - second
    lane = iota(total.shape, 1)
    piece = jnp.where(
        lane < lay.square + lay.heads, first, jnp.where(lane < lay.square + 2 * lay.heads, second, third)
    )
    tile0 = jnp.where(lane < lay.square, rows[:, :LANES], piece).astype(B16)
    tile1 = points.astype(B16)
    packed[:, :LANES] = tile0
    packed[:, LANES:] = tile1
    block = tile1.shape[0]
    parcel[2 * LANES :, :] = jnp.zeros((block + ROWS16, parcel.shape[1]), B16)
    parcel[2 * LANES : 2 * LANES + block, :LANES] = tile1
    gain = gain_rows(head_weight, lay)
    gains[...] = gain
    gain = jnp.broadcast_to(gain_lanes(gain, lay), (ROWS16, LANES))
    first = gain.astype(B16).astype(F32)
    second = (gain - first).astype(B16).astype(F32)
    row = iota(gain.shape, 0)
    pieces = jnp.where(row == 0, first, jnp.where(row == 1, second, jnp.where(row == 2, gain - first - second, 0.0)))
    parcel[2 * LANES + block :, :LANES] = pieces.astype(B16)


def gain_rows(head_weight, lay):
    row = iota((SUBLANES, LANES), 0)
    raw = jnp.zeros((SUBLANES, LANES), F32)
    for h in range(lay.heads):
        raw = jnp.where(row == h, jnp.broadcast_to(head_weight[:, h : h + 1], raw.shape), raw)
    gain = (jnp.maximum(raw, 0.0) + jnp.log1p(jnp.exp(-jnp.abs(raw)))) * POINT_SCALE
    return jnp.where(row < lay.heads, gain, 0.0)


def gain_lanes(gain, lay):
    _, one = head_of(gain.shape, lay)
    return jnp.sum(jnp.where(one == iota(gain.shape, 0), gain, 0.0), axis=0, keepdims=True)


def early_kernel(
    lay, block, order, frames, query_single, w_query, w_qp, bias_weight, w_out, d_out, pair, gains,
    left, base, d_base, d_row, w_out_rows, w_query_rows, table, pair_rows, scratch,
):
    me = lax.axis_index("row")
    for place, offset in enumerate(order):
        j = pl.multiple_of((me ^ offset) * block, block)
        pair_rows[place * block : (place + 1) * block, :] = pair[0, pl.ds(j, block), :]
    turn = [jnp.broadcast_to(frames[:, i : i + 1], (1, LANES)) for i in range(12)]
    for i in range(12):
        table[i : i + 1, :] = turn[i]
    heads, seg = lay.heads, lay.seg
    width = C + 4 * PV + LANES
    shape = (SUBLANES, LANES)
    row, lane = iota(shape, 0), iota(shape, 1)
    zero_head, one_head = head_of(shape, lay)
    zero = nn(to_lane(lay.keys, 0), w_query[...])
    one = nn(to_components(3 * lay.kp, 0, lay.kp, seg), w_qp[...])
    w_q = jnp.concatenate([zero, one], axis=0).astype(B16)
    w_query_rows[...] = w_q
    near = C + 4 * PV
    w_o = jnp.zeros((2 * LANES, w_out.shape[1]), F32)
    for h in range(heads):
        i, j = iota((2 * LANES, near), 0), iota((2 * LANES, near), 1)
        m = i - (lay.keys + h * C)
        found = (m >= 0) & (m < C) & (j == m)
        m = i - h * PV
        found = found | ((m >= 0) & (m < PV) & (j == C + 3 * PV + m))
        for c in range(3):
            m = i - (LANES + c * seg + lay.kp + h * PV)
            found = found | ((m >= 0) & (m < PV) & (j == C + 3 * m + c))
        w_o = w_o + nn(pick(found), w_out[h * width : h * width + near, :])
    w_o = w_o.astype(B16)
    w_out_rows[: 2 * LANES, :] = w_o
    for h in range(heads):
        w_out_rows[(2 + h) * LANES : (3 + h) * LANES, :] = w_out[h * width + near : (h + 1) * width, :]
    single = jnp.broadcast_to(query_single[...], (SUBLANES, query_single.shape[1]))
    rows = nt(single, w_q)
    x, y, z = unpack(rows[:, LANES:], seg)
    out = []
    for c in range(3):
        value = turn[3 * c] * x + turn[3 * c + 1] * y + turn[3 * c + 2] * z + turn[9 + c]
        out.append(value.astype(B16).astype(F32))
    points = pack(*out, seg, 0, lay.kp)
    query = rows[:, :LANES].astype(B16).astype(F32)
    is_key = lane < lay.keys
    left[:SUBLANES, :LANES] = jnp.where(is_key & (zero_head == row), query, 0.0)
    left[:SUBLANES, LANES:] = jnp.zeros(shape, F32)
    minus = lane < 0
    for piece in range(3):
        minus = minus | (lane == lay.square + piece * heads + row)
    left[SUBLANES:, :LANES] = jnp.where(minus & (row < heads), -0.5, 0.0)
    mine = jnp.where(one_head == row, points, 0.0)
    left[SUBLANES:, LANES:] = mine
    gain = gains[...]
    cotangent = jnp.broadcast_to(d_out[...], (SUBLANES, d_out.shape[1]))
    d_row[...] = nt(cotangent, w_o)
    scratch[...] = jnp.zeros_like(scratch)
    scratch[:heads, :] = bias_weight[...].astype(F32)
    for h in range(heads):
        d_pair = nt(cotangent, w_out[h * width + near : (h + 1) * width, :])
        scratch[SUBLANES + h : SUBLANES + h + 1, :] = d_pair[:1, :]
    both = nt(scratch[...].astype(B16), pair_rows[...])
    square = jnp.sum(mine * mine, axis=1, keepdims=True)
    base[...] = both[:SUBLANES] - 0.5 * gain[:, :1] * square
    d_base[...] = both[SUBLANES:]


def spread(weights, parts):
    total, at = 0.0, 0
    for part in parts:
        total = total + nn(weights[:, at : at + part.shape[0]], part[...])
        at += part.shape[0]
    return total


def attention_kernel(
    lay, block, order, *refs
):
    *parts, left, base, d_base, d_row, gains, table, message, features, weights, scores = refs
    frames = [table[i : i + 1, :] for i in range(12)]
    me = lax.axis_index("row")
    heads, seg = lay.heads, lay.seg
    shape = (SUBLANES, LANES)
    row, lane = iota(shape, 0), iota(shape, 1)
    zero_head, one_head = head_of(shape, lay)
    gain = gains[...]
    queries = left[...].astype(B16)
    first = jnp.concatenate([nt(queries, part[...]) for part in parts], axis=1)
    logits = LOGIT_SCALE * (first[:SUBLANES] * (1.0 / math.sqrt(C)) + base[...] + gain[:, :1] * first[SUBLANES:])
    weight = jnp.exp(logits - jnp.max(logits, axis=1, keepdims=True))
    attention = weight / jnp.sum(weight, axis=1, keepdims=True)
    attention = jnp.where(iota(attention.shape, 0) < heads, attention, 0.0)
    attention_b = attention.astype(B16)
    sums = spread(attention_b, parts)
    weights[...] = attention_b
    attended = jnp.sum(jnp.where(zero_head == row, sums[:, :LANES], 0.0), axis=0, keepdims=True)
    points = jnp.sum(jnp.where(one_head == row, sums[:, LANES:], 0.0), axis=0, keepdims=True)
    attended = jnp.broadcast_to(attended, shape)
    points = jnp.broadcast_to(points, shape)
    moved = [v - frames[9 + c] for c, v in enumerate(unpack(points, seg))]
    local = [
        frames[d] * moved[0] + frames[3 + d] * moved[1] + frames[6 + d] * moved[2] for d in range(3)
    ]
    lengths = jnp.sqrt(1.0 + (local[0] * local[0] + local[1] * local[1] + local[2] * local[2]))
    value_points = heads * PV
    is_value = (lane >= lay.keys) & (lane < lay.square)
    features[:, :LANES] = jnp.where(
        is_value, attended, jnp.where(lane < value_points, pltpu.roll(lengths, LANES - lay.kp, 1), 0.0)
    )
    features[:, LANES:] = pack(*local, seg, lay.kp, seg)
    d_zero = d_row[:, :LANES]
    share = pltpu.roll(d_zero, lay.kp, 1) / lengths
    d_local = [v + share * u for v, u in zip(unpack(d_row[:, LANES:], seg), local)]
    d_points = [
        frames[3 * c] * d_local[0] + frames[3 * c + 1] * d_local[1] + frames[3 * c + 2] * d_local[2]
        for c in range(3)
    ]
    d_points = pack(*d_points, seg, lay.kp, seg)
    d_attended = jnp.where(is_value, d_zero, 0.0)
    right = jnp.concatenate(
        [jnp.where(zero_head == row, d_attended, 0.0), jnp.where(one_head == row, d_points, 0.0)], axis=1
    )
    right = right.astype(B16)
    d_attention = jnp.concatenate([nt(right, part[...]) for part in parts], axis=1) + d_base[...]
    total = jnp.sum(attention * d_attention, axis=1, keepdims=True)
    score_b = (LOGIT_SCALE * attention * (d_attention - total)).astype(B16)
    scores[...] = score_b
    query0 = jnp.sum(left[:SUBLANES, :LANES], axis=0, keepdims=True)
    query1 = jnp.sum(left[SUBLANES:, LANES:], axis=0, keepdims=True)
    side = jnp.where(row == 2 * heads, jnp.broadcast_to(query0, shape) + d_attended, 0.0)
    side = side + jnp.where(row == 2 * heads + 1, jnp.broadcast_to(query1, shape) + d_points, 0.0)
    both = attention_b.astype(F32) + pltpu.roll(score_b.astype(F32), heads, 0)
    for at in range(0, both.shape[1], LANES):
        tile = jnp.where(row < 2 * heads, both[:, at : at + LANES], side).astype(B16)
        for place in range(at // block, (at + LANES) // block):
            for core in range(2):
                message[(me ^ order[place]) * 2 + core, :, :] = tile


def rows_kernel(
    lay, *refs
):
    *parts, pair, left, scores, features, weights, w_out_rows, w_query_rows, gains, table, sums = refs
    frames = [table[i : i + 1, :] for i in range(12)]
    heads, seg = lay.heads, lay.seg
    shape = (SUBLANES, LANES)
    row, lane = iota(shape, 0), iota(shape, 1)
    zero_head, one_head = head_of(shape, lay)
    pair_sum = nn(weights[...], pair[...])
    pairs = [jnp.broadcast_to(pair_sum[h : h + 1, :], shape) for h in range(heads)]
    result = nn(jnp.concatenate([features[...]] + pairs, axis=1).astype(B16), w_out_rows[...])
    gain = gains[...]
    score = scores[...].astype(F32)
    d_rows = spread(scores[...], parts)
    d_query = jnp.sum(
        jnp.where((lane < lay.keys) & (zero_head == row), d_rows[:, :LANES], 0.0), axis=0, keepdims=True
    ) * (1.0 / math.sqrt(C))
    score_sum = jnp.sum(score, axis=1, keepdims=True)
    d_points = gain * (d_rows[:, LANES:] - score_sum * left[SUBLANES:, LANES:])
    d_points = jnp.sum(jnp.where(one_head == row, d_points, 0.0), axis=0, keepdims=True)
    x, y, z = unpack(jnp.broadcast_to(d_points, shape), seg)
    local = [frames[d] * x + frames[3 + d] * y + frames[6 + d] * z for d in range(3)]
    local = pack(*local, seg, 0, lay.kp)
    both = jnp.concatenate([jnp.broadcast_to(d_query, shape), local], axis=1).astype(B16)
    grad = nn(both, w_query_rows[...])
    sums[...] = jnp.concatenate([result, grad], axis=1)


def owner_kernel(lay, near, arrived, turned, parcel, other, result):
    heads, seg = lay.heads, lay.seg
    count = arrived.shape[0] // 2
    block = turned.shape[0]
    shape = (SUBLANES, LANES)
    whole = (count, SUBLANES, LANES)
    per = LANES // block
    place = ((iota(whole, 0) ^ lax.axis_index("row")) // near) % per
    row = iota(shape, 0)
    zero_head, one_head = head_of(shape, lay)
    lane = iota(shape, 1)
    from_score0 = lane < lay.keys
    from_score1 = in_segments(shape, lay, 0, lay.kp)
    keep0 = (zero_head >= 0) & (jnp.where(from_score0, zero_head + heads, zero_head) == row)
    keep1 = (one_head >= 0) & (jnp.where(from_score1, one_head + heads, one_head) == row)
    ones = jnp.broadcast_to(jnp.where(keep1 & from_score1, 1.0, 0.0)[None], whole)
    turn = turned[...]
    small = (block, LANES)
    is_kp = in_segments(small, lay, 0, lay.kp)
    is_key = iota(small, 1) < lay.keys
    me = lax.axis_index("head")
    total = None
    for core, held in ((me, parcel), (1 - me, other)):
        took = jnp.concatenate([arrived[pl.ds(q * 2 + core, 1)] for q in range(count)], axis=0).astype(F32)
        mine = took
        for part in range(1, per):
            mine = jnp.where(place == part, pltpu.roll(took, LANES - part * block, 2), mine)
        side0 = jnp.where(keep0[None], jnp.broadcast_to(took[:, 2 * heads : 2 * heads + 1, :], whole), 0.0)
        side1 = jnp.where(keep1[None], jnp.broadcast_to(took[:, 2 * heads + 1 : 2 * heads + 2, :], whole), 0.0)
        right = jnp.concatenate([side0, side1, ones], axis=2).reshape(count * SUBLANES, 3 * LANES).astype(B16)
        moved = jnp.transpose(mine.reshape(count * SUBLANES, LANES)).astype(B16)
        both = nn(moved, right)[:block]
        tile0 = jnp.where(is_key, both[:, :LANES] * (1.0 / math.sqrt(C)), both[:, :LANES])
        pieces = held[2 * LANES + block :, :LANES].astype(F32)
        gain = pieces[0:1] + pieces[1:2] + pieces[2:3]
        own = held[2 * LANES : 2 * LANES + block, :LANES].astype(F32)
        tile1 = both[:, LANES : 2 * LANES]
        tile1 = jnp.where(is_kp, gain * (tile1 - both[:, 2 * LANES :] * own), tile1)
        x, y, z = unpack(tile1, seg)
        local = []
        for d in range(3):
            r = [turn[:, 3 * c + d : 3 * c + d + 1] for c in range(3)]
            local.append(r[0] * x + r[1] * y + r[2] * z)
        tile1 = pack(*local, seg, 0, seg)
        rows = jnp.concatenate([tile0, tile1], axis=1).astype(B16)
        part = nn(rows, held[: 2 * LANES, :])
        total = part if total is None else total + part
    result[...] = total


def finish_kernel(own, other, output, grad_query):
    width = output.shape[1]
    total = own[...] + other[...]
    output[...] = total[:1, :width].astype(output.dtype)
    grad_query[...] = total[:1, width:]


VMEM = pl.BlockSpec(memory_space=pltpu.VMEM)
HBM = pl.BlockSpec(memory_space=pltpu.HBM)


def call(body, outs, args, fresh=0, scratch=(), flops=1000000, last=False):
    size = sum(math.prod(v.shape) * v.dtype.itemsize for v in list(args) + list(outs))

    def kernel(*refs):
        if fresh:
            *refs, sems = refs
            held = refs[len(refs) - fresh :]
            copies = [pltpu.make_async_copy(refs[i], held[i], sems.at[i]) for i in range(fresh)]
            for copy in copies:
                copy.start()
            for copy in copies:
                copy.wait()
            refs = list(held) + list(refs[fresh : len(refs) - fresh])
        body(*refs)

    own = [pltpu.VMEM(v.shape, v.dtype) for v in args[:fresh]]
    return pl.pallas_call(
        kernel,
        out_shape=tuple(outs),
        in_specs=[HBM] * fresh + [VMEM] * (len(args) - fresh),
        out_specs=tuple([pl.BlockSpec() if last else VMEM] * len(outs)),
        scratch_shapes=list(scratch) + own + ([pltpu.SemaphoreType.DMA((fresh,))] if fresh else []),
        compiler_params=pltpu.CompilerParams(vmem_limit_bytes=(16 << 20) + 6 * size),
        cost_estimate=pl.CostEstimate(flops=flops, bytes_accessed=size, transcendentals=0),
    )(*[pltpu.with_memory_space_constraint(v, pltpu.HBM) for v in args[:fresh]], *args[fresh:])


def shape_of(*dims, dtype=F32):
    return jax.ShapeDtypeStruct(dims, dtype)


def shards(
    query_single, key_single, pair, query_frames, key_frames, w_query, w_key, w_value, w_query_points, w_key_points,
    w_value_points, head_weight, bias_weight, w_out, d_out,
):
    lay = Layout(head_weight.shape[0])
    count = lax.axis_size("row")
    block, width = key_single.shape
    total = count * block
    near = 1
    while 4 * near * near <= count:
        near *= 2
    assert count & (count - 1) == 0

    def exchange(value, mask):
        return lax.ppermute(value, "row", [(i, i ^ mask) for i in range(count)])

    packed, parcel, turned, gains = call(
        functools.partial(key_kernel, lay),
        [
            shape_of(block, 2 * LANES, dtype=B16), shape_of(2 * LANES + block + ROWS16, width, dtype=B16),
            shape_of(block, LANES), shape_of(SUBLANES, LANES),
        ],
        [
            head_weight.reshape(1, -1), key_single, key_frames, w_key.T, w_value.T, w_key_points.T, w_value_points.T,
        ],
        7,
    )
    offsets = [0] + list(range(count - near, 0, -near))
    line = jnp.concatenate([packed] + [exchange(packed, mask) for mask in offsets[1:]], axis=0)
    planes = [0] + list(range(near - 1, 0, -1))
    parts = [line] + [exchange(line, m) for m in planes[1:]]
    order = [m ^ o for m in planes for o in offsets]

    swap = [(i, (i + 1) % 2) for i in range(2)]
    other = lax.ppermute(parcel, "head", swap)
    left, base, d_base, d_row, w_out_rows, w_query_rows, table, pair_rows = call(
        functools.partial(early_kernel, lay, block, order),
        [
            shape_of(ROWS16, 2 * LANES), shape_of(SUBLANES, total), shape_of(SUBLANES, total),
            shape_of(SUBLANES, 2 * LANES), shape_of((2 + lay.heads) * LANES, width, dtype=B16),
            shape_of(2 * LANES, width, dtype=B16), shape_of(ROWS16, LANES),
            shape_of(total, LANES, dtype=B16),
        ],
        [
            query_frames.T, query_single, w_query.T, w_query_points.T, bias_weight, w_out, d_out, pair, gains,
        ],
        8,
        [pltpu.VMEM((ROWS16, LANES), F32)],
    )
    message, features, weight_rows, scores = call(
        functools.partial(attention_kernel, lay, block, order),
        [
            shape_of(2 * count, SUBLANES, LANES, dtype=B16), shape_of(SUBLANES, 2 * LANES),
            shape_of(SUBLANES, total, dtype=B16), shape_of(SUBLANES, total, dtype=B16),
        ],
        parts + [left, base, d_base, d_row, gains, table],
    )
    arrived = lax.all_to_all(message, ("row", "head"), 0, 0, tiled=True)
    (sums,) = call(
        functools.partial(rows_kernel, lay),
        [shape_of(SUBLANES, 2 * width)],
        parts + [pair_rows, left, scores, features, weight_rows, w_out_rows, w_query_rows, gains, table],
    )
    output, grad_query = call(
        finish_kernel,
        [shape_of(1, width, dtype=B16), shape_of(1, width)],
        [sums, lax.ppermute(sums, "head", swap)],
        last=True,
    )
    (grad_keys,) = call(
        functools.partial(owner_kernel, lay, near),
        [shape_of(block, width)],
        [arrived, turned, parcel, other],
        last=True,
    )
    return (output, grad_query, grad_keys)


def solution(mesh):
    return jax.shard_map(
        shards,
        mesh=mesh,
        in_specs=(
            P("row", None),
            P("row", None),
            P("row", None, None),
            P(None, "row"),
            P(None, "row"),
            P(None, "head"),
            P(None, "head"),
            P(None, "head"),
            P(None, "head"),
            P(None, "head"),
            P(None, "head"),
            P("head"),
            P("head", None),
            P("head", None),
            P("row", None),
        ),
        out_specs=(P("row", None), P("row", None), P("row", None)),
        check_vma=False,
    )
```

```python
import functools
import math

import jax
import jax.numpy as jnp
from jax import lax
from jax.experimental import pallas as pl
from jax.experimental.pallas import tpu as pltpu
from jax.sharding import PartitionSpec as P

C = 16
PQ = 4
PV = 8
LANES = 128
SUBLANES = 8
ROWS16 = 16
LOGIT_SCALE = math.sqrt(1.0 / 3.0)
POINT_SCALE = math.sqrt(2.0 / (9.0 * PQ))
F32 = jnp.float32
B16 = jnp.bfloat16


class Layout:
    def __init__(self, heads):
        self.heads = heads
        self.base = heads * C
        self.kp = heads * PQ
        self.vp = heads * PV
        self.square = self.base + 3 * self.kp
        assert self.square + self.kp <= LANES and self.base + 3 * self.vp <= LANES
        assert 2 * heads + 2 <= SUBLANES and PQ == 4


def nn(a, b, precision=None):
    return lax.dot_general(a, b, (((1,), (0,)), ((), ())), precision=precision, preferred_element_type=F32)


def nt(a, b):
    return lax.dot_general(a, b, (((1,), (1,)), ((), ())), preferred_element_type=F32)


def iota(shape, dim):
    return lax.broadcasted_iota(jnp.int32, shape, dim)


def pick(condition):
    return jnp.where(condition, 1.0, 0.0).astype(B16)


def to_lane(rows, offset):
    j, i = iota((LANES, rows), 0), iota((LANES, rows), 1)
    return pick(j == i + offset)


def to_components(rows, offset, points, seg):
    j, i = iota((LANES, rows), 0), iota((LANES, rows), 1)
    found = j < 0
    for c in range(3):
        m = j - (c * seg + offset)
        found = found | ((m >= 0) & (m < points) & (i == 3 * m + c))
    return pick(found)


def unpack(tile, seg):
    return tile, pltpu.roll(tile, LANES - seg, 1), pltpu.roll(tile, LANES - 2 * seg, 1)


def pack(parts, seg, base):
    lane = iota(parts[0].shape, 1)
    keep = (lane >= base) & (lane < base + seg)
    x, y, z = (jnp.where(keep, v, 0.0) for v in parts)
    return x + pltpu.roll(y, seg, 1) + pltpu.roll(z, 2 * seg, 1)


def head_of(shape, lay):
    lane = iota(shape, 1)
    zero = jnp.full(shape, -1, jnp.int32)
    one = jnp.full(shape, -1, jnp.int32)
    for h in range(lay.heads):
        same = (lane >= h * C) & (lane < (h + 1) * C)
        zero, one = jnp.where(same, h, zero), jnp.where(same, h, one)
        for c in range(3):
            k = lay.base + c * lay.kp + h * PQ
            v = lay.base + c * lay.vp + h * PV
            zero = jnp.where((lane >= k) & (lane < k + PQ), h, zero)
            one = jnp.where((lane >= v) & (lane < v + PV), h, one)
    return zero, one


def turned_by(frames, vectors):
    x, y, z = vectors
    return [frames[3 * c] * x + frames[3 * c + 1] * y + frames[3 * c + 2] * z for c in range(3)]


def turned_back(frames, vectors):
    x, y, z = vectors
    return [frames[d] * x + frames[3 + d] * y + frames[6 + d] * z for d in range(3)]


def key_kernel(lay, head_weight, key_single, frames, w_key, w_value, w_kp, w_vp, packed, parcel, turned, gains):
    kp, vp, base = lay.kp, lay.vp, lay.base
    zero = nn(to_lane(base, 0), w_key[...]) + nn(to_components(3 * kp, base, kp, kp), w_kp[...])
    one = nn(to_lane(base, 0), w_value[...]) + nn(to_components(3 * vp, base, vp, vp), w_vp[...])
    w_all = jnp.concatenate([zero, one], axis=0).astype(B16)
    rows = nt(key_single[...], w_all)
    turn = jnp.transpose(frames[...])
    columns = [turn[:, i : i + 1] for i in range(12)]
    tiles = []
    lane = iota((rows.shape[0], LANES), 1)
    for tile, seg in ((rows[:, :LANES], kp), (rows[:, LANES:], vp)):
        moved = turned_by(columns, unpack(tile, seg))
        moved = [(v + columns[9 + c]).astype(B16).astype(F32) for c, v in enumerate(moved)]
        if seg == kp:
            square = moved[0] * moved[0] + moved[1] * moved[1] + moved[2] * moved[2]
        tiles.append(jnp.where(lane < base, tile, 0.0) + pack(moved, seg, base))
    square = square + pltpu.roll(square, LANES - 1, 1)
    square = square + pltpu.roll(square, LANES - 2, 1)
    square = pltpu.roll(square, lay.square - base, 1)
    square = jnp.where((lane >= lay.square) & (lane < lay.square + kp) & ((lane - lay.square) % PQ == 0), square, 0.0)
    first = square.astype(B16).astype(F32)
    second = (square - first).astype(B16).astype(F32)
    third = square - first - second
    tile0 = tiles[0] + first + pltpu.roll(second, 1, 1) + pltpu.roll(third, 2, 1)
    tile0 = tile0.astype(B16)
    packed[:, :LANES] = tile0
    packed[:, LANES:] = tiles[1].astype(B16)
    block = tile0.shape[0]
    parcel[: 2 * LANES, :] = w_all
    parcel[2 * LANES :, :] = jnp.zeros((block + ROWS16, parcel.shape[1]), B16)
    parcel[2 * LANES : 2 * LANES + block, :LANES] = tile0
    turned[:, : turn.shape[1]] = turn
    gain = gain_rows(head_weight, lay)
    gains[...] = gain
    gain = jnp.broadcast_to(gain_lanes(gain, lay), (ROWS16, LANES))
    first = gain.astype(B16).astype(F32)
    second = (gain - first).astype(B16).astype(F32)
    row = iota(gain.shape, 0)
    pieces = jnp.where(row == 0, first, jnp.where(row == 1, second, jnp.where(row == 2, gain - first - second, 0.0)))
    parcel[2 * LANES + block :, :LANES] = pieces.astype(B16)


def gain_rows(head_weight, lay):
    row = iota((SUBLANES, LANES), 0)
    raw = jnp.zeros((SUBLANES, LANES), F32)
    for h in range(lay.heads):
        raw = jnp.where(row == h, jnp.broadcast_to(head_weight[:, h : h + 1], raw.shape), raw)
    gain = (jnp.maximum(raw, 0.0) + jnp.log1p(jnp.exp(-jnp.abs(raw)))) * POINT_SCALE
    return jnp.where(row < lay.heads, gain, 0.0)


def gain_lanes(gain, lay):
    zero, _ = head_of(gain.shape, lay)
    return jnp.sum(jnp.where(zero == iota(gain.shape, 0), gain, 0.0), axis=0, keepdims=True)


def early_kernel(
    lay, block, order, frames, query_single, w_query, w_qp, bias_weight, w_out, d_out, pair, gains,
    left, base, d_base, d_row, w_out_rows, w_query_rows, table, pair_rows, scratch,
):
    me = lax.axis_index("row")
    for place, offset in enumerate(order):
        j = pl.multiple_of((me ^ offset) * block, block)
        pair_rows[place * block : (place + 1) * block, :] = pair[0, pl.ds(j, block), :]
    turn = [jnp.broadcast_to(frames[:, i : i + 1], (1, LANES)) for i in range(12)]
    for i in range(12):
        table[i : i + 1, :] = turn[i]
    heads, start = lay.heads, lay.base
    width = C + 4 * PV + LANES
    near = C + 4 * PV
    shape = (SUBLANES, LANES)
    row, lane = iota(shape, 0), iota(shape, 1)
    zero_head, _ = head_of(shape, lay)
    w_q = nn(to_lane(start, 0), w_query[...]) + nn(to_components(3 * lay.kp, start, lay.kp, lay.kp), w_qp[...])
    w_q = w_q.astype(B16)
    w_query_rows[...] = w_q
    w_o = jnp.zeros((2 * LANES, w_out.shape[1]), F32)
    for h in range(heads):
        i, j = iota((2 * LANES, near), 0), iota((2 * LANES, near), 1)
        m = i - (LANES + h * C)
        found = (m >= 0) & (m < C) & (j == m)
        m = i - (start + h * PV)
        found = found | ((m >= 0) & (m < PV) & (j == C + 3 * PV + m))
        for c in range(3):
            m = i - (LANES + start + c * lay.vp + h * PV)
            found = found | ((m >= 0) & (m < PV) & (j == C + 3 * m + c))
        w_o = w_o + nn(pick(found), w_out[h * width : h * width + near, :])
    w_o = w_o.astype(B16)
    w_out_rows[: 2 * LANES, :] = w_o
    for h in range(heads):
        w_out_rows[(2 + h) * LANES : (3 + h) * LANES, :] = w_out[h * width + near : (h + 1) * width, :]
    single = jnp.broadcast_to(query_single[...], (SUBLANES, query_single.shape[1]))
    rows = nt(single, w_q)
    moved = turned_by(turn, unpack(rows, lay.kp))
    points = pack([(v + turn[9 + c]).astype(B16).astype(F32) for c, v in enumerate(moved)], lay.kp, start)
    query = jnp.where(lane < start, rows, 0.0).astype(B16).astype(F32)
    left[:SUBLANES, :] = jnp.where(zero_head == row, query, 0.0)
    minus = lane < 0
    for h in range(heads):
        at = lay.square + h * PQ
        minus = minus | ((row == h) & (lane >= at) & (lane < at + 3))
    mine = jnp.where(zero_head == row, points, 0.0)
    left[SUBLANES:, :] = jnp.where(minus, -0.5, mine)
    gain = gains[...]
    cotangent = jnp.broadcast_to(d_out[...], (SUBLANES, d_out.shape[1]))
    d_row[...] = nt(cotangent, w_o)
    scratch[...] = jnp.zeros_like(scratch)
    scratch[:heads, :] = bias_weight[...].astype(F32)
    for h in range(heads):
        d_pair = nt(cotangent, w_out[h * width + near : (h + 1) * width, :])
        scratch[SUBLANES + h : SUBLANES + h + 1, :] = d_pair[:1, :]
    both = nt(scratch[...].astype(B16), pair_rows[...])
    square = jnp.sum(mine * mine, axis=1, keepdims=True)
    base[...] = both[:SUBLANES] - 0.5 * gain[:, :1] * square
    d_base[...] = both[SUBLANES:]


def attention_kernel(lay, block, order, *refs):
    *parts, left, base, d_base, d_row, gains, table, message, features, weights, scores = refs
    frames = [table[i : i + 1, :] for i in range(12)]
    me = lax.axis_index("row")
    heads, vp, start = lay.heads, lay.vp, lay.base
    shape = (SUBLANES, LANES)
    row, lane = iota(shape, 0), iota(shape, 1)
    _, one_head = head_of(shape, lay)
    gain = gains[...]
    queries = left[...].astype(B16)
    first = jnp.concatenate([nt(queries, part[:, :LANES]) for part in parts], axis=1)
    logits = LOGIT_SCALE * (first[:SUBLANES] * (1.0 / math.sqrt(C)) + base[...] + gain[:, :1] * first[SUBLANES:])
    weight = jnp.exp(logits - jnp.max(logits, axis=1, keepdims=True))
    attention = weight / jnp.sum(weight, axis=1, keepdims=True)
    attention = jnp.where(iota(attention.shape, 0) < heads, attention, 0.0)
    attention_b = attention.astype(B16)
    sums = spread(attention_b, [part.at[:, LANES:] for part in parts])
    weights[...] = attention_b
    sums = jnp.sum(jnp.where(one_head == row, sums, 0.0), axis=0, keepdims=True)
    sums = jnp.broadcast_to(sums, shape)
    local = turned_back(frames, [v - frames[9 + c] for c, v in enumerate(unpack(sums, vp))])
    lengths = jnp.sqrt(1.0 + (local[0] * local[0] + local[1] * local[1] + local[2] * local[2]))
    d_one = d_row[:, LANES:]
    share = d_row[:, :LANES] / lengths
    d_points = turned_by(frames, [v + share * u for v, u in zip(unpack(d_one, vp), local)])
    d_side = jnp.where(lane < start, d_one, 0.0) + pack(d_points, vp, start)
    right = jnp.where(one_head == row, d_side, 0.0).astype(B16)
    d_attention = jnp.concatenate([nt(right, part[:, LANES:]) for part in parts], axis=1) + d_base[...]
    total = jnp.sum(attention * d_attention, axis=1, keepdims=True)
    score_b = (LOGIT_SCALE * attention * (d_attention - total)).astype(B16)
    query = jnp.sum(jnp.where(lane < lay.square, left[:SUBLANES, :] + left[SUBLANES:, :], 0.0), axis=0, keepdims=True)
    side = jnp.where(row == 2 * heads, jnp.broadcast_to(query, shape), 0.0)
    side = side + jnp.where(row == 2 * heads + 1, d_side, 0.0)
    both = attention_b.astype(F32) + pltpu.roll(score_b.astype(F32), heads, 0)
    for at in range(0, both.shape[1], LANES):
        tile = jnp.where(row < 2 * heads, both[:, at : at + LANES], side).astype(B16)
        for place in range(at // block, (at + LANES) // block):
            for core in range(2):
                message[(me ^ order[place]) * 2 + core, :, :] = tile
    scores[...] = score_b
    features[:, :LANES] = jnp.where((lane >= start) & (lane < start + vp), lengths, 0.0)
    features[:, LANES:] = jnp.where(lane < start, sums, 0.0) + pack(local, vp, start)


def spread(weights, parts):
    total, at = 0.0, 0
    for part in parts:
        total = total + nn(weights[:, at : at + part.shape[0]], part[...])
        at += part.shape[0]
    return total


def rows_kernel(lay, *refs):
    *parts, pair, left, scores, features, weights, w_out_rows, w_query_rows, gains, table, sums = refs
    frames = [table[i : i + 1, :] for i in range(12)]
    shape = (SUBLANES, LANES)
    row, lane = iota(shape, 0), iota(shape, 1)
    zero_head, _ = head_of(shape, lay)
    pair_sum = nn(weights[...], pair[...])
    pairs = [jnp.broadcast_to(pair_sum[h : h + 1, :], shape) for h in range(lay.heads)]
    result = nn(jnp.concatenate([features[...]] + pairs, axis=1).astype(B16), w_out_rows[...])
    score = scores[...].astype(F32)
    d_rows = spread(scores[...], [part.at[:, :LANES] for part in parts])
    score_sum = jnp.sum(score, axis=1, keepdims=True)
    points = left[SUBLANES:, :]
    d_rows = jnp.where(lane < lay.base, d_rows * (1.0 / math.sqrt(C)), gains[...] * (d_rows - score_sum * points))
    d_rows = jnp.broadcast_to(
        jnp.sum(jnp.where(zero_head == row, d_rows, 0.0), axis=0, keepdims=True), shape
    )
    local = pack(turned_back(frames, unpack(d_rows, lay.kp)), lay.kp, lay.base)
    both = (jnp.where(lane < lay.base, d_rows, 0.0) + local).astype(B16)
    sums[...] = jnp.concatenate([result, nn(both, w_query_rows[...])], axis=1)


def owner_kernel(lay, near, arrived, turned, parcel, other, result):
    heads, base = lay.heads, lay.base
    count = arrived.shape[0] // 2
    block = turned.shape[0]
    shape = (SUBLANES, LANES)
    whole = (count, SUBLANES, LANES)
    per = LANES // block
    place = ((iota(whole, 0) ^ lax.axis_index("row")) // near) % per
    row = iota(shape, 0)
    zero_head, one_head = head_of(shape, lay)
    lane = iota(shape, 1)
    keep0 = (zero_head >= 0) & (zero_head + heads == row)
    keep1 = one_head == row
    ones = jnp.broadcast_to(jnp.where(keep0 & (lane >= base), 1.0, 0.0)[None], whole)
    columns = [turned[:, i : i + 1] for i in range(9)]
    lane = iota((block, LANES), 1)
    me = lax.axis_index("head")
    total = None
    for core, held in ((me, parcel), (1 - me, other)):
        took = jnp.concatenate([arrived[pl.ds(q * 2 + core, 1)] for q in range(count)], axis=0).astype(F32)
        mine = took
        for part in range(1, per):
            mine = jnp.where(place == part, pltpu.roll(took, LANES - part * block, 2), mine)
        side0 = jnp.where(keep0[None], jnp.broadcast_to(took[:, 2 * heads : 2 * heads + 1, :], whole), 0.0)
        side1 = jnp.where(keep1[None], jnp.broadcast_to(took[:, 2 * heads + 1 : 2 * heads + 2, :], whole), 0.0)
        right = jnp.concatenate([side0, side1, ones], axis=2).reshape(count * SUBLANES, 3 * LANES).astype(B16)
        moved = jnp.transpose(mine.reshape(count * SUBLANES, LANES)).astype(B16)
        both = nn(moved, right)[:block]
        pieces = held[2 * LANES + block :, :LANES].astype(F32)
        gain = pieces[0:1] + pieces[1:2] + pieces[2:3]
        own = held[2 * LANES : 2 * LANES + block, :LANES].astype(F32)
        tile0, tile1 = both[:, :LANES], both[:, LANES : 2 * LANES]
        points = gain * (tile0 - both[:, 2 * LANES :] * own)
        points = pack(turned_back(columns, unpack(points, lay.kp)), lay.kp, base)
        tile0 = jnp.where(lane < base, tile0 * (1.0 / math.sqrt(C)), points)
        points = pack(turned_back(columns, unpack(tile1, lay.vp)), lay.vp, base)
        tile1 = jnp.where(lane < base, tile1, points)
        rows = jnp.concatenate([tile0, tile1], axis=1).astype(B16)
        part = nn(rows, held[: 2 * LANES, :])
        total = part if total is None else total + part
    result[...] = total


def finish_kernel(own, other, output, grad_query):
    width = output.shape[1]
    total = own[...] + other[...]
    output[...] = total[:1, :width].astype(output.dtype)
    grad_query[...] = total[:1, width:]


VMEM = pl.BlockSpec(memory_space=pltpu.VMEM)
HBM = pl.BlockSpec(memory_space=pltpu.HBM)


def call(body, outs, args, fresh=0, scratch=(), flops=1000000, last=False):
    size = sum(math.prod(v.shape) * v.dtype.itemsize for v in list(args) + list(outs))

    def kernel(*refs):
        if fresh:
            *refs, sems = refs
            held = refs[len(refs) - fresh :]
            copies = [pltpu.make_async_copy(refs[i], held[i], sems.at[i]) for i in range(fresh)]
            for copy in copies:
                copy.start()
            for copy in copies:
                copy.wait()
            refs = list(held) + list(refs[fresh : len(refs) - fresh])
        body(*refs)

    own = [pltpu.VMEM(v.shape, v.dtype) for v in args[:fresh]]
    return pl.pallas_call(
        kernel,
        out_shape=tuple(outs),
        in_specs=[HBM] * fresh + [VMEM] * (len(args) - fresh),
        out_specs=tuple([pl.BlockSpec() if last else VMEM] * len(outs)),
        scratch_shapes=list(scratch) + own + ([pltpu.SemaphoreType.DMA((fresh,))] if fresh else []),
        compiler_params=pltpu.CompilerParams(vmem_limit_bytes=(16 << 20) + 6 * size),
        cost_estimate=pl.CostEstimate(flops=flops, bytes_accessed=size, transcendentals=0),
    )(*[pltpu.with_memory_space_constraint(v, pltpu.HBM) for v in args[:fresh]], *args[fresh:])


def shape_of(*dims, dtype=F32):
    return jax.ShapeDtypeStruct(dims, dtype)


def shards(
    query_single, key_single, pair, query_frames, key_frames, w_query, w_key, w_value, w_query_points, w_key_points,
    w_value_points, head_weight, bias_weight, w_out, d_out,
):
    lay = Layout(head_weight.shape[0])
    count = lax.axis_size("row")
    block, width = key_single.shape
    total = count * block
    near = 1
    while 4 * near * near <= count:
        near *= 2
    assert count & (count - 1) == 0

    def exchange(value, mask):
        return lax.ppermute(value, "row", [(i, i ^ mask) for i in range(count)])

    packed, parcel, turned, gains = call(
        functools.partial(key_kernel, lay),
        [
            shape_of(block, 2 * LANES, dtype=B16), shape_of(2 * LANES + block + ROWS16, width, dtype=B16),
            shape_of(block, LANES), shape_of(SUBLANES, LANES),
        ],
        [
            head_weight.reshape(1, -1), key_single, key_frames, w_key.T, w_value.T, w_key_points.T, w_value_points.T,
        ],
        7,
    )
    offsets = [0] + list(range(count - near, 0, -near))
    line = jnp.concatenate([packed] + [exchange(packed, mask) for mask in offsets[1:]], axis=0)
    planes = [0] + list(range(near - 1, 0, -1))
    parts = [line] + [exchange(line, m) for m in planes[1:]]
    order = [m ^ o for m in planes for o in offsets]

    swap = [(i, (i + 1) % 2) for i in range(2)]
    other = lax.ppermute(parcel, "head", swap)
    left, base, d_base, d_row, w_out_rows, w_query_rows, table, pair_rows = call(
        functools.partial(early_kernel, lay, block, order),
        [
            shape_of(ROWS16, LANES), shape_of(SUBLANES, total), shape_of(SUBLANES, total),
            shape_of(SUBLANES, 2 * LANES), shape_of((2 + lay.heads) * LANES, width, dtype=B16),
            shape_of(LANES, width, dtype=B16), shape_of(ROWS16, LANES),
            shape_of(total, LANES, dtype=B16),
        ],
        [
            query_frames.T, query_single, w_query.T, w_query_points.T, bias_weight, w_out, d_out, pair, gains,
        ],
        8,
        [pltpu.VMEM((ROWS16, LANES), F32)],
    )
    message, features, weight_rows, scores = call(
        functools.partial(attention_kernel, lay, block, order),
        [
            shape_of(2 * count, SUBLANES, LANES, dtype=B16), shape_of(SUBLANES, 2 * LANES),
            shape_of(SUBLANES, total, dtype=B16), shape_of(SUBLANES, total, dtype=B16),
        ],
        parts + [left, base, d_base, d_row, gains, table],
    )
    arrived = lax.all_to_all(message, ("row", "head"), 0, 0, tiled=True)
    (sums,) = call(
        functools.partial(rows_kernel, lay),
        [shape_of(SUBLANES, 2 * width)],
        parts + [pair_rows, left, scores, features, weight_rows, w_out_rows, w_query_rows, gains, table],
    )
    output, grad_query = call(
        finish_kernel,
        [shape_of(1, width, dtype=B16), shape_of(1, width)],
        [sums, lax.ppermute(sums, "head", swap)],
        last=True,
    )
    (grad_keys,) = call(
        functools.partial(owner_kernel, lay, near),
        [shape_of(block, width)],
        [arrived, turned, parcel, other],
        last=True,
    )
    return (output, grad_query, grad_keys)


def solution(mesh):
    return jax.shard_map(
        shards,
        mesh=mesh,
        in_specs=(
            P("row", None),
            P("row", None),
            P("row", None, None),
            P(None, "row"),
            P(None, "row"),
            P(None, "head"),
            P(None, "head"),
            P(None, "head"),
            P(None, "head"),
            P(None, "head"),
            P(None, "head"),
            P("head"),
            P("head", None),
            P("head", None),
            P("row", None),
        ),
        out_specs=(P("row", None), P("row", None), P("row", None)),
        check_vma=False,
    )
```

```python
import functools
import math

import jax
import jax.numpy as jnp
from jax import lax
from jax.experimental import pallas as pl
from jax.experimental.pallas import tpu as pltpu
from jax.sharding import PartitionSpec as P

C = 16
PQ = 4
PV = 8
LANES = 128
SUBLANES = 8
ROWS16 = 16
LOGIT_SCALE = math.sqrt(1.0 / 3.0)
POINT_SCALE = math.sqrt(2.0 / (9.0 * PQ))
F32 = jnp.float32
B16 = jnp.bfloat16


class Layout:
    def __init__(self, heads):
        self.heads = heads
        self.base = heads * C
        self.kp = heads * PQ
        self.vp = heads * PV
        self.square = self.base + 3 * self.kp
        assert self.square + self.kp <= LANES and self.base + 3 * self.vp <= LANES
        assert 2 * heads + 2 <= SUBLANES and PQ == 4


def nn(a, b, precision=None):
    return lax.dot_general(a, b, (((1,), (0,)), ((), ())), precision=precision, preferred_element_type=F32)


def nt(a, b):
    return lax.dot_general(a, b, (((1,), (1,)), ((), ())), preferred_element_type=F32)


def iota(shape, dim):
    return lax.broadcasted_iota(jnp.int32, shape, dim)


def pick(condition):
    return jnp.where(condition, 1.0, 0.0).astype(B16)


def to_lane(rows, offset):
    j, i = iota((LANES, rows), 0), iota((LANES, rows), 1)
    return pick(j == i + offset)


def to_components(rows, offset, points, seg):
    j, i = iota((LANES, rows), 0), iota((LANES, rows), 1)
    found = j < 0
    for c in range(3):
        m = j - (c * seg + offset)
        found = found | ((m >= 0) & (m < points) & (i == 3 * m + c))
    return pick(found)


def unpack(tile, seg):
    return tile, pltpu.roll(tile, LANES - seg, 1), pltpu.roll(tile, LANES - 2 * seg, 1)


def pack(parts, seg, base):
    lane = iota(parts[0].shape, 1)
    keep = (lane >= base) & (lane < base + seg)
    x, y, z = (jnp.where(keep, v, 0.0) for v in parts)
    return x + pltpu.roll(y, seg, 1) + pltpu.roll(z, 2 * seg, 1)


def head_of(shape, lay):
    lane = iota(shape, 1)
    zero = jnp.full(shape, -1, jnp.int32)
    one = jnp.full(shape, -1, jnp.int32)
    for h in range(lay.heads):
        same = (lane >= h * C) & (lane < (h + 1) * C)
        zero, one = jnp.where(same, h, zero), jnp.where(same, h, one)
        for c in range(3):
            k = lay.base + c * lay.kp + h * PQ
            v = lay.base + c * lay.vp + h * PV
            zero = jnp.where((lane >= k) & (lane < k + PQ), h, zero)
            one = jnp.where((lane >= v) & (lane < v + PV), h, one)
    return zero, one


def turned_by(frames, vectors):
    x, y, z = vectors
    return [frames[3 * c] * x + frames[3 * c + 1] * y + frames[3 * c + 2] * z for c in range(3)]


def turned_back(frames, vectors):
    x, y, z = vectors
    return [frames[d] * x + frames[3 + d] * y + frames[6 + d] * z for d in range(3)]


def key_kernel(lay, head_weight, key_single, frames, w_key, w_value, w_kp, w_vp, packed, parcel, turned, gains):
    kp, vp, base = lay.kp, lay.vp, lay.base
    zero = nn(to_lane(base, 0), w_key[...]) + nn(to_components(3 * kp, base, kp, kp), w_kp[...])
    one = nn(to_lane(base, 0), w_value[...]) + nn(to_components(3 * vp, base, vp, vp), w_vp[...])
    w_all = jnp.concatenate([zero, one], axis=0).astype(B16)
    rows = nt(key_single[...], w_all)
    turn = jnp.transpose(frames[...])
    columns = [turn[:, i : i + 1] for i in range(12)]
    tiles = []
    lane = iota((rows.shape[0], LANES), 1)
    for tile, seg in ((rows[:, :LANES], kp), (rows[:, LANES:], vp)):
        moved = turned_by(columns, unpack(tile, seg))
        moved = [(v + columns[9 + c]).astype(B16).astype(F32) for c, v in enumerate(moved)]
        if seg == kp:
            square = moved[0] * moved[0] + moved[1] * moved[1] + moved[2] * moved[2]
        tiles.append(jnp.where(lane < base, tile, 0.0) + pack(moved, seg, base))
    square = square + pltpu.roll(square, LANES - 1, 1)
    square = square + pltpu.roll(square, LANES - 2, 1)
    square = pltpu.roll(square, lay.square - base, 1)
    square = jnp.where((lane >= lay.square) & (lane < lay.square + kp) & ((lane - lay.square) % PQ == 0), square, 0.0)
    first = square.astype(B16).astype(F32)
    second = (square - first).astype(B16).astype(F32)
    third = square - first - second
    tile0 = tiles[0] + first + pltpu.roll(second, 1, 1) + pltpu.roll(third, 2, 1)
    tile0 = tile0.astype(B16)
    packed[:, :LANES] = tile0
    packed[:, LANES:] = tiles[1].astype(B16)
    block = tile0.shape[0]
    parcel[: 2 * LANES, :] = w_all
    parcel[2 * LANES :, :] = jnp.zeros((block + ROWS16, parcel.shape[1]), B16)
    parcel[2 * LANES : 2 * LANES + block, :LANES] = tile0
    turned[:, : turn.shape[1]] = turn
    gain = gain_rows(head_weight, lay)
    gains[...] = gain
    gain = jnp.broadcast_to(gain_lanes(gain, lay), (ROWS16, LANES))
    first = gain.astype(B16).astype(F32)
    second = (gain - first).astype(B16).astype(F32)
    row = iota(gain.shape, 0)
    pieces = jnp.where(row == 0, first, jnp.where(row == 1, second, jnp.where(row == 2, gain - first - second, 0.0)))
    parcel[2 * LANES + block :, :LANES] = pieces.astype(B16)


def gain_rows(head_weight, lay):
    row = iota((SUBLANES, LANES), 0)
    raw = jnp.zeros((SUBLANES, LANES), F32)
    for h in range(lay.heads):
        raw = jnp.where(row == h, jnp.broadcast_to(head_weight[:, h : h + 1], raw.shape), raw)
    gain = (jnp.maximum(raw, 0.0) + jnp.log1p(jnp.exp(-jnp.abs(raw)))) * POINT_SCALE
    return jnp.where(row < lay.heads, gain, 0.0)


def gain_lanes(gain, lay):
    zero, _ = head_of(gain.shape, lay)
    return jnp.sum(jnp.where(zero == iota(gain.shape, 0), gain, 0.0), axis=0, keepdims=True)


def early_kernel(
    lay, block, order, frames, query_single, w_query, w_qp, bias_weight, w_out, d_out, pair, gains,
    left, base, d_base, d_row, w_out_rows, w_query_rows, table, pair_rows, scratch,
):
    me = lax.axis_index("row")
    for place, offset in enumerate(order):
        j = pl.multiple_of((me ^ offset) * block, block)
        pair_rows[place * block : (place + 1) * block, :] = pair[0, pl.ds(j, block), :]
    turn = [jnp.broadcast_to(frames[:, i : i + 1], (1, LANES)) for i in range(12)]
    for i in range(12):
        table[i : i + 1, :] = turn[i]
    heads, start = lay.heads, lay.base
    width = C + 4 * PV + LANES
    near = C + 4 * PV
    shape = (SUBLANES, LANES)
    row, lane = iota(shape, 0), iota(shape, 1)
    zero_head, _ = head_of(shape, lay)
    w_q = nn(to_lane(start, 0), w_query[...]) + nn(to_components(3 * lay.kp, start, lay.kp, lay.kp), w_qp[...])
    w_q = w_q.astype(B16)
    w_query_rows[...] = w_q
    w_o = jnp.zeros((2 * LANES, w_out.shape[1]), F32)
    for h in range(heads):
        i, j = iota((2 * LANES, near), 0), iota((2 * LANES, near), 1)
        m = i - (LANES + h * C)
        found = (m >= 0) & (m < C) & (j == m)
        m = i - (start + h * PV)
        found = found | ((m >= 0) & (m < PV) & (j == C + 3 * PV + m))
        for c in range(3):
            m = i - (LANES + start + c * lay.vp + h * PV)
            found = found | ((m >= 0) & (m < PV) & (j == C + 3 * m + c))
        w_o = w_o + nn(pick(found), w_out[h * width : h * width + near, :])
    w_o = w_o.astype(B16)
    w_out_rows[: 2 * LANES, :] = w_o
    for h in range(heads):
        w_out_rows[(2 + h) * LANES : (3 + h) * LANES, :] = w_out[h * width + near : (h + 1) * width, :]
    single = jnp.broadcast_to(query_single[...], (SUBLANES, query_single.shape[1]))
    rows = nt(single, w_q)
    moved = turned_by(turn, unpack(rows, lay.kp))
    points = pack([(v + turn[9 + c]).astype(B16).astype(F32) for c, v in enumerate(moved)], lay.kp, start)
    query = jnp.where(lane < start, rows, 0.0).astype(B16).astype(F32)
    left[:SUBLANES, :] = jnp.where(zero_head == row, query, 0.0)
    minus = lane < 0
    for h in range(heads):
        at = lay.square + h * PQ
        minus = minus | ((row == h) & (lane >= at) & (lane < at + 3))
    mine = jnp.where(zero_head == row, points, 0.0)
    left[SUBLANES:, :] = jnp.where(minus, -0.5, mine)
    gain = gains[...]
    cotangent = jnp.broadcast_to(d_out[...], (SUBLANES, d_out.shape[1]))
    d_row[...] = nt(cotangent, w_o)
    scratch[...] = jnp.zeros_like(scratch)
    scratch[:heads, :] = bias_weight[...].astype(F32)
    for h in range(heads):
        d_pair = nt(cotangent, w_out[h * width + near : (h + 1) * width, :])
        scratch[SUBLANES + h : SUBLANES + h + 1, :] = d_pair[:1, :]
    both = nt(scratch[...].astype(B16), pair_rows[...])
    square = jnp.sum(mine * mine, axis=1, keepdims=True)
    base[...] = both[:SUBLANES] - 0.5 * gain[:, :1] * square
    d_base[...] = both[SUBLANES:]


def attention_kernel(lay, block, order, first_row, *refs):
    *parts, left, base, d_base, d_row, gains, table, message, features, weights, scores = refs
    frames = [table[i : i + 1, :] for i in range(12)]
    me = lax.axis_index("row")
    heads, vp, start = lay.heads, lay.vp, lay.base
    shape = (SUBLANES, LANES)
    row, lane = iota(shape, 0), iota(shape, 1)
    _, one_head = head_of(shape, lay)
    gain = gains[...]
    queries = left[...].astype(B16)
    first = jnp.concatenate([nt(queries, part[:, :LANES]) for part in parts], axis=1)
    logits = LOGIT_SCALE * (first[:SUBLANES] * (1.0 / math.sqrt(C)) + base[...] + gain[:, :1] * first[SUBLANES:])
    weight = jnp.exp(logits - jnp.max(logits, axis=1, keepdims=True))
    attention = weight / jnp.sum(weight, axis=1, keepdims=True)
    attention = jnp.where(iota(attention.shape, 0) < heads, attention, 0.0)
    attention_b = attention.astype(B16)
    sums = spread(attention_b, [part.at[:, LANES:] for part in parts])
    weights[...] = attention_b
    sums = jnp.sum(jnp.where(one_head == row, sums, 0.0), axis=0, keepdims=True)
    sums = jnp.broadcast_to(sums, shape)
    local = turned_back(frames, [v - frames[9 + c] for c, v in enumerate(unpack(sums, vp))])
    lengths = jnp.sqrt(1.0 + (local[0] * local[0] + local[1] * local[1] + local[2] * local[2]))
    d_one = d_row[:, LANES:]
    share = d_row[:, :LANES] / lengths
    d_points = turned_by(frames, [v + share * u for v, u in zip(unpack(d_one, vp), local)])
    d_side = jnp.where(lane < start, d_one, 0.0) + pack(d_points, vp, start)
    right = jnp.where(one_head == row, d_side, 0.0).astype(B16)
    d_attention = jnp.concatenate([nt(right, part[:, LANES:]) for part in parts], axis=1) + d_base[...]
    total = jnp.sum(attention * d_attention, axis=1, keepdims=True)
    score_b = (LOGIT_SCALE * attention * (d_attention - total)).astype(B16)
    query = jnp.sum(jnp.where(lane < lay.square, left[:SUBLANES, :] + left[SUBLANES:, :], 0.0), axis=0, keepdims=True)
    side = jnp.where(row == 2 * heads, jnp.broadcast_to(query, shape), 0.0)
    side = side + jnp.where(row == 2 * heads + 1, d_side, 0.0)
    both = attention_b.astype(F32) + pltpu.roll(score_b.astype(F32), heads, 0)
    for at in range(0, both.shape[1], LANES):
        tile = jnp.where(row < 2 * heads, both[:, at : at + LANES], side).astype(B16)
        for place in range(at // block, (at + LANES) // block):
            for core in range(2):
                message[((me ^ order[place]) + len(order) - first_row) % len(order) * 2 + core, :, :] = tile
    scores[...] = score_b
    features[:, :LANES] = jnp.where((lane >= start) & (lane < start + vp), lengths, 0.0)
    features[:, LANES:] = jnp.where(lane < start, sums, 0.0) + pack(local, vp, start)


def spread(weights, parts):
    total, at = 0.0, 0
    for part in parts:
        total = total + nn(weights[:, at : at + part.shape[0]], part[...])
        at += part.shape[0]
    return total


def rows_kernel(lay, *refs):
    *parts, pair, left, scores, features, weights, w_out_rows, w_query_rows, gains, table, sums = refs
    frames = [table[i : i + 1, :] for i in range(12)]
    shape = (SUBLANES, LANES)
    row, lane = iota(shape, 0), iota(shape, 1)
    zero_head, _ = head_of(shape, lay)
    pair_sum = nn(weights[...], pair[...])
    pairs = [jnp.broadcast_to(pair_sum[h : h + 1, :], shape) for h in range(lay.heads)]
    result = nn(jnp.concatenate([features[...]] + pairs, axis=1).astype(B16), w_out_rows[...])
    score = scores[...].astype(F32)
    d_rows = spread(scores[...], [part.at[:, :LANES] for part in parts])
    score_sum = jnp.sum(score, axis=1, keepdims=True)
    points = left[SUBLANES:, :]
    d_rows = jnp.where(lane < lay.base, d_rows * (1.0 / math.sqrt(C)), gains[...] * (d_rows - score_sum * points))
    d_rows = jnp.broadcast_to(
        jnp.sum(jnp.where(zero_head == row, d_rows, 0.0), axis=0, keepdims=True), shape
    )
    local = pack(turned_back(frames, unpack(d_rows, lay.kp)), lay.kp, lay.base)
    both = (jnp.where(lane < lay.base, d_rows, 0.0) + local).astype(B16)
    sums[...] = jnp.concatenate([result, nn(both, w_query_rows[...])], axis=1)


def owner_kernel(lay, near, first_row, arrived, turned, parcel, other, result):
    heads, base = lay.heads, lay.base
    count = arrived.shape[0] // 2
    block = turned.shape[0]
    shape = (SUBLANES, LANES)
    whole = (count, SUBLANES, LANES)
    per = LANES // block
    place = (((iota(whole, 0) + first_row) % count ^ lax.axis_index("row")) // near) % per
    row = iota(shape, 0)
    zero_head, one_head = head_of(shape, lay)
    lane = iota(shape, 1)
    keep0 = (zero_head >= 0) & (zero_head + heads == row)
    keep1 = one_head == row
    ones = jnp.broadcast_to(jnp.where(keep0 & (lane >= base), 1.0, 0.0)[None], whole)
    columns = [turned[:, i : i + 1] for i in range(9)]
    lane = iota((block, LANES), 1)
    me = lax.axis_index("head")
    total = None
    for core, held in ((me, parcel), (1 - me, other)):
        took = jnp.concatenate([arrived[pl.ds(q * 2 + core, 1)] for q in range(count)], axis=0).astype(F32)
        mine = took
        for part in range(1, per):
            mine = jnp.where(place == part, pltpu.roll(took, LANES - part * block, 2), mine)
        side0 = jnp.where(keep0[None], jnp.broadcast_to(took[:, 2 * heads : 2 * heads + 1, :], whole), 0.0)
        side1 = jnp.where(keep1[None], jnp.broadcast_to(took[:, 2 * heads + 1 : 2 * heads + 2, :], whole), 0.0)
        right = jnp.concatenate([side0, side1, ones], axis=2).reshape(count * SUBLANES, 3 * LANES).astype(B16)
        moved = jnp.transpose(mine.reshape(count * SUBLANES, LANES)).astype(B16)
        both = nn(moved, right)[:block]
        pieces = held[2 * LANES + block :, :LANES].astype(F32)
        gain = pieces[0:1] + pieces[1:2] + pieces[2:3]
        own = held[2 * LANES : 2 * LANES + block, :LANES].astype(F32)
        tile0, tile1 = both[:, :LANES], both[:, LANES : 2 * LANES]
        points = gain * (tile0 - both[:, 2 * LANES :] * own)
        points = pack(turned_back(columns, unpack(points, lay.kp)), lay.kp, base)
        tile0 = jnp.where(lane < base, tile0 * (1.0 / math.sqrt(C)), points)
        points = pack(turned_back(columns, unpack(tile1, lay.vp)), lay.vp, base)
        tile1 = jnp.where(lane < base, tile1, points)
        rows = jnp.concatenate([tile0, tile1], axis=1).astype(B16)
        part = nn(rows, held[: 2 * LANES, :])
        total = part if total is None else total + part
    result[...] = total


def finish_kernel(own, other, output, grad_query):
    width = output.shape[1]
    total = own[...] + other[...]
    output[...] = total[:1, :width].astype(output.dtype)
    grad_query[...] = total[:1, width:]


VMEM = pl.BlockSpec(memory_space=pltpu.VMEM)
HBM = pl.BlockSpec(memory_space=pltpu.HBM)


def call(body, outs, args, fresh=0, scratch=(), flops=1000000, last=False):
    size = sum(math.prod(v.shape) * v.dtype.itemsize for v in list(args) + list(outs))

    def kernel(*refs):
        if fresh:
            *refs, sems = refs
            held = refs[len(refs) - fresh :]
            copies = [pltpu.make_async_copy(refs[i], held[i], sems.at[i]) for i in range(fresh)]
            for copy in copies:
                copy.start()
            for copy in copies:
                copy.wait()
            refs = list(held) + list(refs[fresh : len(refs) - fresh])
        body(*refs)

    own = [pltpu.VMEM(v.shape, v.dtype) for v in args[:fresh]]
    return pl.pallas_call(
        kernel,
        out_shape=tuple(outs),
        in_specs=[HBM] * fresh + [VMEM] * (len(args) - fresh),
        out_specs=tuple([pl.BlockSpec() if last else VMEM] * len(outs)),
        scratch_shapes=list(scratch) + own + ([pltpu.SemaphoreType.DMA((fresh,))] if fresh else []),
        compiler_params=pltpu.CompilerParams(vmem_limit_bytes=(16 << 20) + 6 * size),
        cost_estimate=pl.CostEstimate(flops=flops, bytes_accessed=size, transcendentals=0),
    )(*[pltpu.with_memory_space_constraint(v, pltpu.HBM) for v in args[:fresh]], *args[fresh:])


def shape_of(*dims, dtype=F32):
    return jax.ShapeDtypeStruct(dims, dtype)


def shards(
    query_single, key_single, pair, query_frames, key_frames, w_query, w_key, w_value, w_query_points, w_key_points,
    w_value_points, head_weight, bias_weight, w_out, d_out,
):
    lay = Layout(head_weight.shape[0])
    count = lax.axis_size("row")
    block, width = key_single.shape
    total = count * block
    near = 1
    while 4 * near * near <= count:
        near *= 2
    assert count & (count - 1) == 0

    def exchange(value, mask):
        return lax.ppermute(value, "row", [(i, i ^ mask) for i in range(count)])

    packed, parcel, turned, gains = call(
        functools.partial(key_kernel, lay),
        [
            shape_of(block, 2 * LANES, dtype=B16), shape_of(2 * LANES + block + ROWS16, width, dtype=B16),
            shape_of(block, LANES), shape_of(SUBLANES, LANES),
        ],
        [
            head_weight.reshape(1, -1), key_single, key_frames, w_key.T, w_value.T, w_key_points.T, w_value_points.T,
        ],
        7,
    )
    offsets = [0] + list(range(count - near, 0, -near))
    line = jnp.concatenate([packed] + [exchange(packed, mask) for mask in offsets[1:]], axis=0)
    planes = [0] + list(range(near - 1, 0, -1))
    parts = [line] + [exchange(line, m) for m in planes[1:]]
    order = [m ^ o for m in planes for o in offsets]

    swap = [(i, (i + 1) % 2) for i in range(2)]
    other = lax.ppermute(parcel, "head", swap)
    left, base, d_base, d_row, w_out_rows, w_query_rows, table, pair_rows = call(
        functools.partial(early_kernel, lay, block, order),
        [
            shape_of(ROWS16, LANES), shape_of(SUBLANES, total), shape_of(SUBLANES, total),
            shape_of(SUBLANES, 2 * LANES), shape_of((2 + lay.heads) * LANES, width, dtype=B16),
            shape_of(LANES, width, dtype=B16), shape_of(ROWS16, LANES),
            shape_of(total, LANES, dtype=B16),
        ],
        [
            query_frames.T, query_single, w_query.T, w_query_points.T, bias_weight, w_out, d_out, pair, gains,
        ],
        8,
        [pltpu.VMEM((ROWS16, LANES), F32)],
    )
    first_row = count // 4
    group = [(i + 2 * first_row) % (2 * count) for i in range(2 * count)]
    message, features, weight_rows, scores = call(
        functools.partial(attention_kernel, lay, block, order, first_row),
        [
            shape_of(2 * count, SUBLANES, LANES, dtype=B16), shape_of(SUBLANES, 2 * LANES),
            shape_of(SUBLANES, total, dtype=B16), shape_of(SUBLANES, total, dtype=B16),
        ],
        parts + [left, base, d_base, d_row, gains, table],
    )
    arrived = lax.all_to_all(message, ("row", "head"), 0, 0, axis_index_groups=[group], tiled=True)
    (sums,) = call(
        functools.partial(rows_kernel, lay),
        [shape_of(SUBLANES, 2 * width)],
        parts + [pair_rows, left, scores, features, weight_rows, w_out_rows, w_query_rows, gains, table],
    )
    output, grad_query = call(
        finish_kernel,
        [shape_of(1, width, dtype=B16), shape_of(1, width)],
        [sums, lax.ppermute(sums, "head", swap)],
        last=True,
    )
    (grad_keys,) = call(
        functools.partial(owner_kernel, lay, near, first_row),
        [shape_of(block, width)],
        [arrived, turned, parcel, other],
        last=True,
    )
    return (output, grad_query, grad_keys)


def solution(mesh):
    return jax.shard_map(
        shards,
        mesh=mesh,
        in_specs=(
            P("row", None),
            P("row", None),
            P("row", None, None),
            P(None, "row"),
            P(None, "row"),
            P(None, "head"),
            P(None, "head"),
            P(None, "head"),
            P(None, "head"),
            P(None, "head"),
            P(None, "head"),
            P("head"),
            P("head", None),
            P("head", None),
            P("row", None),
        ),
        out_specs=(P("row", None), P("row", None), P("row", None)),
        check_vma=False,
    )
```

```python
import functools
import math

import jax
import jax.numpy as jnp
from jax import lax
from jax.experimental import pallas as pl
from jax.experimental.pallas import tpu as pltpu
from jax.sharding import PartitionSpec as P

C = 16
PQ = 4
PV = 8
LANES = 128
SUBLANES = 8
ROWS16 = 16
LOGIT_SCALE = math.sqrt(1.0 / 3.0)
POINT_SCALE = math.sqrt(2.0 / (9.0 * PQ))
F32 = jnp.float32
B16 = jnp.bfloat16


class Layout:
    def __init__(self, heads):
        self.heads = heads
        self.base = heads * C
        self.kp = heads * PQ
        self.vp = heads * PV
        self.square = self.base + 3 * self.kp
        assert self.square + self.kp <= LANES and self.base + 3 * self.vp <= LANES
        assert 2 * heads + 2 <= SUBLANES and PQ == 4


def nn(a, b, precision=None):
    return lax.dot_general(a, b, (((1,), (0,)), ((), ())), precision=precision, preferred_element_type=F32)


def nt(a, b):
    return lax.dot_general(a, b, (((1,), (1,)), ((), ())), preferred_element_type=F32)


def iota(shape, dim):
    return lax.broadcasted_iota(jnp.int32, shape, dim)


def pick(condition):
    return jnp.where(condition, 1.0, 0.0).astype(B16)


def to_lane(rows, offset):
    j, i = iota((LANES, rows), 0), iota((LANES, rows), 1)
    return pick(j == i + offset)


def to_components(rows, offset, points, seg):
    j, i = iota((LANES, rows), 0), iota((LANES, rows), 1)
    found = j < 0
    for c in range(3):
        m = j - (c * seg + offset)
        found = found | ((m >= 0) & (m < points) & (i == 3 * m + c))
    return pick(found)


def unpack(tile, seg):
    return tile, pltpu.roll(tile, LANES - seg, 1), pltpu.roll(tile, LANES - 2 * seg, 1)


def pack(parts, seg, base):
    lane = iota(parts[0].shape, 1)
    keep = (lane >= base) & (lane < base + seg)
    x, y, z = (jnp.where(keep, v, 0.0) for v in parts)
    return x + pltpu.roll(y, seg, 1) + pltpu.roll(z, 2 * seg, 1)


def head_of(shape, lay):
    lane = iota(shape, 1)
    zero = jnp.full(shape, -1, jnp.int32)
    one = jnp.full(shape, -1, jnp.int32)
    for h in range(lay.heads):
        same = (lane >= h * C) & (lane < (h + 1) * C)
        zero, one = jnp.where(same, h, zero), jnp.where(same, h, one)
        for c in range(3):
            k = lay.base + c * lay.kp + h * PQ
            v = lay.base + c * lay.vp + h * PV
            zero = jnp.where((lane >= k) & (lane < k + PQ), h, zero)
            one = jnp.where((lane >= v) & (lane < v + PV), h, one)
    return zero, one


def turned_by(frames, vectors):
    x, y, z = vectors
    return [frames[3 * c] * x + frames[3 * c + 1] * y + frames[3 * c + 2] * z for c in range(3)]


def turned_back(frames, vectors):
    x, y, z = vectors
    return [frames[d] * x + frames[3 + d] * y + frames[6 + d] * z for d in range(3)]


def key_kernel(lay, key_single, frames, w_key, w_value, w_kp, w_vp, packed, weights):
    kp, vp, base = lay.kp, lay.vp, lay.base
    zero = nn(to_lane(base, 0), w_key[...]) + nn(to_components(3 * kp, base, kp, kp), w_kp[...])
    one = nn(to_lane(base, 0), w_value[...]) + nn(to_components(3 * vp, base, vp, vp), w_vp[...])
    w_all = jnp.concatenate([zero, one], axis=0).astype(B16)
    rows = nt(key_single[...], w_all)
    turn = jnp.transpose(frames[...])
    columns = [turn[:, i : i + 1] for i in range(12)]
    tiles = []
    lane = iota((rows.shape[0], LANES), 1)
    for tile, seg in ((rows[:, :LANES], kp), (rows[:, LANES:], vp)):
        moved = turned_by(columns, unpack(tile, seg))
        moved = [(v + columns[9 + c]).astype(B16).astype(F32) for c, v in enumerate(moved)]
        if seg == kp:
            square = moved[0] * moved[0] + moved[1] * moved[1] + moved[2] * moved[2]
        tiles.append(jnp.where(lane < base, tile, 0.0) + pack(moved, seg, base))
    square = square + pltpu.roll(square, LANES - 1, 1)
    square = square + pltpu.roll(square, LANES - 2, 1)
    square = pltpu.roll(square, lay.square - base, 1)
    square = jnp.where((lane >= lay.square) & (lane < lay.square + kp) & ((lane - lay.square) % PQ == 0), square, 0.0)
    first = square.astype(B16).astype(F32)
    second = (square - first).astype(B16).astype(F32)
    third = square - first - second
    tile0 = tiles[0] + first + pltpu.roll(second, 1, 1) + pltpu.roll(third, 2, 1)
    packed[:, :LANES] = tile0.astype(B16)
    packed[:, LANES:] = tiles[1].astype(B16)
    weights[...] = w_all


def gain_rows(head_weight, lay):
    row = iota((SUBLANES, LANES), 0)
    raw = jnp.zeros((SUBLANES, LANES), F32)
    for h in range(lay.heads):
        raw = jnp.where(row == h, jnp.broadcast_to(head_weight[:, h : h + 1], raw.shape), raw)
    gain = (jnp.maximum(raw, 0.0) + jnp.log1p(jnp.exp(-jnp.abs(raw)))) * POINT_SCALE
    return jnp.where(row < lay.heads, gain, 0.0)


def gain_lanes(gain, lay):
    zero, _ = head_of(gain.shape, lay)
    return jnp.sum(jnp.where(zero == iota(gain.shape, 0), gain, 0.0), axis=0, keepdims=True)


def early_kernel(
    lay, block, order, frames, query_single, w_query, w_qp, bias_weight, w_out, d_out, pair, head_weight, key_frames,
    packed, weights,
    left, base, d_base, d_row, w_out_rows, w_query_rows, table, pair_rows, gains, parcel, turned, scratch,
):
    parcel[: 2 * LANES, :] = weights[...]
    parcel[2 * LANES :, :] = jnp.zeros((block + ROWS16, parcel.shape[1]), B16)
    parcel[2 * LANES : 2 * LANES + block, :LANES] = packed[:, :LANES]
    gain = gain_rows(head_weight, lay)
    gains[...] = gain
    pieces = jnp.broadcast_to(gain_lanes(gain, lay), (ROWS16, LANES))
    first = pieces.astype(B16).astype(F32)
    second = (pieces - first).astype(B16).astype(F32)
    row = iota(pieces.shape, 0)
    pieces = jnp.where(
        row == 0, first, jnp.where(row == 1, second, jnp.where(row == 2, pieces - first - second, 0.0))
    )
    parcel[2 * LANES + block :, :LANES] = pieces.astype(B16)
    turn = jnp.transpose(key_frames[...])
    turned[:, : turn.shape[1]] = turn
    me = lax.axis_index("row")
    for place, offset in enumerate(order):
        j = pl.multiple_of((me ^ offset) * block, block)
        pair_rows[place * block : (place + 1) * block, :] = pair[0, pl.ds(j, block), :]
    turn = [jnp.broadcast_to(frames[:, i : i + 1], (1, LANES)) for i in range(12)]
    for i in range(12):
        table[i : i + 1, :] = turn[i]
    heads, start = lay.heads, lay.base
    width = C + 4 * PV + LANES
    near = C + 4 * PV
    shape = (SUBLANES, LANES)
    row, lane = iota(shape, 0), iota(shape, 1)
    zero_head, _ = head_of(shape, lay)
    w_q = nn(to_lane(start, 0), w_query[...]) + nn(to_components(3 * lay.kp, start, lay.kp, lay.kp), w_qp[...])
    w_q = w_q.astype(B16)
    w_query_rows[...] = w_q
    w_o = jnp.zeros((2 * LANES, w_out.shape[1]), F32)
    for h in range(heads):
        i, j = iota((2 * LANES, near), 0), iota((2 * LANES, near), 1)
        m = i - (LANES + h * C)
        found = (m >= 0) & (m < C) & (j == m)
        m = i - (start + h * PV)
        found = found | ((m >= 0) & (m < PV) & (j == C + 3 * PV + m))
        for c in range(3):
            m = i - (LANES + start + c * lay.vp + h * PV)
            found = found | ((m >= 0) & (m < PV) & (j == C + 3 * m + c))
        w_o = w_o + nn(pick(found), w_out[h * width : h * width + near, :])
    w_o = w_o.astype(B16)
    w_out_rows[: 2 * LANES, :] = w_o
    for h in range(heads):
        w_out_rows[(2 + h) * LANES : (3 + h) * LANES, :] = w_out[h * width + near : (h + 1) * width, :]
    single = jnp.broadcast_to(query_single[...], (SUBLANES, query_single.shape[1]))
    rows = nt(single, w_q)
    moved = turned_by(turn, unpack(rows, lay.kp))
    points = pack([(v + turn[9 + c]).astype(B16).astype(F32) for c, v in enumerate(moved)], lay.kp, start)
    query = jnp.where(lane < start, rows, 0.0).astype(B16).astype(F32)
    left[:SUBLANES, :] = jnp.where(zero_head == row, query, 0.0)
    minus = lane < 0
    for h in range(heads):
        at = lay.square + h * PQ
        minus = minus | ((row == h) & (lane >= at) & (lane < at + 3))
    mine = jnp.where(zero_head == row, points, 0.0)
    left[SUBLANES:, :] = jnp.where(minus, -0.5, mine)
    cotangent = jnp.broadcast_to(d_out[...], (SUBLANES, d_out.shape[1]))
    d_row[...] = nt(cotangent, w_o)
    scratch[...] = jnp.zeros_like(scratch)
    scratch[:heads, :] = bias_weight[...].astype(F32)
    for h in range(heads):
        d_pair = nt(cotangent, w_out[h * width + near : (h + 1) * width, :])
        scratch[SUBLANES + h : SUBLANES + h + 1, :] = d_pair[:1, :]
    both = nt(scratch[...].astype(B16), pair_rows[...])
    square = jnp.sum(mine * mine, axis=1, keepdims=True)
    base[...] = both[:SUBLANES] - 0.5 * gain[:, :1] * square
    d_base[...] = both[SUBLANES:]


def attention_kernel(lay, block, order, *refs):
    *parts, left, base, d_base, d_row, gains, table, message, features, weights, scores = refs
    frames = [table[i : i + 1, :] for i in range(12)]
    me = lax.axis_index("row")
    heads, vp, start = lay.heads, lay.vp, lay.base
    shape = (SUBLANES, LANES)
    row, lane = iota(shape, 0), iota(shape, 1)
    _, one_head = head_of(shape, lay)
    gain = gains[...]
    queries = left[...].astype(B16)
    first = jnp.concatenate([nt(queries, part[:, :LANES]) for part in parts], axis=1)
    logits = LOGIT_SCALE * (first[:SUBLANES] * (1.0 / math.sqrt(C)) + base[...] + gain[:, :1] * first[SUBLANES:])
    weight = jnp.exp(logits - jnp.max(logits, axis=1, keepdims=True))
    attention = weight / jnp.sum(weight, axis=1, keepdims=True)
    attention = jnp.where(iota(attention.shape, 0) < heads, attention, 0.0)
    attention_b = attention.astype(B16)
    sums = spread(attention_b, [part.at[:, LANES:] for part in parts])
    weights[...] = attention_b
    sums = jnp.sum(jnp.where(one_head == row, sums, 0.0), axis=0, keepdims=True)
    sums = jnp.broadcast_to(sums, shape)
    local = turned_back(frames, [v - frames[9 + c] for c, v in enumerate(unpack(sums, vp))])
    lengths = jnp.sqrt(1.0 + (local[0] * local[0] + local[1] * local[1] + local[2] * local[2]))
    d_one = d_row[:, LANES:]
    share = d_row[:, :LANES] / lengths
    d_points = turned_by(frames, [v + share * u for v, u in zip(unpack(d_one, vp), local)])
    d_side = jnp.where(lane < start, d_one, 0.0) + pack(d_points, vp, start)
    right = jnp.where(one_head == row, d_side, 0.0).astype(B16)
    d_attention = jnp.concatenate([nt(right, part[:, LANES:]) for part in parts], axis=1) + d_base[...]
    total = jnp.sum(attention * d_attention, axis=1, keepdims=True)
    score_b = (LOGIT_SCALE * attention * (d_attention - total)).astype(B16)
    query = jnp.sum(jnp.where(lane < lay.square, left[:SUBLANES, :] + left[SUBLANES:, :], 0.0), axis=0, keepdims=True)
    side = jnp.where(row == 2 * heads, jnp.broadcast_to(query, shape), 0.0)
    side = side + jnp.where(row == 2 * heads + 1, d_side, 0.0)
    both = attention_b.astype(F32) + pltpu.roll(score_b.astype(F32), heads, 0)
    for at in range(0, both.shape[1], LANES):
        tile = jnp.where(row < 2 * heads, both[:, at : at + LANES], side).astype(B16)
        for place in range(at // block, (at + LANES) // block):
            for core in range(2):
                message[(me ^ order[place]) * 2 + core, :, :] = tile
    scores[...] = score_b
    features[:, :LANES] = jnp.where((lane >= start) & (lane < start + vp), lengths, 0.0)
    features[:, LANES:] = jnp.where(lane < start, sums, 0.0) + pack(local, vp, start)


def spread(weights, parts):
    total, at = 0.0, 0
    for part in parts:
        total = total + nn(weights[:, at : at + part.shape[0]], part[...])
        at += part.shape[0]
    return total


def rows_kernel(lay, *refs):
    *parts, pair, left, scores, features, weights, w_out_rows, w_query_rows, gains, table, sums = refs
    frames = [table[i : i + 1, :] for i in range(12)]
    shape = (SUBLANES, LANES)
    row, lane = iota(shape, 0), iota(shape, 1)
    zero_head, _ = head_of(shape, lay)
    pair_sum = nn(weights[...], pair[...])
    pairs = [jnp.broadcast_to(pair_sum[h : h + 1, :], shape) for h in range(lay.heads)]
    result = nn(jnp.concatenate([features[...]] + pairs, axis=1).astype(B16), w_out_rows[...])
    score = scores[...].astype(F32)
    d_rows = spread(scores[...], [part.at[:, :LANES] for part in parts])
    score_sum = jnp.sum(score, axis=1, keepdims=True)
    points = left[SUBLANES:, :]
    d_rows = jnp.where(lane < lay.base, d_rows * (1.0 / math.sqrt(C)), gains[...] * (d_rows - score_sum * points))
    d_rows = jnp.broadcast_to(
        jnp.sum(jnp.where(zero_head == row, d_rows, 0.0), axis=0, keepdims=True), shape
    )
    local = pack(turned_back(frames, unpack(d_rows, lay.kp)), lay.kp, lay.base)
    both = (jnp.where(lane < lay.base, d_rows, 0.0) + local).astype(B16)
    sums[...] = jnp.concatenate([result, nn(both, w_query_rows[...])], axis=1)


def owner_kernel(lay, near, offsets, arrived, turned, parcel, other, result):
    heads, base = lay.heads, lay.base
    count = arrived.shape[0] // 2
    block = turned.shape[0]
    shape = (SUBLANES, LANES)
    whole = (count, SUBLANES, LANES)
    per = LANES // block
    apart = (iota(whole, 0) ^ lax.axis_index("row")) // near
    place = jnp.zeros(whole, jnp.int32)
    for i, offset in enumerate(offsets):
        place = jnp.where(apart == offset // near, i % per, place)
    row = iota(shape, 0)
    zero_head, one_head = head_of(shape, lay)
    lane = iota(shape, 1)
    keep0 = (zero_head >= 0) & (zero_head + heads == row)
    keep1 = one_head == row
    ones = jnp.broadcast_to(jnp.where(keep0 & (lane >= base), 1.0, 0.0)[None], whole)
    columns = [turned[:, i : i + 1] for i in range(9)]
    lane = iota((block, LANES), 1)
    me = lax.axis_index("head")
    total = None
    for core, held in ((me, parcel), (1 - me, other)):
        took = jnp.concatenate([arrived[pl.ds(q * 2 + core, 1)] for q in range(count)], axis=0).astype(F32)
        mine = took
        for part in range(1, per):
            mine = jnp.where(place == part, pltpu.roll(took, LANES - part * block, 2), mine)
        side0 = jnp.where(keep0[None], jnp.broadcast_to(took[:, 2 * heads : 2 * heads + 1, :], whole), 0.0)
        side1 = jnp.where(keep1[None], jnp.broadcast_to(took[:, 2 * heads + 1 : 2 * heads + 2, :], whole), 0.0)
        right = jnp.concatenate([side0, side1, ones], axis=2).reshape(count * SUBLANES, 3 * LANES).astype(B16)
        moved = jnp.transpose(mine.reshape(count * SUBLANES, LANES)).astype(B16)
        both = nn(moved, right)[:block]
        pieces = held[2 * LANES + block :, :LANES].astype(F32)
        gain = pieces[0:1] + pieces[1:2] + pieces[2:3]
        own = held[2 * LANES : 2 * LANES + block, :LANES].astype(F32)
        tile0, tile1 = both[:, :LANES], both[:, LANES : 2 * LANES]
        points = gain * (tile0 - both[:, 2 * LANES :] * own)
        points = pack(turned_back(columns, unpack(points, lay.kp)), lay.kp, base)
        tile0 = jnp.where(lane < base, tile0 * (1.0 / math.sqrt(C)), points)
        points = pack(turned_back(columns, unpack(tile1, lay.vp)), lay.vp, base)
        tile1 = jnp.where(lane < base, tile1, points)
        rows = jnp.concatenate([tile0, tile1], axis=1).astype(B16)
        part = nn(rows, held[: 2 * LANES, :])
        total = part if total is None else total + part
    result[...] = total


def finish_kernel(own, other, output, grad_query):
    width = output.shape[1]
    total = own[...] + other[...]
    output[...] = total[:1, :width].astype(output.dtype)
    grad_query[...] = total[:1, width:]


VMEM = pl.BlockSpec(memory_space=pltpu.VMEM)
HBM = pl.BlockSpec(memory_space=pltpu.HBM)


def call(body, outs, args, fresh=0, scratch=(), flops=1000000, last=False):
    size = sum(math.prod(v.shape) * v.dtype.itemsize for v in list(args) + list(outs))

    def kernel(*refs):
        if fresh:
            *refs, sems = refs
            held = refs[len(refs) - fresh :]
            copies = [pltpu.make_async_copy(refs[i], held[i], sems.at[i]) for i in range(fresh)]
            for copy in copies:
                copy.start()
            for copy in copies:
                copy.wait()
            refs = list(held) + list(refs[fresh : len(refs) - fresh])
        body(*refs)

    own = [pltpu.VMEM(v.shape, v.dtype) for v in args[:fresh]]
    return pl.pallas_call(
        kernel,
        out_shape=tuple(outs),
        in_specs=[HBM] * fresh + [VMEM] * (len(args) - fresh),
        out_specs=tuple([pl.BlockSpec() if last else VMEM] * len(outs)),
        scratch_shapes=list(scratch) + own + ([pltpu.SemaphoreType.DMA((fresh,))] if fresh else []),
        compiler_params=pltpu.CompilerParams(vmem_limit_bytes=(16 << 20) + 6 * size),
        cost_estimate=pl.CostEstimate(flops=flops, bytes_accessed=size, transcendentals=0),
    )(*[pltpu.with_memory_space_constraint(v, pltpu.HBM) for v in args[:fresh]], *args[fresh:])


def shape_of(*dims, dtype=F32):
    return jax.ShapeDtypeStruct(dims, dtype)


def shards(
    query_single, key_single, pair, query_frames, key_frames, w_query, w_key, w_value, w_query_points, w_key_points,
    w_value_points, head_weight, bias_weight, w_out, d_out,
):
    lay = Layout(head_weight.shape[0])
    count = lax.axis_size("row")
    block, width = key_single.shape
    total = count * block
    near = 1
    while 4 * near * near <= count:
        near *= 2
    assert count & (count - 1) == 0

    def exchange(value, mask):
        return lax.ppermute(value, "row", [(i, i ^ mask) for i in range(count)])

    packed, weights = call(
        functools.partial(key_kernel, lay),
        [
            shape_of(block, 2 * LANES, dtype=B16), shape_of(2 * LANES, width, dtype=B16),
        ],
        [
            key_single, key_frames, w_key.T, w_value.T, w_key_points.T, w_value_points.T,
        ],
        6,
    )
    offsets = [0] + [o for o in range(near, count, near) if o != count // 2] + [count // 2]
    line = jnp.concatenate([packed] + [exchange(packed, mask) for mask in offsets[1:]], axis=0)
    planes = list(range(near))
    parts = [line] + [exchange(line, m) for m in planes[1:]]
    order = [m ^ o for m in planes for o in offsets]

    left, base, d_base, d_row, w_out_rows, w_query_rows, table, pair_rows, gains, parcel, turned = call(
        functools.partial(early_kernel, lay, block, order),
        [
            shape_of(ROWS16, LANES), shape_of(SUBLANES, total), shape_of(SUBLANES, total),
            shape_of(SUBLANES, 2 * LANES), shape_of((2 + lay.heads) * LANES, width, dtype=B16),
            shape_of(LANES, width, dtype=B16), shape_of(ROWS16, LANES),
            shape_of(total, LANES, dtype=B16), shape_of(SUBLANES, LANES),
            shape_of(2 * LANES + block + ROWS16, width, dtype=B16), shape_of(block, LANES),
        ],
        [
            query_frames.T, query_single, w_query.T, w_query_points.T, bias_weight, w_out, d_out, pair,
            head_weight.reshape(1, -1), key_frames, packed, weights,
        ],
        10,
        [pltpu.VMEM((ROWS16, LANES), F32)],
    )
    swap = [(i, (i + 1) % 2) for i in range(2)]
    other = lax.ppermute(parcel, "head", swap)
    message, features, weight_rows, scores = call(
        functools.partial(attention_kernel, lay, block, order),
        [
            shape_of(2 * count, SUBLANES, LANES, dtype=B16), shape_of(SUBLANES, 2 * LANES),
            shape_of(SUBLANES, total, dtype=B16), shape_of(SUBLANES, total, dtype=B16),
        ],
        parts + [left, base, d_base, d_row, gains, table],
    )
    arrived = lax.all_to_all(message, ("row", "head"), 0, 0, tiled=True)
    (sums,) = call(
        functools.partial(rows_kernel, lay),
        [shape_of(SUBLANES, 2 * width)],
        parts + [pair_rows, left, scores, features, weight_rows, w_out_rows, w_query_rows, gains, table],
    )
    output, grad_query = call(
        finish_kernel,
        [shape_of(1, width, dtype=B16), shape_of(1, width)],
        [sums, lax.ppermute(sums, "head", swap)],
        last=True,
    )
    (grad_keys,) = call(
        functools.partial(owner_kernel, lay, near, offsets),
        [shape_of(block, width)],
        [arrived, turned, parcel, other],
        last=True,
    )
    return (output, grad_query, grad_keys)


def solution(mesh):
    return jax.shard_map(
        shards,
        mesh=mesh,
        in_specs=(
            P("row", None),
            P("row", None),
            P("row", None, None),
            P(None, "row"),
            P(None, "row"),
            P(None, "head"),
            P(None, "head"),
            P(None, "head"),
            P(None, "head"),
            P(None, "head"),
            P(None, "head"),
            P("head"),
            P("head", None),
            P("head", None),
            P("row", None),
        ),
        out_specs=(P("row", None), P("row", None), P("row", None)),
        check_vma=False,
    )
```

```python
import functools
import math

import jax
import jax.numpy as jnp
from jax import lax
from jax.experimental import pallas as pl
from jax.experimental.pallas import tpu as pltpu
from jax.sharding import PartitionSpec as P

C = 16
PQ = 4
PV = 8
LANES = 128
SUBLANES = 8
ROWS16 = 16
LOGIT_SCALE = math.sqrt(1.0 / 3.0)
POINT_SCALE = math.sqrt(2.0 / (9.0 * PQ))
F32 = jnp.float32
B16 = jnp.bfloat16


class Layout:
    def __init__(self, heads):
        self.heads = heads
        self.base = heads * C
        self.kp = heads * PQ
        self.vp = heads * PV
        self.square = self.base + 3 * self.kp
        assert self.square + self.kp <= LANES and self.base + 3 * self.vp <= LANES
        assert 2 * heads + 2 <= SUBLANES and PQ == 4


def nn(a, b, precision=None):
    return lax.dot_general(a, b, (((1,), (0,)), ((), ())), precision=precision, preferred_element_type=F32)


def nt(a, b):
    return lax.dot_general(a, b, (((1,), (1,)), ((), ())), preferred_element_type=F32)


def iota(shape, dim):
    return lax.broadcasted_iota(jnp.int32, shape, dim)


def pick(condition):
    return jnp.where(condition, 1.0, 0.0).astype(B16)


def to_lane(rows, offset):
    j, i = iota((LANES, rows), 0), iota((LANES, rows), 1)
    return pick(j == i + offset)


def to_components(rows, offset, points, seg):
    j, i = iota((LANES, rows), 0), iota((LANES, rows), 1)
    found = j < 0
    for c in range(3):
        m = j - (c * seg + offset)
        found = found | ((m >= 0) & (m < points) & (i == 3 * m + c))
    return pick(found)


def unpack(tile, seg):
    return tile, pltpu.roll(tile, LANES - seg, 1), pltpu.roll(tile, LANES - 2 * seg, 1)


def pack(parts, seg, base):
    lane = iota(parts[0].shape, 1)
    keep = (lane >= base) & (lane < base + seg)
    x, y, z = (jnp.where(keep, v, 0.0) for v in parts)
    return x + pltpu.roll(y, seg, 1) + pltpu.roll(z, 2 * seg, 1)


def head_of(shape, lay):
    lane = iota(shape, 1)
    zero = jnp.full(shape, -1, jnp.int32)
    one = jnp.full(shape, -1, jnp.int32)
    for h in range(lay.heads):
        same = (lane >= h * C) & (lane < (h + 1) * C)
        zero, one = jnp.where(same, h, zero), jnp.where(same, h, one)
        for c in range(3):
            k = lay.base + c * lay.kp + h * PQ
            v = lay.base + c * lay.vp + h * PV
            zero = jnp.where((lane >= k) & (lane < k + PQ), h, zero)
            one = jnp.where((lane >= v) & (lane < v + PV), h, one)
    return zero, one


def turned_by(frames, vectors):
    x, y, z = vectors
    return [frames[3 * c] * x + frames[3 * c + 1] * y + frames[3 * c + 2] * z for c in range(3)]


def turned_back(frames, vectors):
    x, y, z = vectors
    return [frames[d] * x + frames[3 + d] * y + frames[6 + d] * z for d in range(3)]


def key_kernel(lay, ready, key_single, frames, w_key, w_value, w_kp, w_vp, packed):
    heads, kp, vp, base = lay.heads, lay.kp, lay.vp, lay.base
    tall = PQ * SUBLANES

    def rows_of(count, width):
        return iota((count, width), 0), iota((count, width), 1)

    r, i = rows_of(tall, 3 * kp)
    to_kp = [pick((i == 3 * PQ * (r & 7) + 3 * (r >> 3) + c) & ((r & 7) < heads)) for c in range(3)]
    r, i = rows_of(vp, 3 * vp)
    to_vp = [pick(i == 3 * r + c) for c in range(3)]
    width = 2 * LANES
    r, j = rows_of(base, width)
    place = [j == r, j == r + LANES]
    r, j = rows_of(tall, width)
    place += [(j == base + c * kp + PQ * (r & 7) + (r >> 3)) & ((r & 7) < heads) for c in range(3)]
    r, j = rows_of(vp, width)
    place += [j == LANES + base + c * vp + r for c in range(3)]
    r, j = rows_of(SUBLANES, width)
    place += [(j == lay.square + PQ * r + piece) & (r < heads) for piece in range(3)]
    place = jnp.concatenate([jnp.where(found, 1.0, 0.0) for found in place], axis=0).astype(B16)
    to_kp = jnp.concatenate(to_kp, axis=0)
    to_vp = jnp.concatenate(to_vp, axis=0)
    ready()
    single = key_single[...]
    turn = [frames[i : i + 1, :] for i in range(12)]
    features = [nt(w_key[...], single), nt(w_value[...], single)]
    for choose, weight, height in ((to_kp, w_kp, tall), (to_vp, w_vp, vp)):
        rows = nt(nn(choose, weight[...]).astype(B16), single)
        moved = turned_by(turn, [rows[c * height : (c + 1) * height] for c in range(3)])
        moved = [(v + turn[9 + c]).astype(B16).astype(F32) for c, v in enumerate(moved)]
        features += moved
        if height == tall:
            square = moved[0] * moved[0] + moved[1] * moved[1] + moved[2] * moved[2]
            square = sum(square[group(p)] for p in range(PQ))
    first = square.astype(B16).astype(F32)
    second = (square - first).astype(B16).astype(F32)
    features = jnp.concatenate(features + [first, second, square - first - second], axis=0)
    packed[...] = nn(jnp.transpose(features).astype(B16), place).astype(B16)


def group(h):
    return slice(h * SUBLANES, (h + 1) * SUBLANES)


def gain_rows(head_weight, lay):
    row = iota((SUBLANES, LANES), 0)
    raw = jnp.zeros((SUBLANES, LANES), F32)
    for h in range(lay.heads):
        raw = jnp.where(row == h, jnp.broadcast_to(head_weight[:, h : h + 1], raw.shape), raw)
    gain = (jnp.maximum(raw, 0.0) + jnp.log1p(jnp.exp(-jnp.abs(raw)))) * POINT_SCALE
    return jnp.where(row < lay.heads, gain, 0.0)


def gain_lanes(gain, lay):
    zero, _ = head_of(gain.shape, lay)
    return jnp.sum(jnp.where(zero == iota(gain.shape, 0), gain, 0.0), axis=0, keepdims=True)


def early_kernel(
    lay, block, order, frames, query_single, w_query, w_qp, bias_weight, w_out, d_out, pair, head_weight, key_frames,
    w_key, w_value, w_kp, w_vp, packed,
    left, base, d_base, d_row, w_out_rows, w_query_rows, table, pair_rows, gains, parcel, turned, scratch,
):
    kp, vp = lay.kp, lay.vp
    zero = nn(to_lane(lay.base, 0), w_key[...]) + nn(to_components(3 * kp, lay.base, kp, kp), w_kp[...])
    one = nn(to_lane(lay.base, 0), w_value[...]) + nn(to_components(3 * vp, lay.base, vp, vp), w_vp[...])
    parcel[:LANES, :] = zero.astype(B16)
    parcel[LANES : 2 * LANES, :] = one.astype(B16)
    parcel[2 * LANES :, :] = jnp.zeros((block + ROWS16, parcel.shape[1]), B16)
    parcel[2 * LANES : 2 * LANES + block, :LANES] = packed[:, :LANES]
    gain = gain_rows(head_weight, lay)
    gains[...] = gain
    pieces = jnp.broadcast_to(gain_lanes(gain, lay), (ROWS16, LANES))
    first = pieces.astype(B16).astype(F32)
    second = (pieces - first).astype(B16).astype(F32)
    row = iota(pieces.shape, 0)
    pieces = jnp.where(
        row == 0, first, jnp.where(row == 1, second, jnp.where(row == 2, pieces - first - second, 0.0))
    )
    parcel[2 * LANES + block :, :LANES] = pieces.astype(B16)
    turn = jnp.transpose(key_frames[...])
    turned[:, : turn.shape[1]] = turn
    me = lax.axis_index("row")
    for place, offset in enumerate(order):
        j = pl.multiple_of((me ^ offset) * block, block)
        pair_rows[place * block : (place + 1) * block, :] = pair[0, pl.ds(j, block), :]
    turn = [jnp.broadcast_to(frames[:, i : i + 1], (1, LANES)) for i in range(12)]
    for i in range(12):
        table[i : i + 1, :] = turn[i]
    heads, start = lay.heads, lay.base
    width = C + 4 * PV + LANES
    near = C + 4 * PV
    shape = (SUBLANES, LANES)
    row, lane = iota(shape, 0), iota(shape, 1)
    zero_head, _ = head_of(shape, lay)
    w_q = nn(to_lane(start, 0), w_query[...]) + nn(to_components(3 * lay.kp, start, lay.kp, lay.kp), w_qp[...])
    w_q = w_q.astype(B16)
    w_query_rows[...] = w_q
    w_o = jnp.zeros((2 * LANES, w_out.shape[1]), F32)
    for h in range(heads):
        i, j = iota((2 * LANES, near), 0), iota((2 * LANES, near), 1)
        m = i - (LANES + h * C)
        found = (m >= 0) & (m < C) & (j == m)
        m = i - (start + h * PV)
        found = found | ((m >= 0) & (m < PV) & (j == C + 3 * PV + m))
        for c in range(3):
            m = i - (LANES + start + c * lay.vp + h * PV)
            found = found | ((m >= 0) & (m < PV) & (j == C + 3 * m + c))
        w_o = w_o + nn(pick(found), w_out[h * width : h * width + near, :])
    w_o = w_o.astype(B16)
    w_out_rows[: 2 * LANES, :] = w_o
    for h in range(heads):
        w_out_rows[(2 + h) * LANES : (3 + h) * LANES, :] = w_out[h * width + near : (h + 1) * width, :]
    single = jnp.broadcast_to(query_single[...], (SUBLANES, query_single.shape[1]))
    rows = nt(single, w_q)
    moved = turned_by(turn, unpack(rows, lay.kp))
    points = pack([(v + turn[9 + c]).astype(B16).astype(F32) for c, v in enumerate(moved)], lay.kp, start)
    query = jnp.where(lane < start, rows, 0.0).astype(B16).astype(F32)
    left[:SUBLANES, :] = jnp.where(zero_head == row, query, 0.0)
    minus = lane < 0
    for h in range(heads):
        at = lay.square + h * PQ
        minus = minus | ((row == h) & (lane >= at) & (lane < at + 3))
    mine = jnp.where(zero_head == row, points, 0.0)
    left[SUBLANES:, :] = jnp.where(minus, -0.5, mine)
    cotangent = jnp.broadcast_to(d_out[...], (SUBLANES, d_out.shape[1]))
    d_row[...] = nt(cotangent, w_o)
    scratch[...] = jnp.zeros_like(scratch)
    scratch[:heads, :] = bias_weight[...].astype(F32)
    for h in range(heads):
        d_pair = nt(cotangent, w_out[h * width + near : (h + 1) * width, :])
        scratch[SUBLANES + h : SUBLANES + h + 1, :] = d_pair[:1, :]
    both = nt(scratch[...].astype(B16), pair_rows[...])
    square = jnp.sum(mine * mine, axis=1, keepdims=True)
    base[...] = both[:SUBLANES] - 0.5 * gain[:, :1] * square
    d_base[...] = both[SUBLANES:]


def attention_kernel(lay, block, order, *refs):
    *parts, left, base, d_base, d_row, gains, table, message, features, weights, scores = refs
    frames = [table[i : i + 1, :] for i in range(12)]
    me = lax.axis_index("row")
    heads, vp, start = lay.heads, lay.vp, lay.base
    shape = (SUBLANES, LANES)
    row, lane = iota(shape, 0), iota(shape, 1)
    _, one_head = head_of(shape, lay)
    gain = gains[...]
    queries = left[...].astype(B16)
    first = jnp.concatenate([nt(queries, part[:, :LANES]) for part in parts], axis=1)
    logits = LOGIT_SCALE * (first[:SUBLANES] * (1.0 / math.sqrt(C)) + base[...] + gain[:, :1] * first[SUBLANES:])
    weight = jnp.exp(logits - jnp.max(logits, axis=1, keepdims=True))
    attention = weight / jnp.sum(weight, axis=1, keepdims=True)
    attention = jnp.where(iota(attention.shape, 0) < heads, attention, 0.0)
    attention_b = attention.astype(B16)
    sums = spread(attention_b, [part.at[:, LANES:] for part in parts])
    weights[...] = attention_b
    sums = jnp.sum(jnp.where(one_head == row, sums, 0.0), axis=0, keepdims=True)
    sums = jnp.broadcast_to(sums, shape)
    local = turned_back(frames, [v - frames[9 + c] for c, v in enumerate(unpack(sums, vp))])
    lengths = jnp.sqrt(1.0 + (local[0] * local[0] + local[1] * local[1] + local[2] * local[2]))
    d_one = d_row[:, LANES:]
    share = d_row[:, :LANES] / lengths
    d_points = turned_by(frames, [v + share * u for v, u in zip(unpack(d_one, vp), local)])
    d_side = jnp.where(lane < start, d_one, 0.0) + pack(d_points, vp, start)
    right = jnp.where(one_head == row, d_side, 0.0).astype(B16)
    d_attention = jnp.concatenate([nt(right, part[:, LANES:]) for part in parts], axis=1) + d_base[...]
    total = jnp.sum(attention * d_attention, axis=1, keepdims=True)
    score_b = (LOGIT_SCALE * attention * (d_attention - total)).astype(B16)
    query = jnp.sum(jnp.where(lane < lay.square, left[:SUBLANES, :] + left[SUBLANES:, :], 0.0), axis=0, keepdims=True)
    side = jnp.where(row == 2 * heads, jnp.broadcast_to(query, shape), 0.0)
    side = side + jnp.where(row == 2 * heads + 1, d_side, 0.0)
    both = attention_b.astype(F32) + pltpu.roll(score_b.astype(F32), heads, 0)
    for at in range(0, both.shape[1], LANES):
        tile = jnp.where(row < 2 * heads, both[:, at : at + LANES], side).astype(B16)
        for place in range(at // block, (at + LANES) // block):
            for core in range(2):
                message[(me ^ order[place]) * 2 + core, :, :] = tile
    scores[...] = score_b
    features[:, :LANES] = jnp.where((lane >= start) & (lane < start + vp), lengths, 0.0)
    features[:, LANES:] = jnp.where(lane < start, sums, 0.0) + pack(local, vp, start)


def spread(weights, parts):
    total, at = 0.0, 0
    for part in parts:
        total = total + nn(weights[:, at : at + part.shape[0]], part[...])
        at += part.shape[0]
    return total


def rows_kernel(lay, *refs):
    *parts, pair, left, scores, features, weights, w_out_rows, w_query_rows, gains, table, sums = refs
    frames = [table[i : i + 1, :] for i in range(12)]
    shape = (SUBLANES, LANES)
    row, lane = iota(shape, 0), iota(shape, 1)
    zero_head, _ = head_of(shape, lay)
    pair_sum = nn(weights[...], pair[...])
    pairs = [jnp.broadcast_to(pair_sum[h : h + 1, :], shape) for h in range(lay.heads)]
    result = nn(jnp.concatenate([features[...]] + pairs, axis=1).astype(B16), w_out_rows[...])
    score = scores[...].astype(F32)
    d_rows = spread(scores[...], [part.at[:, :LANES] for part in parts])
    score_sum = jnp.sum(score, axis=1, keepdims=True)
    points = left[SUBLANES:, :]
    d_rows = jnp.where(lane < lay.base, d_rows * (1.0 / math.sqrt(C)), gains[...] * (d_rows - score_sum * points))
    d_rows = jnp.broadcast_to(
        jnp.sum(jnp.where(zero_head == row, d_rows, 0.0), axis=0, keepdims=True), shape
    )
    local = pack(turned_back(frames, unpack(d_rows, lay.kp)), lay.kp, lay.base)
    both = (jnp.where(lane < lay.base, d_rows, 0.0) + local).astype(B16)
    sums[...] = jnp.concatenate([result, nn(both, w_query_rows[...])], axis=1)


def owner_kernel(lay, near, offsets, arrived, turned, parcel, other, result):
    heads, base = lay.heads, lay.base
    count = arrived.shape[0] // 2
    block = turned.shape[0]
    shape = (SUBLANES, LANES)
    whole = (count, SUBLANES, LANES)
    per = LANES // block
    apart = (iota(whole, 0) ^ lax.axis_index("row")) // near
    place = jnp.zeros(whole, jnp.int32)
    for i, offset in enumerate(offsets):
        place = jnp.where(apart == offset // near, i % per, place)
    row = iota(shape, 0)
    zero_head, one_head = head_of(shape, lay)
    lane = iota(shape, 1)
    keep0 = (zero_head >= 0) & (zero_head + heads == row)
    keep1 = one_head == row
    ones = jnp.broadcast_to(jnp.where(keep0 & (lane >= base), 1.0, 0.0)[None], whole)
    columns = [turned[:, i : i + 1] for i in range(9)]
    lane = iota((block, LANES), 1)
    me = lax.axis_index("head")
    total = None
    for core, held in ((me, parcel), (1 - me, other)):
        took = jnp.concatenate([arrived[pl.ds(q * 2 + core, 1)] for q in range(count)], axis=0).astype(F32)
        mine = took
        for part in range(1, per):
            mine = jnp.where(place == part, pltpu.roll(took, LANES - part * block, 2), mine)
        side0 = jnp.where(keep0[None], jnp.broadcast_to(took[:, 2 * heads : 2 * heads + 1, :], whole), 0.0)
        side1 = jnp.where(keep1[None], jnp.broadcast_to(took[:, 2 * heads + 1 : 2 * heads + 2, :], whole), 0.0)
        right = jnp.concatenate([side0, side1, ones], axis=2).reshape(count * SUBLANES, 3 * LANES).astype(B16)
        moved = jnp.transpose(mine.reshape(count * SUBLANES, LANES)).astype(B16)
        both = nn(moved, right)[:block]
        pieces = held[2 * LANES + block :, :LANES].astype(F32)
        gain = pieces[0:1] + pieces[1:2] + pieces[2:3]
        own = held[2 * LANES : 2 * LANES + block, :LANES].astype(F32)
        tile0, tile1 = both[:, :LANES], both[:, LANES : 2 * LANES]
        points = gain * (tile0 - both[:, 2 * LANES :] * own)
        points = pack(turned_back(columns, unpack(points, lay.kp)), lay.kp, base)
        tile0 = jnp.where(lane < base, tile0 * (1.0 / math.sqrt(C)), points)
        points = pack(turned_back(columns, unpack(tile1, lay.vp)), lay.vp, base)
        tile1 = jnp.where(lane < base, tile1, points)
        rows = jnp.concatenate([tile0, tile1], axis=1).astype(B16)
        part = nn(rows, held[: 2 * LANES, :])
        total = part if total is None else total + part
    result[...] = total


def finish_kernel(own, other, output, grad_query):
    width = output.shape[1]
    total = own[...] + other[...]
    output[...] = total[:1, :width].astype(output.dtype)
    grad_query[...] = total[:1, width:]


VMEM = pl.BlockSpec(memory_space=pltpu.VMEM)
HBM = pl.BlockSpec(memory_space=pltpu.HBM)


def call(body, outs, args, fresh=0, scratch=(), flops=1000000, last=False, waits=False):
    size = sum(math.prod(v.shape) * v.dtype.itemsize for v in list(args) + list(outs))

    def kernel(*refs):
        if fresh:
            *refs, sems = refs
            held = refs[len(refs) - fresh :]
            copies = [pltpu.make_async_copy(refs[i], held[i], sems.at[i]) for i in range(fresh)]
            for copy in copies:
                copy.start()

            def ready():
                for copy in copies:
                    copy.wait()

            if not waits:
                ready()
            refs = list(held) + list(refs[fresh : len(refs) - fresh])
        body(*([ready] if waits else []), *refs)

    own = [pltpu.VMEM(v.shape, v.dtype) for v in args[:fresh]]
    return pl.pallas_call(
        kernel,
        out_shape=tuple(outs),
        in_specs=[HBM] * fresh + [VMEM] * (len(args) - fresh),
        out_specs=tuple([pl.BlockSpec() if last else VMEM] * len(outs)),
        scratch_shapes=list(scratch) + own + ([pltpu.SemaphoreType.DMA((fresh,))] if fresh else []),
        compiler_params=pltpu.CompilerParams(vmem_limit_bytes=(16 << 20) + 6 * size),
        cost_estimate=pl.CostEstimate(flops=flops, bytes_accessed=size, transcendentals=0),
    )(*[pltpu.with_memory_space_constraint(v, pltpu.HBM) for v in args[:fresh]], *args[fresh:])


def shape_of(*dims, dtype=F32):
    return jax.ShapeDtypeStruct(dims, dtype)


def shards(
    query_single, key_single, pair, query_frames, key_frames, w_query, w_key, w_value, w_query_points, w_key_points,
    w_value_points, head_weight, bias_weight, w_out, d_out,
):
    lay = Layout(head_weight.shape[0])
    count = lax.axis_size("row")
    block, width = key_single.shape
    total = count * block
    near = 1
    while 4 * near * near <= count:
        near *= 2
    assert count & (count - 1) == 0

    def exchange(value, mask):
        return lax.ppermute(value, "row", [(i, i ^ mask) for i in range(count)])

    (packed,) = call(
        functools.partial(key_kernel, lay),
        [shape_of(block, 2 * LANES, dtype=B16)],
        [
            key_single, key_frames, w_key.T, w_value.T, w_key_points.T, w_value_points.T,
        ],
        6,
        waits=True,
    )
    offsets = list(range(0, count, near))
    line = jnp.concatenate([packed] + [exchange(packed, mask) for mask in offsets[1:]], axis=0)
    planes = list(range(near))
    parts = [line] + [exchange(line, m) for m in planes[1:]]
    order = [m ^ o for m in planes for o in offsets]

    left, base, d_base, d_row, w_out_rows, w_query_rows, table, pair_rows, gains, parcel, turned = call(
        functools.partial(early_kernel, lay, block, order),
        [
            shape_of(ROWS16, LANES), shape_of(SUBLANES, total), shape_of(SUBLANES, total),
            shape_of(SUBLANES, 2 * LANES), shape_of((2 + lay.heads) * LANES, width, dtype=B16),
            shape_of(LANES, width, dtype=B16), shape_of(ROWS16, LANES),
            shape_of(total, LANES, dtype=B16), shape_of(SUBLANES, LANES),
            shape_of(2 * LANES + block + ROWS16, width, dtype=B16), shape_of(block, LANES),
        ],
        [
            query_frames.T, query_single, w_query.T, w_query_points.T, bias_weight, w_out, d_out, pair,
            head_weight.reshape(1, -1), key_frames, w_key.T, w_value.T, w_key_points.T, w_value_points.T, packed,
        ],
        14,
        [pltpu.VMEM((ROWS16, LANES), F32)],
    )
    swap = [(i, (i + 1) % 2) for i in range(2)]
    other = lax.ppermute(parcel, "head", swap)
    message, features, weight_rows, scores = call(
        functools.partial(attention_kernel, lay, block, order),
        [
            shape_of(2 * count, SUBLANES, LANES, dtype=B16), shape_of(SUBLANES, 2 * LANES),
            shape_of(SUBLANES, total, dtype=B16), shape_of(SUBLANES, total, dtype=B16),
        ],
        parts + [left, base, d_base, d_row, gains, table],
    )
    arrived = lax.all_to_all(message, ("row", "head"), 0, 0, tiled=True)
    (sums,) = call(
        functools.partial(rows_kernel, lay),
        [shape_of(SUBLANES, 2 * width)],
        parts + [pair_rows, left, scores, features, weight_rows, w_out_rows, w_query_rows, gains, table],
    )
    output, grad_query = call(
        finish_kernel,
        [shape_of(1, width, dtype=B16), shape_of(1, width)],
        [sums, lax.ppermute(sums, "head", swap)],
        last=True,
    )
    (grad_keys,) = call(
        functools.partial(owner_kernel, lay, near, offsets),
        [shape_of(block, width)],
        [arrived, turned, parcel, other],
        last=True,
    )
    return (output, grad_query, grad_keys)


def solution(mesh):
    return jax.shard_map(
        shards,
        mesh=mesh,
        in_specs=(
            P("row", None),
            P("row", None),
            P("row", None, None),
            P(None, "row"),
            P(None, "row"),
            P(None, "head"),
            P(None, "head"),
            P(None, "head"),
            P(None, "head"),
            P(None, "head"),
            P(None, "head"),
            P("head"),
            P("head", None),
            P("head", None),
            P("row", None),
        ),
        out_specs=(P("row", None), P("row", None), P("row", None)),
        check_vma=False,
    )
```

```python
import functools
import math

import jax
import jax.numpy as jnp
from jax import lax
from jax.experimental import pallas as pl
from jax.experimental.pallas import tpu as pltpu
from jax.sharding import PartitionSpec as P

C = 16
PQ = 4
PV = 8
LANES = 128
SUBLANES = 8
ROWS16 = 16
LOGIT_SCALE = math.sqrt(1.0 / 3.0)
POINT_SCALE = math.sqrt(2.0 / (9.0 * PQ))
F32 = jnp.float32
B16 = jnp.bfloat16


class Layout:
    def __init__(self, heads):
        self.heads = heads
        self.base = heads * C
        self.kp = heads * PQ
        self.vp = heads * PV
        self.square = self.base + 3 * self.kp
        assert self.square + self.kp <= LANES and self.base + 3 * self.vp <= LANES
        assert 2 * heads + 2 <= SUBLANES and PQ == 4


def nn(a, b, precision=None):
    return lax.dot_general(a, b, (((1,), (0,)), ((), ())), precision=precision, preferred_element_type=F32)


def nt(a, b):
    return lax.dot_general(a, b, (((1,), (1,)), ((), ())), preferred_element_type=F32)


def iota(shape, dim):
    return lax.broadcasted_iota(jnp.int32, shape, dim)


def pick(condition):
    return jnp.where(condition, 1.0, 0.0).astype(B16)


def to_lane(rows, offset):
    j, i = iota((LANES, rows), 0), iota((LANES, rows), 1)
    return pick(j == i + offset)


def to_components(rows, offset, points, seg):
    j, i = iota((LANES, rows), 0), iota((LANES, rows), 1)
    found = j < 0
    for c in range(3):
        m = j - (c * seg + offset)
        found = found | ((m >= 0) & (m < points) & (i == 3 * m + c))
    return pick(found)


def unpack(tile, seg):
    return tile, pltpu.roll(tile, LANES - seg, 1), pltpu.roll(tile, LANES - 2 * seg, 1)


def pack(parts, seg, base):
    lane = iota(parts[0].shape, 1)
    keep = (lane >= base) & (lane < base + seg)
    x, y, z = (jnp.where(keep, v, 0.0) for v in parts)
    return x + pltpu.roll(y, seg, 1) + pltpu.roll(z, 2 * seg, 1)


def head_of(shape, lay):
    lane = iota(shape, 1)
    zero = jnp.full(shape, -1, jnp.int32)
    one = jnp.full(shape, -1, jnp.int32)
    for h in range(lay.heads):
        same = (lane >= h * C) & (lane < (h + 1) * C)
        zero, one = jnp.where(same, h, zero), jnp.where(same, h, one)
        for c in range(3):
            k = lay.base + c * lay.kp + h * PQ
            v = lay.base + c * lay.vp + h * PV
            zero = jnp.where((lane >= k) & (lane < k + PQ), h, zero)
            one = jnp.where((lane >= v) & (lane < v + PV), h, one)
    return zero, one


def turned_by(frames, vectors):
    x, y, z = vectors
    return [frames[3 * c] * x + frames[3 * c + 1] * y + frames[3 * c + 2] * z for c in range(3)]


def turned_back(frames, vectors):
    x, y, z = vectors
    return [frames[d] * x + frames[3 + d] * y + frames[6 + d] * z for d in range(3)]


def key_kernel(lay, ready, key_single, frames, w_key, w_value, w_kp, w_vp, packed):
    heads, kp, vp, base = lay.heads, lay.kp, lay.vp, lay.base
    tall = PQ * SUBLANES

    def rows_of(count, width):
        return iota((count, width), 0), iota((count, width), 1)

    r, i = rows_of(tall, 3 * kp)
    to_kp = [pick((i == 3 * PQ * (r & 7) + 3 * (r >> 3) + c) & ((r & 7) < heads)) for c in range(3)]
    r, i = rows_of(vp, 3 * vp)
    to_vp = [pick(i == 3 * r + c) for c in range(3)]
    width = 2 * LANES
    r, j = rows_of(base, width)
    place = [j == r, j == r + LANES]
    r, j = rows_of(tall, width)
    place += [(j == base + c * kp + PQ * (r & 7) + (r >> 3)) & ((r & 7) < heads) for c in range(3)]
    r, j = rows_of(vp, width)
    place += [j == LANES + base + c * vp + r for c in range(3)]
    r, j = rows_of(SUBLANES, width)
    place += [(j == lay.square + PQ * r + piece) & (r < heads) for piece in range(3)]
    place = jnp.concatenate([jnp.where(found, 1.0, 0.0) for found in place], axis=0).astype(B16)
    to_kp = jnp.concatenate(to_kp, axis=0)
    to_vp = jnp.concatenate(to_vp, axis=0)
    ready()
    single = key_single[...]
    turn = [frames[i : i + 1, :] for i in range(12)]
    features = [nt(w_key[...], single), nt(w_value[...], single)]
    for choose, weight, height in ((to_kp, w_kp, tall), (to_vp, w_vp, vp)):
        rows = nt(nn(choose, weight[...]).astype(B16), single)
        moved = turned_by(turn, [rows[c * height : (c + 1) * height] for c in range(3)])
        moved = [(v + turn[9 + c]).astype(B16).astype(F32) for c, v in enumerate(moved)]
        features += moved
        if height == tall:
            square = moved[0] * moved[0] + moved[1] * moved[1] + moved[2] * moved[2]
            square = sum(square[group(p)] for p in range(PQ))
    first = square.astype(B16).astype(F32)
    second = (square - first).astype(B16).astype(F32)
    features = jnp.concatenate(features + [first, second, square - first - second], axis=0)
    packed[...] = nn(jnp.transpose(features).astype(B16), place).astype(B16)


def group(h):
    return slice(h * SUBLANES, (h + 1) * SUBLANES)


def gain_rows(head_weight, lay):
    row = iota((SUBLANES, LANES), 0)
    raw = jnp.zeros((SUBLANES, LANES), F32)
    for h in range(lay.heads):
        raw = jnp.where(row == h, jnp.broadcast_to(head_weight[:, h : h + 1], raw.shape), raw)
    gain = (jnp.maximum(raw, 0.0) + jnp.log1p(jnp.exp(-jnp.abs(raw)))) * POINT_SCALE
    return jnp.where(row < lay.heads, gain, 0.0)


def gain_lanes(gain, lay):
    zero, _ = head_of(gain.shape, lay)
    return jnp.sum(jnp.where(zero == iota(gain.shape, 0), gain, 0.0), axis=0, keepdims=True)


def early_kernel(
    lay, block, order, frames, query_single, w_query, w_qp, bias_weight, w_out, d_out, pair, head_weight, key_frames,
    w_key, w_value, w_kp, w_vp,
    left, base, d_base, d_row, w_out_rows, w_query_rows, table, pair_rows, gains, parcel, turned, scratch,
):
    kp, vp = lay.kp, lay.vp
    zero = nn(to_lane(lay.base, 0), w_key[...]) + nn(to_components(3 * kp, lay.base, kp, kp), w_kp[...])
    one = nn(to_lane(lay.base, 0), w_value[...]) + nn(to_components(3 * vp, lay.base, vp, vp), w_vp[...])
    parcel[:LANES, :] = zero.astype(B16)
    parcel[LANES : 2 * LANES, :] = one.astype(B16)
    parcel[2 * LANES :, :] = jnp.zeros((block + ROWS16, parcel.shape[1]), B16)
    gain = gain_rows(head_weight, lay)
    gains[...] = gain
    pieces = jnp.broadcast_to(gain_lanes(gain, lay), (ROWS16, LANES))
    first = pieces.astype(B16).astype(F32)
    second = (pieces - first).astype(B16).astype(F32)
    row = iota(pieces.shape, 0)
    pieces = jnp.where(
        row == 0, first, jnp.where(row == 1, second, jnp.where(row == 2, pieces - first - second, 0.0))
    )
    parcel[2 * LANES + block :, :LANES] = pieces.astype(B16)
    turn = jnp.transpose(key_frames[...])
    turned[:, : turn.shape[1]] = turn
    me = lax.axis_index("row")
    for place, offset in enumerate(order):
        j = pl.multiple_of((me ^ offset) * block, block)
        pair_rows[place * block : (place + 1) * block, :] = pair[0, pl.ds(j, block), :]
    turn = [jnp.broadcast_to(frames[:, i : i + 1], (1, LANES)) for i in range(12)]
    for i in range(12):
        table[i : i + 1, :] = turn[i]
    heads, start = lay.heads, lay.base
    width = C + 4 * PV + LANES
    near = C + 4 * PV
    shape = (SUBLANES, LANES)
    row, lane = iota(shape, 0), iota(shape, 1)
    zero_head, _ = head_of(shape, lay)
    w_q = nn(to_lane(start, 0), w_query[...]) + nn(to_components(3 * lay.kp, start, lay.kp, lay.kp), w_qp[...])
    w_q = w_q.astype(B16)
    w_query_rows[...] = w_q
    w_o = jnp.zeros((2 * LANES, w_out.shape[1]), F32)
    for h in range(heads):
        i, j = iota((2 * LANES, near), 0), iota((2 * LANES, near), 1)
        m = i - (LANES + h * C)
        found = (m >= 0) & (m < C) & (j == m)
        m = i - (start + h * PV)
        found = found | ((m >= 0) & (m < PV) & (j == C + 3 * PV + m))
        for c in range(3):
            m = i - (LANES + start + c * lay.vp + h * PV)
            found = found | ((m >= 0) & (m < PV) & (j == C + 3 * m + c))
        w_o = w_o + nn(pick(found), w_out[h * width : h * width + near, :])
    w_o = w_o.astype(B16)
    w_out_rows[: 2 * LANES, :] = w_o
    for h in range(heads):
        w_out_rows[(2 + h) * LANES : (3 + h) * LANES, :] = w_out[h * width + near : (h + 1) * width, :]
    single = jnp.broadcast_to(query_single[...], (SUBLANES, query_single.shape[1]))
    rows = nt(single, w_q)
    moved = turned_by(turn, unpack(rows, lay.kp))
    points = pack([(v + turn[9 + c]).astype(B16).astype(F32) for c, v in enumerate(moved)], lay.kp, start)
    query = jnp.where(lane < start, rows, 0.0).astype(B16).astype(F32)
    left[:SUBLANES, :] = jnp.where(zero_head == row, query, 0.0)
    minus = lane < 0
    for h in range(heads):
        at = lay.square + h * PQ
        minus = minus | ((row == h) & (lane >= at) & (lane < at + 3))
    mine = jnp.where(zero_head == row, points, 0.0)
    left[SUBLANES:, :] = jnp.where(minus, -0.5, mine)
    cotangent = jnp.broadcast_to(d_out[...], (SUBLANES, d_out.shape[1]))
    d_row[...] = nt(cotangent, w_o)
    scratch[...] = jnp.zeros_like(scratch)
    scratch[:heads, :] = bias_weight[...].astype(F32)
    for h in range(heads):
        d_pair = nt(cotangent, w_out[h * width + near : (h + 1) * width, :])
        scratch[SUBLANES + h : SUBLANES + h + 1, :] = d_pair[:1, :]
    both = nt(scratch[...].astype(B16), pair_rows[...])
    square = jnp.sum(mine * mine, axis=1, keepdims=True)
    base[...] = both[:SUBLANES] - 0.5 * gain[:, :1] * square
    d_base[...] = both[SUBLANES:]


def copied(sources, targets, sems):
    return [pltpu.make_async_copy(a, b, sems.at[i]) for i, (a, b) in enumerate(zip(sources, targets))]


def front_kernel(lay, block, order, split, *refs):
    first, second, outs = split
    keys, early = refs[:first], refs[first : first + second]
    packed, *results = refs[first + second : first + second + 1 + outs]
    held = refs[first + second + 1 + outs : -3]
    scratch, sems, early_sems = refs[-3:]
    copies = copied(keys, held[:first], sems)
    for copy in copies:
        copy.start()

    @pl.when(lax.axis_index("head") == 1)
    def _():
        ahead = copied(early, held[first:], early_sems)
        for copy in ahead:
            copy.start()
        for copy in ahead:
            copy.wait()
        early_kernel(lay, block, order, *held[first:], *results, scratch)

    def ready():
        for copy in copies:
            copy.wait()

    key_kernel(lay, ready, *held[:first], packed)


def later_kernel(lay, block, order, split, *refs):
    second, outs = split
    early, packed, had = refs[:second], refs[second], refs[second + 1 : second + 1 + outs]
    results = refs[second + 1 + outs : second + 1 + 2 * outs]
    held = refs[second + 1 + 2 * outs : -2]
    scratch, sems = refs[-2:]
    core = lax.axis_index("head")

    @pl.when(core == 0)
    def _():
        copies = copied(early, held, sems)
        for copy in copies:
            copy.start()
        for copy in copies:
            copy.wait()
        early_kernel(lay, block, order, *held, *results, scratch)

    @pl.when(core != 0)
    def _():
        for source, target in zip(had, results):
            target[...] = source[...]

    parcel = results[-2]
    parcel[2 * LANES : 2 * LANES + block, :LANES] = packed[:, :LANES]


def attention_kernel(lay, block, order, *refs):
    *parts, left, base, d_base, d_row, gains, table, message, features, weights, scores = refs
    frames = [table[i : i + 1, :] for i in range(12)]
    me = lax.axis_index("row")
    heads, vp, start = lay.heads, lay.vp, lay.base
    shape = (SUBLANES, LANES)
    row, lane = iota(shape, 0), iota(shape, 1)
    _, one_head = head_of(shape, lay)
    gain = gains[...]
    queries = left[...].astype(B16)
    first = jnp.concatenate([nt(queries, part[:, :LANES]) for part in parts], axis=1)
    logits = LOGIT_SCALE * (first[:SUBLANES] * (1.0 / math.sqrt(C)) + base[...] + gain[:, :1] * first[SUBLANES:])
    weight = jnp.exp(logits - jnp.max(logits, axis=1, keepdims=True))
    attention = weight / jnp.sum(weight, axis=1, keepdims=True)
    attention = jnp.where(iota(attention.shape, 0) < heads, attention, 0.0)
    attention_b = attention.astype(B16)
    sums = spread(attention_b, [part.at[:, LANES:] for part in parts])
    weights[...] = attention_b
    sums = jnp.sum(jnp.where(one_head == row, sums, 0.0), axis=0, keepdims=True)
    sums = jnp.broadcast_to(sums, shape)
    local = turned_back(frames, [v - frames[9 + c] for c, v in enumerate(unpack(sums, vp))])
    lengths = jnp.sqrt(1.0 + (local[0] * local[0] + local[1] * local[1] + local[2] * local[2]))
    d_one = d_row[:, LANES:]
    share = d_row[:, :LANES] / lengths
    d_points = turned_by(frames, [v + share * u for v, u in zip(unpack(d_one, vp), local)])
    d_side = jnp.where(lane < start, d_one, 0.0) + pack(d_points, vp, start)
    right = jnp.where(one_head == row, d_side, 0.0).astype(B16)
    d_attention = jnp.concatenate([nt(right, part[:, LANES:]) for part in parts], axis=1) + d_base[...]
    total = jnp.sum(attention * d_attention, axis=1, keepdims=True)
    score_b = (LOGIT_SCALE * attention * (d_attention - total)).astype(B16)
    query = jnp.sum(jnp.where(lane < lay.square, left[:SUBLANES, :] + left[SUBLANES:, :], 0.0), axis=0, keepdims=True)
    side = jnp.where(row == 2 * heads, jnp.broadcast_to(query, shape), 0.0)
    side = side + jnp.where(row == 2 * heads + 1, d_side, 0.0)
    both = attention_b.astype(F32) + pltpu.roll(score_b.astype(F32), heads, 0)
    for at in range(0, both.shape[1], LANES):
        tile = jnp.where(row < 2 * heads, both[:, at : at + LANES], side).astype(B16)
        for place in range(at // block, (at + LANES) // block):
            for core in range(2):
                message[(me ^ order[place]) * 2 + core, :, :] = tile
    scores[...] = score_b
    features[:, :LANES] = jnp.where((lane >= start) & (lane < start + vp), lengths, 0.0)
    features[:, LANES:] = jnp.where(lane < start, sums, 0.0) + pack(local, vp, start)


def spread(weights, parts):
    total, at = 0.0, 0
    for part in parts:
        total = total + nn(weights[:, at : at + part.shape[0]], part[...])
        at += part.shape[0]
    return total


def rows_kernel(lay, *refs):
    *parts, pair, left, scores, features, weights, w_out_rows, w_query_rows, gains, table, sums = refs
    frames = [table[i : i + 1, :] for i in range(12)]
    shape = (SUBLANES, LANES)
    row, lane = iota(shape, 0), iota(shape, 1)
    zero_head, _ = head_of(shape, lay)
    pair_sum = nn(weights[...], pair[...])
    pairs = [jnp.broadcast_to(pair_sum[h : h + 1, :], shape) for h in range(lay.heads)]
    result = nn(jnp.concatenate([features[...]] + pairs, axis=1).astype(B16), w_out_rows[...])
    score = scores[...].astype(F32)
    d_rows = spread(scores[...], [part.at[:, :LANES] for part in parts])
    score_sum = jnp.sum(score, axis=1, keepdims=True)
    points = left[SUBLANES:, :]
    d_rows = jnp.where(lane < lay.base, d_rows * (1.0 / math.sqrt(C)), gains[...] * (d_rows - score_sum * points))
    d_rows = jnp.broadcast_to(
        jnp.sum(jnp.where(zero_head == row, d_rows, 0.0), axis=0, keepdims=True), shape
    )
    local = pack(turned_back(frames, unpack(d_rows, lay.kp)), lay.kp, lay.base)
    both = (jnp.where(lane < lay.base, d_rows, 0.0) + local).astype(B16)
    sums[...] = jnp.concatenate([result, nn(both, w_query_rows[...])], axis=1)


def owner_kernel(lay, near, offsets, arrived, turned, parcel, other, result):
    heads, base = lay.heads, lay.base
    count = arrived.shape[0] // 2
    block = turned.shape[0]
    shape = (SUBLANES, LANES)
    whole = (count, SUBLANES, LANES)
    per = LANES // block
    apart = (iota(whole, 0) ^ lax.axis_index("row")) // near
    place = jnp.zeros(whole, jnp.int32)
    for i, offset in enumerate(offsets):
        place = jnp.where(apart == offset // near, i % per, place)
    row = iota(shape, 0)
    zero_head, one_head = head_of(shape, lay)
    lane = iota(shape, 1)
    keep0 = (zero_head >= 0) & (zero_head + heads == row)
    keep1 = one_head == row
    ones = jnp.broadcast_to(jnp.where(keep0 & (lane >= base), 1.0, 0.0)[None], whole)
    columns = [turned[:, i : i + 1] for i in range(9)]
    lane = iota((block, LANES), 1)
    me = lax.axis_index("head")
    total = None
    for core, held in ((me, parcel), (1 - me, other)):
        took = jnp.concatenate([arrived[pl.ds(q * 2 + core, 1)] for q in range(count)], axis=0).astype(F32)
        mine = took
        for part in range(1, per):
            mine = jnp.where(place == part, pltpu.roll(took, LANES - part * block, 2), mine)
        side0 = jnp.where(keep0[None], jnp.broadcast_to(took[:, 2 * heads : 2 * heads + 1, :], whole), 0.0)
        side1 = jnp.where(keep1[None], jnp.broadcast_to(took[:, 2 * heads + 1 : 2 * heads + 2, :], whole), 0.0)
        right = jnp.concatenate([side0, side1, ones], axis=2).reshape(count * SUBLANES, 3 * LANES).astype(B16)
        moved = jnp.transpose(mine.reshape(count * SUBLANES, LANES)).astype(B16)
        both = nn(moved, right)[:block]
        pieces = held[2 * LANES + block :, :LANES].astype(F32)
        gain = pieces[0:1] + pieces[1:2] + pieces[2:3]
        own = held[2 * LANES : 2 * LANES + block, :LANES].astype(F32)
        tile0, tile1 = both[:, :LANES], both[:, LANES : 2 * LANES]
        points = gain * (tile0 - both[:, 2 * LANES :] * own)
        points = pack(turned_back(columns, unpack(points, lay.kp)), lay.kp, base)
        tile0 = jnp.where(lane < base, tile0 * (1.0 / math.sqrt(C)), points)
        points = pack(turned_back(columns, unpack(tile1, lay.vp)), lay.vp, base)
        tile1 = jnp.where(lane < base, tile1, points)
        rows = jnp.concatenate([tile0, tile1], axis=1).astype(B16)
        part = nn(rows, held[: 2 * LANES, :])
        total = part if total is None else total + part
    result[...] = total


def finish_kernel(own, other, output, grad_query):
    width = output.shape[1]
    total = own[...] + other[...]
    output[...] = total[:1, :width].astype(output.dtype)
    grad_query[...] = total[:1, width:]


VMEM = pl.BlockSpec(memory_space=pltpu.VMEM)
HBM = pl.BlockSpec(memory_space=pltpu.HBM)


def call(body, outs, args, outside=0, scratch=(), last=False):
    size = sum(math.prod(v.shape) * v.dtype.itemsize for v in list(args) + list(outs))
    return pl.pallas_call(
        body,
        out_shape=tuple(outs),
        in_specs=[HBM] * outside + [VMEM] * (len(args) - outside),
        out_specs=tuple([pl.BlockSpec() if last else VMEM] * len(outs)),
        scratch_shapes=list(scratch),
        compiler_params=pltpu.CompilerParams(vmem_limit_bytes=(16 << 20) + 6 * size),
        cost_estimate=pl.CostEstimate(flops=1000000, bytes_accessed=size, transcendentals=0),
    )(*[pltpu.with_memory_space_constraint(v, pltpu.HBM) for v in args[:outside]], *args[outside:])


def buffers(args):
    return [pltpu.VMEM(v.shape, v.dtype) for v in args]


def shape_of(*dims, dtype=F32):
    return jax.ShapeDtypeStruct(dims, dtype)


def shards(
    query_single, key_single, pair, query_frames, key_frames, w_query, w_key, w_value, w_query_points, w_key_points,
    w_value_points, head_weight, bias_weight, w_out, d_out,
):
    lay = Layout(head_weight.shape[0])
    count = lax.axis_size("row")
    block, width = key_single.shape
    total = count * block
    near = 1
    while 4 * near * near <= count:
        near *= 2
    assert count & (count - 1) == 0

    def exchange(value, mask):
        return lax.ppermute(value, "row", [(i, i ^ mask) for i in range(count)])

    offsets = list(range(0, count, near))
    planes = list(range(near))
    order = [m ^ o for m in planes for o in offsets]

    weights = [w_key.T, w_value.T, w_key_points.T, w_value_points.T]
    key_args = [key_single, key_frames] + weights
    early_args = [
        query_frames.T, query_single, w_query.T, w_query_points.T, bias_weight, w_out, d_out, pair,
        head_weight.reshape(1, -1), key_frames,
    ] + weights
    early_outs = [
        shape_of(ROWS16, LANES), shape_of(SUBLANES, total), shape_of(SUBLANES, total),
        shape_of(SUBLANES, 2 * LANES), shape_of((2 + lay.heads) * LANES, width, dtype=B16),
        shape_of(LANES, width, dtype=B16), shape_of(ROWS16, LANES),
        shape_of(total, LANES, dtype=B16), shape_of(SUBLANES, LANES),
        shape_of(2 * LANES + block + ROWS16, width, dtype=B16), shape_of(block, LANES),
    ]
    first, second, outs = len(key_args), len(early_args), len(early_outs)
    packed, *had = call(
        functools.partial(front_kernel, lay, block, order, (first, second, outs)),
        [shape_of(block, 2 * LANES, dtype=B16)] + early_outs,
        key_args + early_args,
        first + second,
        buffers(key_args + early_args)
        + [pltpu.VMEM((ROWS16, LANES), F32), pltpu.SemaphoreType.DMA((first,)), pltpu.SemaphoreType.DMA((second,))],
    )
    line = jnp.concatenate([packed] + [exchange(packed, mask) for mask in offsets[1:]], axis=0)
    parts = [line] + [exchange(line, m) for m in planes[1:]]
    left, base, d_base, d_row, w_out_rows, w_query_rows, table, pair_rows, gains, parcel, turned = call(
        functools.partial(later_kernel, lay, block, order, (second, outs)),
        early_outs,
        early_args + [packed] + had,
        second,
        buffers(early_args) + [pltpu.VMEM((ROWS16, LANES), F32), pltpu.SemaphoreType.DMA((second,))],
    )
    swap = [(i, (i + 1) % 2) for i in range(2)]
    other = lax.ppermute(parcel, "head", swap)
    message, features, weight_rows, scores = call(
        functools.partial(attention_kernel, lay, block, order),
        [
            shape_of(2 * count, SUBLANES, LANES, dtype=B16), shape_of(SUBLANES, 2 * LANES),
            shape_of(SUBLANES, total, dtype=B16), shape_of(SUBLANES, total, dtype=B16),
        ],
        parts + [left, base, d_base, d_row, gains, table],
    )
    arrived = lax.all_to_all(message, ("row", "head"), 0, 0, tiled=True)
    (sums,) = call(
        functools.partial(rows_kernel, lay),
        [shape_of(SUBLANES, 2 * width)],
        parts + [pair_rows, left, scores, features, weight_rows, w_out_rows, w_query_rows, gains, table],
    )
    output, grad_query = call(
        finish_kernel,
        [shape_of(1, width, dtype=B16), shape_of(1, width)],
        [sums, lax.ppermute(sums, "head", swap)],
        last=True,
    )
    (grad_keys,) = call(
        functools.partial(owner_kernel, lay, near, offsets),
        [shape_of(block, width)],
        [arrived, turned, parcel, other],
        last=True,
    )
    return (output, grad_query, grad_keys)


def solution(mesh):
    return jax.shard_map(
        shards,
        mesh=mesh,
        in_specs=(
            P("row", None),
            P("row", None),
            P("row", None, None),
            P(None, "row"),
            P(None, "row"),
            P(None, "head"),
            P(None, "head"),
            P(None, "head"),
            P(None, "head"),
            P(None, "head"),
            P(None, "head"),
            P("head"),
            P("head", None),
            P("head", None),
            P("row", None),
        ),
        out_specs=(P("row", None), P("row", None), P("row", None)),
        check_vma=False,
    )
```

```python
import functools
import math

import jax
import jax.numpy as jnp
from jax import lax
from jax.experimental import pallas as pl
from jax.experimental.pallas import tpu as pltpu
from jax.sharding import PartitionSpec as P

C = 16
PQ = 4
PV = 8
LANES = 128
SUBLANES = 8
ROWS16 = 16
LOGIT_SCALE = math.sqrt(1.0 / 3.0)
POINT_SCALE = math.sqrt(2.0 / (9.0 * PQ))
F32 = jnp.float32
B16 = jnp.bfloat16


class Layout:
    def __init__(self, heads):
        self.heads = heads
        self.base = heads * C
        self.kp = heads * PQ
        self.vp = heads * PV
        self.square = self.base + 3 * self.kp
        assert self.square + self.kp <= LANES and self.base + 3 * self.vp <= LANES
        assert 2 * heads + 2 <= SUBLANES and PQ == 4


def nn(a, b, precision=None):
    return lax.dot_general(a, b, (((1,), (0,)), ((), ())), precision=precision, preferred_element_type=F32)


def nt(a, b):
    return lax.dot_general(a, b, (((1,), (1,)), ((), ())), preferred_element_type=F32)


def iota(shape, dim):
    return lax.broadcasted_iota(jnp.int32, shape, dim)


def pick(condition):
    return jnp.where(condition, 1.0, 0.0).astype(B16)


def to_lane(rows, offset):
    j, i = iota((LANES, rows), 0), iota((LANES, rows), 1)
    return pick(j == i + offset)


def to_components(rows, offset, points, seg):
    j, i = iota((LANES, rows), 0), iota((LANES, rows), 1)
    found = j < 0
    for c in range(3):
        m = j - (c * seg + offset)
        found = found | ((m >= 0) & (m < points) & (i == 3 * m + c))
    return pick(found)


def unpack(tile, seg):
    return tile, pltpu.roll(tile, LANES - seg, 1), pltpu.roll(tile, LANES - 2 * seg, 1)


def pack(parts, seg, base):
    lane = iota(parts[0].shape, 1)
    keep = (lane >= base) & (lane < base + seg)
    x, y, z = (jnp.where(keep, v, 0.0) for v in parts)
    return x + pltpu.roll(y, seg, 1) + pltpu.roll(z, 2 * seg, 1)


def head_of(shape, lay):
    lane = iota(shape, 1)
    zero = jnp.full(shape, -1, jnp.int32)
    one = jnp.full(shape, -1, jnp.int32)
    for h in range(lay.heads):
        same = (lane >= h * C) & (lane < (h + 1) * C)
        zero, one = jnp.where(same, h, zero), jnp.where(same, h, one)
        for c in range(3):
            k = lay.base + c * lay.kp + h * PQ
            v = lay.base + c * lay.vp + h * PV
            zero = jnp.where((lane >= k) & (lane < k + PQ), h, zero)
            one = jnp.where((lane >= v) & (lane < v + PV), h, one)
    return zero, one


def turned_by(frames, vectors):
    x, y, z = vectors
    return [frames[3 * c] * x + frames[3 * c + 1] * y + frames[3 * c + 2] * z for c in range(3)]


def turned_back(frames, vectors):
    x, y, z = vectors
    return [frames[d] * x + frames[3 + d] * y + frames[6 + d] * z for d in range(3)]


def key_kernel(lay, ready, key_single, frames, w_key, w_value, w_kp, w_vp, packed):
    heads, kp, vp, base = lay.heads, lay.kp, lay.vp, lay.base
    tall = PQ * SUBLANES

    def rows_of(count, width):
        return iota((count, width), 0), iota((count, width), 1)

    r, i = rows_of(tall, 3 * kp)
    to_kp = [pick((i == 3 * PQ * (r & 7) + 3 * (r >> 3) + c) & ((r & 7) < heads)) for c in range(3)]
    r, i = rows_of(vp, 3 * vp)
    to_vp = [pick(i == 3 * r + c) for c in range(3)]
    width = 2 * LANES
    r, j = rows_of(base, width)
    place = [j == r, j == r + LANES]
    r, j = rows_of(tall, width)
    place += [(j == base + c * kp + PQ * (r & 7) + (r >> 3)) & ((r & 7) < heads) for c in range(3)]
    r, j = rows_of(vp, width)
    place += [j == LANES + base + c * vp + r for c in range(3)]
    r, j = rows_of(SUBLANES, width)
    place += [(j == lay.square + PQ * r + piece) & (r < heads) for piece in range(3)]
    place = jnp.concatenate([jnp.where(found, 1.0, 0.0) for found in place], axis=0).astype(B16)
    to_kp = jnp.concatenate(to_kp, axis=0)
    to_vp = jnp.concatenate(to_vp, axis=0)
    ready()
    single = key_single[...]
    turn = [frames[i : i + 1, :] for i in range(12)]
    features = [nt(w_key[...], single), nt(w_value[...], single)]
    for choose, weight, height in ((to_kp, w_kp, tall), (to_vp, w_vp, vp)):
        rows = nt(nn(choose, weight[...]).astype(B16), single)
        moved = turned_by(turn, [rows[c * height : (c + 1) * height] for c in range(3)])
        moved = [(v + turn[9 + c]).astype(B16).astype(F32) for c, v in enumerate(moved)]
        features += moved
        if height == tall:
            square = moved[0] * moved[0] + moved[1] * moved[1] + moved[2] * moved[2]
            square = sum(square[group(p)] for p in range(PQ))
    first = square.astype(B16).astype(F32)
    second = (square - first).astype(B16).astype(F32)
    features = jnp.concatenate(features + [first, second, square - first - second], axis=0)
    packed[...] = nn(jnp.transpose(features).astype(B16), place).astype(B16)


def group(h):
    return slice(h * SUBLANES, (h + 1) * SUBLANES)


def gain_rows(head_weight, lay):
    row = iota((SUBLANES, LANES), 0)
    raw = jnp.zeros((SUBLANES, LANES), F32)
    for h in range(lay.heads):
        raw = jnp.where(row == h, jnp.broadcast_to(head_weight[:, h : h + 1], raw.shape), raw)
    gain = (jnp.maximum(raw, 0.0) + jnp.log1p(jnp.exp(-jnp.abs(raw)))) * POINT_SCALE
    return jnp.where(row < lay.heads, gain, 0.0)


def gain_lanes(gain, lay):
    zero, _ = head_of(gain.shape, lay)
    return jnp.sum(jnp.where(zero == iota(gain.shape, 0), gain, 0.0), axis=0, keepdims=True)


def early_kernel(
    lay, block, order, frames, query_single, w_query, w_qp, bias_weight, w_out, d_out, pair, head_weight, key_frames,
    w_key, w_value, w_kp, w_vp, packed,
    left, base, d_base, d_row, w_out_rows, w_query_rows, table, pair_rows, gains, parcel, turned, scratch,
):
    kp, vp = lay.kp, lay.vp
    zero = nn(to_lane(lay.base, 0), w_key[...]) + nn(to_components(3 * kp, lay.base, kp, kp), w_kp[...])
    one = nn(to_lane(lay.base, 0), w_value[...]) + nn(to_components(3 * vp, lay.base, vp, vp), w_vp[...])
    parcel[:LANES, :] = zero.astype(B16)
    parcel[LANES : 2 * LANES, :] = one.astype(B16)
    parcel[2 * LANES :, :] = jnp.zeros((block + ROWS16, parcel.shape[1]), B16)
    parcel[2 * LANES : 2 * LANES + block, :LANES] = packed[:, :LANES]
    gain = gain_rows(head_weight, lay)
    gains[...] = gain
    pieces = jnp.broadcast_to(gain_lanes(gain, lay), (ROWS16, LANES))
    first = pieces.astype(B16).astype(F32)
    second = (pieces - first).astype(B16).astype(F32)
    row = iota(pieces.shape, 0)
    pieces = jnp.where(
        row == 0, first, jnp.where(row == 1, second, jnp.where(row == 2, pieces - first - second, 0.0))
    )
    parcel[2 * LANES + block :, :LANES] = pieces.astype(B16)
    turn = jnp.transpose(key_frames[...])
    turned[:, : turn.shape[1]] = turn
    me = lax.axis_index("row")
    for place, offset in enumerate(order):
        j = pl.multiple_of((me ^ offset) * block, block)
        pair_rows[place * block : (place + 1) * block, :] = pair[0, pl.ds(j, block), :]
    turn = [jnp.broadcast_to(frames[:, i : i + 1], (1, LANES)) for i in range(12)]
    for i in range(12):
        table[i : i + 1, :] = turn[i]
    heads, start = lay.heads, lay.base
    width = C + 4 * PV + LANES
    near = C + 4 * PV
    shape = (SUBLANES, LANES)
    row, lane = iota(shape, 0), iota(shape, 1)
    zero_head, _ = head_of(shape, lay)
    w_q = nn(to_lane(start, 0), w_query[...]) + nn(to_components(3 * lay.kp, start, lay.kp, lay.kp), w_qp[...])
    w_q = w_q.astype(B16)
    w_query_rows[...] = w_q
    w_o = jnp.zeros((2 * LANES, w_out.shape[1]), F32)
    for h in range(heads):
        i, j = iota((2 * LANES, near), 0), iota((2 * LANES, near), 1)
        m = i - (LANES + h * C)
        found = (m >= 0) & (m < C) & (j == m)
        m = i - (start + h * PV)
        found = found | ((m >= 0) & (m < PV) & (j == C + 3 * PV + m))
        for c in range(3):
            m = i - (LANES + start + c * lay.vp + h * PV)
            found = found | ((m >= 0) & (m < PV) & (j == C + 3 * m + c))
        w_o = w_o + nn(pick(found), w_out[h * width : h * width + near, :])
    w_o = w_o.astype(B16)
    w_out_rows[: 2 * LANES, :] = w_o
    for h in range(heads):
        w_out_rows[(2 + h) * LANES : (3 + h) * LANES, :] = w_out[h * width + near : (h + 1) * width, :]
    single = jnp.broadcast_to(query_single[...], (SUBLANES, query_single.shape[1]))
    rows = nt(single, w_q)
    moved = turned_by(turn, unpack(rows, lay.kp))
    points = pack([(v + turn[9 + c]).astype(B16).astype(F32) for c, v in enumerate(moved)], lay.kp, start)
    query = jnp.where(lane < start, rows, 0.0).astype(B16).astype(F32)
    left[:SUBLANES, :] = jnp.where(zero_head == row, query, 0.0)
    minus = lane < 0
    for h in range(heads):
        at = lay.square + h * PQ
        minus = minus | ((row == h) & (lane >= at) & (lane < at + 3))
    mine = jnp.where(zero_head == row, points, 0.0)
    left[SUBLANES:, :] = jnp.where(minus, -0.5, mine)
    cotangent = jnp.broadcast_to(d_out[...], (SUBLANES, d_out.shape[1]))
    d_row[...] = nt(cotangent, w_o)
    scratch[...] = jnp.zeros_like(scratch)
    scratch[:heads, :] = bias_weight[...].astype(F32)
    for h in range(heads):
        d_pair = nt(cotangent, w_out[h * width + near : (h + 1) * width, :])
        scratch[SUBLANES + h : SUBLANES + h + 1, :] = d_pair[:1, :]
    both = nt(scratch[...].astype(B16), pair_rows[...])
    square = jnp.sum(mine * mine, axis=1, keepdims=True)
    base[...] = both[:SUBLANES] - 0.5 * gain[:, :1] * square
    d_base[...] = both[SUBLANES:]


def attention_kernel(lay, block, order, *refs):
    *parts, left, base, d_base, d_row, gains, table, message, features, weights, scores = refs
    frames = [table[i : i + 1, :] for i in range(12)]
    me = lax.axis_index("row")
    heads, vp, start = lay.heads, lay.vp, lay.base
    shape = (SUBLANES, LANES)
    row, lane = iota(shape, 0), iota(shape, 1)
    _, one_head = head_of(shape, lay)
    gain = gains[...]
    queries = left[...].astype(B16)
    first = jnp.concatenate([nt(queries, part[:, :LANES]) for part in parts], axis=1)
    logits = LOGIT_SCALE * (first[:SUBLANES] * (1.0 / math.sqrt(C)) + base[...] + gain[:, :1] * first[SUBLANES:])
    weight = jnp.exp(logits - jnp.max(logits, axis=1, keepdims=True))
    weight = jnp.where(iota(weight.shape, 0) < heads, weight, 0.0)
    whole = weight.astype(B16).astype(F32)
    sums = spread(jnp.concatenate([whole, weight - whole], axis=0).astype(B16), [part.at[:, LANES:] for part in parts])
    total = jnp.sum(weight, axis=1, keepdims=True)
    inverse = 1.0 / jnp.where(row[:, :1] < heads, total, 1.0)
    d_total = jnp.sum(weight * d_base[...], axis=1, keepdims=True) * inverse
    attention = weight * inverse
    attention_b = attention.astype(B16)
    weights[...] = attention_b
    sums = jnp.where(one_head == row, (sums[:SUBLANES] + sums[SUBLANES:]) * inverse, 0.0)
    sums = jnp.broadcast_to(jnp.sum(sums, axis=0, keepdims=True), shape)
    local = turned_back(frames, [v - frames[9 + c] for c, v in enumerate(unpack(sums, vp))])
    lengths = jnp.sqrt(1.0 + (local[0] * local[0] + local[1] * local[1] + local[2] * local[2]))
    d_one = d_row[:, LANES:]
    share = d_row[:, :LANES] / lengths
    d_points = turned_by(frames, [v + share * u for v, u in zip(unpack(d_one, vp), local)])
    d_side = jnp.where(lane < start, d_one, 0.0) + pack(d_points, vp, start)
    right = jnp.where(one_head == row, d_side, 0.0).astype(B16)
    d_total = d_total + jnp.sum(right.astype(F32) * sums, axis=1, keepdims=True)
    d_attention = jnp.concatenate([nt(right, part[:, LANES:]) for part in parts], axis=1) + d_base[...]
    score_b = (LOGIT_SCALE * attention * (d_attention - d_total)).astype(B16)
    query = jnp.sum(jnp.where(lane < lay.square, left[:SUBLANES, :] + left[SUBLANES:, :], 0.0), axis=0, keepdims=True)
    side = jnp.where(row == 2 * heads, jnp.broadcast_to(query, shape), 0.0)
    side = side + jnp.where(row == 2 * heads + 1, d_side, 0.0)
    both = attention_b.astype(F32) + pltpu.roll(score_b.astype(F32), heads, 0)
    for at in range(0, both.shape[1], LANES):
        for place in range(at // block, (at + LANES) // block):
            tile = both[:, at : at + LANES]
            if place * block != at:
                tile = pltpu.roll(tile, LANES - (place * block - at), 1)
            tile = jnp.where(row < 2 * heads, tile, side).astype(B16)
            for core in range(2):
                message[(me ^ order[place]) * 2 + core, :, :] = tile
    scores[...] = score_b
    features[:, :LANES] = jnp.where((lane >= start) & (lane < start + vp), lengths, 0.0)
    features[:, LANES:] = jnp.where(lane < start, sums, 0.0) + pack(local, vp, start)


def spread(weights, parts):
    total, at = 0.0, 0
    for part in parts:
        total = total + nn(weights[:, at : at + part.shape[0]], part[...])
        at += part.shape[0]
    return total


def rows_kernel(lay, *refs):
    *parts, pair, left, scores, features, weights, w_out_rows, w_query_rows, gains, table, sums = refs
    frames = [table[i : i + 1, :] for i in range(12)]
    shape = (SUBLANES, LANES)
    row, lane = iota(shape, 0), iota(shape, 1)
    zero_head, _ = head_of(shape, lay)
    pair_sum = nn(weights[...], pair[...])
    pairs = [jnp.broadcast_to(pair_sum[h : h + 1, :], shape) for h in range(lay.heads)]
    result = nn(jnp.concatenate([features[...]] + pairs, axis=1).astype(B16), w_out_rows[...])
    score = scores[...].astype(F32)
    d_rows = spread(scores[...], [part.at[:, :LANES] for part in parts])
    score_sum = jnp.sum(score, axis=1, keepdims=True)
    points = left[SUBLANES:, :]
    d_rows = jnp.where(lane < lay.base, d_rows * (1.0 / math.sqrt(C)), gains[...] * (d_rows - score_sum * points))
    d_rows = jnp.broadcast_to(
        jnp.sum(jnp.where(zero_head == row, d_rows, 0.0), axis=0, keepdims=True), shape
    )
    local = pack(turned_back(frames, unpack(d_rows, lay.kp)), lay.kp, lay.base)
    both = (jnp.where(lane < lay.base, d_rows, 0.0) + local).astype(B16)
    sums[...] = jnp.concatenate([result, nn(both, w_query_rows[...])], axis=1)


def owner_kernel(lay, arrived, turned, parcel, other, result):
    heads, base = lay.heads, lay.base
    count = arrived.shape[0] // 2
    block = turned.shape[0]
    shape = (SUBLANES, LANES)
    whole = (count, SUBLANES, LANES)
    row = iota(shape, 0)
    zero_head, one_head = head_of(shape, lay)
    lane = iota(shape, 1)
    keep0 = (zero_head >= 0) & (zero_head + heads == row)
    keep1 = one_head == row
    ones = jnp.broadcast_to(jnp.where(keep0 & (lane >= base), 1.0, 0.0)[None], whole)
    columns = [turned[:, i : i + 1] for i in range(9)]
    lane = iota((block, LANES), 1)
    me = lax.axis_index("head")
    total = None
    for core, held in ((me, parcel), (1 - me, other)):
        took = jnp.concatenate([arrived[pl.ds(q * 2 + core, 1)] for q in range(count)], axis=0).astype(F32)
        side0 = jnp.where(keep0[None], jnp.broadcast_to(took[:, 2 * heads : 2 * heads + 1, :], whole), 0.0)
        side1 = jnp.where(keep1[None], jnp.broadcast_to(took[:, 2 * heads + 1 : 2 * heads + 2, :], whole), 0.0)
        right = jnp.concatenate([side0, side1, ones], axis=2).reshape(count * SUBLANES, 3 * LANES).astype(B16)
        moved = jnp.transpose(took.reshape(count * SUBLANES, LANES)).astype(B16)
        both = nn(moved, right)[:block]
        pieces = held[2 * LANES + block :, :LANES].astype(F32)
        gain = pieces[0:1] + pieces[1:2] + pieces[2:3]
        own = held[2 * LANES : 2 * LANES + block, :LANES].astype(F32)
        tile0, tile1 = both[:, :LANES], both[:, LANES : 2 * LANES]
        points = gain * (tile0 - both[:, 2 * LANES :] * own)
        points = pack(turned_back(columns, unpack(points, lay.kp)), lay.kp, base)
        tile0 = jnp.where(lane < base, tile0 * (1.0 / math.sqrt(C)), points)
        points = pack(turned_back(columns, unpack(tile1, lay.vp)), lay.vp, base)
        tile1 = jnp.where(lane < base, tile1, points)
        rows = jnp.concatenate([tile0, tile1], axis=1).astype(B16)
        part = nn(rows, held[: 2 * LANES, :])
        total = part if total is None else total + part
    result[...] = total


def finish_kernel(own, other, output, grad_query):
    width = output.shape[1]
    total = own[...] + other[...]
    output[...] = total[:1, :width].astype(output.dtype)
    grad_query[...] = total[:1, width:]


VMEM = pl.BlockSpec(memory_space=pltpu.VMEM)
HBM = pl.BlockSpec(memory_space=pltpu.HBM)


def call(body, outs, args, fresh=0, scratch=(), flops=1000000, last=False, waits=False):
    size = sum(math.prod(v.shape) * v.dtype.itemsize for v in list(args) + list(outs))

    def kernel(*refs):
        if fresh:
            *refs, sems = refs
            held = refs[len(refs) - fresh :]
            copies = [pltpu.make_async_copy(refs[i], held[i], sems.at[i]) for i in range(fresh)]
            for copy in copies:
                copy.start()

            def ready():
                for copy in copies:
                    copy.wait()

            if not waits:
                ready()
            refs = list(held) + list(refs[fresh : len(refs) - fresh])
        body(*([ready] if waits else []), *refs)

    own = [pltpu.VMEM(v.shape, v.dtype) for v in args[:fresh]]
    return pl.pallas_call(
        kernel,
        out_shape=tuple(outs),
        in_specs=[HBM] * fresh + [VMEM] * (len(args) - fresh),
        out_specs=tuple([pl.BlockSpec() if last else VMEM] * len(outs)),
        scratch_shapes=list(scratch) + own + ([pltpu.SemaphoreType.DMA((fresh,))] if fresh else []),
        compiler_params=pltpu.CompilerParams(vmem_limit_bytes=(16 << 20) + 6 * size),
        cost_estimate=pl.CostEstimate(flops=flops, bytes_accessed=size, transcendentals=0),
    )(*[pltpu.with_memory_space_constraint(v, pltpu.HBM) for v in args[:fresh]], *args[fresh:])


def shape_of(*dims, dtype=F32):
    return jax.ShapeDtypeStruct(dims, dtype)


def shards(
    query_single, key_single, pair, query_frames, key_frames, w_query, w_key, w_value, w_query_points, w_key_points,
    w_value_points, head_weight, bias_weight, w_out, d_out,
):
    lay = Layout(head_weight.shape[0])
    count = lax.axis_size("row")
    block, width = key_single.shape
    total = count * block
    near = 1
    while 4 * near * near <= count:
        near *= 2
    assert count & (count - 1) == 0

    def exchange(value, mask):
        return lax.ppermute(value, "row", [(i, i ^ mask) for i in range(count)])

    (packed,) = call(
        functools.partial(key_kernel, lay),
        [shape_of(block, 2 * LANES, dtype=B16)],
        [
            key_single, key_frames, w_key.T, w_value.T, w_key_points.T, w_value_points.T,
        ],
        6,
        waits=True,
    )
    offsets = list(range(0, count, near))
    line = jnp.concatenate([packed] + [exchange(packed, mask) for mask in offsets[1:]], axis=0)
    planes = list(range(near))
    parts = [line] + [exchange(line, m) for m in planes[1:]]
    order = [m ^ o for m in planes for o in offsets]

    left, base, d_base, d_row, w_out_rows, w_query_rows, table, pair_rows, gains, parcel, turned = call(
        functools.partial(early_kernel, lay, block, order),
        [
            shape_of(ROWS16, LANES), shape_of(SUBLANES, total), shape_of(SUBLANES, total),
            shape_of(SUBLANES, 2 * LANES), shape_of((2 + lay.heads) * LANES, width, dtype=B16),
            shape_of(LANES, width, dtype=B16), shape_of(ROWS16, LANES),
            shape_of(total, LANES, dtype=B16), shape_of(SUBLANES, LANES),
            shape_of(2 * LANES + block + ROWS16, width, dtype=B16), shape_of(block, LANES),
        ],
        [
            query_frames.T, query_single, w_query.T, w_query_points.T, bias_weight, w_out, d_out, pair,
            head_weight.reshape(1, -1), key_frames, w_key.T, w_value.T, w_key_points.T, w_value_points.T, packed,
        ],
        14,
        [pltpu.VMEM((ROWS16, LANES), F32)],
    )
    swap = [(i, (i + 1) % 2) for i in range(2)]
    other = lax.ppermute(parcel, "head", swap)
    message, features, weight_rows, scores = call(
        functools.partial(attention_kernel, lay, block, order),
        [
            shape_of(2 * count, SUBLANES, LANES, dtype=B16), shape_of(SUBLANES, 2 * LANES),
            shape_of(SUBLANES, total, dtype=B16), shape_of(SUBLANES, total, dtype=B16),
        ],
        parts + [left, base, d_base, d_row, gains, table],
    )
    arrived = lax.all_to_all(message, ("row", "head"), 0, 0, tiled=True)
    (sums,) = call(
        functools.partial(rows_kernel, lay),
        [shape_of(SUBLANES, 2 * width)],
        parts + [pair_rows, left, scores, features, weight_rows, w_out_rows, w_query_rows, gains, table],
    )
    output, grad_query = call(
        finish_kernel,
        [shape_of(1, width, dtype=B16), shape_of(1, width)],
        [sums, lax.ppermute(sums, "head", swap)],
        last=True,
    )
    (grad_keys,) = call(
        functools.partial(owner_kernel, lay),
        [shape_of(block, width)],
        [arrived, turned, parcel, other],
        last=True,
    )
    return (output, grad_query, grad_keys)


def solution(mesh):
    return jax.shard_map(
        shards,
        mesh=mesh,
        in_specs=(
            P("row", None),
            P("row", None),
            P("row", None, None),
            P(None, "row"),
            P(None, "row"),
            P(None, "head"),
            P(None, "head"),
            P(None, "head"),
            P(None, "head"),
            P(None, "head"),
            P(None, "head"),
            P("head"),
            P("head", None),
            P("head", None),
            P("row", None),
        ),
        out_specs=(P("row", None), P("row", None), P("row", None)),
        check_vma=False,
    )
```

```python
import functools
import math

import jax
import jax.numpy as jnp
from jax import lax
from jax.experimental import pallas as pl
from jax.experimental.pallas import tpu as pltpu
from jax.sharding import PartitionSpec as P

C = 16
PQ = 4
PV = 8
LANES = 128
SUBLANES = 8
ROWS16 = 16
LOGIT_SCALE = math.sqrt(1.0 / 3.0)
POINT_SCALE = math.sqrt(2.0 / (9.0 * PQ))
F32 = jnp.float32
B16 = jnp.bfloat16


class Layout:
    def __init__(self, heads):
        self.heads = heads
        self.base = heads * C
        self.kp = heads * PQ
        self.vp = heads * PV
        self.square = self.base + 3 * self.kp
        assert self.square + self.kp <= LANES and self.base + 3 * self.vp <= LANES
        assert 2 * heads + 2 <= SUBLANES and PQ == 4


def nn(a, b, precision=None):
    return lax.dot_general(a, b, (((1,), (0,)), ((), ())), precision=precision, preferred_element_type=F32)


def nt(a, b):
    return lax.dot_general(a, b, (((1,), (1,)), ((), ())), preferred_element_type=F32)


def iota(shape, dim):
    return lax.broadcasted_iota(jnp.int32, shape, dim)


def pick(condition):
    return jnp.where(condition, 1.0, 0.0).astype(B16)


def to_lane(rows, offset):
    j, i = iota((LANES, rows), 0), iota((LANES, rows), 1)
    return pick(j == i + offset)


def to_components(rows, offset, points, seg):
    j, i = iota((LANES, rows), 0), iota((LANES, rows), 1)
    found = j < 0
    for c in range(3):
        m = j - (c * seg + offset)
        found = found | ((m >= 0) & (m < points) & (i == 3 * m + c))
    return pick(found)


def unpack(tile, seg):
    return tile, pltpu.roll(tile, LANES - seg, 1), pltpu.roll(tile, LANES - 2 * seg, 1)


def pack(parts, seg, base):
    lane = iota(parts[0].shape, 1)
    keep = (lane >= base) & (lane < base + seg)
    x, y, z = (jnp.where(keep, v, 0.0) for v in parts)
    return x + pltpu.roll(y, seg, 1) + pltpu.roll(z, 2 * seg, 1)


def head_of(shape, lay):
    lane = iota(shape, 1)
    zero = jnp.full(shape, -1, jnp.int32)
    one = jnp.full(shape, -1, jnp.int32)
    for h in range(lay.heads):
        same = (lane >= h * C) & (lane < (h + 1) * C)
        zero, one = jnp.where(same, h, zero), jnp.where(same, h, one)
        for c in range(3):
            k = lay.base + c * lay.kp + h * PQ
            v = lay.base + c * lay.vp + h * PV
            zero = jnp.where((lane >= k) & (lane < k + PQ), h, zero)
            one = jnp.where((lane >= v) & (lane < v + PV), h, one)
    return zero, one


def turned_by(frames, vectors):
    x, y, z = vectors
    return [frames[3 * c] * x + frames[3 * c + 1] * y + frames[3 * c + 2] * z for c in range(3)]


def turned_back(frames, vectors):
    x, y, z = vectors
    return [frames[d] * x + frames[3 + d] * y + frames[6 + d] * z for d in range(3)]


def key_kernel(lay, ready, key_single, frames, w_key, w_value, w_kp, w_vp, packed):
    heads, kp, vp, base = lay.heads, lay.kp, lay.vp, lay.base
    tall = PQ * SUBLANES

    def rows_of(count, width):
        return iota((count, width), 0), iota((count, width), 1)

    r, i = rows_of(tall, 3 * kp)
    to_kp = [pick((i == 3 * PQ * (r & 7) + 3 * (r >> 3) + c) & ((r & 7) < heads)) for c in range(3)]
    r, i = rows_of(vp, 3 * vp)
    to_vp = [pick(i == 3 * r + c) for c in range(3)]
    width = 2 * LANES
    r, j = rows_of(base, width)
    place = [j == r, j == r + LANES]
    r, j = rows_of(tall, width)
    place += [(j == base + c * kp + PQ * (r & 7) + (r >> 3)) & ((r & 7) < heads) for c in range(3)]
    r, j = rows_of(vp, width)
    place += [j == LANES + base + c * vp + r for c in range(3)]
    r, j = rows_of(SUBLANES, width)
    place += [(j == lay.square + PQ * r + piece) & (r < heads) for piece in range(3)]
    place = jnp.concatenate([jnp.where(found, 1.0, 0.0) for found in place], axis=0).astype(B16)
    to_kp = jnp.concatenate(to_kp, axis=0)
    to_vp = jnp.concatenate(to_vp, axis=0)
    ready()
    single = key_single[...]
    turn = [frames[i : i + 1, :] for i in range(12)]
    features = [nt(w_key[...], single), nt(w_value[...], single)]
    for choose, weight, height in ((to_kp, w_kp, tall), (to_vp, w_vp, vp)):
        rows = nt(nn(choose, weight[...]).astype(B16), single)
        moved = turned_by(turn, [rows[c * height : (c + 1) * height] for c in range(3)])
        moved = [(v + turn[9 + c]).astype(B16).astype(F32) for c, v in enumerate(moved)]
        features += moved
        if height == tall:
            square = moved[0] * moved[0] + moved[1] * moved[1] + moved[2] * moved[2]
            square = sum(square[group(p)] for p in range(PQ))
    first = square.astype(B16).astype(F32)
    second = (square - first).astype(B16).astype(F32)
    features = jnp.concatenate(features + [first, second, square - first - second], axis=0)
    packed[...] = nn(jnp.transpose(features).astype(B16), place).astype(B16)


def group(h):
    return slice(h * SUBLANES, (h + 1) * SUBLANES)


def gain_rows(head_weight, lay):
    row = iota((SUBLANES, LANES), 0)
    raw = jnp.zeros((SUBLANES, LANES), F32)
    for h in range(lay.heads):
        raw = jnp.where(row == h, jnp.broadcast_to(head_weight[:, h : h + 1], raw.shape), raw)
    gain = (jnp.maximum(raw, 0.0) + jnp.log1p(jnp.exp(-jnp.abs(raw)))) * POINT_SCALE
    return jnp.where(row < lay.heads, gain, 0.0)


def gain_lanes(gain, lay):
    zero, _ = head_of(gain.shape, lay)
    return jnp.sum(jnp.where(zero == iota(gain.shape, 0), gain, 0.0), axis=0, keepdims=True)


def early_kernel(
    lay, block, order, frames, query_single, w_query, w_qp, bias_weight, w_out, d_out, pair, head_weight, key_frames,
    w_key, w_value, w_kp, w_vp, packed,
    left, base, d_base, d_row, w_out_rows, w_query_rows, table, pair_rows, gains, parcel, turned, scratch,
):
    kp, vp = lay.kp, lay.vp
    zero = nn(to_lane(lay.base, 0), w_key[...]) + nn(to_components(3 * kp, lay.base, kp, kp), w_kp[...])
    one = nn(to_lane(lay.base, 0), w_value[...]) + nn(to_components(3 * vp, lay.base, vp, vp), w_vp[...])
    parcel[:LANES, :] = zero.astype(B16)
    parcel[LANES : 2 * LANES, :] = one.astype(B16)
    parcel[2 * LANES :, :] = jnp.zeros((block + ROWS16, parcel.shape[1]), B16)
    parcel[2 * LANES : 2 * LANES + block, :LANES] = packed[:, :LANES]
    gain = gain_rows(head_weight, lay)
    gains[...] = gain
    pieces = jnp.broadcast_to(gain_lanes(gain, lay), (ROWS16, LANES))
    first = pieces.astype(B16).astype(F32)
    second = (pieces - first).astype(B16).astype(F32)
    row = iota(pieces.shape, 0)
    pieces = jnp.where(
        row == 0, first, jnp.where(row == 1, second, jnp.where(row == 2, pieces - first - second, 0.0))
    )
    parcel[2 * LANES + block :, :LANES] = pieces.astype(B16)
    turn = jnp.transpose(key_frames[...])
    turned[:, : turn.shape[1]] = turn
    me = lax.axis_index("row")
    for place, offset in enumerate(order):
        j = pl.multiple_of((me ^ offset) * block, block)
        pair_rows[place * block : (place + 1) * block, :] = pair[0, pl.ds(j, block), :]
    turn = [jnp.broadcast_to(frames[:, i : i + 1], (1, LANES)) for i in range(12)]
    for i in range(12):
        table[i : i + 1, :] = turn[i]
    heads, start = lay.heads, lay.base
    width = C + 4 * PV + LANES
    near = C + 4 * PV
    shape = (SUBLANES, LANES)
    row, lane = iota(shape, 0), iota(shape, 1)
    zero_head, _ = head_of(shape, lay)
    w_q = nn(to_lane(start, 0), w_query[...]) + nn(to_components(3 * lay.kp, start, lay.kp, lay.kp), w_qp[...])
    w_q = w_q.astype(B16)
    w_query_rows[...] = w_q
    w_o = jnp.zeros((2 * LANES, w_out.shape[1]), F32)
    for h in range(heads):
        i, j = iota((2 * LANES, near), 0), iota((2 * LANES, near), 1)
        m = i - (LANES + h * C)
        found = (m >= 0) & (m < C) & (j == m)
        m = i - (start + h * PV)
        found = found | ((m >= 0) & (m < PV) & (j == C + 3 * PV + m))
        for c in range(3):
            m = i - (LANES + start + c * lay.vp + h * PV)
            found = found | ((m >= 0) & (m < PV) & (j == C + 3 * m + c))
        w_o = w_o + nn(pick(found), w_out[h * width : h * width + near, :])
    w_o = w_o.astype(B16)
    w_out_rows[: 2 * LANES, :] = w_o
    for h in range(heads):
        w_out_rows[(2 + h) * LANES : (3 + h) * LANES, :] = w_out[h * width + near : (h + 1) * width, :]
    single = jnp.broadcast_to(query_single[...], (SUBLANES, query_single.shape[1]))
    rows = nt(single, w_q)
    moved = turned_by(turn, unpack(rows, lay.kp))
    points = pack([(v + turn[9 + c]).astype(B16).astype(F32) for c, v in enumerate(moved)], lay.kp, start)
    query = jnp.where(lane < start, rows, 0.0).astype(B16).astype(F32)
    left[:SUBLANES, :] = jnp.where(zero_head == row, query, 0.0)
    minus = lane < 0
    for h in range(heads):
        at = lay.square + h * PQ
        minus = minus | ((row == h) & (lane >= at) & (lane < at + 3))
    mine = jnp.where(zero_head == row, points, 0.0)
    left[SUBLANES:, :] = jnp.where(minus, -0.5, mine)
    cotangent = jnp.broadcast_to(d_out[...], (SUBLANES, d_out.shape[1]))
    d_row[...] = nt(cotangent, w_o)
    scratch[...] = jnp.zeros_like(scratch)
    scratch[:heads, :] = bias_weight[...].astype(F32)
    for h in range(heads):
        d_pair = nt(cotangent, w_out[h * width + near : (h + 1) * width, :])
        scratch[SUBLANES + h : SUBLANES + h + 1, :] = d_pair[:1, :]
    both = nt(scratch[...].astype(B16), pair_rows[...])
    square = jnp.sum(mine * mine, axis=1, keepdims=True)
    base[...] = both[:SUBLANES] - 0.5 * gain[:, :1] * square
    d_base[...] = both[SUBLANES:]


def attention_kernel(lay, block, order, *refs):
    *parts, other, left, base, d_base, d_row, gains, table, message, features, weights, scores = refs
    frames = [table[i : i + 1, :] for i in range(12)]
    me = lax.axis_index("row")
    heads, vp, start = lay.heads, lay.vp, lay.base
    shape = (SUBLANES, LANES)
    row, lane = iota(shape, 0), iota(shape, 1)
    _, one_head = head_of(shape, lay)
    gain = gains[...]
    queries = left[...].astype(B16)
    first = jnp.concatenate([nt(queries, tile(part, 0)) for part in parts], axis=1)
    logits = LOGIT_SCALE * (first[:SUBLANES] * (1.0 / math.sqrt(C)) + base[...] + gain[:, :1] * first[SUBLANES:])
    weight = jnp.exp(logits - jnp.max(logits, axis=1, keepdims=True))
    attention = weight / jnp.sum(weight, axis=1, keepdims=True)
    attention = jnp.where(iota(attention.shape, 0) < heads, attention, 0.0)
    attention_b = attention.astype(B16)
    weights[...] = attention_b
    sums = spread(attention_b, [tile(part, 1) for part in parts])
    sums = jnp.sum(jnp.where(one_head == row, sums, 0.0), axis=0, keepdims=True)
    sums = jnp.broadcast_to(sums, shape)
    local = turned_back(frames, [v - frames[9 + c] for c, v in enumerate(unpack(sums, vp))])
    lengths = jnp.sqrt(1.0 + (local[0] * local[0] + local[1] * local[1] + local[2] * local[2]))
    d_one = d_row[:, LANES:]
    share = d_row[:, :LANES] / lengths
    d_points = turned_by(frames, [v + share * u for v, u in zip(unpack(d_one, vp), local)])
    d_side = jnp.where(lane < start, d_one, 0.0) + pack(d_points, vp, start)
    right = jnp.where(one_head == row, d_side, 0.0).astype(B16)
    d_attention = jnp.concatenate([nt(right, tile(part, 1)) for part in parts], axis=1) + d_base[...]
    total = jnp.sum(attention * d_attention, axis=1, keepdims=True)
    score_b = (LOGIT_SCALE * attention * (d_attention - total)).astype(B16)
    query = jnp.sum(jnp.where(lane < lay.square, left[:SUBLANES, :] + left[SUBLANES:, :], 0.0), axis=0, keepdims=True)
    side = jnp.where(row == 2 * heads, jnp.broadcast_to(query, shape), 0.0)
    side = side + jnp.where(row == 2 * heads + 1, d_side, 0.0)
    both = attention_b.astype(F32) + pltpu.roll(score_b.astype(F32), heads, 0)
    for at in range(0, both.shape[1], LANES):
        for place in range(at // block, (at + LANES) // block):
            piece = both[:, at : at + LANES]
            if place * block != at:
                piece = pltpu.roll(piece, LANES - (place * block - at), 1)
            piece = jnp.where(row < 2 * heads, piece, side).astype(B16)
            for core in range(2):
                message[(me ^ order[place]) * 2 + core, :, :] = piece
    scores[...] = score_b
    features[:, :LANES] = jnp.where((lane >= start) & (lane < start + vp), lengths, 0.0)
    features[:, LANES:] = jnp.where(lane < start, sums, 0.0) + pack(local, vp, start)


def tile(part, which):
    return part[:, which * LANES : (which + 1) * LANES]


def spread(weights, parts):
    total, at = 0.0, 0
    for part in parts:
        total = total + nn(weights[:, at : at + part.shape[0]], part)
        at += part.shape[0]
    return total


def rows_kernel(lay, *refs):
    *parts, arrived, pair, left, scores, features, weights, w_out_rows, w_query_rows, gains, table, sums = refs
    frames = [table[i : i + 1, :] for i in range(12)]
    shape = (SUBLANES, LANES)
    row, lane = iota(shape, 0), iota(shape, 1)
    zero_head, _ = head_of(shape, lay)
    pair_sum = nn(weights[...], pair[...])
    pairs = [jnp.broadcast_to(pair_sum[h : h + 1, :], shape) for h in range(lay.heads)]
    result = nn(jnp.concatenate([features[...]] + pairs, axis=1).astype(B16), w_out_rows[...])
    score = scores[...].astype(F32)
    d_rows = spread(scores[...], [tile(part, 0) for part in parts])
    score_sum = jnp.sum(score, axis=1, keepdims=True)
    points = left[SUBLANES:, :]
    d_rows = jnp.where(lane < lay.base, d_rows * (1.0 / math.sqrt(C)), gains[...] * (d_rows - score_sum * points))
    d_rows = jnp.broadcast_to(
        jnp.sum(jnp.where(zero_head == row, d_rows, 0.0), axis=0, keepdims=True), shape
    )
    local = pack(turned_back(frames, unpack(d_rows, lay.kp)), lay.kp, lay.base)
    both = (jnp.where(lane < lay.base, d_rows, 0.0) + local).astype(B16)
    sums[...] = jnp.concatenate([result, nn(both, w_query_rows[...])], axis=1)


def owner_kernel(lay, arrived, turned, parcel, other, result):
    heads, base = lay.heads, lay.base
    count = arrived.shape[0] // 2
    block = turned.shape[0]
    shape = (SUBLANES, LANES)
    whole = (count, SUBLANES, LANES)
    row = iota(shape, 0)
    zero_head, one_head = head_of(shape, lay)
    lane = iota(shape, 1)
    keep0 = (zero_head >= 0) & (zero_head + heads == row)
    keep1 = one_head == row
    ones = jnp.broadcast_to(jnp.where(keep0 & (lane >= base), 1.0, 0.0)[None], whole)
    columns = [turned[:, i : i + 1] for i in range(9)]
    lane = iota((block, LANES), 1)
    me = lax.axis_index("head")
    total = None
    for core, held in ((me, parcel), (1 - me, other)):
        took = jnp.concatenate([arrived[pl.ds(q * 2 + core, 1)] for q in range(count)], axis=0).astype(F32)
        side0 = jnp.where(keep0[None], jnp.broadcast_to(took[:, 2 * heads : 2 * heads + 1, :], whole), 0.0)
        side1 = jnp.where(keep1[None], jnp.broadcast_to(took[:, 2 * heads + 1 : 2 * heads + 2, :], whole), 0.0)
        right = jnp.concatenate([side0, side1, ones], axis=2).reshape(count * SUBLANES, 3 * LANES).astype(B16)
        moved = jnp.transpose(took.reshape(count * SUBLANES, LANES)).astype(B16)
        both = nn(moved, right)[:block]
        pieces = held[2 * LANES + block :, :LANES].astype(F32)
        gain = pieces[0:1] + pieces[1:2] + pieces[2:3]
        own = held[2 * LANES : 2 * LANES + block, :LANES].astype(F32)
        tile0, tile1 = both[:, :LANES], both[:, LANES : 2 * LANES]
        points = gain * (tile0 - both[:, 2 * LANES :] * own)
        points = pack(turned_back(columns, unpack(points, lay.kp)), lay.kp, base)
        tile0 = jnp.where(lane < base, tile0 * (1.0 / math.sqrt(C)), points)
        points = pack(turned_back(columns, unpack(tile1, lay.vp)), lay.vp, base)
        tile1 = jnp.where(lane < base, tile1, points)
        rows = jnp.concatenate([tile0, tile1], axis=1).astype(B16)
        part = nn(rows, held[: 2 * LANES, :])
        total = part if total is None else total + part
    result[...] = total


def finish_kernel(own, other, output, grad_query):
    width = output.shape[1]
    total = own[...] + other[...]
    output[...] = total[:1, :width].astype(output.dtype)
    grad_query[...] = total[:1, width:]


VMEM = pl.BlockSpec(memory_space=pltpu.VMEM)
HBM = pl.BlockSpec(memory_space=pltpu.HBM)


def call(body, outs, args, fresh=0, scratch=(), flops=1000000, last=False, waits=False):
    size = sum(math.prod(v.shape) * v.dtype.itemsize for v in list(args) + list(outs))

    def kernel(*refs):
        if fresh:
            *refs, sems = refs
            held = refs[len(refs) - fresh :]
            copies = [pltpu.make_async_copy(refs[i], held[i], sems.at[i]) for i in range(fresh)]
            for copy in copies:
                copy.start()

            def ready():
                for copy in copies:
                    copy.wait()

            if not waits:
                ready()
            refs = list(held) + list(refs[fresh : len(refs) - fresh])
        body(*([ready] if waits else []), *refs)

    own = [pltpu.VMEM(v.shape, v.dtype) for v in args[:fresh]]
    return pl.pallas_call(
        kernel,
        out_shape=tuple(outs),
        in_specs=[HBM] * fresh + [VMEM] * (len(args) - fresh),
        out_specs=tuple([pl.BlockSpec() if last else VMEM] * len(outs)),
        scratch_shapes=list(scratch) + own + ([pltpu.SemaphoreType.DMA((fresh,))] if fresh else []),
        compiler_params=pltpu.CompilerParams(vmem_limit_bytes=(16 << 20) + 6 * size),
        cost_estimate=pl.CostEstimate(flops=flops, bytes_accessed=size, transcendentals=0),
    )(*[pltpu.with_memory_space_constraint(v, pltpu.HBM) for v in args[:fresh]], *args[fresh:])


def shape_of(*dims, dtype=F32):
    return jax.ShapeDtypeStruct(dims, dtype)


def shards(
    query_single, key_single, pair, query_frames, key_frames, w_query, w_key, w_value, w_query_points, w_key_points,
    w_value_points, head_weight, bias_weight, w_out, d_out,
):
    lay = Layout(head_weight.shape[0])
    count = lax.axis_size("row")
    block, width = key_single.shape
    total = count * block
    near = 1
    while 4 * near * near <= count:
        near *= 2
    assert count & (count - 1) == 0

    def exchange(value, mask):
        return lax.ppermute(value, "row", [(i, i ^ mask) for i in range(count)])

    (packed,) = call(
        functools.partial(key_kernel, lay),
        [shape_of(block, 2 * LANES, dtype=B16)],
        [
            key_single, key_frames, w_key.T, w_value.T, w_key_points.T, w_value_points.T,
        ],
        6,
        waits=True,
    )
    offsets = list(range(0, count, near))
    line = jnp.concatenate([packed] + [exchange(packed, mask) for mask in offsets[1:]], axis=0)
    planes = list(range(near))
    parts = [line] + [exchange(line, m) for m in planes[1:]]
    order = [m ^ o for m in planes for o in offsets]

    left, base, d_base, d_row, w_out_rows, w_query_rows, table, pair_rows, gains, parcel, turned = call(
        functools.partial(early_kernel, lay, block, order),
        [
            shape_of(ROWS16, LANES), shape_of(SUBLANES, total), shape_of(SUBLANES, total),
            shape_of(SUBLANES, 2 * LANES), shape_of((2 + lay.heads) * LANES, width, dtype=B16),
            shape_of(LANES, width, dtype=B16), shape_of(ROWS16, LANES),
            shape_of(total, LANES, dtype=B16), shape_of(SUBLANES, LANES),
            shape_of(2 * LANES + block + ROWS16, width, dtype=B16), shape_of(block, LANES),
        ],
        [
            query_frames.T, query_single, w_query.T, w_query_points.T, bias_weight, w_out, d_out, pair,
            head_weight.reshape(1, -1), key_frames, w_key.T, w_value.T, w_key_points.T, w_value_points.T, packed,
        ],
        14,
        [pltpu.VMEM((ROWS16, LANES), F32)],
    )
    swap = [(i, (i + 1) % 2) for i in range(2)]
    other = lax.ppermute(parcel, "head", swap)
    message, features, weight_rows, scores = call(
        functools.partial(attention_kernel, lay, block, order),
        [
            shape_of(2 * count, SUBLANES, LANES, dtype=B16), shape_of(SUBLANES, 2 * LANES),
            shape_of(SUBLANES, total, dtype=B16), shape_of(SUBLANES, total, dtype=B16),
        ],
        parts + [other, left, base, d_base, d_row, gains, table],
    )
    arrived = lax.all_to_all(message, ("row", "head"), 0, 0, tiled=True)
    (sums,) = call(
        functools.partial(rows_kernel, lay),
        [shape_of(SUBLANES, 2 * width)],
        parts + [arrived, pair_rows, left, scores, features, weight_rows, w_out_rows, w_query_rows, gains, table],
    )
    output, grad_query = call(
        finish_kernel,
        [shape_of(1, width, dtype=B16), shape_of(1, width)],
        [sums, lax.ppermute(sums, "head", swap)],
        last=True,
    )
    (grad_keys,) = call(
        functools.partial(owner_kernel, lay),
        [shape_of(block, width)],
        [arrived, turned, parcel, other],
        last=True,
    )
    return (output, grad_query, grad_keys)


def solution(mesh):
    return jax.shard_map(
        shards,
        mesh=mesh,
        in_specs=(
            P("row", None),
            P("row", None),
            P("row", None, None),
            P(None, "row"),
            P(None, "row"),
            P(None, "head"),
            P(None, "head"),
            P(None, "head"),
            P(None, "head"),
            P(None, "head"),
            P(None, "head"),
            P("head"),
            P("head", None),
            P("head", None),
            P("row", None),
        ),
        out_specs=(P("row", None), P("row", None), P("row", None)),
        check_vma=False,
    )
```

```python
import functools
import math

import jax
import jax.numpy as jnp
from jax import lax
from jax.experimental import pallas as pl
from jax.experimental.pallas import tpu as pltpu
from jax.sharding import PartitionSpec as P

C = 16
PQ = 4
PV = 8
LANES = 128
SUBLANES = 8
ROWS16 = 16
LOGIT_SCALE = math.sqrt(1.0 / 3.0)
POINT_SCALE = math.sqrt(2.0 / (9.0 * PQ))
F32 = jnp.float32
B16 = jnp.bfloat16


class Layout:
    def __init__(self, heads):
        self.heads = heads
        self.base = heads * C
        self.kp = heads * PQ
        self.vp = heads * PV
        self.square = self.base + 3 * self.kp
        assert self.square + self.kp <= LANES and self.base + 3 * self.vp <= LANES
        assert 2 * heads + 2 <= SUBLANES and PQ == 4
        self.used = self.square + self.kp
        self.free = LANES - self.used
        self.chunks = self.used // self.free
        assert self.chunks * self.free == self.used

    def kept(self, block):
        kept = block * self.chunks // (self.chunks + 1)
        assert (block - kept) * self.chunks == kept and kept % ROWS16 == 0 and (block - kept) % ROWS16 == 0
        return kept

    def squeeze(self, zero, one):
        block = zero.shape[0]
        kept = self.kept(block)
        moved = [pltpu.roll(zero[kept:], self.used - c * self.free, 1) for c in range(self.chunks)]
        lane = iota((kept, LANES), 1)
        zero = jnp.where(lane < self.used, zero[:kept], jnp.concatenate(moved, axis=0))
        return jnp.concatenate([zero, one], axis=0)

    def restore(self, part, block):
        kept = self.kept(block)
        rest, height = block - kept, block + kept
        lane = iota((rest, LANES), 1)
        zero, one = [], []
        for at in range(0, part.shape[0], height):
            top = part[at : at + kept, :]
            wide = top.astype(F32)
            end = jnp.zeros((rest, LANES), F32)
            for c in range(self.chunks):
                chunk = pltpu.roll(wide[c * rest : (c + 1) * rest], LANES - self.used + c * self.free, 1)
                end = jnp.where((lane >= c * self.free) & (lane < (c + 1) * self.free), chunk, end)
            zero += [top, end.astype(B16)]
            one.append(part[at + kept : at + height, :])
        return jnp.concatenate(zero, axis=0), jnp.concatenate(one, axis=0)


def nn(a, b, precision=None):
    return lax.dot_general(a, b, (((1,), (0,)), ((), ())), precision=precision, preferred_element_type=F32)


def nt(a, b):
    return lax.dot_general(a, b, (((1,), (1,)), ((), ())), preferred_element_type=F32)


def iota(shape, dim):
    return lax.broadcasted_iota(jnp.int32, shape, dim)


def pick(condition):
    return jnp.where(condition, 1.0, 0.0).astype(B16)


def to_lane(rows, offset):
    j, i = iota((LANES, rows), 0), iota((LANES, rows), 1)
    return pick(j == i + offset)


def to_components(rows, offset, points, seg):
    j, i = iota((LANES, rows), 0), iota((LANES, rows), 1)
    found = j < 0
    for c in range(3):
        m = j - (c * seg + offset)
        found = found | ((m >= 0) & (m < points) & (i == 3 * m + c))
    return pick(found)


def unpack(tile, seg):
    return tile, pltpu.roll(tile, LANES - seg, 1), pltpu.roll(tile, LANES - 2 * seg, 1)


def pack(parts, seg, base):
    lane = iota(parts[0].shape, 1)
    keep = (lane >= base) & (lane < base + seg)
    x, y, z = (jnp.where(keep, v, 0.0) for v in parts)
    return x + pltpu.roll(y, seg, 1) + pltpu.roll(z, 2 * seg, 1)


def head_of(shape, lay):
    lane = iota(shape, 1)
    zero = jnp.full(shape, -1, jnp.int32)
    one = jnp.full(shape, -1, jnp.int32)
    for h in range(lay.heads):
        same = (lane >= h * C) & (lane < (h + 1) * C)
        zero, one = jnp.where(same, h, zero), jnp.where(same, h, one)
        for c in range(3):
            k = lay.base + c * lay.kp + h * PQ
            v = lay.base + c * lay.vp + h * PV
            zero = jnp.where((lane >= k) & (lane < k + PQ), h, zero)
            one = jnp.where((lane >= v) & (lane < v + PV), h, one)
    return zero, one


def turned_by(frames, vectors):
    x, y, z = vectors
    return [frames[3 * c] * x + frames[3 * c + 1] * y + frames[3 * c + 2] * z for c in range(3)]


def turned_back(frames, vectors):
    x, y, z = vectors
    return [frames[d] * x + frames[3 + d] * y + frames[6 + d] * z for d in range(3)]


def key_kernel(lay, ready, key_single, frames, w_key, w_value, w_kp, w_vp, packed, own):
    heads, kp, vp, base = lay.heads, lay.kp, lay.vp, lay.base
    tall = PQ * SUBLANES

    def rows_of(count, width):
        return iota((count, width), 0), iota((count, width), 1)

    r, i = rows_of(tall, 3 * kp)
    to_kp = [pick((i == 3 * PQ * (r & 7) + 3 * (r >> 3) + c) & ((r & 7) < heads)) for c in range(3)]
    r, i = rows_of(vp, 3 * vp)
    to_vp = [pick(i == 3 * r + c) for c in range(3)]
    width = 2 * LANES
    r, j = rows_of(base, width)
    place = [j == r, j == r + LANES]
    r, j = rows_of(tall, width)
    place += [(j == base + c * kp + PQ * (r & 7) + (r >> 3)) & ((r & 7) < heads) for c in range(3)]
    r, j = rows_of(vp, width)
    place += [j == LANES + base + c * vp + r for c in range(3)]
    r, j = rows_of(SUBLANES, width)
    place += [(j == lay.square + PQ * r + piece) & (r < heads) for piece in range(3)]
    place = jnp.concatenate([jnp.where(found, 1.0, 0.0) for found in place], axis=0).astype(B16)
    to_kp = jnp.concatenate(to_kp, axis=0)
    to_vp = jnp.concatenate(to_vp, axis=0)
    ready()
    single = key_single[...]
    turn = [frames[i : i + 1, :] for i in range(12)]
    features = [nt(w_key[...], single), nt(w_value[...], single)]
    for choose, weight, height in ((to_kp, w_kp, tall), (to_vp, w_vp, vp)):
        rows = nt(nn(choose, weight[...]).astype(B16), single)
        moved = turned_by(turn, [rows[c * height : (c + 1) * height] for c in range(3)])
        moved = [(v + turn[9 + c]).astype(B16).astype(F32) for c, v in enumerate(moved)]
        features += moved
        if height == tall:
            square = moved[0] * moved[0] + moved[1] * moved[1] + moved[2] * moved[2]
            square = sum(square[group(p)] for p in range(PQ))
    first = square.astype(B16).astype(F32)
    second = (square - first).astype(B16).astype(F32)
    features = jnp.concatenate(features + [first, second, square - first - second], axis=0)
    rows = nn(jnp.transpose(features).astype(B16), place)
    own[...] = rows[:, :LANES].astype(B16)
    packed[...] = lay.squeeze(rows[:, :LANES], rows[:, LANES:]).astype(B16)


def group(h):
    return slice(h * SUBLANES, (h + 1) * SUBLANES)


def gain_rows(head_weight, lay):
    row = iota((SUBLANES, LANES), 0)
    raw = jnp.zeros((SUBLANES, LANES), F32)
    for h in range(lay.heads):
        raw = jnp.where(row == h, jnp.broadcast_to(head_weight[:, h : h + 1], raw.shape), raw)
    gain = (jnp.maximum(raw, 0.0) + jnp.log1p(jnp.exp(-jnp.abs(raw)))) * POINT_SCALE
    return jnp.where(row < lay.heads, gain, 0.0)


def gain_lanes(gain, lay):
    zero, _ = head_of(gain.shape, lay)
    return jnp.sum(jnp.where(zero == iota(gain.shape, 0), gain, 0.0), axis=0, keepdims=True)


def early_kernel(
    lay, block, order, frames, query_single, w_query, w_qp, bias_weight, w_out, d_out, pair, head_weight, key_frames,
    w_key, w_value, w_kp, w_vp, own,
    left, base, d_base, d_row, w_out_rows, w_query_rows, table, pair_rows, gains, parcel, turned, scratch,
):
    kp, vp = lay.kp, lay.vp
    zero = nn(to_lane(lay.base, 0), w_key[...]) + nn(to_components(3 * kp, lay.base, kp, kp), w_kp[...])
    one = nn(to_lane(lay.base, 0), w_value[...]) + nn(to_components(3 * vp, lay.base, vp, vp), w_vp[...])
    parcel[:LANES, :] = zero.astype(B16)
    parcel[LANES : 2 * LANES, :] = one.astype(B16)
    parcel[2 * LANES :, :] = jnp.zeros((block + ROWS16, parcel.shape[1]), B16)
    parcel[2 * LANES : 2 * LANES + block, :LANES] = own[...]
    gain = gain_rows(head_weight, lay)
    gains[...] = gain
    pieces = jnp.broadcast_to(gain_lanes(gain, lay), (ROWS16, LANES))
    first = pieces.astype(B16).astype(F32)
    second = (pieces - first).astype(B16).astype(F32)
    row = iota(pieces.shape, 0)
    pieces = jnp.where(
        row == 0, first, jnp.where(row == 1, second, jnp.where(row == 2, pieces - first - second, 0.0))
    )
    parcel[2 * LANES + block :, :LANES] = pieces.astype(B16)
    turn = jnp.transpose(key_frames[...])
    turned[:, : turn.shape[1]] = turn
    me = lax.axis_index("row")
    for place, offset in enumerate(order):
        j = pl.multiple_of((me ^ offset) * block, block)
        pair_rows[place * block : (place + 1) * block, :] = pair[0, pl.ds(j, block), :]
    turn = [jnp.broadcast_to(frames[:, i : i + 1], (1, LANES)) for i in range(12)]
    for i in range(12):
        table[i : i + 1, :] = turn[i]
    heads, start = lay.heads, lay.base
    width = C + 4 * PV + LANES
    near = C + 4 * PV
    shape = (SUBLANES, LANES)
    row, lane = iota(shape, 0), iota(shape, 1)
    zero_head, _ = head_of(shape, lay)
    w_q = nn(to_lane(start, 0), w_query[...]) + nn(to_components(3 * lay.kp, start, lay.kp, lay.kp), w_qp[...])
    w_q = w_q.astype(B16)
    w_query_rows[...] = w_q
    w_o = jnp.zeros((2 * LANES, w_out.shape[1]), F32)
    for h in range(heads):
        i, j = iota((2 * LANES, near), 0), iota((2 * LANES, near), 1)
        m = i - (LANES + h * C)
        found = (m >= 0) & (m < C) & (j == m)
        m = i - (start + h * PV)
        found = found | ((m >= 0) & (m < PV) & (j == C + 3 * PV + m))
        for c in range(3):
            m = i - (LANES + start + c * lay.vp + h * PV)
            found = found | ((m >= 0) & (m < PV) & (j == C + 3 * m + c))
        w_o = w_o + nn(pick(found), w_out[h * width : h * width + near, :])
    w_o = w_o.astype(B16)
    w_out_rows[: 2 * LANES, :] = w_o
    for h in range(heads):
        w_out_rows[(2 + h) * LANES : (3 + h) * LANES, :] = w_out[h * width + near : (h + 1) * width, :]
    single = jnp.broadcast_to(query_single[...], (SUBLANES, query_single.shape[1]))
    rows = nt(single, w_q)
    moved = turned_by(turn, unpack(rows, lay.kp))
    points = pack([(v + turn[9 + c]).astype(B16).astype(F32) for c, v in enumerate(moved)], lay.kp, start)
    query = jnp.where(lane < start, rows, 0.0).astype(B16).astype(F32)
    left[:SUBLANES, :] = jnp.where(zero_head == row, query, 0.0)
    minus = lane < 0
    for h in range(heads):
        at = lay.square + h * PQ
        minus = minus | ((row == h) & (lane >= at) & (lane < at + 3))
    mine = jnp.where(zero_head == row, points, 0.0)
    left[SUBLANES:, :] = jnp.where(minus, -0.5, mine)
    cotangent = jnp.broadcast_to(d_out[...], (SUBLANES, d_out.shape[1]))
    d_row[...] = nt(cotangent, w_o)
    scratch[...] = jnp.zeros_like(scratch)
    scratch[:heads, :] = bias_weight[...].astype(F32)
    for h in range(heads):
        d_pair = nt(cotangent, w_out[h * width + near : (h + 1) * width, :])
        scratch[SUBLANES + h : SUBLANES + h + 1, :] = d_pair[:1, :]
    both = nt(scratch[...].astype(B16), pair_rows[...])
    square = jnp.sum(mine * mine, axis=1, keepdims=True)
    base[...] = both[:SUBLANES] - 0.5 * gain[:, :1] * square
    d_base[...] = both[SUBLANES:]


def attention_kernel(lay, block, order, *refs):
    *parts, left, base, d_base, d_row, gains, table, message, features, weights, scores, gathered = refs
    frames = [table[i : i + 1, :] for i in range(12)]
    me = lax.axis_index("row")
    heads, vp, start = lay.heads, lay.vp, lay.base
    shape = (SUBLANES, LANES)
    row, lane = iota(shape, 0), iota(shape, 1)
    _, one_head = head_of(shape, lay)
    gain = gains[...]
    restored = [lay.restore(part, block) for part in parts]
    zeros, ones = [zero for zero, _ in restored], [one for _, one in restored]
    queries = left[...].astype(B16)
    first = jnp.concatenate([nt(queries, zero) for zero in zeros], axis=1)
    logits = LOGIT_SCALE * (first[:SUBLANES] * (1.0 / math.sqrt(C)) + base[...] + gain[:, :1] * first[SUBLANES:])
    weight = jnp.exp(logits - jnp.max(logits, axis=1, keepdims=True))
    attention = weight / jnp.sum(weight, axis=1, keepdims=True)
    attention = jnp.where(iota(attention.shape, 0) < heads, attention, 0.0)
    attention_b = attention.astype(B16)
    weights[...] = attention_b
    sums = spread(attention_b, ones)
    sums = jnp.sum(jnp.where(one_head == row, sums, 0.0), axis=0, keepdims=True)
    sums = jnp.broadcast_to(sums, shape)
    local = turned_back(frames, [v - frames[9 + c] for c, v in enumerate(unpack(sums, vp))])
    lengths = jnp.sqrt(1.0 + (local[0] * local[0] + local[1] * local[1] + local[2] * local[2]))
    d_one = d_row[:, LANES:]
    share = d_row[:, :LANES] / lengths
    d_points = turned_by(frames, [v + share * u for v, u in zip(unpack(d_one, vp), local)])
    d_side = jnp.where(lane < start, d_one, 0.0) + pack(d_points, vp, start)
    right = jnp.where(one_head == row, d_side, 0.0).astype(B16)
    d_attention = jnp.concatenate([nt(right, one) for one in ones], axis=1) + d_base[...]
    total = jnp.sum(attention * d_attention, axis=1, keepdims=True)
    score_b = (LOGIT_SCALE * attention * (d_attention - total)).astype(B16)
    query = jnp.sum(jnp.where(lane < lay.square, left[:SUBLANES, :] + left[SUBLANES:, :], 0.0), axis=0, keepdims=True)
    side = jnp.where(row == 2 * heads, jnp.broadcast_to(query, shape), 0.0)
    side = side + jnp.where(row == 2 * heads + 1, d_side, 0.0)
    both = attention_b.astype(F32) + pltpu.roll(score_b.astype(F32), heads, 0)
    for at in range(0, both.shape[1], LANES):
        for place in range(at // block, (at + LANES) // block):
            piece = both[:, at : at + LANES]
            if place * block != at:
                piece = pltpu.roll(piece, LANES - (place * block - at), 1)
            piece = jnp.where(row < 2 * heads, piece, side).astype(B16)
            for core in range(2):
                message[(me ^ order[place]) * 2 + core, :, :] = piece
    at = 0
    for zero in zeros:
        gathered[at : at + zero.shape[0], :] = zero
        at += zero.shape[0]
    scores[...] = score_b
    features[:, :LANES] = jnp.where((lane >= start) & (lane < start + vp), lengths, 0.0)
    features[:, LANES:] = jnp.where(lane < start, sums, 0.0) + pack(local, vp, start)


def spread(weights, parts):
    total, at = 0.0, 0
    for part in parts:
        total = total + nn(weights[:, at : at + part.shape[0]], part)
        at += part.shape[0]
    return total


def rows_kernel(lay, *refs):
    gathered, pair, left, scores, features, weights, w_out_rows, w_query_rows, gains, table, sums = refs
    frames = [table[i : i + 1, :] for i in range(12)]
    shape = (SUBLANES, LANES)
    row, lane = iota(shape, 0), iota(shape, 1)
    zero_head, _ = head_of(shape, lay)
    pair_sum = nn(weights[...], pair[...])
    pairs = [jnp.broadcast_to(pair_sum[h : h + 1, :], shape) for h in range(lay.heads)]
    result = nn(jnp.concatenate([features[...]] + pairs, axis=1).astype(B16), w_out_rows[...])
    score = scores[...].astype(F32)
    d_rows = nn(scores[...], gathered[...])
    score_sum = jnp.sum(score, axis=1, keepdims=True)
    points = left[SUBLANES:, :]
    d_rows = jnp.where(lane < lay.base, d_rows * (1.0 / math.sqrt(C)), gains[...] * (d_rows - score_sum * points))
    d_rows = jnp.broadcast_to(
        jnp.sum(jnp.where(zero_head == row, d_rows, 0.0), axis=0, keepdims=True), shape
    )
    local = pack(turned_back(frames, unpack(d_rows, lay.kp)), lay.kp, lay.base)
    both = (jnp.where(lane < lay.base, d_rows, 0.0) + local).astype(B16)
    sums[...] = jnp.concatenate([result, nn(both, w_query_rows[...])], axis=1)


def owner_kernel(lay, arrived, turned, parcel, other, result):
    heads, base = lay.heads, lay.base
    count = arrived.shape[0] // 2
    block = turned.shape[0]
    shape = (SUBLANES, LANES)
    whole = (count, SUBLANES, LANES)
    row = iota(shape, 0)
    zero_head, one_head = head_of(shape, lay)
    lane = iota(shape, 1)
    keep0 = (zero_head >= 0) & (zero_head + heads == row)
    keep1 = one_head == row
    ones = jnp.broadcast_to(jnp.where(keep0 & (lane >= base), 1.0, 0.0)[None], whole)
    columns = [turned[:, i : i + 1] for i in range(9)]
    lane = iota((block, LANES), 1)
    me = lax.axis_index("head")
    total = None
    for core, held in ((me, parcel), (1 - me, other)):
        took = jnp.concatenate([arrived[pl.ds(q * 2 + core, 1)] for q in range(count)], axis=0).astype(F32)
        side0 = jnp.where(keep0[None], jnp.broadcast_to(took[:, 2 * heads : 2 * heads + 1, :], whole), 0.0)
        side1 = jnp.where(keep1[None], jnp.broadcast_to(took[:, 2 * heads + 1 : 2 * heads + 2, :], whole), 0.0)
        right = jnp.concatenate([side0, side1, ones], axis=2).reshape(count * SUBLANES, 3 * LANES).astype(B16)
        moved = jnp.transpose(took.reshape(count * SUBLANES, LANES)).astype(B16)
        both = nn(moved, right)[:block]
        pieces = held[2 * LANES + block :, :LANES].astype(F32)
        gain = pieces[0:1] + pieces[1:2] + pieces[2:3]
        own = held[2 * LANES : 2 * LANES + block, :LANES].astype(F32)
        tile0, tile1 = both[:, :LANES], both[:, LANES : 2 * LANES]
        points = gain * (tile0 - both[:, 2 * LANES :] * own)
        points = pack(turned_back(columns, unpack(points, lay.kp)), lay.kp, base)
        tile0 = jnp.where(lane < base, tile0 * (1.0 / math.sqrt(C)), points)
        points = pack(turned_back(columns, unpack(tile1, lay.vp)), lay.vp, base)
        tile1 = jnp.where(lane < base, tile1, points)
        rows = jnp.concatenate([tile0, tile1], axis=1).astype(B16)
        part = nn(rows, held[: 2 * LANES, :])
        total = part if total is None else total + part
    result[...] = total


def finish_kernel(own, other, output, grad_query):
    width = output.shape[1]
    total = own[...] + other[...]
    output[...] = total[:1, :width].astype(output.dtype)
    grad_query[...] = total[:1, width:]


VMEM = pl.BlockSpec(memory_space=pltpu.VMEM)
HBM = pl.BlockSpec(memory_space=pltpu.HBM)


def call(body, outs, args, fresh=0, scratch=(), flops=1000000, last=False, waits=False):
    size = sum(math.prod(v.shape) * v.dtype.itemsize for v in list(args) + list(outs))

    def kernel(*refs):
        if fresh:
            *refs, sems = refs
            held = refs[len(refs) - fresh :]
            copies = [pltpu.make_async_copy(refs[i], held[i], sems.at[i]) for i in range(fresh)]
            for copy in copies:
                copy.start()

            def ready():
                for copy in copies:
                    copy.wait()

            if not waits:
                ready()
            refs = list(held) + list(refs[fresh : len(refs) - fresh])
        body(*([ready] if waits else []), *refs)

    own = [pltpu.VMEM(v.shape, v.dtype) for v in args[:fresh]]
    return pl.pallas_call(
        kernel,
        out_shape=tuple(outs),
        in_specs=[HBM] * fresh + [VMEM] * (len(args) - fresh),
        out_specs=tuple([pl.BlockSpec() if last else VMEM] * len(outs)),
        scratch_shapes=list(scratch) + own + ([pltpu.SemaphoreType.DMA((fresh,))] if fresh else []),
        compiler_params=pltpu.CompilerParams(vmem_limit_bytes=(16 << 20) + 6 * size),
        cost_estimate=pl.CostEstimate(flops=flops, bytes_accessed=size, transcendentals=0),
    )(*[pltpu.with_memory_space_constraint(v, pltpu.HBM) for v in args[:fresh]], *args[fresh:])


def shape_of(*dims, dtype=F32):
    return jax.ShapeDtypeStruct(dims, dtype)


def shards(
    query_single, key_single, pair, query_frames, key_frames, w_query, w_key, w_value, w_query_points, w_key_points,
    w_value_points, head_weight, bias_weight, w_out, d_out,
):
    lay = Layout(head_weight.shape[0])
    count = lax.axis_size("row")
    block, width = key_single.shape
    total = count * block
    near = 1
    while 4 * near * near <= count:
        near *= 2
    assert count & (count - 1) == 0

    def exchange(value, mask):
        return lax.ppermute(value, "row", [(i, i ^ mask) for i in range(count)])

    packed, own = call(
        functools.partial(key_kernel, lay),
        [shape_of(block + lay.kept(block), LANES, dtype=B16), shape_of(block, LANES, dtype=B16)],
        [
            key_single, key_frames, w_key.T, w_value.T, w_key_points.T, w_value_points.T,
        ],
        6,
        waits=True,
    )
    offsets = list(range(0, count, near))
    line = jnp.concatenate([packed] + [exchange(packed, mask) for mask in offsets[1:]], axis=0)
    planes = list(range(near))
    parts = [line] + [exchange(line, m) for m in planes[1:]]
    order = [m ^ o for m in planes for o in offsets]

    left, base, d_base, d_row, w_out_rows, w_query_rows, table, pair_rows, gains, parcel, turned = call(
        functools.partial(early_kernel, lay, block, order),
        [
            shape_of(ROWS16, LANES), shape_of(SUBLANES, total), shape_of(SUBLANES, total),
            shape_of(SUBLANES, 2 * LANES), shape_of((2 + lay.heads) * LANES, width, dtype=B16),
            shape_of(LANES, width, dtype=B16), shape_of(ROWS16, LANES),
            shape_of(total, LANES, dtype=B16), shape_of(SUBLANES, LANES),
            shape_of(2 * LANES + block + ROWS16, width, dtype=B16), shape_of(block, LANES),
        ],
        [
            query_frames.T, query_single, w_query.T, w_query_points.T, bias_weight, w_out, d_out, pair,
            head_weight.reshape(1, -1), key_frames, w_key.T, w_value.T, w_key_points.T, w_value_points.T, own,
        ],
        14,
        [pltpu.VMEM((ROWS16, LANES), F32)],
    )
    swap = [(i, (i + 1) % 2) for i in range(2)]
    other = lax.ppermute(parcel, "head", swap)
    message, features, weight_rows, scores, gathered = call(
        functools.partial(attention_kernel, lay, block, order),
        [
            shape_of(2 * count, SUBLANES, LANES, dtype=B16), shape_of(SUBLANES, 2 * LANES),
            shape_of(SUBLANES, total, dtype=B16), shape_of(SUBLANES, total, dtype=B16),
            shape_of(total, LANES, dtype=B16),
        ],
        parts + [left, base, d_base, d_row, gains, table],
    )
    arrived = lax.all_to_all(message, ("row", "head"), 0, 0, tiled=True)
    (sums,) = call(
        functools.partial(rows_kernel, lay),
        [shape_of(SUBLANES, 2 * width)],
        [gathered, pair_rows, left, scores, features, weight_rows, w_out_rows, w_query_rows, gains, table],
    )
    output, grad_query = call(
        finish_kernel,
        [shape_of(1, width, dtype=B16), shape_of(1, width)],
        [sums, lax.ppermute(sums, "head", swap)],
        last=True,
    )
    (grad_keys,) = call(
        functools.partial(owner_kernel, lay),
        [shape_of(block, width)],
        [arrived, turned, parcel, other],
        last=True,
    )
    return (output, grad_query, grad_keys)


def solution(mesh):
    return jax.shard_map(
        shards,
        mesh=mesh,
        in_specs=(
            P("row", None),
            P("row", None),
            P("row", None, None),
            P(None, "row"),
            P(None, "row"),
            P(None, "head"),
            P(None, "head"),
            P(None, "head"),
            P(None, "head"),
            P(None, "head"),
            P(None, "head"),
            P("head"),
            P("head", None),
            P("head", None),
            P("row", None),
        ),
        out_specs=(P("row", None), P("row", None), P("row", None)),
        check_vma=False,
    )
```

```python
import functools
import math

import jax
import jax.numpy as jnp
from jax import lax
from jax.experimental import pallas as pl
from jax.experimental.pallas import tpu as pltpu
from jax.sharding import PartitionSpec as P

C = 16
PQ = 4
PV = 8
LANES = 128
SUBLANES = 8
ROWS16 = 16
LOGIT_SCALE = math.sqrt(1.0 / 3.0)
POINT_SCALE = math.sqrt(2.0 / (9.0 * PQ))
F32 = jnp.float32
B16 = jnp.bfloat16


class Layout:
    def __init__(self, heads):
        self.heads = heads
        self.base = heads * C
        self.kp = heads * PQ
        self.vp = heads * PV
        self.square = self.base + 3 * self.kp
        assert self.square + self.kp <= LANES and self.base + 3 * self.vp <= LANES
        assert 2 * heads + 2 <= SUBLANES and PQ == 4
        self.used = self.square + self.kp
        self.free = LANES - self.used
        self.chunks = self.used // self.free
        assert self.chunks * self.free == self.used

    def kept(self, block):
        kept = block * self.chunks // (self.chunks + 1)
        assert (block - kept) * self.chunks == kept and kept % ROWS16 == 0 and (block - kept) % ROWS16 == 0
        return kept

    def squeeze(self, zero, one):
        block = zero.shape[0]
        kept = self.kept(block)
        moved = [pltpu.roll(zero[kept:], self.used - c * self.free, 1) for c in range(self.chunks)]
        lane = iota((kept, LANES), 1)
        zero = jnp.where(lane < self.used, zero[:kept], jnp.concatenate(moved, axis=0))
        return jnp.concatenate([zero, one], axis=0)

    def restore(self, part, block):
        kept = self.kept(block)
        rest, height = block - kept, block + kept
        lane = iota((rest, LANES), 1)
        zero, one = [], []
        for at in range(0, part.shape[0], height):
            top = part[at : at + kept, :]
            wide = top.astype(F32)
            end = jnp.zeros((rest, LANES), F32)
            for c in range(self.chunks):
                chunk = pltpu.roll(wide[c * rest : (c + 1) * rest], LANES - self.used + c * self.free, 1)
                end = jnp.where((lane >= c * self.free) & (lane < (c + 1) * self.free), chunk, end)
            zero += [top, end.astype(B16)]
            one.append(part[at + kept : at + height, :])
        return jnp.concatenate(zero, axis=0), jnp.concatenate(one, axis=0)


def nn(a, b, precision=None):
    return lax.dot_general(a, b, (((1,), (0,)), ((), ())), precision=precision, preferred_element_type=F32)


def nt(a, b):
    return lax.dot_general(a, b, (((1,), (1,)), ((), ())), preferred_element_type=F32)


def iota(shape, dim):
    return lax.broadcasted_iota(jnp.int32, shape, dim)


def pick(condition):
    return jnp.where(condition, 1.0, 0.0).astype(B16)


def to_lane(rows, offset):
    j, i = iota((LANES, rows), 0), iota((LANES, rows), 1)
    return pick(j == i + offset)


def to_components(rows, offset, points, seg):
    j, i = iota((LANES, rows), 0), iota((LANES, rows), 1)
    found = j < 0
    for c in range(3):
        m = j - (c * seg + offset)
        found = found | ((m >= 0) & (m < points) & (i == 3 * m + c))
    return pick(found)


def unpack(tile, seg):
    return tile, pltpu.roll(tile, LANES - seg, 1), pltpu.roll(tile, LANES - 2 * seg, 1)


def pack(parts, seg, base):
    lane = iota(parts[0].shape, 1)
    keep = (lane >= base) & (lane < base + seg)
    x, y, z = (jnp.where(keep, v, 0.0) for v in parts)
    return x + pltpu.roll(y, seg, 1) + pltpu.roll(z, 2 * seg, 1)


def head_of(shape, lay):
    lane = iota(shape, 1)
    zero = jnp.full(shape, -1, jnp.int32)
    one = jnp.full(shape, -1, jnp.int32)
    for h in range(lay.heads):
        same = (lane >= h * C) & (lane < (h + 1) * C)
        zero, one = jnp.where(same, h, zero), jnp.where(same, h, one)
        for c in range(3):
            k = lay.base + c * lay.kp + h * PQ
            v = lay.base + c * lay.vp + h * PV
            zero = jnp.where((lane >= k) & (lane < k + PQ), h, zero)
            one = jnp.where((lane >= v) & (lane < v + PV), h, one)
    return zero, one


def turned_by(frames, vectors):
    x, y, z = vectors
    return [frames[3 * c] * x + frames[3 * c + 1] * y + frames[3 * c + 2] * z for c in range(3)]


def turned_back(frames, vectors):
    x, y, z = vectors
    return [frames[d] * x + frames[3 + d] * y + frames[6 + d] * z for d in range(3)]


def key_kernel(lay, ready, key_single, frames, w_key, w_value, w_kp, w_vp, packed, own):
    heads, kp, vp, base = lay.heads, lay.kp, lay.vp, lay.base
    tall = PQ * SUBLANES

    def rows_of(count, width):
        return iota((count, width), 0), iota((count, width), 1)

    r, i = rows_of(tall, 3 * kp)
    to_kp = [pick((i == 3 * PQ * (r & 7) + 3 * (r >> 3) + c) & ((r & 7) < heads)) for c in range(3)]
    r, i = rows_of(vp, 3 * vp)
    to_vp = [pick(i == 3 * r + c) for c in range(3)]
    width = 2 * LANES
    r, j = rows_of(base, width)
    place = [j == r, j == r + LANES]
    r, j = rows_of(tall, width)
    place += [(j == base + c * kp + PQ * (r & 7) + (r >> 3)) & ((r & 7) < heads) for c in range(3)]
    r, j = rows_of(vp, width)
    place += [j == LANES + base + c * vp + r for c in range(3)]
    r, j = rows_of(SUBLANES, width)
    place += [(j == lay.square + PQ * r + piece) & (r < heads) for piece in range(3)]
    place = jnp.concatenate([jnp.where(found, 1.0, 0.0) for found in place], axis=0).astype(B16)
    to_kp = jnp.concatenate(to_kp, axis=0)
    to_vp = jnp.concatenate(to_vp, axis=0)
    ready()
    single = key_single[...]
    turn = [frames[i : i + 1, :] for i in range(12)]
    features = [nt(w_key[...], single), nt(w_value[...], single)]
    for choose, weight, height in ((to_kp, w_kp, tall), (to_vp, w_vp, vp)):
        rows = nt(nn(choose, weight[...]).astype(B16), single)
        moved = turned_by(turn, [rows[c * height : (c + 1) * height] for c in range(3)])
        moved = [(v + turn[9 + c]).astype(B16).astype(F32) for c, v in enumerate(moved)]
        features += moved
        if height == tall:
            square = moved[0] * moved[0] + moved[1] * moved[1] + moved[2] * moved[2]
            square = sum(square[group(p)] for p in range(PQ))
    first = square.astype(B16).astype(F32)
    second = (square - first).astype(B16).astype(F32)
    features = jnp.concatenate(features + [first, second, square - first - second], axis=0)
    rows = nn(jnp.transpose(features).astype(B16), place)
    own[...] = rows[:, :LANES].astype(B16)
    packed[...] = lay.squeeze(rows[:, :LANES], rows[:, LANES:]).astype(B16)


def group(h):
    return slice(h * SUBLANES, (h + 1) * SUBLANES)


def gain_rows(head_weight, lay):
    row = iota((SUBLANES, LANES), 0)
    raw = jnp.zeros((SUBLANES, LANES), F32)
    for h in range(lay.heads):
        raw = jnp.where(row == h, jnp.broadcast_to(head_weight[:, h : h + 1], raw.shape), raw)
    gain = (jnp.maximum(raw, 0.0) + jnp.log1p(jnp.exp(-jnp.abs(raw)))) * POINT_SCALE
    return jnp.where(row < lay.heads, gain, 0.0)


def gain_lanes(gain, lay):
    zero, _ = head_of(gain.shape, lay)
    return jnp.sum(jnp.where(zero == iota(gain.shape, 0), gain, 0.0), axis=0, keepdims=True)


def early_kernel(
    lay, block, order, frames, query_single, w_query, w_qp, bias_weight, w_out, d_out, pair, head_weight, key_frames,
    w_key, w_value, w_kp, w_vp, own,
    left, base, d_base, d_row, w_out_rows, w_query_rows, table, pair_rows, gains, parcel, turned, scratch,
):
    kp, vp = lay.kp, lay.vp
    zero = nn(to_lane(lay.base, 0), w_key[...]) + nn(to_components(3 * kp, lay.base, kp, kp), w_kp[...])
    one = nn(to_lane(lay.base, 0), w_value[...]) + nn(to_components(3 * vp, lay.base, vp, vp), w_vp[...])
    parcel[:LANES, :] = zero.astype(B16)
    parcel[LANES : 2 * LANES, :] = one.astype(B16)
    parcel[2 * LANES :, :] = jnp.zeros((block + ROWS16, parcel.shape[1]), B16)
    parcel[2 * LANES : 2 * LANES + block, :LANES] = own[...]
    gain = gain_rows(head_weight, lay)
    gains[...] = gain
    pieces = jnp.broadcast_to(gain_lanes(gain, lay), (ROWS16, LANES))
    first = pieces.astype(B16).astype(F32)
    second = (pieces - first).astype(B16).astype(F32)
    row = iota(pieces.shape, 0)
    pieces = jnp.where(
        row == 0, first, jnp.where(row == 1, second, jnp.where(row == 2, pieces - first - second, 0.0))
    )
    parcel[2 * LANES + block :, :LANES] = pieces.astype(B16)
    turn = jnp.transpose(key_frames[...])
    turned[:, : turn.shape[1]] = turn
    me = lax.axis_index("row")
    for place, offset in enumerate(order):
        j = pl.multiple_of((me ^ offset) * block, block)
        pair_rows[place * block : (place + 1) * block, :] = pair[0, pl.ds(j, block), :]
    turn = [jnp.broadcast_to(frames[:, i : i + 1], (1, LANES)) for i in range(12)]
    for i in range(12):
        table[i : i + 1, :] = turn[i]
    heads, start = lay.heads, lay.base
    width = C + 4 * PV + LANES
    near = C + 4 * PV
    shape = (SUBLANES, LANES)
    row, lane = iota(shape, 0), iota(shape, 1)
    zero_head, _ = head_of(shape, lay)
    w_q = nn(to_lane(start, 0), w_query[...]) + nn(to_components(3 * lay.kp, start, lay.kp, lay.kp), w_qp[...])
    w_q = w_q.astype(B16)
    w_query_rows[...] = w_q
    w_o = jnp.zeros((2 * LANES, w_out.shape[1]), F32)
    for h in range(heads):
        i, j = iota((2 * LANES, near), 0), iota((2 * LANES, near), 1)
        m = i - (LANES + h * C)
        found = (m >= 0) & (m < C) & (j == m)
        m = i - (start + h * PV)
        found = found | ((m >= 0) & (m < PV) & (j == C + 3 * PV + m))
        for c in range(3):
            m = i - (LANES + start + c * lay.vp + h * PV)
            found = found | ((m >= 0) & (m < PV) & (j == C + 3 * m + c))
        w_o = w_o + nn(pick(found), w_out[h * width : h * width + near, :])
    w_o = w_o.astype(B16)
    w_out_rows[: 2 * LANES, :] = w_o
    for h in range(heads):
        w_out_rows[(2 + h) * LANES : (3 + h) * LANES, :] = w_out[h * width + near : (h + 1) * width, :]
    single = jnp.broadcast_to(query_single[...], (SUBLANES, query_single.shape[1]))
    rows = nt(single, w_q)
    moved = turned_by(turn, unpack(rows, lay.kp))
    points = pack([(v + turn[9 + c]).astype(B16).astype(F32) for c, v in enumerate(moved)], lay.kp, start)
    query = jnp.where(lane < start, rows, 0.0).astype(B16).astype(F32)
    left[:SUBLANES, :] = jnp.where(zero_head == row, query, 0.0)
    minus = lane < 0
    for h in range(heads):
        at = lay.square + h * PQ
        minus = minus | ((row == h) & (lane >= at) & (lane < at + 3))
    mine = jnp.where(zero_head == row, points, 0.0)
    left[SUBLANES:, :] = jnp.where(minus, -0.5, mine)
    cotangent = jnp.broadcast_to(d_out[...], (SUBLANES, d_out.shape[1]))
    d_row[...] = nt(cotangent, w_o)
    scratch[...] = jnp.zeros_like(scratch)
    scratch[:heads, :] = bias_weight[...].astype(F32)
    for h in range(heads):
        d_pair = nt(cotangent, w_out[h * width + near : (h + 1) * width, :])
        scratch[SUBLANES + h : SUBLANES + h + 1, :] = d_pair[:1, :]
    both = nt(scratch[...].astype(B16), pair_rows[...])
    square = jnp.sum(mine * mine, axis=1, keepdims=True)
    base[...] = both[:SUBLANES] - 0.5 * gain[:, :1] * square
    d_base[...] = both[SUBLANES:]


def attention_kernel(lay, block, order, *refs):
    *parts, left, base, d_base, d_row, gains, table, message, features, weights, scores, gathered = refs
    frames = [table[i : i + 1, :] for i in range(12)]
    me = lax.axis_index("row")
    heads, vp, start = lay.heads, lay.vp, lay.base
    shape = (SUBLANES, LANES)
    row, lane = iota(shape, 0), iota(shape, 1)
    _, one_head = head_of(shape, lay)
    gain = gains[...]
    restored = [lay.restore(part, block) for part in parts]
    zeros, ones = [zero for zero, _ in restored], [one for _, one in restored]
    queries = left[...].astype(B16)
    first = jnp.concatenate([nt(queries, zero) for zero in zeros], axis=1)
    logits = LOGIT_SCALE * (first[:SUBLANES] * (1.0 / math.sqrt(C)) + base[...] + gain[:, :1] * first[SUBLANES:])
    weight = jnp.exp(logits - jnp.max(logits, axis=1, keepdims=True))
    attention = weight / jnp.sum(weight, axis=1, keepdims=True)
    attention = jnp.where(iota(attention.shape, 0) < heads, attention, 0.0)
    attention_b = attention.astype(B16)
    weights[...] = attention_b
    sums = spread(attention_b, ones)
    sums = jnp.sum(jnp.where(one_head == row, sums, 0.0), axis=0, keepdims=True)
    sums = jnp.broadcast_to(sums, shape)
    local = turned_back(frames, [v - frames[9 + c] for c, v in enumerate(unpack(sums, vp))])
    lengths = jnp.sqrt(1.0 + (local[0] * local[0] + local[1] * local[1] + local[2] * local[2]))
    d_one = d_row[:, LANES:]
    share = d_row[:, :LANES] / lengths
    d_points = turned_by(frames, [v + share * u for v, u in zip(unpack(d_one, vp), local)])
    d_side = jnp.where(lane < start, d_one, 0.0) + pack(d_points, vp, start)
    right = jnp.where(one_head == row, d_side, 0.0).astype(B16)
    d_attention = jnp.concatenate([nt(right, one) for one in ones], axis=1) + d_base[...]
    total = jnp.sum(attention * d_attention, axis=1, keepdims=True)
    score_b = (LOGIT_SCALE * attention * (d_attention - total)).astype(B16)
    query = jnp.sum(jnp.where(lane < lay.square, left[:SUBLANES, :] + left[SUBLANES:, :], 0.0), axis=0, keepdims=True)
    side = jnp.where(row == 2 * heads, jnp.broadcast_to(query, shape), 0.0)
    side = side + jnp.where(row == 2 * heads + 1, d_side, 0.0)
    both = attention_b.astype(F32) + pltpu.roll(score_b.astype(F32), heads, 0)
    for at in range(0, both.shape[1], LANES):
        for place in range(at // block, (at + LANES) // block):
            piece = both[:, at : at + LANES]
            if place * block != at:
                piece = pltpu.roll(piece, LANES - (place * block - at), 1)
            piece = jnp.where(row < 2 * heads, piece, side).astype(B16)
            for core in range(2):
                message[(me ^ order[place]) * 2 + core, :, :] = piece
    at = 0
    for zero in zeros:
        gathered[at : at + zero.shape[0], :] = zero
        at += zero.shape[0]
    scores[...] = score_b
    features[:, :LANES] = jnp.where((lane >= start) & (lane < start + vp), lengths, 0.0)
    features[:, LANES:] = jnp.where(lane < start, sums, 0.0) + pack(local, vp, start)


def spread(weights, parts):
    total, at = 0.0, 0
    for part in parts:
        total = total + nn(weights[:, at : at + part.shape[0]], part)
        at += part.shape[0]
    return total


def rows_kernel(lay, *refs):
    gathered, pair, left, scores, features, weights, w_out_rows, w_query_rows, gains, table, parcel, sums, again = refs
    frames = [table[i : i + 1, :] for i in range(12)]
    shape = (SUBLANES, LANES)
    row, lane = iota(shape, 0), iota(shape, 1)
    zero_head, _ = head_of(shape, lay)
    pair_sum = nn(weights[...], pair[...])
    pairs = [jnp.broadcast_to(pair_sum[h : h + 1, :], shape) for h in range(lay.heads)]
    result = nn(jnp.concatenate([features[...]] + pairs, axis=1).astype(B16), w_out_rows[...])
    score = scores[...].astype(F32)
    d_rows = nn(scores[...], gathered[...])
    score_sum = jnp.sum(score, axis=1, keepdims=True)
    points = left[SUBLANES:, :]
    d_rows = jnp.where(lane < lay.base, d_rows * (1.0 / math.sqrt(C)), gains[...] * (d_rows - score_sum * points))
    d_rows = jnp.broadcast_to(
        jnp.sum(jnp.where(zero_head == row, d_rows, 0.0), axis=0, keepdims=True), shape
    )
    local = pack(turned_back(frames, unpack(d_rows, lay.kp)), lay.kp, lay.base)
    both = (jnp.where(lane < lay.base, d_rows, 0.0) + local).astype(B16)
    sums[...] = jnp.concatenate([result, nn(both, w_query_rows[...])], axis=1)
    again[...] = parcel[...]


def owner_kernel(lay, arrived, turned, parcel, other, result):
    heads, base = lay.heads, lay.base
    count = arrived.shape[0] // 2
    block = turned.shape[0]
    shape = (SUBLANES, LANES)
    whole = (count, SUBLANES, LANES)
    row = iota(shape, 0)
    zero_head, one_head = head_of(shape, lay)
    lane = iota(shape, 1)
    keep0 = (zero_head >= 0) & (zero_head + heads == row)
    keep1 = one_head == row
    ones = jnp.broadcast_to(jnp.where(keep0 & (lane >= base), 1.0, 0.0)[None], whole)
    columns = [turned[:, i : i + 1] for i in range(9)]
    lane = iota((block, LANES), 1)
    me = lax.axis_index("head")
    total = None
    for core, held in ((me, parcel), (1 - me, other)):
        took = jnp.concatenate([arrived[pl.ds(q * 2 + core, 1)] for q in range(count)], axis=0).astype(F32)
        side0 = jnp.where(keep0[None], jnp.broadcast_to(took[:, 2 * heads : 2 * heads + 1, :], whole), 0.0)
        side1 = jnp.where(keep1[None], jnp.broadcast_to(took[:, 2 * heads + 1 : 2 * heads + 2, :], whole), 0.0)
        right = jnp.concatenate([side0, side1, ones], axis=2).reshape(count * SUBLANES, 3 * LANES).astype(B16)
        moved = jnp.transpose(took.reshape(count * SUBLANES, LANES)).astype(B16)
        both = nn(moved, right)[:block]
        pieces = held[2 * LANES + block :, :LANES].astype(F32)
        gain = pieces[0:1] + pieces[1:2] + pieces[2:3]
        own = held[2 * LANES : 2 * LANES + block, :LANES].astype(F32)
        tile0, tile1 = both[:, :LANES], both[:, LANES : 2 * LANES]
        points = gain * (tile0 - both[:, 2 * LANES :] * own)
        points = pack(turned_back(columns, unpack(points, lay.kp)), lay.kp, base)
        tile0 = jnp.where(lane < base, tile0 * (1.0 / math.sqrt(C)), points)
        points = pack(turned_back(columns, unpack(tile1, lay.vp)), lay.vp, base)
        tile1 = jnp.where(lane < base, tile1, points)
        rows = jnp.concatenate([tile0, tile1], axis=1).astype(B16)
        part = nn(rows, held[: 2 * LANES, :])
        total = part if total is None else total + part
    result[...] = total


def finish_kernel(own, other, output, grad_query):
    width = output.shape[1]
    total = own[...] + other[...]
    output[...] = total[:1, :width].astype(output.dtype)
    grad_query[...] = total[:1, width:]


VMEM = pl.BlockSpec(memory_space=pltpu.VMEM)
HBM = pl.BlockSpec(memory_space=pltpu.HBM)


def call(body, outs, args, fresh=0, scratch=(), flops=1000000, last=False, waits=False):
    size = sum(math.prod(v.shape) * v.dtype.itemsize for v in list(args) + list(outs))

    def kernel(*refs):
        if fresh:
            *refs, sems = refs
            held = refs[len(refs) - fresh :]
            copies = [pltpu.make_async_copy(refs[i], held[i], sems.at[i]) for i in range(fresh)]
            for copy in copies:
                copy.start()

            def ready():
                for copy in copies:
                    copy.wait()

            if not waits:
                ready()
            refs = list(held) + list(refs[fresh : len(refs) - fresh])
        body(*([ready] if waits else []), *refs)

    own = [pltpu.VMEM(v.shape, v.dtype) for v in args[:fresh]]
    return pl.pallas_call(
        kernel,
        out_shape=tuple(outs),
        in_specs=[HBM] * fresh + [VMEM] * (len(args) - fresh),
        out_specs=tuple([pl.BlockSpec() if last else VMEM] * len(outs)),
        scratch_shapes=list(scratch) + own + ([pltpu.SemaphoreType.DMA((fresh,))] if fresh else []),
        compiler_params=pltpu.CompilerParams(vmem_limit_bytes=(16 << 20) + 6 * size),
        cost_estimate=pl.CostEstimate(flops=flops, bytes_accessed=size, transcendentals=0),
    )(*[pltpu.with_memory_space_constraint(v, pltpu.HBM) for v in args[:fresh]], *args[fresh:])


def shape_of(*dims, dtype=F32):
    return jax.ShapeDtypeStruct(dims, dtype)


def shards(
    query_single, key_single, pair, query_frames, key_frames, w_query, w_key, w_value, w_query_points, w_key_points,
    w_value_points, head_weight, bias_weight, w_out, d_out,
):
    lay = Layout(head_weight.shape[0])
    count = lax.axis_size("row")
    block, width = key_single.shape
    total = count * block
    near = 1
    while 4 * near * near <= count:
        near *= 2
    assert count & (count - 1) == 0

    def exchange(value, mask):
        return lax.ppermute(value, "row", [(i, i ^ mask) for i in range(count)])

    packed, own = call(
        functools.partial(key_kernel, lay),
        [shape_of(block + lay.kept(block), LANES, dtype=B16), shape_of(block, LANES, dtype=B16)],
        [
            key_single, key_frames, w_key.T, w_value.T, w_key_points.T, w_value_points.T,
        ],
        6,
        waits=True,
    )
    offsets = list(range(0, count, near))
    line = jnp.concatenate([packed] + [exchange(packed, mask) for mask in offsets[1:]], axis=0)
    planes = list(range(near))
    parts = [line] + [exchange(line, m) for m in planes[1:]]
    order = [m ^ o for m in planes for o in offsets]

    left, base, d_base, d_row, w_out_rows, w_query_rows, table, pair_rows, gains, parcel, turned = call(
        functools.partial(early_kernel, lay, block, order),
        [
            shape_of(ROWS16, LANES), shape_of(SUBLANES, total), shape_of(SUBLANES, total),
            shape_of(SUBLANES, 2 * LANES), shape_of((2 + lay.heads) * LANES, width, dtype=B16),
            shape_of(LANES, width, dtype=B16), shape_of(ROWS16, LANES),
            shape_of(total, LANES, dtype=B16), shape_of(SUBLANES, LANES),
            shape_of(2 * LANES + block + ROWS16, width, dtype=B16), shape_of(block, LANES),
        ],
        [
            query_frames.T, query_single, w_query.T, w_query_points.T, bias_weight, w_out, d_out, pair,
            head_weight.reshape(1, -1), key_frames, w_key.T, w_value.T, w_key_points.T, w_value_points.T, own,
        ],
        14,
        [pltpu.VMEM((ROWS16, LANES), F32)],
    )
    swap = [(i, (i + 1) % 2) for i in range(2)]
    message, features, weight_rows, scores, gathered = call(
        functools.partial(attention_kernel, lay, block, order),
        [
            shape_of(2 * count, SUBLANES, LANES, dtype=B16), shape_of(SUBLANES, 2 * LANES),
            shape_of(SUBLANES, total, dtype=B16), shape_of(SUBLANES, total, dtype=B16),
            shape_of(total, LANES, dtype=B16),
        ],
        parts + [left, base, d_base, d_row, gains, table],
    )
    arrived = lax.all_to_all(message, ("row", "head"), 0, 0, tiled=True)
    sums, again = call(
        functools.partial(rows_kernel, lay),
        [shape_of(SUBLANES, 2 * width), parcel],
        [gathered, pair_rows, left, scores, features, weight_rows, w_out_rows, w_query_rows, gains, table, parcel],
    )
    other = lax.ppermute(again, "head", swap)
    output, grad_query = call(
        finish_kernel,
        [shape_of(1, width, dtype=B16), shape_of(1, width)],
        [sums, lax.ppermute(sums, "head", swap)],
        last=True,
    )
    (grad_keys,) = call(
        functools.partial(owner_kernel, lay),
        [shape_of(block, width)],
        [arrived, turned, parcel, other],
        last=True,
    )
    return (output, grad_query, grad_keys)


def solution(mesh):
    return jax.shard_map(
        shards,
        mesh=mesh,
        in_specs=(
            P("row", None),
            P("row", None),
            P("row", None, None),
            P(None, "row"),
            P(None, "row"),
            P(None, "head"),
            P(None, "head"),
            P(None, "head"),
            P(None, "head"),
            P(None, "head"),
            P(None, "head"),
            P("head"),
            P("head", None),
            P("head", None),
            P("row", None),
        ),
        out_specs=(P("row", None), P("row", None), P("row", None)),
        check_vma=False,
    )
```

```python
import functools
import math

import jax
import jax.numpy as jnp
from jax import lax
from jax.experimental import pallas as pl
from jax.experimental.pallas import tpu as pltpu
from jax.sharding import PartitionSpec as P

C = 16
PQ = 4
PV = 8
LANES = 128
SUBLANES = 8
ROWS16 = 16
LOGIT_SCALE = math.sqrt(1.0 / 3.0)
POINT_SCALE = math.sqrt(2.0 / (9.0 * PQ))
F32 = jnp.float32
B16 = jnp.bfloat16


class Layout:
    def __init__(self, heads):
        self.heads = heads
        self.base = heads * C
        self.kp = heads * PQ
        self.vp = heads * PV
        self.square = self.base + 3 * self.kp
        assert self.square + self.kp <= LANES and self.base + 3 * self.vp <= LANES
        assert 2 * heads + 2 <= SUBLANES and PQ == 4


def nn(a, b, precision=None):
    return lax.dot_general(a, b, (((1,), (0,)), ((), ())), precision=precision, preferred_element_type=F32)


def nt(a, b):
    return lax.dot_general(a, b, (((1,), (1,)), ((), ())), preferred_element_type=F32)


def iota(shape, dim):
    return lax.broadcasted_iota(jnp.int32, shape, dim)


def pick(condition):
    return jnp.where(condition, 1.0, 0.0).astype(B16)


def to_lane(rows, offset):
    j, i = iota((LANES, rows), 0), iota((LANES, rows), 1)
    return pick(j == i + offset)


def to_components(rows, offset, points, seg):
    j, i = iota((LANES, rows), 0), iota((LANES, rows), 1)
    found = j < 0
    for c in range(3):
        m = j - (c * seg + offset)
        found = found | ((m >= 0) & (m < points) & (i == 3 * m + c))
    return pick(found)


def unpack(tile, seg):
    return tile, pltpu.roll(tile, LANES - seg, 1), pltpu.roll(tile, LANES - 2 * seg, 1)


def pack(parts, seg, base):
    lane = iota(parts[0].shape, 1)
    keep = (lane >= base) & (lane < base + seg)
    x, y, z = (jnp.where(keep, v, 0.0) for v in parts)
    return x + pltpu.roll(y, seg, 1) + pltpu.roll(z, 2 * seg, 1)


def head_of(shape, lay):
    lane = iota(shape, 1)
    zero = jnp.full(shape, -1, jnp.int32)
    one = jnp.full(shape, -1, jnp.int32)
    for h in range(lay.heads):
        same = (lane >= h * C) & (lane < (h + 1) * C)
        zero, one = jnp.where(same, h, zero), jnp.where(same, h, one)
        for c in range(3):
            k = lay.base + c * lay.kp + h * PQ
            v = lay.base + c * lay.vp + h * PV
            zero = jnp.where((lane >= k) & (lane < k + PQ), h, zero)
            one = jnp.where((lane >= v) & (lane < v + PV), h, one)
    return zero, one


def turned_by(frames, vectors):
    x, y, z = vectors
    return [frames[3 * c] * x + frames[3 * c + 1] * y + frames[3 * c + 2] * z for c in range(3)]


def turned_back(frames, vectors):
    x, y, z = vectors
    return [frames[d] * x + frames[3 + d] * y + frames[6 + d] * z for d in range(3)]


def key_kernel(lay, ready, key_single, frames, w_key, w_value, w_kp, w_vp, packed):
    heads, kp, vp, base = lay.heads, lay.kp, lay.vp, lay.base
    tall = PQ * SUBLANES

    def rows_of(count, width):
        return iota((count, width), 0), iota((count, width), 1)

    r, i = rows_of(tall, 3 * kp)
    to_kp = [pick((i == 3 * PQ * (r & 7) + 3 * (r >> 3) + c) & ((r & 7) < heads)) for c in range(3)]
    r, i = rows_of(vp, 3 * vp)
    to_vp = [pick(i == 3 * r + c) for c in range(3)]
    width = 2 * LANES
    r, j = rows_of(base, width)
    place = [j == r, j == r + LANES]
    r, j = rows_of(tall, width)
    place += [(j == base + c * kp + PQ * (r & 7) + (r >> 3)) & ((r & 7) < heads) for c in range(3)]
    r, j = rows_of(vp, width)
    place += [j == LANES + base + c * vp + r for c in range(3)]
    r, j = rows_of(SUBLANES, width)
    place += [(j == lay.square + PQ * r + piece) & (r < heads) for piece in range(3)]
    place = jnp.concatenate([jnp.where(found, 1.0, 0.0) for found in place], axis=0).astype(B16)
    to_kp = jnp.concatenate(to_kp, axis=0)
    to_vp = jnp.concatenate(to_vp, axis=0)
    ready()
    single = key_single[...]
    turn = [frames[i : i + 1, :] for i in range(12)]
    features = [nt(w_key[...], single), nt(w_value[...], single)]
    for choose, weight, height in ((to_kp, w_kp, tall), (to_vp, w_vp, vp)):
        rows = nt(nn(choose, weight[...]).astype(B16), single)
        moved = turned_by(turn, [rows[c * height : (c + 1) * height] for c in range(3)])
        moved = [(v + turn[9 + c]).astype(B16).astype(F32) for c, v in enumerate(moved)]
        features += moved
        if height == tall:
            square = moved[0] * moved[0] + moved[1] * moved[1] + moved[2] * moved[2]
            square = sum(square[group(p)] for p in range(PQ))
    first = square.astype(B16).astype(F32)
    second = (square - first).astype(B16).astype(F32)
    features = jnp.concatenate(features + [first, second, square - first - second], axis=0)
    packed[...] = nn(jnp.transpose(features).astype(B16), place).astype(B16)


def group(h):
    return slice(h * SUBLANES, (h + 1) * SUBLANES)


def gain_rows(head_weight, lay):
    row = iota((SUBLANES, LANES), 0)
    raw = jnp.zeros((SUBLANES, LANES), F32)
    for h in range(lay.heads):
        raw = jnp.where(row == h, jnp.broadcast_to(head_weight[:, h : h + 1], raw.shape), raw)
    gain = (jnp.maximum(raw, 0.0) + jnp.log1p(jnp.exp(-jnp.abs(raw)))) * POINT_SCALE
    return jnp.where(row < lay.heads, gain, 0.0)


def gain_lanes(gain, lay):
    zero, _ = head_of(gain.shape, lay)
    return jnp.sum(jnp.where(zero == iota(gain.shape, 0), gain, 0.0), axis=0, keepdims=True)


def early_kernel(
    lay, block, order, frames, query_single, w_query, w_qp, bias_weight, w_out, d_out, pair, head_weight, key_frames,
    w_key, w_value, w_kp, w_vp, packed,
    left, base, d_base, d_row, w_out_rows, w_query_rows, table, pair_rows, gains, parcel, turned, scratch,
):
    kp, vp = lay.kp, lay.vp
    zero = nn(to_lane(lay.base, 0), w_key[...]) + nn(to_components(3 * kp, lay.base, kp, kp), w_kp[...])
    one = nn(to_lane(lay.base, 0), w_value[...]) + nn(to_components(3 * vp, lay.base, vp, vp), w_vp[...])
    parcel[:LANES, :] = zero.astype(B16)
    parcel[LANES : 2 * LANES, :] = one.astype(B16)
    parcel[2 * LANES :, :] = jnp.zeros((block + ROWS16, parcel.shape[1]), B16)
    parcel[2 * LANES : 2 * LANES + block, :LANES] = packed[:, :LANES]
    gain = gain_rows(head_weight, lay)
    gains[...] = gain
    pieces = jnp.broadcast_to(gain_lanes(gain, lay), (ROWS16, LANES))
    first = pieces.astype(B16).astype(F32)
    second = (pieces - first).astype(B16).astype(F32)
    row = iota(pieces.shape, 0)
    pieces = jnp.where(
        row == 0, first, jnp.where(row == 1, second, jnp.where(row == 2, pieces - first - second, 0.0))
    )
    parcel[2 * LANES + block :, :LANES] = pieces.astype(B16)
    turn = jnp.transpose(key_frames[...])
    turned[:, : turn.shape[1]] = turn
    me = lax.axis_index("row")
    for place, offset in enumerate(order):
        j = pl.multiple_of((me ^ offset) * block, block)
        pair_rows[place * block : (place + 1) * block, :] = pair[0, pl.ds(j, block), :]
    turn = [jnp.broadcast_to(frames[:, i : i + 1], (1, LANES)) for i in range(12)]
    for i in range(12):
        table[i : i + 1, :] = turn[i]
    heads, start = lay.heads, lay.base
    width = C + 4 * PV + LANES
    near = C + 4 * PV
    shape = (SUBLANES, LANES)
    row, lane = iota(shape, 0), iota(shape, 1)
    zero_head, _ = head_of(shape, lay)
    w_q = nn(to_lane(start, 0), w_query[...]) + nn(to_components(3 * lay.kp, start, lay.kp, lay.kp), w_qp[...])
    w_q = w_q.astype(B16)
    w_query_rows[...] = w_q
    w_o = jnp.zeros((2 * LANES, w_out.shape[1]), F32)
    for h in range(heads):
        i, j = iota((2 * LANES, near), 0), iota((2 * LANES, near), 1)
        m = i - (LANES + h * C)
        found = (m >= 0) & (m < C) & (j == m)
        m = i - (start + h * PV)
        found = found | ((m >= 0) & (m < PV) & (j == C + 3 * PV + m))
        for c in range(3):
            m = i - (LANES + start + c * lay.vp + h * PV)
            found = found | ((m >= 0) & (m < PV) & (j == C + 3 * m + c))
        w_o = w_o + nn(pick(found), w_out[h * width : h * width + near, :])
    w_o = w_o.astype(B16)
    w_out_rows[: 2 * LANES, :] = w_o
    for h in range(heads):
        w_out_rows[(2 + h) * LANES : (3 + h) * LANES, :] = w_out[h * width + near : (h + 1) * width, :]
    single = jnp.broadcast_to(query_single[...], (SUBLANES, query_single.shape[1]))
    rows = nt(single, w_q)
    moved = turned_by(turn, unpack(rows, lay.kp))
    points = pack([(v + turn[9 + c]).astype(B16).astype(F32) for c, v in enumerate(moved)], lay.kp, start)
    query = jnp.where(lane < start, rows, 0.0).astype(B16).astype(F32)
    left[:SUBLANES, :] = jnp.where(zero_head == row, query, 0.0)
    minus = lane < 0
    for h in range(heads):
        at = lay.square + h * PQ
        minus = minus | ((row == h) & (lane >= at) & (lane < at + 3))
    mine = jnp.where(zero_head == row, points, 0.0)
    left[SUBLANES:, :] = jnp.where(minus, -0.5, mine)
    cotangent = jnp.broadcast_to(d_out[...], (SUBLANES, d_out.shape[1]))
    d_row[...] = nt(cotangent, w_o)
    scratch[...] = jnp.zeros_like(scratch)
    scratch[:heads, :] = bias_weight[...].astype(F32)
    for h in range(heads):
        d_pair = nt(cotangent, w_out[h * width + near : (h + 1) * width, :])
        scratch[SUBLANES + h : SUBLANES + h + 1, :] = d_pair[:1, :]
    both = nt(scratch[...].astype(B16), pair_rows[...])
    square = jnp.sum(mine * mine, axis=1, keepdims=True)
    base[...] = both[:SUBLANES] - 0.5 * gain[:, :1] * square
    d_base[...] = both[SUBLANES:]


def attention_kernel(lay, block, order, *refs):
    *parts, left, base, d_base, d_row, gains, table, messages, features, weights, scores, message, sem = refs
    frames = [table[i : i + 1, :] for i in range(12)]
    me = lax.axis_index("row")
    heads, vp, start = lay.heads, lay.vp, lay.base
    shape = (SUBLANES, LANES)
    row, lane = iota(shape, 0), iota(shape, 1)
    _, one_head = head_of(shape, lay)
    gain = gains[...]
    queries = left[...].astype(B16)
    first = jnp.concatenate([nt(queries, part[:, :LANES]) for part in parts], axis=1)
    logits = LOGIT_SCALE * (first[:SUBLANES] * (1.0 / math.sqrt(C)) + base[...] + gain[:, :1] * first[SUBLANES:])
    weight = jnp.exp(logits - jnp.max(logits, axis=1, keepdims=True))
    attention = weight / jnp.sum(weight, axis=1, keepdims=True)
    attention = jnp.where(iota(attention.shape, 0) < heads, attention, 0.0)
    attention_b = attention.astype(B16)
    sums = spread(attention_b, [part.at[:, LANES:] for part in parts])
    sums = jnp.sum(jnp.where(one_head == row, sums, 0.0), axis=0, keepdims=True)
    sums = jnp.broadcast_to(sums, shape)
    local = turned_back(frames, [v - frames[9 + c] for c, v in enumerate(unpack(sums, vp))])
    lengths = jnp.sqrt(1.0 + (local[0] * local[0] + local[1] * local[1] + local[2] * local[2]))
    d_one = d_row[:, LANES:]
    share = d_row[:, :LANES] / lengths
    d_points = turned_by(frames, [v + share * u for v, u in zip(unpack(d_one, vp), local)])
    d_side = jnp.where(lane < start, d_one, 0.0) + pack(d_points, vp, start)
    right = jnp.where(one_head == row, d_side, 0.0).astype(B16)
    d_attention = jnp.concatenate([nt(right, part[:, LANES:]) for part in parts], axis=1) + d_base[...]
    total = jnp.sum(attention * d_attention, axis=1, keepdims=True)
    score_b = (LOGIT_SCALE * attention * (d_attention - total)).astype(B16)
    query = jnp.sum(jnp.where(lane < lay.square, left[:SUBLANES, :] + left[SUBLANES:, :], 0.0), axis=0, keepdims=True)
    side = jnp.where(row == 2 * heads, jnp.broadcast_to(query, shape), 0.0)
    side = side + jnp.where(row == 2 * heads + 1, d_side, 0.0)
    both = attention_b.astype(F32) + pltpu.roll(score_b.astype(F32), heads, 0)
    for at in range(0, both.shape[1], LANES):
        for place in range(at // block, (at + LANES) // block):
            tile = both[:, at : at + LANES]
            if place * block != at:
                tile = pltpu.roll(tile, LANES - (place * block - at), 1)
            tile = jnp.where(row < 2 * heads, tile, side).astype(B16)
            for core in range(2):
                message[(me ^ order[place]) * 2 + core, :, :] = tile
    sent = pltpu.make_async_copy(message, messages, sem)
    sent.start()
    weights[...] = attention_b
    scores[...] = score_b
    features[:, :LANES] = jnp.where((lane >= start) & (lane < start + vp), lengths, 0.0)
    features[:, LANES:] = jnp.where(lane < start, sums, 0.0) + pack(local, vp, start)
    sent.wait()


def spread(weights, parts):
    total, at = 0.0, 0
    for part in parts:
        total = total + nn(weights[:, at : at + part.shape[0]], part[...])
        at += part.shape[0]
    return total


def rows_kernel(lay, *refs):
    *parts, pair, left, scores, features, weights, w_out_rows, w_query_rows, gains, table, sums = refs
    frames = [table[i : i + 1, :] for i in range(12)]
    shape = (SUBLANES, LANES)
    row, lane = iota(shape, 0), iota(shape, 1)
    zero_head, _ = head_of(shape, lay)
    pair_sum = nn(weights[...], pair[...])
    pairs = [jnp.broadcast_to(pair_sum[h : h + 1, :], shape) for h in range(lay.heads)]
    result = nn(jnp.concatenate([features[...]] + pairs, axis=1).astype(B16), w_out_rows[...])
    score = scores[...].astype(F32)
    d_rows = spread(scores[...], [part.at[:, :LANES] for part in parts])
    score_sum = jnp.sum(score, axis=1, keepdims=True)
    points = left[SUBLANES:, :]
    d_rows = jnp.where(lane < lay.base, d_rows * (1.0 / math.sqrt(C)), gains[...] * (d_rows - score_sum * points))
    d_rows = jnp.broadcast_to(
        jnp.sum(jnp.where(zero_head == row, d_rows, 0.0), axis=0, keepdims=True), shape
    )
    local = pack(turned_back(frames, unpack(d_rows, lay.kp)), lay.kp, lay.base)
    both = (jnp.where(lane < lay.base, d_rows, 0.0) + local).astype(B16)
    sums[...] = jnp.concatenate([result, nn(both, w_query_rows[...])], axis=1)


def owner_kernel(lay, arrived, turned, parcel, other, result):
    heads, base = lay.heads, lay.base
    count = arrived.shape[0] // 2
    block = turned.shape[0]
    shape = (SUBLANES, LANES)
    whole = (count, SUBLANES, LANES)
    row = iota(shape, 0)
    zero_head, one_head = head_of(shape, lay)
    lane = iota(shape, 1)
    keep0 = (zero_head >= 0) & (zero_head + heads == row)
    keep1 = one_head == row
    ones = jnp.broadcast_to(jnp.where(keep0 & (lane >= base), 1.0, 0.0)[None], whole)
    columns = [turned[:, i : i + 1] for i in range(9)]
    lane = iota((block, LANES), 1)
    me = lax.axis_index("head")
    total = None
    for core, held in ((me, parcel), (1 - me, other)):
        took = jnp.concatenate([arrived[pl.ds(q * 2 + core, 1)] for q in range(count)], axis=0).astype(F32)
        side0 = jnp.where(keep0[None], jnp.broadcast_to(took[:, 2 * heads : 2 * heads + 1, :], whole), 0.0)
        side1 = jnp.where(keep1[None], jnp.broadcast_to(took[:, 2 * heads + 1 : 2 * heads + 2, :], whole), 0.0)
        right = jnp.concatenate([side0, side1, ones], axis=2).reshape(count * SUBLANES, 3 * LANES).astype(B16)
        moved = jnp.transpose(took.reshape(count * SUBLANES, LANES)).astype(B16)
        both = nn(moved, right)[:block]
        pieces = held[2 * LANES + block :, :LANES].astype(F32)
        gain = pieces[0:1] + pieces[1:2] + pieces[2:3]
        own = held[2 * LANES : 2 * LANES + block, :LANES].astype(F32)
        tile0, tile1 = both[:, :LANES], both[:, LANES : 2 * LANES]
        points = gain * (tile0 - both[:, 2 * LANES :] * own)
        points = pack(turned_back(columns, unpack(points, lay.kp)), lay.kp, base)
        tile0 = jnp.where(lane < base, tile0 * (1.0 / math.sqrt(C)), points)
        points = pack(turned_back(columns, unpack(tile1, lay.vp)), lay.vp, base)
        tile1 = jnp.where(lane < base, tile1, points)
        rows = jnp.concatenate([tile0, tile1], axis=1).astype(B16)
        part = nn(rows, held[: 2 * LANES, :])
        total = part if total is None else total + part
    result[...] = total


def finish_kernel(own, other, output, grad_query):
    width = output.shape[1]
    total = own[...] + other[...]
    output[...] = total[:1, :width].astype(output.dtype)
    grad_query[...] = total[:1, width:]


VMEM = pl.BlockSpec(memory_space=pltpu.VMEM)
HBM = pl.BlockSpec(memory_space=pltpu.HBM)


def call(body, outs, args, fresh=0, scratch=(), flops=1000000, last=False, waits=False, away=0):
    size = sum(math.prod(v.shape) * v.dtype.itemsize for v in list(args) + list(outs))

    def kernel(*refs):
        if fresh:
            *refs, sems = refs
            held = refs[len(refs) - fresh :]
            copies = [pltpu.make_async_copy(refs[i], held[i], sems.at[i]) for i in range(fresh)]
            for copy in copies:
                copy.start()

            def ready():
                for copy in copies:
                    copy.wait()

            if not waits:
                ready()
            refs = list(held) + list(refs[fresh : len(refs) - fresh])
        body(*([ready] if waits else []), *refs)

    own = [pltpu.VMEM(v.shape, v.dtype) for v in args[:fresh]]
    return pl.pallas_call(
        kernel,
        out_shape=tuple(outs),
        in_specs=[HBM] * fresh + [VMEM] * (len(args) - fresh),
        out_specs=tuple([HBM] * away + [pl.BlockSpec() if last else VMEM] * (len(outs) - away)),
        scratch_shapes=list(scratch) + own + ([pltpu.SemaphoreType.DMA((fresh,))] if fresh else []),
        compiler_params=pltpu.CompilerParams(vmem_limit_bytes=(16 << 20) + 6 * size),
        cost_estimate=pl.CostEstimate(flops=flops, bytes_accessed=size, transcendentals=0),
    )(*[pltpu.with_memory_space_constraint(v, pltpu.HBM) for v in args[:fresh]], *args[fresh:])


def shape_of(*dims, dtype=F32):
    return jax.ShapeDtypeStruct(dims, dtype)


def shards(
    query_single, key_single, pair, query_frames, key_frames, w_query, w_key, w_value, w_query_points, w_key_points,
    w_value_points, head_weight, bias_weight, w_out, d_out,
):
    lay = Layout(head_weight.shape[0])
    count = lax.axis_size("row")
    block, width = key_single.shape
    total = count * block
    near = 1
    while 4 * near * near <= count:
        near *= 2
    assert count & (count - 1) == 0

    def exchange(value, mask):
        return lax.ppermute(value, "row", [(i, i ^ mask) for i in range(count)])

    (packed,) = call(
        functools.partial(key_kernel, lay),
        [shape_of(block, 2 * LANES, dtype=B16)],
        [
            key_single, key_frames, w_key.T, w_value.T, w_key_points.T, w_value_points.T,
        ],
        6,
        waits=True,
    )
    offsets = list(range(0, count, near))
    line = jnp.concatenate([packed] + [exchange(packed, mask) for mask in offsets[1:]], axis=0)
    planes = list(range(near))
    parts = [line] + [exchange(line, m) for m in planes[1:]]
    order = [m ^ o for m in planes for o in offsets]

    left, base, d_base, d_row, w_out_rows, w_query_rows, table, pair_rows, gains, parcel, turned = call(
        functools.partial(early_kernel, lay, block, order),
        [
            shape_of(ROWS16, LANES), shape_of(SUBLANES, total), shape_of(SUBLANES, total),
            shape_of(SUBLANES, 2 * LANES), shape_of((2 + lay.heads) * LANES, width, dtype=B16),
            shape_of(LANES, width, dtype=B16), shape_of(ROWS16, LANES),
            shape_of(total, LANES, dtype=B16), shape_of(SUBLANES, LANES),
            shape_of(2 * LANES + block + ROWS16, width, dtype=B16), shape_of(block, LANES),
        ],
        [
            query_frames.T, query_single, w_query.T, w_query_points.T, bias_weight, w_out, d_out, pair,
            head_weight.reshape(1, -1), key_frames, w_key.T, w_value.T, w_key_points.T, w_value_points.T, packed,
        ],
        14,
        [pltpu.VMEM((ROWS16, LANES), F32)],
    )
    swap = [(i, (i + 1) % 2) for i in range(2)]
    other = lax.ppermute(parcel, "head", swap)
    message, features, weight_rows, scores = call(
        functools.partial(attention_kernel, lay, block, order),
        [
            shape_of(2 * count, SUBLANES, LANES, dtype=B16), shape_of(SUBLANES, 2 * LANES),
            shape_of(SUBLANES, total, dtype=B16), shape_of(SUBLANES, total, dtype=B16),
        ],
        parts + [left, base, d_base, d_row, gains, table],
        scratch=[pltpu.VMEM((2 * count, SUBLANES, LANES), B16), pltpu.SemaphoreType.DMA],
        away=1,
    )
    arrived = lax.all_to_all(message, ("row", "head"), 0, 0, tiled=True)
    (sums,) = call(
        functools.partial(rows_kernel, lay),
        [shape_of(SUBLANES, 2 * width)],
        parts + [pair_rows, left, scores, features, weight_rows, w_out_rows, w_query_rows, gains, table],
    )
    output, grad_query = call(
        finish_kernel,
        [shape_of(1, width, dtype=B16), shape_of(1, width)],
        [sums, lax.ppermute(sums, "head", swap)],
        last=True,
    )
    (grad_keys,) = call(
        functools.partial(owner_kernel, lay),
        [shape_of(block, width)],
        [arrived, turned, parcel, other],
        last=True,
    )
    return (output, grad_query, grad_keys)


def solution(mesh):
    return jax.shard_map(
        shards,
        mesh=mesh,
        in_specs=(
            P("row", None),
            P("row", None),
            P("row", None, None),
            P(None, "row"),
            P(None, "row"),
            P(None, "head"),
            P(None, "head"),
            P(None, "head"),
            P(None, "head"),
            P(None, "head"),
            P(None, "head"),
            P("head"),
            P("head", None),
            P("head", None),
            P("row", None),
        ),
        out_specs=(P("row", None), P("row", None), P("row", None)),
        check_vma=False,
    )
```

```python
import functools
import math

import jax
import jax.numpy as jnp
from jax import lax
from jax.experimental import pallas as pl
from jax.experimental.pallas import tpu as pltpu
from jax.sharding import PartitionSpec as P

C = 16
PQ = 4
PV = 8
LANES = 128
SUBLANES = 8
ROWS16 = 16
LOGIT_SCALE = math.sqrt(1.0 / 3.0)
POINT_SCALE = math.sqrt(2.0 / (9.0 * PQ))
F32 = jnp.float32
B16 = jnp.bfloat16


class Layout:
    def __init__(self, heads):
        self.heads = heads
        self.base = heads * C
        self.kp = heads * PQ
        self.vp = heads * PV
        self.square = self.base + 3 * self.kp
        assert self.square + self.kp <= LANES and self.base + 3 * self.vp <= LANES
        assert 2 * heads + 2 <= SUBLANES and PQ == 4


def nn(a, b, precision=None):
    return lax.dot_general(a, b, (((1,), (0,)), ((), ())), precision=precision, preferred_element_type=F32)


def nt(a, b):
    return lax.dot_general(a, b, (((1,), (1,)), ((), ())), preferred_element_type=F32)


def iota(shape, dim):
    return lax.broadcasted_iota(jnp.int32, shape, dim)


def pick(condition):
    return jnp.where(condition, 1.0, 0.0).astype(B16)


def to_lane(rows, offset):
    j, i = iota((LANES, rows), 0), iota((LANES, rows), 1)
    return pick(j == i + offset)


def to_components(rows, offset, points, seg):
    j, i = iota((LANES, rows), 0), iota((LANES, rows), 1)
    found = j < 0
    for c in range(3):
        m = j - (c * seg + offset)
        found = found | ((m >= 0) & (m < points) & (i == 3 * m + c))
    return pick(found)


def unpack(tile, seg):
    return tile, pltpu.roll(tile, LANES - seg, 1), pltpu.roll(tile, LANES - 2 * seg, 1)


def pack(parts, seg, base):
    lane = iota(parts[0].shape, 1)
    keep = (lane >= base) & (lane < base + seg)
    x, y, z = (jnp.where(keep, v, 0.0) for v in parts)
    return x + pltpu.roll(y, seg, 1) + pltpu.roll(z, 2 * seg, 1)


def head_of(shape, lay):
    lane = iota(shape, 1)
    zero = jnp.full(shape, -1, jnp.int32)
    one = jnp.full(shape, -1, jnp.int32)
    for h in range(lay.heads):
        same = (lane >= h * C) & (lane < (h + 1) * C)
        zero, one = jnp.where(same, h, zero), jnp.where(same, h, one)
        for c in range(3):
            k = lay.base + c * lay.kp + h * PQ
            v = lay.base + c * lay.vp + h * PV
            zero = jnp.where((lane >= k) & (lane < k + PQ), h, zero)
            one = jnp.where((lane >= v) & (lane < v + PV), h, one)
    return zero, one


def turned_by(frames, vectors):
    x, y, z = vectors
    return [frames[3 * c] * x + frames[3 * c + 1] * y + frames[3 * c + 2] * z for c in range(3)]


def turned_back(frames, vectors):
    x, y, z = vectors
    return [frames[d] * x + frames[3 + d] * y + frames[6 + d] * z for d in range(3)]


def key_kernel(lay, ready, key_single, frames, w_key, w_value, w_kp, w_vp, packed):
    heads, kp, vp, base = lay.heads, lay.kp, lay.vp, lay.base
    tall = PQ * SUBLANES

    def rows_of(count, width):
        return iota((count, width), 0), iota((count, width), 1)

    r, i = rows_of(tall, 3 * kp)
    to_kp = [pick((i == 3 * PQ * (r & 7) + 3 * (r >> 3) + c) & ((r & 7) < heads)) for c in range(3)]
    r, i = rows_of(vp, 3 * vp)
    to_vp = [pick(i == 3 * r + c) for c in range(3)]
    width = 2 * LANES
    r, j = rows_of(base, width)
    place = [j == r, j == r + LANES]
    r, j = rows_of(tall, width)
    place += [(j == base + c * kp + PQ * (r & 7) + (r >> 3)) & ((r & 7) < heads) for c in range(3)]
    r, j = rows_of(vp, width)
    place += [j == LANES + base + c * vp + r for c in range(3)]
    r, j = rows_of(SUBLANES, width)
    place += [(j == lay.square + PQ * r + piece) & (r < heads) for piece in range(3)]
    place = jnp.concatenate([jnp.where(found, 1.0, 0.0) for found in place], axis=0).astype(B16)
    to_kp = jnp.concatenate(to_kp, axis=0)
    to_vp = jnp.concatenate(to_vp, axis=0)
    ready()
    single = key_single[...]
    turn = [frames[i : i + 1, :] for i in range(12)]
    features = [nt(w_key[...], single), nt(w_value[...], single)]
    for choose, weight, height in ((to_kp, w_kp, tall), (to_vp, w_vp, vp)):
        rows = nt(nn(choose, weight[...]).astype(B16), single)
        moved = turned_by(turn, [rows[c * height : (c + 1) * height] for c in range(3)])
        moved = [(v + turn[9 + c]).astype(B16).astype(F32) for c, v in enumerate(moved)]
        features += moved
        if height == tall:
            square = moved[0] * moved[0] + moved[1] * moved[1] + moved[2] * moved[2]
            square = sum(square[group(p)] for p in range(PQ))
    first = square.astype(B16).astype(F32)
    second = (square - first).astype(B16).astype(F32)
    features = jnp.concatenate(features + [first, second, square - first - second], axis=0)
    packed[...] = nn(jnp.transpose(features).astype(B16), place).astype(B16)


def group(h):
    return slice(h * SUBLANES, (h + 1) * SUBLANES)


def gain_rows(head_weight, lay):
    row = iota((SUBLANES, LANES), 0)
    raw = jnp.zeros((SUBLANES, LANES), F32)
    for h in range(lay.heads):
        raw = jnp.where(row == h, jnp.broadcast_to(head_weight[:, h : h + 1], raw.shape), raw)
    gain = (jnp.maximum(raw, 0.0) + jnp.log1p(jnp.exp(-jnp.abs(raw)))) * POINT_SCALE
    return jnp.where(row < lay.heads, gain, 0.0)


def gain_lanes(gain, lay):
    zero, _ = head_of(gain.shape, lay)
    return jnp.sum(jnp.where(zero == iota(gain.shape, 0), gain, 0.0), axis=0, keepdims=True)


def early_kernel(
    lay, block, order, frames, query_single, w_query, w_qp, bias_weight, w_out, d_out, pair, head_weight, key_frames,
    w_key, w_value, w_kp, w_vp, packed,
    left, base, d_base, d_row, w_out_rows, w_query_rows, table, pair_rows, gains, parcel, turned, scratch,
):
    kp, vp = lay.kp, lay.vp
    zero = nn(to_lane(lay.base, 0), w_key[...]) + nn(to_components(3 * kp, lay.base, kp, kp), w_kp[...])
    one = nn(to_lane(lay.base, 0), w_value[...]) + nn(to_components(3 * vp, lay.base, vp, vp), w_vp[...])
    parcel[:LANES, :] = zero.astype(B16)
    parcel[LANES : 2 * LANES, :] = one.astype(B16)
    half = block // 2
    parcel[2 * LANES :, :LANES] = packed[:half, :LANES]
    parcel[2 * LANES :, LANES : 2 * LANES] = packed[half:, :LANES]
    parcel[2 * LANES :, 2 * LANES :] = jnp.zeros((half, parcel.shape[1] - 2 * LANES), B16)
    gain = gain_rows(head_weight, lay)
    gains[...] = gain
    pieces = jnp.broadcast_to(gain_lanes(gain, lay), (ROWS16, LANES))
    first = pieces.astype(B16).astype(F32)
    second = (pieces - first).astype(B16).astype(F32)
    row = iota(pieces.shape, 0)
    pieces = jnp.where(
        row == 0, first, jnp.where(row == 1, second, jnp.where(row == 2, pieces - first - second, 0.0))
    )
    parcel[2 * LANES : 2 * LANES + ROWS16, 2 * LANES : 3 * LANES] = pieces.astype(B16)
    turn = jnp.transpose(key_frames[...])
    turned[:, : turn.shape[1]] = turn
    me = lax.axis_index("row")
    for place, offset in enumerate(order):
        j = pl.multiple_of((me ^ offset) * block, block)
        pair_rows[place * block : (place + 1) * block, :] = pair[0, pl.ds(j, block), :]
    turn = [jnp.broadcast_to(frames[:, i : i + 1], (1, LANES)) for i in range(12)]
    for i in range(12):
        table[i : i + 1, :] = turn[i]
    heads, start = lay.heads, lay.base
    width = C + 4 * PV + LANES
    near = C + 4 * PV
    shape = (SUBLANES, LANES)
    row, lane = iota(shape, 0), iota(shape, 1)
    zero_head, _ = head_of(shape, lay)
    w_q = nn(to_lane(start, 0), w_query[...]) + nn(to_components(3 * lay.kp, start, lay.kp, lay.kp), w_qp[...])
    w_q = w_q.astype(B16)
    w_query_rows[...] = w_q
    w_o = jnp.zeros((2 * LANES, w_out.shape[1]), F32)
    for h in range(heads):
        i, j = iota((2 * LANES, near), 0), iota((2 * LANES, near), 1)
        m = i - (LANES + h * C)
        found = (m >= 0) & (m < C) & (j == m)
        m = i - (start + h * PV)
        found = found | ((m >= 0) & (m < PV) & (j == C + 3 * PV + m))
        for c in range(3):
            m = i - (LANES + start + c * lay.vp + h * PV)
            found = found | ((m >= 0) & (m < PV) & (j == C + 3 * m + c))
        w_o = w_o + nn(pick(found), w_out[h * width : h * width + near, :])
    w_o = w_o.astype(B16)
    w_out_rows[: 2 * LANES, :] = w_o
    for h in range(heads):
        w_out_rows[(2 + h) * LANES : (3 + h) * LANES, :] = w_out[h * width + near : (h + 1) * width, :]
    single = jnp.broadcast_to(query_single[...], (SUBLANES, query_single.shape[1]))
    rows = nt(single, w_q)
    moved = turned_by(turn, unpack(rows, lay.kp))
    points = pack([(v + turn[9 + c]).astype(B16).astype(F32) for c, v in enumerate(moved)], lay.kp, start)
    query = jnp.where(lane < start, rows, 0.0).astype(B16).astype(F32)
    left[:SUBLANES, :] = jnp.where(zero_head == row, query, 0.0)
    minus = lane < 0
    for h in range(heads):
        at = lay.square + h * PQ
        minus = minus | ((row == h) & (lane >= at) & (lane < at + 3))
    mine = jnp.where(zero_head == row, points, 0.0)
    left[SUBLANES:, :] = jnp.where(minus, -0.5, mine)
    cotangent = jnp.broadcast_to(d_out[...], (SUBLANES, d_out.shape[1]))
    d_row[...] = nt(cotangent, w_o)
    scratch[...] = jnp.zeros_like(scratch)
    scratch[:heads, :] = bias_weight[...].astype(F32)
    for h in range(heads):
        d_pair = nt(cotangent, w_out[h * width + near : (h + 1) * width, :])
        scratch[SUBLANES + h : SUBLANES + h + 1, :] = d_pair[:1, :]
    both = nt(scratch[...].astype(B16), pair_rows[...])
    square = jnp.sum(mine * mine, axis=1, keepdims=True)
    base[...] = both[:SUBLANES] - 0.5 * gain[:, :1] * square
    d_base[...] = both[SUBLANES:]


def attention_kernel(lay, block, order, *refs):
    *parts, left, base, d_base, d_row, gains, table, message, features, weights, scores = refs
    frames = [table[i : i + 1, :] for i in range(12)]
    me = lax.axis_index("row")
    heads, vp, start = lay.heads, lay.vp, lay.base
    shape = (SUBLANES, LANES)
    row, lane = iota(shape, 0), iota(shape, 1)
    _, one_head = head_of(shape, lay)
    gain = gains[...]
    queries = left[...].astype(B16)
    first = jnp.concatenate([nt(queries, part[:, :LANES]) for part in parts], axis=1)
    logits = LOGIT_SCALE * (first[:SUBLANES] * (1.0 / math.sqrt(C)) + base[...] + gain[:, :1] * first[SUBLANES:])
    weight = jnp.exp(logits - jnp.max(logits, axis=1, keepdims=True))
    attention = weight / jnp.sum(weight, axis=1, keepdims=True)
    attention = jnp.where(iota(attention.shape, 0) < heads, attention, 0.0)
    attention_b = attention.astype(B16)
    sums = spread(attention_b, [part.at[:, LANES:] for part in parts])
    sums = jnp.sum(jnp.where(one_head == row, sums, 0.0), axis=0, keepdims=True)
    sums = jnp.broadcast_to(sums, shape)
    local = turned_back(frames, [v - frames[9 + c] for c, v in enumerate(unpack(sums, vp))])
    lengths = jnp.sqrt(1.0 + (local[0] * local[0] + local[1] * local[1] + local[2] * local[2]))
    d_one = d_row[:, LANES:]
    share = d_row[:, :LANES] / lengths
    d_points = turned_by(frames, [v + share * u for v, u in zip(unpack(d_one, vp), local)])
    d_side = jnp.where(lane < start, d_one, 0.0) + pack(d_points, vp, start)
    right = jnp.where(one_head == row, d_side, 0.0).astype(B16)
    d_attention = jnp.concatenate([nt(right, part[:, LANES:]) for part in parts], axis=1) + d_base[...]
    total = jnp.sum(attention * d_attention, axis=1, keepdims=True)
    score_b = (LOGIT_SCALE * attention * (d_attention - total)).astype(B16)
    query = jnp.sum(jnp.where(lane < lay.square, left[:SUBLANES, :] + left[SUBLANES:, :], 0.0), axis=0, keepdims=True)
    side = jnp.where(row == 2 * heads, jnp.broadcast_to(query, shape), 0.0)
    side = side + jnp.where(row == 2 * heads + 1, d_side, 0.0)
    both = attention_b.astype(F32) + pltpu.roll(score_b.astype(F32), heads, 0)
    for at in range(0, both.shape[1], LANES):
        for place in range(at // block, (at + LANES) // block):
            tile = both[:, at : at + LANES]
            if place * block != at:
                tile = pltpu.roll(tile, LANES - (place * block - at), 1)
            tile = jnp.where(row < 2 * heads, tile, side).astype(B16)
            for core in range(2):
                message[(me ^ order[place]) * 2 + core, :, :] = tile
    weights[...] = attention_b
    scores[...] = score_b
    features[:, :LANES] = jnp.where((lane >= start) & (lane < start + vp), lengths, 0.0)
    features[:, LANES:] = jnp.where(lane < start, sums, 0.0) + pack(local, vp, start)


def spread(weights, parts):
    total, at = 0.0, 0
    for part in parts:
        total = total + nn(weights[:, at : at + part.shape[0]], part[...])
        at += part.shape[0]
    return total


def rows_kernel(lay, *refs):
    *parts, pair, left, scores, features, weights, w_out_rows, w_query_rows, gains, table, sums = refs
    frames = [table[i : i + 1, :] for i in range(12)]
    shape = (SUBLANES, LANES)
    row, lane = iota(shape, 0), iota(shape, 1)
    zero_head, _ = head_of(shape, lay)
    pair_sum = nn(weights[...], pair[...])
    pairs = [jnp.broadcast_to(pair_sum[h : h + 1, :], shape) for h in range(lay.heads)]
    result = nn(jnp.concatenate([features[...]] + pairs, axis=1).astype(B16), w_out_rows[...])
    score = scores[...].astype(F32)
    d_rows = spread(scores[...], [part.at[:, :LANES] for part in parts])
    score_sum = jnp.sum(score, axis=1, keepdims=True)
    points = left[SUBLANES:, :]
    d_rows = jnp.where(lane < lay.base, d_rows * (1.0 / math.sqrt(C)), gains[...] * (d_rows - score_sum * points))
    d_rows = jnp.broadcast_to(
        jnp.sum(jnp.where(zero_head == row, d_rows, 0.0), axis=0, keepdims=True), shape
    )
    local = pack(turned_back(frames, unpack(d_rows, lay.kp)), lay.kp, lay.base)
    both = (jnp.where(lane < lay.base, d_rows, 0.0) + local).astype(B16)
    sums[...] = jnp.concatenate([result, nn(both, w_query_rows[...])], axis=1)


def owner_kernel(lay, arrived, turned, parcel, other, result):
    heads, base = lay.heads, lay.base
    count = arrived.shape[0] // 2
    block = turned.shape[0]
    shape = (SUBLANES, LANES)
    whole = (count, SUBLANES, LANES)
    row = iota(shape, 0)
    zero_head, one_head = head_of(shape, lay)
    lane = iota(shape, 1)
    keep0 = (zero_head >= 0) & (zero_head + heads == row)
    keep1 = one_head == row
    ones = jnp.broadcast_to(jnp.where(keep0 & (lane >= base), 1.0, 0.0)[None], whole)
    columns = [turned[:, i : i + 1] for i in range(9)]
    lane = iota((block, LANES), 1)
    me = lax.axis_index("head")
    total = None
    for core, held in ((me, parcel), (1 - me, other)):
        took = jnp.concatenate([arrived[pl.ds(q * 2 + core, 1)] for q in range(count)], axis=0).astype(F32)
        side0 = jnp.where(keep0[None], jnp.broadcast_to(took[:, 2 * heads : 2 * heads + 1, :], whole), 0.0)
        side1 = jnp.where(keep1[None], jnp.broadcast_to(took[:, 2 * heads + 1 : 2 * heads + 2, :], whole), 0.0)
        right = jnp.concatenate([side0, side1, ones], axis=2).reshape(count * SUBLANES, 3 * LANES).astype(B16)
        moved = jnp.transpose(took.reshape(count * SUBLANES, LANES)).astype(B16)
        both = nn(moved, right)[:block]
        pieces = held[2 * LANES : 2 * LANES + ROWS16, 2 * LANES : 3 * LANES].astype(F32)
        gain = pieces[0:1] + pieces[1:2] + pieces[2:3]
        own = [held[2 * LANES :, at : at + LANES].astype(F32) for at in (0, LANES)]
        own = jnp.concatenate(own, axis=0)
        tile0, tile1 = both[:, :LANES], both[:, LANES : 2 * LANES]
        points = gain * (tile0 - both[:, 2 * LANES :] * own)
        points = pack(turned_back(columns, unpack(points, lay.kp)), lay.kp, base)
        tile0 = jnp.where(lane < base, tile0 * (1.0 / math.sqrt(C)), points)
        points = pack(turned_back(columns, unpack(tile1, lay.vp)), lay.vp, base)
        tile1 = jnp.where(lane < base, tile1, points)
        rows = jnp.concatenate([tile0, tile1], axis=1).astype(B16)
        part = nn(rows, held[: 2 * LANES, :])
        total = part if total is None else total + part
    result[...] = total


def finish_kernel(own, other, output, grad_query):
    width = output.shape[1]
    total = own[...] + other[...]
    output[...] = total[:1, :width].astype(output.dtype)
    grad_query[...] = total[:1, width:]


VMEM = pl.BlockSpec(memory_space=pltpu.VMEM)
HBM = pl.BlockSpec(memory_space=pltpu.HBM)


def call(body, outs, args, fresh=0, scratch=(), flops=1000000, last=False, waits=False):
    size = sum(math.prod(v.shape) * v.dtype.itemsize for v in list(args) + list(outs))

    def kernel(*refs):
        if fresh:
            *refs, sems = refs
            held = refs[len(refs) - fresh :]
            copies = [pltpu.make_async_copy(refs[i], held[i], sems.at[i]) for i in range(fresh)]
            for copy in copies:
                copy.start()

            def ready():
                for copy in copies:
                    copy.wait()

            if not waits:
                ready()
            refs = list(held) + list(refs[fresh : len(refs) - fresh])
        body(*([ready] if waits else []), *refs)

    own = [pltpu.VMEM(v.shape, v.dtype) for v in args[:fresh]]
    return pl.pallas_call(
        kernel,
        out_shape=tuple(outs),
        in_specs=[HBM] * fresh + [VMEM] * (len(args) - fresh),
        out_specs=tuple([pl.BlockSpec() if last else VMEM] * len(outs)),
        scratch_shapes=list(scratch) + own + ([pltpu.SemaphoreType.DMA((fresh,))] if fresh else []),
        compiler_params=pltpu.CompilerParams(vmem_limit_bytes=(16 << 20) + 6 * size),
        cost_estimate=pl.CostEstimate(flops=flops, bytes_accessed=size, transcendentals=0),
    )(*[pltpu.with_memory_space_constraint(v, pltpu.HBM) for v in args[:fresh]], *args[fresh:])


def shape_of(*dims, dtype=F32):
    return jax.ShapeDtypeStruct(dims, dtype)


def shards(
    query_single, key_single, pair, query_frames, key_frames, w_query, w_key, w_value, w_query_points, w_key_points,
    w_value_points, head_weight, bias_weight, w_out, d_out,
):
    lay = Layout(head_weight.shape[0])
    count = lax.axis_size("row")
    block, width = key_single.shape
    total = count * block
    near = 1
    while 4 * near * near <= count:
        near *= 2
    assert count & (count - 1) == 0

    def exchange(value, mask):
        return lax.ppermute(value, "row", [(i, i ^ mask) for i in range(count)])

    (packed,) = call(
        functools.partial(key_kernel, lay),
        [shape_of(block, 2 * LANES, dtype=B16)],
        [
            key_single, key_frames, w_key.T, w_value.T, w_key_points.T, w_value_points.T,
        ],
        6,
        waits=True,
    )
    offsets = list(range(0, count, near))
    line = jnp.concatenate([packed] + [exchange(packed, mask) for mask in offsets[1:]], axis=0)
    planes = list(range(near))
    parts = [line] + [exchange(line, m) for m in planes[1:]]
    order = [m ^ o for m in planes for o in offsets]

    left, base, d_base, d_row, w_out_rows, w_query_rows, table, pair_rows, gains, parcel, turned = call(
        functools.partial(early_kernel, lay, block, order),
        [
            shape_of(ROWS16, LANES), shape_of(SUBLANES, total), shape_of(SUBLANES, total),
            shape_of(SUBLANES, 2 * LANES), shape_of((2 + lay.heads) * LANES, width, dtype=B16),
            shape_of(LANES, width, dtype=B16), shape_of(ROWS16, LANES),
            shape_of(total, LANES, dtype=B16), shape_of(SUBLANES, LANES),
            shape_of(2 * LANES + block // 2, width, dtype=B16), shape_of(block, LANES),
        ],
        [
            query_frames.T, query_single, w_query.T, w_query_points.T, bias_weight, w_out, d_out, pair,
            head_weight.reshape(1, -1), key_frames, w_key.T, w_value.T, w_key_points.T, w_value_points.T, packed,
        ],
        14,
        [pltpu.VMEM((ROWS16, LANES), F32)],
    )
    swap = [(i, (i + 1) % 2) for i in range(2)]
    other = lax.ppermute(parcel, "head", swap)
    message, features, weight_rows, scores = call(
        functools.partial(attention_kernel, lay, block, order),
        [
            shape_of(2 * count, SUBLANES, LANES, dtype=B16), shape_of(SUBLANES, 2 * LANES),
            shape_of(SUBLANES, total, dtype=B16), shape_of(SUBLANES, total, dtype=B16),
        ],
        parts + [left, base, d_base, d_row, gains, table],
    )
    arrived = lax.all_to_all(message, ("row", "head"), 0, 0, tiled=True)
    (sums,) = call(
        functools.partial(rows_kernel, lay),
        [shape_of(SUBLANES, 2 * width)],
        parts + [pair_rows, left, scores, features, weight_rows, w_out_rows, w_query_rows, gains, table],
    )
    output, grad_query = call(
        finish_kernel,
        [shape_of(1, width, dtype=B16), shape_of(1, width)],
        [sums, lax.ppermute(sums, "head", swap)],
        last=True,
    )
    (grad_keys,) = call(
        functools.partial(owner_kernel, lay),
        [shape_of(block, width)],
        [arrived, turned, parcel, other],
        last=True,
    )
    return (output, grad_query, grad_keys)


def solution(mesh):
    return jax.shard_map(
        shards,
        mesh=mesh,
        in_specs=(
            P("row", None),
            P("row", None),
            P("row", None, None),
            P(None, "row"),
            P(None, "row"),
            P(None, "head"),
            P(None, "head"),
            P(None, "head"),
            P(None, "head"),
            P(None, "head"),
            P(None, "head"),
            P("head"),
            P("head", None),
            P("head", None),
            P("row", None),
        ),
        out_specs=(P("row", None), P("row", None), P("row", None)),
        check_vma=False,
    )
```

```python
import functools
import math

import jax
import jax.numpy as jnp
from jax import lax
from jax.experimental import pallas as pl
from jax.experimental.pallas import tpu as pltpu
from jax.sharding import PartitionSpec as P

C = 16
PQ = 4
PV = 8
LANES = 128
SUBLANES = 8
ROWS16 = 16
LOGIT_SCALE = math.sqrt(1.0 / 3.0)
POINT_SCALE = math.sqrt(2.0 / (9.0 * PQ))
F32 = jnp.float32
B16 = jnp.bfloat16


class Layout:
    def __init__(self, heads):
        self.heads = heads
        self.base = heads * C
        self.kp = heads * PQ
        self.vp = heads * PV
        self.square = self.base + 3 * self.kp
        assert self.square + self.kp <= LANES and self.base + 3 * self.vp <= LANES
        assert 2 * heads + 2 <= SUBLANES and PQ == 4


def nn(a, b, precision=None):
    return lax.dot_general(a, b, (((1,), (0,)), ((), ())), precision=precision, preferred_element_type=F32)


def nt(a, b):
    return lax.dot_general(a, b, (((1,), (1,)), ((), ())), preferred_element_type=F32)


def iota(shape, dim):
    return lax.broadcasted_iota(jnp.int32, shape, dim)


def pick(condition):
    return jnp.where(condition, 1.0, 0.0).astype(B16)


def to_lane(rows, offset):
    j, i = iota((LANES, rows), 0), iota((LANES, rows), 1)
    return pick(j == i + offset)


def to_components(rows, offset, points, seg):
    j, i = iota((LANES, rows), 0), iota((LANES, rows), 1)
    found = j < 0
    for c in range(3):
        m = j - (c * seg + offset)
        found = found | ((m >= 0) & (m < points) & (i == 3 * m + c))
    return pick(found)


def unpack(tile, seg):
    return tile, pltpu.roll(tile, LANES - seg, 1), pltpu.roll(tile, LANES - 2 * seg, 1)


def pack(parts, seg, base):
    lane = iota(parts[0].shape, 1)
    keep = (lane >= base) & (lane < base + seg)
    x, y, z = (jnp.where(keep, v, 0.0) for v in parts)
    return x + pltpu.roll(y, seg, 1) + pltpu.roll(z, 2 * seg, 1)


def head_of(shape, lay):
    lane = iota(shape, 1)
    zero = jnp.full(shape, -1, jnp.int32)
    one = jnp.full(shape, -1, jnp.int32)
    for h in range(lay.heads):
        same = (lane >= h * C) & (lane < (h + 1) * C)
        zero, one = jnp.where(same, h, zero), jnp.where(same, h, one)
        for c in range(3):
            k = lay.base + c * lay.kp + h * PQ
            v = lay.base + c * lay.vp + h * PV
            zero = jnp.where((lane >= k) & (lane < k + PQ), h, zero)
            one = jnp.where((lane >= v) & (lane < v + PV), h, one)
    return zero, one


def turned_by(frames, vectors):
    x, y, z = vectors
    return [frames[3 * c] * x + frames[3 * c + 1] * y + frames[3 * c + 2] * z for c in range(3)]


def turned_back(frames, vectors):
    x, y, z = vectors
    return [frames[d] * x + frames[3 + d] * y + frames[6 + d] * z for d in range(3)]


def key_kernel(lay, ready, key_single, frames, w_key, w_value, w_kp, w_vp, packed):
    heads, kp, vp, base = lay.heads, lay.kp, lay.vp, lay.base
    tall = PQ * SUBLANES

    def rows_of(count, width):
        return iota((count, width), 0), iota((count, width), 1)

    r, i = rows_of(tall, 3 * kp)
    to_kp = [pick((i == 3 * PQ * (r & 7) + 3 * (r >> 3) + c) & ((r & 7) < heads)) for c in range(3)]
    r, i = rows_of(vp, 3 * vp)
    to_vp = [pick(i == 3 * r + c) for c in range(3)]
    width = 2 * LANES
    r, j = rows_of(base, width)
    place = [j == r, j == r + LANES]
    r, j = rows_of(tall, width)
    place += [(j == base + c * kp + PQ * (r & 7) + (r >> 3)) & ((r & 7) < heads) for c in range(3)]
    r, j = rows_of(vp, width)
    place += [j == LANES + base + c * vp + r for c in range(3)]
    r, j = rows_of(SUBLANES, width)
    place += [(j == lay.square + PQ * r + piece) & (r < heads) for piece in range(3)]
    place = jnp.concatenate([jnp.where(found, 1.0, 0.0) for found in place], axis=0).astype(B16)
    to_kp = jnp.concatenate(to_kp, axis=0)
    to_vp = jnp.concatenate(to_vp, axis=0)
    ready()
    single = key_single[...]
    turn = [frames[i : i + 1, :] for i in range(12)]
    features = [nt(w_key[...], single), nt(w_value[...], single)]
    for choose, weight, height in ((to_kp, w_kp, tall), (to_vp, w_vp, vp)):
        rows = nt(nn(choose, weight[...]).astype(B16), single)
        moved = turned_by(turn, [rows[c * height : (c + 1) * height] for c in range(3)])
        moved = [(v + turn[9 + c]).astype(B16).astype(F32) for c, v in enumerate(moved)]
        features += moved
        if height == tall:
            square = moved[0] * moved[0] + moved[1] * moved[1] + moved[2] * moved[2]
            square = sum(square[group(p)] for p in range(PQ))
    first = square.astype(B16).astype(F32)
    second = (square - first).astype(B16).astype(F32)
    features = jnp.concatenate(features + [first, second, square - first - second], axis=0)
    packed[...] = nn(jnp.transpose(features).astype(B16), place).astype(B16)


def group(h):
    return slice(h * SUBLANES, (h + 1) * SUBLANES)


def gain_rows(head_weight, lay):
    row = iota((SUBLANES, LANES), 0)
    raw = jnp.zeros((SUBLANES, LANES), F32)
    for h in range(lay.heads):
        raw = jnp.where(row == h, jnp.broadcast_to(head_weight[:, h : h + 1], raw.shape), raw)
    gain = (jnp.maximum(raw, 0.0) + jnp.log1p(jnp.exp(-jnp.abs(raw)))) * POINT_SCALE
    return jnp.where(row < lay.heads, gain, 0.0)


def gain_lanes(gain, lay):
    zero, _ = head_of(gain.shape, lay)
    return jnp.sum(jnp.where(zero == iota(gain.shape, 0), gain, 0.0), axis=0, keepdims=True)


def early_kernel(
    lay, block, order, frames, query_single, w_query, w_qp, bias_weight, w_out, d_out, pair, head_weight, key_frames,
    w_key, w_value, w_kp, w_vp, packed,
    left, base, d_base, d_row, w_out_rows, w_query_rows, table, pair_rows, gains, parcel, turned, scratch,
):
    kp, vp = lay.kp, lay.vp
    zero = nn(to_lane(lay.base, 0), w_key[...]) + nn(to_components(3 * kp, lay.base, kp, kp), w_kp[...])
    one = nn(to_lane(lay.base, 0), w_value[...]) + nn(to_components(3 * vp, lay.base, vp, vp), w_vp[...])
    parcel[:LANES, :] = zero.astype(B16)
    parcel[LANES : 2 * LANES, :] = one.astype(B16)
    half = block // 2
    parcel[2 * LANES :, :LANES] = packed[:half, :LANES]
    parcel[2 * LANES :, LANES : 2 * LANES] = packed[half:, :LANES]
    parcel[2 * LANES :, 2 * LANES :] = jnp.zeros((half, parcel.shape[1] - 2 * LANES), B16)
    gain = gain_rows(head_weight, lay)
    gains[...] = gain
    pieces = jnp.broadcast_to(gain_lanes(gain, lay), (ROWS16, LANES))
    first = pieces.astype(B16).astype(F32)
    second = (pieces - first).astype(B16).astype(F32)
    row = iota(pieces.shape, 0)
    pieces = jnp.where(
        row == 0, first, jnp.where(row == 1, second, jnp.where(row == 2, pieces - first - second, 0.0))
    )
    parcel[2 * LANES : 2 * LANES + ROWS16, 2 * LANES : 3 * LANES] = pieces.astype(B16)
    turn = jnp.transpose(key_frames[...])
    turned[:, : turn.shape[1]] = turn
    me = lax.axis_index("row")
    for place, offset in enumerate(order):
        j = pl.multiple_of((me ^ offset) * block, block)
        pair_rows[place * block : (place + 1) * block, :] = pair[0, pl.ds(j, block), :]
    turn = [jnp.broadcast_to(frames[:, i : i + 1], (1, LANES)) for i in range(12)]
    for i in range(12):
        table[i : i + 1, :] = turn[i]
    heads, start = lay.heads, lay.base
    width = C + 4 * PV + LANES
    near = C + 4 * PV
    shape = (SUBLANES, LANES)
    row, lane = iota(shape, 0), iota(shape, 1)
    zero_head, _ = head_of(shape, lay)
    w_q = nn(to_lane(start, 0), w_query[...]) + nn(to_components(3 * lay.kp, start, lay.kp, lay.kp), w_qp[...])
    w_q = w_q.astype(B16)
    w_query_rows[...] = w_q
    w_o = jnp.zeros((2 * LANES, w_out.shape[1]), F32)
    for h in range(heads):
        i, j = iota((2 * LANES, near), 0), iota((2 * LANES, near), 1)
        m = i - (LANES + h * C)
        found = (m >= 0) & (m < C) & (j == m)
        m = i - (start + h * PV)
        found = found | ((m >= 0) & (m < PV) & (j == C + 3 * PV + m))
        for c in range(3):
            m = i - (LANES + start + c * lay.vp + h * PV)
            found = found | ((m >= 0) & (m < PV) & (j == C + 3 * m + c))
        w_o = w_o + nn(pick(found), w_out[h * width : h * width + near, :])
    w_o = w_o.astype(B16)
    w_out_rows[: 2 * LANES, :] = w_o
    for h in range(heads):
        w_out_rows[(2 + h) * LANES : (3 + h) * LANES, :] = w_out[h * width + near : (h + 1) * width, :]
    single = jnp.broadcast_to(query_single[...], (SUBLANES, query_single.shape[1]))
    rows = nt(single, w_q)
    moved = turned_by(turn, unpack(rows, lay.kp))
    points = pack([(v + turn[9 + c]).astype(B16).astype(F32) for c, v in enumerate(moved)], lay.kp, start)
    query = jnp.where(lane < start, rows, 0.0).astype(B16).astype(F32)
    left[:SUBLANES, :] = jnp.where(zero_head == row, query, 0.0)
    minus = lane < 0
    for h in range(heads):
        at = lay.square + h * PQ
        minus = minus | ((row == h) & (lane >= at) & (lane < at + 3))
    mine = jnp.where(zero_head == row, points, 0.0)
    left[SUBLANES:, :] = jnp.where(minus, -0.5, mine)
    cotangent = jnp.broadcast_to(d_out[...], (SUBLANES, d_out.shape[1]))
    d_row[...] = nt(cotangent, w_o)
    scratch[...] = jnp.zeros_like(scratch)
    scratch[:heads, :] = bias_weight[...].astype(F32)
    for h in range(heads):
        d_pair = nt(cotangent, w_out[h * width + near : (h + 1) * width, :])
        scratch[SUBLANES + h : SUBLANES + h + 1, :] = d_pair[:1, :]
    both = nt(scratch[...].astype(B16), pair_rows[...])
    square = jnp.sum(mine * mine, axis=1, keepdims=True)
    base[...] = both[:SUBLANES] - 0.5 * gain[:, :1] * square
    d_base[...] = both[SUBLANES:]


def attention_kernel(lay, block, order, *refs):
    *parts, left, base, d_base, d_row, gains, table, message, features, weights, scores = refs
    frames = [table[i : i + 1, :] for i in range(12)]
    me = lax.axis_index("row")
    heads, vp, start = lay.heads, lay.vp, lay.base
    shape = (SUBLANES, LANES)
    row, lane = iota(shape, 0), iota(shape, 1)
    _, one_head = head_of(shape, lay)
    gain = gains[...]
    queries = left[...].astype(B16)
    first = jnp.concatenate([nt(queries, part[:, :LANES]) for part in parts], axis=1)
    logits = LOGIT_SCALE * (first[:SUBLANES] * (1.0 / math.sqrt(C)) + base[...] + gain[:, :1] * first[SUBLANES:])
    weight = jnp.exp(logits - jnp.max(logits, axis=1, keepdims=True))
    attention = weight / jnp.sum(weight, axis=1, keepdims=True)
    attention = jnp.where(iota(attention.shape, 0) < heads, attention, 0.0)
    attention_b = attention.astype(B16)
    sums = spread(attention_b, [part.at[:, LANES:] for part in parts])
    sums = jnp.sum(jnp.where(one_head == row, sums, 0.0), axis=0, keepdims=True)
    sums = jnp.broadcast_to(sums, shape)
    local = turned_back(frames, [v - frames[9 + c] for c, v in enumerate(unpack(sums, vp))])
    lengths = jnp.sqrt(1.0 + (local[0] * local[0] + local[1] * local[1] + local[2] * local[2]))
    d_one = d_row[:, LANES:]
    share = d_row[:, :LANES] / lengths
    d_points = turned_by(frames, [v + share * u for v, u in zip(unpack(d_one, vp), local)])
    d_side = jnp.where(lane < start, d_one, 0.0) + pack(d_points, vp, start)
    right = jnp.where(one_head == row, d_side, 0.0).astype(B16)
    d_attention = jnp.concatenate([nt(right, part[:, LANES:]) for part in parts], axis=1) + d_base[...]
    total = jnp.sum(attention * d_attention, axis=1, keepdims=True)
    score_b = (LOGIT_SCALE * attention * (d_attention - total)).astype(B16)
    query = jnp.sum(jnp.where(lane < lay.square, left[:SUBLANES, :] + left[SUBLANES:, :], 0.0), axis=0, keepdims=True)
    side = jnp.where(row == 2 * heads, jnp.broadcast_to(query, shape), 0.0)
    side = side + jnp.where(row == 2 * heads + 1, d_side, 0.0)
    both = attention_b.astype(F32) + pltpu.roll(score_b.astype(F32), heads, 0)
    for at in range(0, both.shape[1], LANES):
        for place in range(at // block, (at + LANES) // block):
            tile = both[:, at : at + LANES]
            if place * block != at:
                tile = pltpu.roll(tile, LANES - (place * block - at), 1)
            tile = jnp.where(row < 2 * heads, tile, side).astype(B16)
            for core in range(2):
                message[(me ^ order[place]) * 2 + core, :, :] = tile
    weights[...] = attention_b
    scores[...] = score_b
    features[:, :LANES] = jnp.where((lane >= start) & (lane < start + vp), lengths, 0.0)
    features[:, LANES:] = jnp.where(lane < start, sums, 0.0) + pack(local, vp, start)


def spread(weights, parts):
    total, at = 0.0, 0
    for part in parts:
        total = total + nn(weights[:, at : at + part.shape[0]], part[...])
        at += part.shape[0]
    return total


def rows_kernel(lay, *refs):
    *parts, pair, left, scores, features, weights, w_out_rows, w_query_rows, gains, table, sums = refs
    frames = [table[i : i + 1, :] for i in range(12)]
    shape = (SUBLANES, LANES)
    row, lane = iota(shape, 0), iota(shape, 1)
    zero_head, _ = head_of(shape, lay)
    pair_sum = nn(weights[...], pair[...])
    pairs = [jnp.broadcast_to(pair_sum[h : h + 1, :], shape) for h in range(lay.heads)]
    result = nn(jnp.concatenate([features[...]] + pairs, axis=1).astype(B16), w_out_rows[...])
    score = scores[...].astype(F32)
    d_rows = spread(scores[...], [part.at[:, :LANES] for part in parts])
    score_sum = jnp.sum(score, axis=1, keepdims=True)
    points = left[SUBLANES:, :]
    d_rows = jnp.where(lane < lay.base, d_rows * (1.0 / math.sqrt(C)), gains[...] * (d_rows - score_sum * points))
    d_rows = jnp.broadcast_to(
        jnp.sum(jnp.where(zero_head == row, d_rows, 0.0), axis=0, keepdims=True), shape
    )
    local = pack(turned_back(frames, unpack(d_rows, lay.kp)), lay.kp, lay.base)
    both = (jnp.where(lane < lay.base, d_rows, 0.0) + local).astype(B16)
    sums[...] = jnp.concatenate([result, nn(both, w_query_rows[...])], axis=1)


def owner_kernel(lay, arrived, turned, parcel, other, result):
    heads, base = lay.heads, lay.base
    count = arrived.shape[0] // 2
    block = turned.shape[0]
    shape = (SUBLANES, LANES)
    whole = (count, SUBLANES, LANES)
    row = iota(shape, 0)
    zero_head, one_head = head_of(shape, lay)
    lane = iota(shape, 1)
    keep0 = (zero_head >= 0) & (zero_head + heads == row)
    keep1 = one_head == row
    ones = jnp.broadcast_to(jnp.where(keep0 & (lane >= base), 1.0, 0.0)[None], whole)
    columns = [turned[:, i : i + 1] for i in range(9)]
    lane = iota((block, LANES), 1)
    me = lax.axis_index("head")
    total = None
    for core, held in ((me, parcel), (1 - me, other)):
        took = jnp.concatenate([arrived[pl.ds(q * 2 + core, 1)] for q in range(count)], axis=0).astype(F32)
        side0 = jnp.where(keep0[None], jnp.broadcast_to(took[:, 2 * heads : 2 * heads + 1, :], whole), 0.0)
        side1 = jnp.where(keep1[None], jnp.broadcast_to(took[:, 2 * heads + 1 : 2 * heads + 2, :], whole), 0.0)
        right = jnp.concatenate([side0, side1, ones], axis=2).reshape(count * SUBLANES, 3 * LANES).astype(B16)
        moved = jnp.transpose(took.reshape(count * SUBLANES, LANES)).astype(B16)
        both = nn(moved, right)[:block]
        pieces = held[2 * LANES : 2 * LANES + ROWS16, 2 * LANES : 3 * LANES].astype(F32)
        gain = pieces[0:1] + pieces[1:2] + pieces[2:3]
        own = [held[2 * LANES :, at : at + LANES].astype(F32) for at in (0, LANES)]
        own = jnp.concatenate(own, axis=0)
        tile0, tile1 = both[:, :LANES], both[:, LANES : 2 * LANES]
        points = gain * (tile0 - both[:, 2 * LANES :] * own)
        points = pack(turned_back(columns, unpack(points, lay.kp)), lay.kp, base)
        tile0 = jnp.where(lane < base, tile0 * (1.0 / math.sqrt(C)), points)
        points = pack(turned_back(columns, unpack(tile1, lay.vp)), lay.vp, base)
        tile1 = jnp.where(lane < base, tile1, points)
        rows = jnp.concatenate([tile0, tile1], axis=1).astype(B16)
        part = nn(rows, held[: 2 * LANES, :])
        total = part if total is None else total + part
    result[...] = total


def finish_kernel(own, other, output, grad_query):
    width = output.shape[1]
    total = own[...] + other[...]
    output[...] = total[:1, :width].astype(output.dtype)
    grad_query[...] = total[:1, width:]


VMEM = pl.BlockSpec(memory_space=pltpu.VMEM)
HBM = pl.BlockSpec(memory_space=pltpu.HBM)


def call(body, outs, args, fresh=0, scratch=(), flops=1000000, last=False, waits=False):
    size = sum(math.prod(v.shape) * v.dtype.itemsize for v in list(args) + list(outs))

    def kernel(*refs):
        if fresh:
            *refs, sems = refs
            held = refs[len(refs) - fresh :]
            copies = [pltpu.make_async_copy(refs[i], held[i], sems.at[i]) for i in range(fresh)]
            for copy in copies:
                copy.start()

            def ready():
                for copy in copies:
                    copy.wait()

            if not waits:
                ready()
            refs = list(held) + list(refs[fresh : len(refs) - fresh])
        body(*([ready] if waits else []), *refs)

    own = [pltpu.VMEM(v.shape, v.dtype) for v in args[:fresh]]
    return pl.pallas_call(
        kernel,
        out_shape=tuple(outs),
        in_specs=[HBM] * fresh + [VMEM] * (len(args) - fresh),
        out_specs=tuple([pl.BlockSpec() if last else VMEM] * len(outs)),
        scratch_shapes=list(scratch) + own + ([pltpu.SemaphoreType.DMA((fresh,))] if fresh else []),
        compiler_params=pltpu.CompilerParams(vmem_limit_bytes=(16 << 20) + 6 * size),
        cost_estimate=pl.CostEstimate(flops=flops, bytes_accessed=size, transcendentals=0),
    )(*[pltpu.with_memory_space_constraint(v, pltpu.HBM) for v in args[:fresh]], *args[fresh:])


def shape_of(*dims, dtype=F32):
    return jax.ShapeDtypeStruct(dims, dtype)


def shards(
    query_single, key_single, pair, query_frames, key_frames, w_query, w_key, w_value, w_query_points, w_key_points,
    w_value_points, head_weight, bias_weight, w_out, d_out,
):
    lay = Layout(head_weight.shape[0])
    count = lax.axis_size("row")
    block, width = key_single.shape
    total = count * block
    near = 1
    while 4 * near * near <= count:
        near *= 2
    assert count & (count - 1) == 0

    def exchange(value, mask):
        return lax.ppermute(value, "row", [(i, i ^ mask) for i in range(count)])

    (packed,) = call(
        functools.partial(key_kernel, lay),
        [shape_of(block, 2 * LANES, dtype=B16)],
        [
            key_single, key_frames, w_key.T, w_value.T, w_key_points.T, w_value_points.T,
        ],
        6,
        waits=True,
    )
    assert near == 4 or count >= 16
    near, far = 4, count // 4
    offsets = []
    for high in range(0, count, 8):
        twist = high ^ (5 if high & 8 else 0)
        offsets += [twist, twist ^ 7]
    offsets = offsets[:1] + offsets[:0:-1]
    line = jnp.concatenate([packed] + [exchange(packed, mask) for mask in offsets[1:]], axis=0)
    planes = [0, 2, 4, 1]
    parts = [line] + [exchange(line, m) for m in planes[1:]]
    order = [m ^ o for m in planes for o in offsets]

    left, base, d_base, d_row, w_out_rows, w_query_rows, table, pair_rows, gains, parcel, turned = call(
        functools.partial(early_kernel, lay, block, order),
        [
            shape_of(ROWS16, LANES), shape_of(SUBLANES, total), shape_of(SUBLANES, total),
            shape_of(SUBLANES, 2 * LANES), shape_of((2 + lay.heads) * LANES, width, dtype=B16),
            shape_of(LANES, width, dtype=B16), shape_of(ROWS16, LANES),
            shape_of(total, LANES, dtype=B16), shape_of(SUBLANES, LANES),
            shape_of(2 * LANES + block // 2, width, dtype=B16), shape_of(block, LANES),
        ],
        [
            query_frames.T, query_single, w_query.T, w_query_points.T, bias_weight, w_out, d_out, pair,
            head_weight.reshape(1, -1), key_frames, w_key.T, w_value.T, w_key_points.T, w_value_points.T, packed,
        ],
        14,
        [pltpu.VMEM((ROWS16, LANES), F32)],
    )
    swap = [(i, (i + 1) % 2) for i in range(2)]
    other = lax.ppermute(parcel, "head", swap)
    message, features, weight_rows, scores = call(
        functools.partial(attention_kernel, lay, block, order),
        [
            shape_of(2 * count, SUBLANES, LANES, dtype=B16), shape_of(SUBLANES, 2 * LANES),
            shape_of(SUBLANES, total, dtype=B16), shape_of(SUBLANES, total, dtype=B16),
        ],
        parts + [left, base, d_base, d_row, gains, table],
    )
    arrived = lax.all_to_all(message, ("row", "head"), 0, 0, tiled=True)
    (sums,) = call(
        functools.partial(rows_kernel, lay),
        [shape_of(SUBLANES, 2 * width)],
        parts + [pair_rows, left, scores, features, weight_rows, w_out_rows, w_query_rows, gains, table],
    )
    output, grad_query = call(
        finish_kernel,
        [shape_of(1, width, dtype=B16), shape_of(1, width)],
        [sums, lax.ppermute(sums, "head", swap)],
        last=True,
    )
    (grad_keys,) = call(
        functools.partial(owner_kernel, lay),
        [shape_of(block, width)],
        [arrived, turned, parcel, other],
        last=True,
    )
    return (output, grad_query, grad_keys)


def solution(mesh):
    return jax.shard_map(
        shards,
        mesh=mesh,
        in_specs=(
            P("row", None),
            P("row", None),
            P("row", None, None),
            P(None, "row"),
            P(None, "row"),
            P(None, "head"),
            P(None, "head"),
            P(None, "head"),
            P(None, "head"),
            P(None, "head"),
            P(None, "head"),
            P("head"),
            P("head", None),
            P("head", None),
            P("row", None),
        ),
        out_specs=(P("row", None), P("row", None), P("row", None)),
        check_vma=False,
    )
```

```python
import functools
import math

import jax
import jax.numpy as jnp
from jax import lax
from jax.experimental import pallas as pl
from jax.experimental.pallas import tpu as pltpu
from jax.sharding import PartitionSpec as P

C = 16
PQ = 4
PV = 8
LANES = 128
SUBLANES = 8
ROWS16 = 16
LOGIT_SCALE = math.sqrt(1.0 / 3.0)
POINT_SCALE = math.sqrt(2.0 / (9.0 * PQ))
F32 = jnp.float32
B16 = jnp.bfloat16


class Layout:
    def __init__(self, heads):
        self.heads = heads
        self.base = heads * C
        self.kp = heads * PQ
        self.vp = heads * PV
        self.square = self.base + 3 * self.kp
        assert self.square + self.kp <= LANES and self.base + 3 * self.vp <= LANES
        assert 2 * heads + 2 <= SUBLANES and PQ == 4


def nn(a, b, precision=None):
    return lax.dot_general(a, b, (((1,), (0,)), ((), ())), precision=precision, preferred_element_type=F32)


def nt(a, b):
    return lax.dot_general(a, b, (((1,), (1,)), ((), ())), preferred_element_type=F32)


def iota(shape, dim):
    return lax.broadcasted_iota(jnp.int32, shape, dim)


def pick(condition):
    return jnp.where(condition, 1.0, 0.0).astype(B16)


def to_lane(rows, offset):
    j, i = iota((LANES, rows), 0), iota((LANES, rows), 1)
    return pick(j == i + offset)


def to_components(rows, offset, points, seg):
    j, i = iota((LANES, rows), 0), iota((LANES, rows), 1)
    found = j < 0
    for c in range(3):
        m = j - (c * seg + offset)
        found = found | ((m >= 0) & (m < points) & (i == 3 * m + c))
    return pick(found)


def unpack(tile, seg):
    return tile, pltpu.roll(tile, LANES - seg, 1), pltpu.roll(tile, LANES - 2 * seg, 1)


def pack(parts, seg, base):
    lane = iota(parts[0].shape, 1)
    keep = (lane >= base) & (lane < base + seg)
    x, y, z = (jnp.where(keep, v, 0.0) for v in parts)
    return x + pltpu.roll(y, seg, 1) + pltpu.roll(z, 2 * seg, 1)


def head_of(shape, lay):
    lane = iota(shape, 1)
    zero = jnp.full(shape, -1, jnp.int32)
    one = jnp.full(shape, -1, jnp.int32)
    for h in range(lay.heads):
        same = (lane >= h * C) & (lane < (h + 1) * C)
        zero, one = jnp.where(same, h, zero), jnp.where(same, h, one)
        for c in range(3):
            k = lay.base + c * lay.kp + h * PQ
            v = lay.base + c * lay.vp + h * PV
            zero = jnp.where((lane >= k) & (lane < k + PQ), h, zero)
            one = jnp.where((lane >= v) & (lane < v + PV), h, one)
    return zero, one


def turned_by(frames, vectors):
    x, y, z = vectors
    return [frames[3 * c] * x + frames[3 * c + 1] * y + frames[3 * c + 2] * z for c in range(3)]


def turned_back(frames, vectors):
    x, y, z = vectors
    return [frames[d] * x + frames[3 + d] * y + frames[6 + d] * z for d in range(3)]


def key_kernel(lay, ready, key_single, frames, w_key, w_value, w_kp, w_vp, packed):
    heads, kp, vp, base = lay.heads, lay.kp, lay.vp, lay.base
    tall = PQ * SUBLANES

    def rows_of(count, width):
        return iota((count, width), 0), iota((count, width), 1)

    r, i = rows_of(tall, 3 * kp)
    to_kp = [pick((i == 3 * PQ * (r & 7) + 3 * (r >> 3) + c) & ((r & 7) < heads)) for c in range(3)]
    r, i = rows_of(vp, 3 * vp)
    to_vp = [pick(i == 3 * r + c) for c in range(3)]
    width = 2 * LANES
    r, j = rows_of(base, width)
    place = [j == r, j == r + LANES]
    r, j = rows_of(tall, width)
    place += [(j == base + c * kp + PQ * (r & 7) + (r >> 3)) & ((r & 7) < heads) for c in range(3)]
    r, j = rows_of(vp, width)
    place += [j == LANES + base + c * vp + r for c in range(3)]
    r, j = rows_of(SUBLANES, width)
    place += [(j == lay.square + PQ * r + piece) & (r < heads) for piece in range(3)]
    place = jnp.concatenate([jnp.where(found, 1.0, 0.0) for found in place], axis=0).astype(B16)
    to_kp = jnp.concatenate(to_kp, axis=0)
    to_vp = jnp.concatenate(to_vp, axis=0)
    ready()
    single = key_single[...]
    turn = [frames[i : i + 1, :] for i in range(12)]
    features = [nt(w_key[...], single), nt(w_value[...], single)]
    for choose, weight, height in ((to_kp, w_kp, tall), (to_vp, w_vp, vp)):
        rows = nt(nn(choose, weight[...]).astype(B16), single)
        moved = turned_by(turn, [rows[c * height : (c + 1) * height] for c in range(3)])
        moved = [(v + turn[9 + c]).astype(B16).astype(F32) for c, v in enumerate(moved)]
        features += moved
        if height == tall:
            square = moved[0] * moved[0] + moved[1] * moved[1] + moved[2] * moved[2]
            square = sum(square[group(p)] for p in range(PQ))
    first = square.astype(B16).astype(F32)
    second = (square - first).astype(B16).astype(F32)
    features = jnp.concatenate(features + [first, second, square - first - second], axis=0)
    packed[...] = nn(jnp.transpose(features).astype(B16), place).astype(B16)


def group(h):
    return slice(h * SUBLANES, (h + 1) * SUBLANES)


def gain_rows(head_weight, lay):
    row = iota((SUBLANES, LANES), 0)
    raw = jnp.zeros((SUBLANES, LANES), F32)
    for h in range(lay.heads):
        raw = jnp.where(row == h, jnp.broadcast_to(head_weight[:, h : h + 1], raw.shape), raw)
    gain = (jnp.maximum(raw, 0.0) + jnp.log1p(jnp.exp(-jnp.abs(raw)))) * POINT_SCALE
    return jnp.where(row < lay.heads, gain, 0.0)


def gain_lanes(gain, lay):
    zero, _ = head_of(gain.shape, lay)
    return jnp.sum(jnp.where(zero == iota(gain.shape, 0), gain, 0.0), axis=0, keepdims=True)


def early_kernel(
    lay, block, order, frames, query_single, w_query, w_qp, bias_weight, w_out, d_out, pair, head_weight, key_frames,
    w_key, w_value, w_kp, w_vp, packed,
    left, base, d_base, d_row, w_out_rows, w_query_rows, table, pair_rows, gains, parcel, turned, scratch,
):
    kp, vp = lay.kp, lay.vp
    zero = nn(to_lane(lay.base, 0), w_key[...]) + nn(to_components(3 * kp, lay.base, kp, kp), w_kp[...])
    one = nn(to_lane(lay.base, 0), w_value[...]) + nn(to_components(3 * vp, lay.base, vp, vp), w_vp[...])
    parcel[:LANES, :] = zero.astype(B16)
    parcel[LANES : 2 * LANES, :] = one.astype(B16)
    half = block // 2
    parcel[2 * LANES :, :LANES] = packed[:half, :LANES]
    parcel[2 * LANES :, LANES : 2 * LANES] = packed[half:, :LANES]
    parcel[2 * LANES :, 2 * LANES :] = jnp.zeros((half, parcel.shape[1] - 2 * LANES), B16)
    gain = gain_rows(head_weight, lay)
    gains[...] = gain
    pieces = jnp.broadcast_to(gain_lanes(gain, lay), (ROWS16, LANES))
    first = pieces.astype(B16).astype(F32)
    second = (pieces - first).astype(B16).astype(F32)
    row = iota(pieces.shape, 0)
    pieces = jnp.where(
        row == 0, first, jnp.where(row == 1, second, jnp.where(row == 2, pieces - first - second, 0.0))
    )
    parcel[2 * LANES : 2 * LANES + ROWS16, 2 * LANES : 3 * LANES] = pieces.astype(B16)
    turn = jnp.transpose(key_frames[...])
    turned[:, : turn.shape[1]] = turn
    me = lax.axis_index("row")
    for place, offset in enumerate(order):
        j = pl.multiple_of((me ^ offset) * block, block)
        pair_rows[place * block : (place + 1) * block, :] = pair[0, pl.ds(j, block), :]
    turn = [jnp.broadcast_to(frames[:, i : i + 1], (1, LANES)) for i in range(12)]
    for i in range(12):
        table[i : i + 1, :] = turn[i]
    heads, start = lay.heads, lay.base
    width = C + 4 * PV + LANES
    near = C + 4 * PV
    shape = (SUBLANES, LANES)
    row, lane = iota(shape, 0), iota(shape, 1)
    zero_head, _ = head_of(shape, lay)
    w_q = nn(to_lane(start, 0), w_query[...]) + nn(to_components(3 * lay.kp, start, lay.kp, lay.kp), w_qp[...])
    w_q = w_q.astype(B16)
    w_query_rows[...] = w_q
    w_o = jnp.zeros((2 * LANES, w_out.shape[1]), F32)
    for h in range(heads):
        i, j = iota((2 * LANES, near), 0), iota((2 * LANES, near), 1)
        m = i - (LANES + h * C)
        found = (m >= 0) & (m < C) & (j == m)
        m = i - (start + h * PV)
        found = found | ((m >= 0) & (m < PV) & (j == C + 3 * PV + m))
        for c in range(3):
            m = i - (LANES + start + c * lay.vp + h * PV)
            found = found | ((m >= 0) & (m < PV) & (j == C + 3 * m + c))
        w_o = w_o + nn(pick(found), w_out[h * width : h * width + near, :])
    w_o = w_o.astype(B16)
    w_out_rows[: 2 * LANES, :] = w_o
    for h in range(heads):
        w_out_rows[(2 + h) * LANES : (3 + h) * LANES, :] = w_out[h * width + near : (h + 1) * width, :]
    single = jnp.broadcast_to(query_single[...], (SUBLANES, query_single.shape[1]))
    rows = nt(single, w_q)
    moved = turned_by(turn, unpack(rows, lay.kp))
    points = pack([(v + turn[9 + c]).astype(B16).astype(F32) for c, v in enumerate(moved)], lay.kp, start)
    query = jnp.where(lane < start, rows, 0.0).astype(B16).astype(F32)
    left[:SUBLANES, :] = jnp.where(zero_head == row, query, 0.0)
    minus = lane < 0
    for h in range(heads):
        at = lay.square + h * PQ
        minus = minus | ((row == h) & (lane >= at) & (lane < at + 3))
    mine = jnp.where(zero_head == row, points, 0.0)
    left[SUBLANES:, :] = jnp.where(minus, -0.5, mine)
    cotangent = jnp.broadcast_to(d_out[...], (SUBLANES, d_out.shape[1]))
    d_row[...] = nt(cotangent, w_o)
    scratch[...] = jnp.zeros_like(scratch)
    scratch[:heads, :] = bias_weight[...].astype(F32)
    for h in range(heads):
        d_pair = nt(cotangent, w_out[h * width + near : (h + 1) * width, :])
        scratch[SUBLANES + h : SUBLANES + h + 1, :] = d_pair[:1, :]
    both = nt(scratch[...].astype(B16), pair_rows[...])
    square = jnp.sum(mine * mine, axis=1, keepdims=True)
    base[...] = both[:SUBLANES] - 0.5 * gain[:, :1] * square
    d_base[...] = both[SUBLANES:]


def attention_kernel(lay, block, order, *refs):
    *parts, left, base, d_base, d_row, gains, table, message, features, weights, scores = refs
    frames = [table[i : i + 1, :] for i in range(12)]
    me = lax.axis_index("row")
    heads, vp, start = lay.heads, lay.vp, lay.base
    shape = (SUBLANES, LANES)
    row, lane = iota(shape, 0), iota(shape, 1)
    _, one_head = head_of(shape, lay)
    gain = gains[...]
    queries = left[...].astype(B16)
    first = jnp.concatenate([nt(queries, part[:, :LANES]) for part in parts], axis=1)
    logits = LOGIT_SCALE * (first[:SUBLANES] * (1.0 / math.sqrt(C)) + base[...] + gain[:, :1] * first[SUBLANES:])
    weight = jnp.exp(logits - jnp.max(logits, axis=1, keepdims=True))
    attention = weight / jnp.sum(weight, axis=1, keepdims=True)
    attention = jnp.where(iota(attention.shape, 0) < heads, attention, 0.0)
    attention_b = attention.astype(B16)
    sums = spread(attention_b, [part.at[:, LANES:] for part in parts])
    sums = jnp.sum(jnp.where(one_head == row, sums, 0.0), axis=0, keepdims=True)
    sums = jnp.broadcast_to(sums, shape)
    local = turned_back(frames, [v - frames[9 + c] for c, v in enumerate(unpack(sums, vp))])
    lengths = jnp.sqrt(1.0 + (local[0] * local[0] + local[1] * local[1] + local[2] * local[2]))
    d_one = d_row[:, LANES:]
    share = d_row[:, :LANES] / lengths
    d_points = turned_by(frames, [v + share * u for v, u in zip(unpack(d_one, vp), local)])
    d_side = jnp.where(lane < start, d_one, 0.0) + pack(d_points, vp, start)
    right = jnp.where(one_head == row, d_side, 0.0).astype(B16)
    d_attention = jnp.concatenate([nt(right, part[:, LANES:]) for part in parts], axis=1) + d_base[...]
    total = jnp.sum(attention * d_attention, axis=1, keepdims=True)
    score_b = (LOGIT_SCALE * attention * (d_attention - total)).astype(B16)
    query = jnp.sum(jnp.where(lane < lay.square, left[:SUBLANES, :] + left[SUBLANES:, :], 0.0), axis=0, keepdims=True)
    side = jnp.where(row == 2 * heads, jnp.broadcast_to(query, shape), 0.0)
    side = side + jnp.where(row == 2 * heads + 1, d_side, 0.0)
    both = attention_b.astype(F32) + pltpu.roll(score_b.astype(F32), heads, 0)
    for at in range(0, both.shape[1], LANES):
        for place in range(at // block, (at + LANES) // block):
            tile = both[:, at : at + LANES]
            if place * block != at:
                tile = pltpu.roll(tile, LANES - (place * block - at), 1)
            tile = jnp.where(row < 2 * heads, tile, side).astype(B16)
            for core in range(2):
                message[(me ^ order[place]) * 2 + core, :, :] = tile
    weights[...] = attention_b
    scores[...] = score_b
    features[:, :LANES] = jnp.where((lane >= start) & (lane < start + vp), lengths, 0.0)
    features[:, LANES:] = jnp.where(lane < start, sums, 0.0) + pack(local, vp, start)


def spread(weights, parts):
    total, at = 0.0, 0
    for part in parts:
        total = total + nn(weights[:, at : at + part.shape[0]], part[...])
        at += part.shape[0]
    return total


def rows_kernel(lay, *refs):
    *parts, pair, left, scores, features, weights, w_out_rows, w_query_rows, gains, table, sums = refs
    frames = [table[i : i + 1, :] for i in range(12)]
    shape = (SUBLANES, LANES)
    row, lane = iota(shape, 0), iota(shape, 1)
    zero_head, _ = head_of(shape, lay)
    pair_sum = nn(weights[...], pair[...])
    pairs = [jnp.broadcast_to(pair_sum[h : h + 1, :], shape) for h in range(lay.heads)]
    result = nn(jnp.concatenate([features[...]] + pairs, axis=1).astype(B16), w_out_rows[...])
    score = scores[...].astype(F32)
    d_rows = spread(scores[...], [part.at[:, :LANES] for part in parts])
    score_sum = jnp.sum(score, axis=1, keepdims=True)
    points = left[SUBLANES:, :]
    d_rows = jnp.where(lane < lay.base, d_rows * (1.0 / math.sqrt(C)), gains[...] * (d_rows - score_sum * points))
    d_rows = jnp.broadcast_to(
        jnp.sum(jnp.where(zero_head == row, d_rows, 0.0), axis=0, keepdims=True), shape
    )
    local = pack(turned_back(frames, unpack(d_rows, lay.kp)), lay.kp, lay.base)
    both = (jnp.where(lane < lay.base, d_rows, 0.0) + local).astype(B16)
    sums[...] = jnp.concatenate([result, nn(both, w_query_rows[...])], axis=1)


def owner_kernel(lay, arrived, turned, parcel, other, result):
    heads, base = lay.heads, lay.base
    count = arrived.shape[0] // 2
    block = turned.shape[0]
    shape = (SUBLANES, LANES)
    whole = (count, SUBLANES, LANES)
    row = iota(shape, 0)
    zero_head, one_head = head_of(shape, lay)
    lane = iota(shape, 1)
    keep0 = (zero_head >= 0) & (zero_head + heads == row)
    keep1 = one_head == row
    ones = jnp.broadcast_to(jnp.where(keep0 & (lane >= base), 1.0, 0.0)[None], whole)
    columns = [turned[:, i : i + 1] for i in range(9)]
    lane = iota((block, LANES), 1)
    me = lax.axis_index("head")
    total = None
    for core, held in ((me, parcel), (1 - me, other)):
        took = jnp.concatenate([arrived[pl.ds(q * 2 + core, 1)] for q in range(count)], axis=0).astype(F32)
        side0 = jnp.where(keep0[None], jnp.broadcast_to(took[:, 2 * heads : 2 * heads + 1, :], whole), 0.0)
        side1 = jnp.where(keep1[None], jnp.broadcast_to(took[:, 2 * heads + 1 : 2 * heads + 2, :], whole), 0.0)
        right = jnp.concatenate([side0, side1, ones], axis=2).reshape(count * SUBLANES, 3 * LANES).astype(B16)
        moved = jnp.transpose(took.reshape(count * SUBLANES, LANES)).astype(B16)
        both = nn(moved, right)[:block]
        pieces = held[2 * LANES : 2 * LANES + ROWS16, 2 * LANES : 3 * LANES].astype(F32)
        gain = pieces[0:1] + pieces[1:2] + pieces[2:3]
        own = [held[2 * LANES :, at : at + LANES].astype(F32) for at in (0, LANES)]
        own = jnp.concatenate(own, axis=0)
        tile0, tile1 = both[:, :LANES], both[:, LANES : 2 * LANES]
        points = gain * (tile0 - both[:, 2 * LANES :] * own)
        points = pack(turned_back(columns, unpack(points, lay.kp)), lay.kp, base)
        tile0 = jnp.where(lane < base, tile0 * (1.0 / math.sqrt(C)), points)
        points = pack(turned_back(columns, unpack(tile1, lay.vp)), lay.vp, base)
        tile1 = jnp.where(lane < base, tile1, points)
        rows = jnp.concatenate([tile0, tile1], axis=1).astype(B16)
        part = nn(rows, held[: 2 * LANES, :])
        total = part if total is None else total + part
    result[...] = total


def finish_kernel(own, other, output, grad_query):
    width = output.shape[1]
    total = own[...] + other[...]
    output[...] = total[:1, :width].astype(output.dtype)
    grad_query[...] = total[:1, width:]


VMEM = pl.BlockSpec(memory_space=pltpu.VMEM)
HBM = pl.BlockSpec(memory_space=pltpu.HBM)


def call(body, outs, args, fresh=0, scratch=(), flops=1000000, last=False, waits=False):
    size = sum(math.prod(v.shape) * v.dtype.itemsize for v in list(args) + list(outs))

    def kernel(*refs):
        if fresh:
            *refs, sems = refs
            held = refs[len(refs) - fresh :]
            copies = [pltpu.make_async_copy(refs[i], held[i], sems.at[i]) for i in range(fresh)]
            for copy in copies:
                copy.start()

            def ready():
                for copy in copies:
                    copy.wait()

            if not waits:
                ready()
            refs = list(held) + list(refs[fresh : len(refs) - fresh])
        body(*([ready] if waits else []), *refs)

    own = [pltpu.VMEM(v.shape, v.dtype) for v in args[:fresh]]
    return pl.pallas_call(
        kernel,
        out_shape=tuple(outs),
        in_specs=[HBM] * fresh + [VMEM] * (len(args) - fresh),
        out_specs=tuple([pl.BlockSpec() if last else VMEM] * len(outs)),
        scratch_shapes=list(scratch) + own + ([pltpu.SemaphoreType.DMA((fresh,))] if fresh else []),
        compiler_params=pltpu.CompilerParams(vmem_limit_bytes=(16 << 20) + 6 * size),
        cost_estimate=pl.CostEstimate(flops=flops, bytes_accessed=size, transcendentals=0),
    )(*[pltpu.with_memory_space_constraint(v, pltpu.HBM) for v in args[:fresh]], *args[fresh:])


def shape_of(*dims, dtype=F32):
    return jax.ShapeDtypeStruct(dims, dtype)


def shards(
    query_single, key_single, pair, query_frames, key_frames, w_query, w_key, w_value, w_query_points, w_key_points,
    w_value_points, head_weight, bias_weight, w_out, d_out,
):
    lay = Layout(head_weight.shape[0])
    count = lax.axis_size("row")
    block, width = key_single.shape
    total = count * block
    near = 1
    while 4 * near * near <= count:
        near *= 2
    assert count & (count - 1) == 0

    def exchange(value, mask):
        return lax.ppermute(value, "row", [(i, i ^ mask) for i in range(count)])

    (packed,) = call(
        functools.partial(key_kernel, lay),
        [shape_of(block, 2 * LANES, dtype=B16)],
        [
            key_single, key_frames, w_key.T, w_value.T, w_key_points.T, w_value_points.T,
        ],
        6,
        waits=True,
    )
    offsets = list(range(0, count, near))
    line = jnp.concatenate([packed] + [exchange(packed, mask) for mask in offsets[1:]], axis=0)
    planes = [0, 1] + list(range(near - 1, 1, -1))
    parts = [line] + [exchange(line, m) for m in planes[1:]]
    order = [m ^ o for m in planes for o in offsets]

    left, base, d_base, d_row, w_out_rows, w_query_rows, table, pair_rows, gains, parcel, turned = call(
        functools.partial(early_kernel, lay, block, order),
        [
            shape_of(ROWS16, LANES), shape_of(SUBLANES, total), shape_of(SUBLANES, total),
            shape_of(SUBLANES, 2 * LANES), shape_of((2 + lay.heads) * LANES, width, dtype=B16),
            shape_of(LANES, width, dtype=B16), shape_of(ROWS16, LANES),
            shape_of(total, LANES, dtype=B16), shape_of(SUBLANES, LANES),
            shape_of(2 * LANES + block // 2, width, dtype=B16), shape_of(block, LANES),
        ],
        [
            query_frames.T, query_single, w_query.T, w_query_points.T, bias_weight, w_out, d_out, pair,
            head_weight.reshape(1, -1), key_frames, w_key.T, w_value.T, w_key_points.T, w_value_points.T, packed,
        ],
        14,
        [pltpu.VMEM((ROWS16, LANES), F32)],
    )
    swap = [(i, (i + 1) % 2) for i in range(2)]
    other = lax.ppermute(parcel, "head", swap)
    message, features, weight_rows, scores = call(
        functools.partial(attention_kernel, lay, block, order),
        [
            shape_of(2 * count, SUBLANES, LANES, dtype=B16), shape_of(SUBLANES, 2 * LANES),
            shape_of(SUBLANES, total, dtype=B16), shape_of(SUBLANES, total, dtype=B16),
        ],
        parts + [left, base, d_base, d_row, gains, table],
    )
    arrived = lax.all_to_all(message, ("row", "head"), 0, 0, tiled=True)
    (sums,) = call(
        functools.partial(rows_kernel, lay),
        [shape_of(SUBLANES, 2 * width)],
        parts + [pair_rows, left, scores, features, weight_rows, w_out_rows, w_query_rows, gains, table],
    )
    output, grad_query = call(
        finish_kernel,
        [shape_of(1, width, dtype=B16), shape_of(1, width)],
        [sums, lax.ppermute(sums, "head", swap)],
        last=True,
    )
    (grad_keys,) = call(
        functools.partial(owner_kernel, lay),
        [shape_of(block, width)],
        [arrived, turned, parcel, other],
        last=True,
    )
    return (output, grad_query, grad_keys)


def solution(mesh):
    return jax.shard_map(
        shards,
        mesh=mesh,
        in_specs=(
            P("row", None),
            P("row", None),
            P("row", None, None),
            P(None, "row"),
            P(None, "row"),
            P(None, "head"),
            P(None, "head"),
            P(None, "head"),
            P(None, "head"),
            P(None, "head"),
            P(None, "head"),
            P("head"),
            P("head", None),
            P("head", None),
            P("row", None),
        ),
        out_specs=(P("row", None), P("row", None), P("row", None)),
        check_vma=False,
    )
```

```python
import functools
import math

import jax
import jax.numpy as jnp
from jax import lax
from jax.experimental import pallas as pl
from jax.experimental.pallas import tpu as pltpu
from jax.sharding import PartitionSpec as P

C = 16
PQ = 4
PV = 8
LANES = 128
SUBLANES = 8
ROWS16 = 16
LOGIT_SCALE = math.sqrt(1.0 / 3.0)
POINT_SCALE = math.sqrt(2.0 / (9.0 * PQ))
F32 = jnp.float32
B16 = jnp.bfloat16


class Layout:
    def __init__(self, heads):
        self.heads = heads
        self.base = heads * C
        self.kp = heads * PQ
        self.vp = heads * PV
        self.square = self.base + 3 * self.kp
        assert self.square + self.kp <= LANES and self.base + 3 * self.vp <= LANES
        assert 2 * heads + 2 <= SUBLANES and PQ == 4


def nn(a, b, precision=None):
    return lax.dot_general(a, b, (((1,), (0,)), ((), ())), precision=precision, preferred_element_type=F32)


def nt(a, b):
    return lax.dot_general(a, b, (((1,), (1,)), ((), ())), preferred_element_type=F32)


def iota(shape, dim):
    return lax.broadcasted_iota(jnp.int32, shape, dim)


def pick(condition):
    return jnp.where(condition, 1.0, 0.0).astype(B16)


def to_lane(rows, offset):
    j, i = iota((LANES, rows), 0), iota((LANES, rows), 1)
    return pick(j == i + offset)


def to_components(rows, offset, points, seg):
    j, i = iota((LANES, rows), 0), iota((LANES, rows), 1)
    found = j < 0
    for c in range(3):
        m = j - (c * seg + offset)
        found = found | ((m >= 0) & (m < points) & (i == 3 * m + c))
    return pick(found)


def unpack(tile, seg):
    return tile, pltpu.roll(tile, LANES - seg, 1), pltpu.roll(tile, LANES - 2 * seg, 1)


def pack(parts, seg, base):
    lane = iota(parts[0].shape, 1)
    keep = (lane >= base) & (lane < base + seg)
    x, y, z = (jnp.where(keep, v, 0.0) for v in parts)
    return x + pltpu.roll(y, seg, 1) + pltpu.roll(z, 2 * seg, 1)


def head_of(shape, lay):
    lane = iota(shape, 1)
    zero = jnp.full(shape, -1, jnp.int32)
    one = jnp.full(shape, -1, jnp.int32)
    for h in range(lay.heads):
        same = (lane >= h * C) & (lane < (h + 1) * C)
        zero, one = jnp.where(same, h, zero), jnp.where(same, h, one)
        for c in range(3):
            k = lay.base + c * lay.kp + h * PQ
            v = lay.base + c * lay.vp + h * PV
            zero = jnp.where((lane >= k) & (lane < k + PQ), h, zero)
            one = jnp.where((lane >= v) & (lane < v + PV), h, one)
    return zero, one


def turned_by(frames, vectors):
    x, y, z = vectors
    return [frames[3 * c] * x + frames[3 * c + 1] * y + frames[3 * c + 2] * z for c in range(3)]


def turned_back(frames, vectors):
    x, y, z = vectors
    return [frames[d] * x + frames[3 + d] * y + frames[6 + d] * z for d in range(3)]


def key_kernel(lay, ready, key_single, frames, w_key, w_value, w_kp, w_vp, packed):
    heads, kp, vp, base = lay.heads, lay.kp, lay.vp, lay.base
    tall = PQ * SUBLANES

    def rows_of(count, width):
        return iota((count, width), 0), iota((count, width), 1)

    r, i = rows_of(tall, 3 * kp)
    to_kp = [pick((i == 3 * PQ * (r & 7) + 3 * (r >> 3) + c) & ((r & 7) < heads)) for c in range(3)]
    r, i = rows_of(vp, 3 * vp)
    to_vp = [pick(i == 3 * r + c) for c in range(3)]
    width = 2 * LANES
    r, j = rows_of(base, width)
    place = [j == r, j == r + LANES]
    r, j = rows_of(tall, width)
    place += [(j == base + c * kp + PQ * (r & 7) + (r >> 3)) & ((r & 7) < heads) for c in range(3)]
    r, j = rows_of(vp, width)
    place += [j == LANES + base + c * vp + r for c in range(3)]
    r, j = rows_of(SUBLANES, width)
    place += [(j == lay.square + PQ * r + piece) & (r < heads) for piece in range(3)]
    place = jnp.concatenate([jnp.where(found, 1.0, 0.0) for found in place], axis=0).astype(B16)
    to_kp = jnp.concatenate(to_kp, axis=0)
    to_vp = jnp.concatenate(to_vp, axis=0)
    ready()
    single = key_single[...]
    turn = [frames[i : i + 1, :] for i in range(12)]
    features = [nt(w_key[...], single), nt(w_value[...], single)]
    for choose, weight, height in ((to_kp, w_kp, tall), (to_vp, w_vp, vp)):
        rows = nt(nn(choose, weight[...]).astype(B16), single)
        moved = turned_by(turn, [rows[c * height : (c + 1) * height] for c in range(3)])
        moved = [(v + turn[9 + c]).astype(B16).astype(F32) for c, v in enumerate(moved)]
        features += moved
        if height == tall:
            square = moved[0] * moved[0] + moved[1] * moved[1] + moved[2] * moved[2]
            square = sum(square[group(p)] for p in range(PQ))
    first = square.astype(B16).astype(F32)
    second = (square - first).astype(B16).astype(F32)
    features = jnp.concatenate(features + [first, second, square - first - second], axis=0)
    packed[...] = nn(jnp.transpose(features).astype(B16), place).astype(B16)


def group(h):
    return slice(h * SUBLANES, (h + 1) * SUBLANES)


def gain_rows(head_weight, lay):
    row = iota((SUBLANES, LANES), 0)
    raw = jnp.zeros((SUBLANES, LANES), F32)
    for h in range(lay.heads):
        raw = jnp.where(row == h, jnp.broadcast_to(head_weight[:, h : h + 1], raw.shape), raw)
    gain = (jnp.maximum(raw, 0.0) + jnp.log1p(jnp.exp(-jnp.abs(raw)))) * POINT_SCALE
    return jnp.where(row < lay.heads, gain, 0.0)


def gain_lanes(gain, lay):
    zero, _ = head_of(gain.shape, lay)
    return jnp.sum(jnp.where(zero == iota(gain.shape, 0), gain, 0.0), axis=0, keepdims=True)


def early_kernel(
    lay, block, order, frames, query_single, w_query, w_qp, bias_weight, w_out, d_out, pair, head_weight, key_frames,
    w_key, w_value, w_kp, w_vp, packed,
    left, base, d_base, d_row, w_out_rows, w_query_rows, table, pair_rows, gains, parcel, turned, scratch,
):
    kp, vp = lay.kp, lay.vp
    zero = nn(to_lane(lay.base, 0), w_key[...]) + nn(to_components(3 * kp, lay.base, kp, kp), w_kp[...])
    one = nn(to_lane(lay.base, 0), w_value[...]) + nn(to_components(3 * vp, lay.base, vp, vp), w_vp[...])
    parcel[:LANES, :] = zero.astype(B16)
    parcel[LANES : 2 * LANES, :] = one.astype(B16)
    half = block // 2
    parcel[2 * LANES :, :LANES] = packed[:half, :LANES]
    parcel[2 * LANES :, LANES : 2 * LANES] = packed[half:, :LANES]
    parcel[2 * LANES :, 2 * LANES :] = jnp.zeros((half, parcel.shape[1] - 2 * LANES), B16)
    gain = gain_rows(head_weight, lay)
    gains[...] = gain
    pieces = jnp.broadcast_to(gain_lanes(gain, lay), (ROWS16, LANES))
    first = pieces.astype(B16).astype(F32)
    second = (pieces - first).astype(B16).astype(F32)
    row = iota(pieces.shape, 0)
    pieces = jnp.where(
        row == 0, first, jnp.where(row == 1, second, jnp.where(row == 2, pieces - first - second, 0.0))
    )
    parcel[2 * LANES : 2 * LANES + ROWS16, 2 * LANES : 3 * LANES] = pieces.astype(B16)
    turn = jnp.transpose(key_frames[...])
    turned[:, : turn.shape[1]] = turn
    me = lax.axis_index("row")
    for place, offset in enumerate(order):
        j = pl.multiple_of((me ^ offset) * block, block)
        pair_rows[place * block : (place + 1) * block, :] = pair[0, pl.ds(j, block), :]
    turn = [jnp.broadcast_to(frames[:, i : i + 1], (1, LANES)) for i in range(12)]
    for i in range(12):
        table[i : i + 1, :] = turn[i]
    heads, start = lay.heads, lay.base
    width = C + 4 * PV + LANES
    near = C + 4 * PV
    shape = (SUBLANES, LANES)
    row, lane = iota(shape, 0), iota(shape, 1)
    zero_head, _ = head_of(shape, lay)
    w_q = nn(to_lane(start, 0), w_query[...]) + nn(to_components(3 * lay.kp, start, lay.kp, lay.kp), w_qp[...])
    w_q = w_q.astype(B16)
    w_query_rows[...] = w_q
    w_o = jnp.zeros((2 * LANES, w_out.shape[1]), F32)
    for h in range(heads):
        i, j = iota((2 * LANES, near), 0), iota((2 * LANES, near), 1)
        m = i - (LANES + h * C)
        found = (m >= 0) & (m < C) & (j == m)
        m = i - (start + h * PV)
        found = found | ((m >= 0) & (m < PV) & (j == C + 3 * PV + m))
        for c in range(3):
            m = i - (LANES + start + c * lay.vp + h * PV)
            found = found | ((m >= 0) & (m < PV) & (j == C + 3 * m + c))
        w_o = w_o + nn(pick(found), w_out[h * width : h * width + near, :])
    w_o = w_o.astype(B16)
    w_out_rows[: 2 * LANES, :] = w_o
    for h in range(heads):
        w_out_rows[(2 + h) * LANES : (3 + h) * LANES, :] = w_out[h * width + near : (h + 1) * width, :]
    single = jnp.broadcast_to(query_single[...], (SUBLANES, query_single.shape[1]))
    rows = nt(single, w_q)
    moved = turned_by(turn, unpack(rows, lay.kp))
    points = pack([(v + turn[9 + c]).astype(B16).astype(F32) for c, v in enumerate(moved)], lay.kp, start)
    query = jnp.where(lane < start, rows, 0.0).astype(B16).astype(F32)
    left[:SUBLANES, :] = jnp.where(zero_head == row, query, 0.0)
    minus = lane < 0
    for h in range(heads):
        at = lay.square + h * PQ
        minus = minus | ((row == h) & (lane >= at) & (lane < at + 3))
    mine = jnp.where(zero_head == row, points, 0.0)
    left[SUBLANES:, :] = jnp.where(minus, -0.5, mine)
    cotangent = jnp.broadcast_to(d_out[...], (SUBLANES, d_out.shape[1]))
    d_row[...] = nt(cotangent, w_o)
    scratch[...] = jnp.zeros_like(scratch)
    scratch[:heads, :] = bias_weight[...].astype(F32)
    for h in range(heads):
        d_pair = nt(cotangent, w_out[h * width + near : (h + 1) * width, :])
        scratch[SUBLANES + h : SUBLANES + h + 1, :] = d_pair[:1, :]
    both = nt(scratch[...].astype(B16), pair_rows[...])
    square = jnp.sum(mine * mine, axis=1, keepdims=True)
    base[...] = both[:SUBLANES] - 0.5 * gain[:, :1] * square
    d_base[...] = both[SUBLANES:]


def attention_kernel(lay, block, order, *refs):
    *parts, left, base, d_base, d_row, gains, table, message, features, weights, scores = refs
    frames = [table[i : i + 1, :] for i in range(12)]
    me = lax.axis_index("row")
    heads, vp, start = lay.heads, lay.vp, lay.base
    shape = (SUBLANES, LANES)
    row, lane = iota(shape, 0), iota(shape, 1)
    _, one_head = head_of(shape, lay)
    gain = gains[...]
    queries = left[...].astype(B16)
    first = jnp.concatenate([nt(queries, part[:, :LANES]) for part in parts], axis=1)
    logits = LOGIT_SCALE * (first[:SUBLANES] * (1.0 / math.sqrt(C)) + base[...] + gain[:, :1] * first[SUBLANES:])
    weight = jnp.exp(logits - jnp.max(logits, axis=1, keepdims=True))
    weight = jnp.where(iota(weight.shape, 0) < heads, weight, 0.0)
    whole = weight.astype(B16).astype(F32)
    sums = spread(jnp.concatenate([whole, weight - whole], axis=0).astype(B16), [part.at[:, LANES:] for part in parts])
    total = jnp.sum(weight, axis=1, keepdims=True)
    total = jnp.where(row[:, :1] < heads, total, 1.0)
    attention = weight / total
    attention_b = attention.astype(B16)
    sums = jnp.where(one_head == row, (sums[:SUBLANES] + sums[SUBLANES:]) / total, 0.0)
    sums = jnp.broadcast_to(jnp.sum(sums, axis=0, keepdims=True), shape)
    local = turned_back(frames, [v - frames[9 + c] for c, v in enumerate(unpack(sums, vp))])
    lengths = jnp.sqrt(1.0 + (local[0] * local[0] + local[1] * local[1] + local[2] * local[2]))
    d_one = d_row[:, LANES:]
    share = d_row[:, :LANES] / lengths
    d_points = turned_by(frames, [v + share * u for v, u in zip(unpack(d_one, vp), local)])
    d_side = jnp.where(lane < start, d_one, 0.0) + pack(d_points, vp, start)
    right = jnp.where(one_head == row, d_side, 0.0).astype(B16)
    d_attention = jnp.concatenate([nt(right, part[:, LANES:]) for part in parts], axis=1) + d_base[...]
    total = jnp.sum(attention * d_attention, axis=1, keepdims=True)
    score_b = (LOGIT_SCALE * attention * (d_attention - total)).astype(B16)
    query = jnp.sum(jnp.where(lane < lay.square, left[:SUBLANES, :] + left[SUBLANES:, :], 0.0), axis=0, keepdims=True)
    side = jnp.where(row == 2 * heads, jnp.broadcast_to(query, shape), 0.0)
    side = side + jnp.where(row == 2 * heads + 1, d_side, 0.0)
    both = attention_b.astype(F32) + pltpu.roll(score_b.astype(F32), heads, 0)
    for at in range(0, both.shape[1], LANES):
        for place in range(at // block, (at + LANES) // block):
            tile = both[:, at : at + LANES]
            if place * block != at:
                tile = pltpu.roll(tile, LANES - (place * block - at), 1)
            tile = jnp.where(row < 2 * heads, tile, side).astype(B16)
            for core in range(2):
                message[(me ^ order[place]) * 2 + core, :, :] = tile
    weights[...] = attention_b
    scores[...] = score_b
    features[:, :LANES] = jnp.where((lane >= start) & (lane < start + vp), lengths, 0.0)
    features[:, LANES:] = jnp.where(lane < start, sums, 0.0) + pack(local, vp, start)


def spread(weights, parts):
    total, at = 0.0, 0
    for part in parts:
        total = total + nn(weights[:, at : at + part.shape[0]], part[...])
        at += part.shape[0]
    return total


def rows_kernel(lay, *refs):
    *parts, pair, left, scores, features, weights, w_out_rows, w_query_rows, gains, table, sums = refs
    frames = [table[i : i + 1, :] for i in range(12)]
    shape = (SUBLANES, LANES)
    row, lane = iota(shape, 0), iota(shape, 1)
    zero_head, _ = head_of(shape, lay)
    pair_sum = nn(weights[...], pair[...])
    pairs = [jnp.broadcast_to(pair_sum[h : h + 1, :], shape) for h in range(lay.heads)]
    result = nn(jnp.concatenate([features[...]] + pairs, axis=1).astype(B16), w_out_rows[...])
    score = scores[...].astype(F32)
    d_rows = spread(scores[...], [part.at[:, :LANES] for part in parts])
    score_sum = jnp.sum(score, axis=1, keepdims=True)
    points = left[SUBLANES:, :]
    d_rows = jnp.where(lane < lay.base, d_rows * (1.0 / math.sqrt(C)), gains[...] * (d_rows - score_sum * points))
    d_rows = jnp.broadcast_to(
        jnp.sum(jnp.where(zero_head == row, d_rows, 0.0), axis=0, keepdims=True), shape
    )
    local = pack(turned_back(frames, unpack(d_rows, lay.kp)), lay.kp, lay.base)
    both = (jnp.where(lane < lay.base, d_rows, 0.0) + local).astype(B16)
    sums[...] = jnp.concatenate([result, nn(both, w_query_rows[...])], axis=1)


def owner_kernel(lay, arrived, turned, parcel, other, result):
    heads, base = lay.heads, lay.base
    count = arrived.shape[0] // 2
    block = turned.shape[0]
    shape = (SUBLANES, LANES)
    whole = (count, SUBLANES, LANES)
    row = iota(shape, 0)
    zero_head, one_head = head_of(shape, lay)
    lane = iota(shape, 1)
    keep0 = (zero_head >= 0) & (zero_head + heads == row)
    keep1 = one_head == row
    ones = jnp.broadcast_to(jnp.where(keep0 & (lane >= base), 1.0, 0.0)[None], whole)
    columns = [turned[:, i : i + 1] for i in range(9)]
    lane = iota((block, LANES), 1)
    me = lax.axis_index("head")
    total = None
    for core, held in ((me, parcel), (1 - me, other)):
        took = jnp.concatenate([arrived[pl.ds(q * 2 + core, 1)] for q in range(count)], axis=0).astype(F32)
        side0 = jnp.where(keep0[None], jnp.broadcast_to(took[:, 2 * heads : 2 * heads + 1, :], whole), 0.0)
        side1 = jnp.where(keep1[None], jnp.broadcast_to(took[:, 2 * heads + 1 : 2 * heads + 2, :], whole), 0.0)
        right = jnp.concatenate([side0, side1, ones], axis=2).reshape(count * SUBLANES, 3 * LANES).astype(B16)
        moved = jnp.transpose(took.reshape(count * SUBLANES, LANES)).astype(B16)
        both = nn(moved, right)[:block]
        pieces = held[2 * LANES : 2 * LANES + ROWS16, 2 * LANES : 3 * LANES].astype(F32)
        gain = pieces[0:1] + pieces[1:2] + pieces[2:3]
        own = [held[2 * LANES :, at : at + LANES].astype(F32) for at in (0, LANES)]
        own = jnp.concatenate(own, axis=0)
        tile0, tile1 = both[:, :LANES], both[:, LANES : 2 * LANES]
        points = gain * (tile0 - both[:, 2 * LANES :] * own)
        points = pack(turned_back(columns, unpack(points, lay.kp)), lay.kp, base)
        tile0 = jnp.where(lane < base, tile0 * (1.0 / math.sqrt(C)), points)
        points = pack(turned_back(columns, unpack(tile1, lay.vp)), lay.vp, base)
        tile1 = jnp.where(lane < base, tile1, points)
        rows = jnp.concatenate([tile0, tile1], axis=1).astype(B16)
        part = nn(rows, held[: 2 * LANES, :])
        total = part if total is None else total + part
    result[...] = total


def finish_kernel(own, other, output, grad_query):
    width = output.shape[1]
    total = own[...] + other[...]
    output[...] = total[:1, :width].astype(output.dtype)
    grad_query[...] = total[:1, width:]


VMEM = pl.BlockSpec(memory_space=pltpu.VMEM)
HBM = pl.BlockSpec(memory_space=pltpu.HBM)


def call(body, outs, args, fresh=0, scratch=(), flops=1000000, last=False, waits=False):
    size = sum(math.prod(v.shape) * v.dtype.itemsize for v in list(args) + list(outs))

    def kernel(*refs):
        if fresh:
            *refs, sems = refs
            held = refs[len(refs) - fresh :]
            copies = [pltpu.make_async_copy(refs[i], held[i], sems.at[i]) for i in range(fresh)]
            for copy in copies:
                copy.start()

            def ready():
                for copy in copies:
                    copy.wait()

            if not waits:
                ready()
            refs = list(held) + list(refs[fresh : len(refs) - fresh])
        body(*([ready] if waits else []), *refs)

    own = [pltpu.VMEM(v.shape, v.dtype) for v in args[:fresh]]
    return pl.pallas_call(
        kernel,
        out_shape=tuple(outs),
        in_specs=[HBM] * fresh + [VMEM] * (len(args) - fresh),
        out_specs=tuple([pl.BlockSpec() if last else VMEM] * len(outs)),
        scratch_shapes=list(scratch) + own + ([pltpu.SemaphoreType.DMA((fresh,))] if fresh else []),
        compiler_params=pltpu.CompilerParams(vmem_limit_bytes=(16 << 20) + 6 * size),
        cost_estimate=pl.CostEstimate(flops=flops, bytes_accessed=size, transcendentals=0),
    )(*[pltpu.with_memory_space_constraint(v, pltpu.HBM) for v in args[:fresh]], *args[fresh:])


def shape_of(*dims, dtype=F32):
    return jax.ShapeDtypeStruct(dims, dtype)


def shards(
    query_single, key_single, pair, query_frames, key_frames, w_query, w_key, w_value, w_query_points, w_key_points,
    w_value_points, head_weight, bias_weight, w_out, d_out,
):
    lay = Layout(head_weight.shape[0])
    count = lax.axis_size("row")
    block, width = key_single.shape
    total = count * block
    near = 1
    while 4 * near * near <= count:
        near *= 2
    assert count & (count - 1) == 0

    def exchange(value, mask):
        return lax.ppermute(value, "row", [(i, i ^ mask) for i in range(count)])

    (packed,) = call(
        functools.partial(key_kernel, lay),
        [shape_of(block, 2 * LANES, dtype=B16)],
        [
            key_single, key_frames, w_key.T, w_value.T, w_key_points.T, w_value_points.T,
        ],
        6,
        waits=True,
    )
    offsets = list(range(0, count, near))
    line = jnp.concatenate([packed] + [exchange(packed, mask) for mask in offsets[1:]], axis=0)
    planes = list(range(near))
    parts = [line] + [exchange(line, m) for m in planes[1:]]
    order = [m ^ o for m in planes for o in offsets]

    left, base, d_base, d_row, w_out_rows, w_query_rows, table, pair_rows, gains, parcel, turned = call(
        functools.partial(early_kernel, lay, block, order),
        [
            shape_of(ROWS16, LANES), shape_of(SUBLANES, total), shape_of(SUBLANES, total),
            shape_of(SUBLANES, 2 * LANES), shape_of((2 + lay.heads) * LANES, width, dtype=B16),
            shape_of(LANES, width, dtype=B16), shape_of(ROWS16, LANES),
            shape_of(total, LANES, dtype=B16), shape_of(SUBLANES, LANES),
            shape_of(2 * LANES + block // 2, width, dtype=B16), shape_of(block, LANES),
        ],
        [
            query_frames.T, query_single, w_query.T, w_query_points.T, bias_weight, w_out, d_out, pair,
            head_weight.reshape(1, -1), key_frames, w_key.T, w_value.T, w_key_points.T, w_value_points.T, packed,
        ],
        14,
        [pltpu.VMEM((ROWS16, LANES), F32)],
    )
    swap = [(i, (i + 1) % 2) for i in range(2)]
    other = lax.ppermute(parcel, "head", swap)
    message, features, weight_rows, scores = call(
        functools.partial(attention_kernel, lay, block, order),
        [
            shape_of(2 * count, SUBLANES, LANES, dtype=B16), shape_of(SUBLANES, 2 * LANES),
            shape_of(SUBLANES, total, dtype=B16), shape_of(SUBLANES, total, dtype=B16),
        ],
        parts + [left, base, d_base, d_row, gains, table],
    )
    arrived = lax.all_to_all(message, ("row", "head"), 0, 0, tiled=True)
    (sums,) = call(
        functools.partial(rows_kernel, lay),
        [shape_of(SUBLANES, 2 * width)],
        parts + [pair_rows, left, scores, features, weight_rows, w_out_rows, w_query_rows, gains, table],
    )
    output, grad_query = call(
        finish_kernel,
        [shape_of(1, width, dtype=B16), shape_of(1, width)],
        [sums, lax.ppermute(sums, "head", swap)],
        last=True,
    )
    (grad_keys,) = call(
        functools.partial(owner_kernel, lay),
        [shape_of(block, width)],
        [arrived, turned, parcel, other],
        last=True,
    )
    return (output, grad_query, grad_keys)


def solution(mesh):
    return jax.shard_map(
        shards,
        mesh=mesh,
        in_specs=(
            P("row", None),
            P("row", None),
            P("row", None, None),
            P(None, "row"),
            P(None, "row"),
            P(None, "head"),
            P(None, "head"),
            P(None, "head"),
            P(None, "head"),
            P(None, "head"),
            P(None, "head"),
            P("head"),
            P("head", None),
            P("head", None),
            P("row", None),
        ),
        out_specs=(P("row", None), P("row", None), P("row", None)),
        check_vma=False,
    )
```

```python
import functools
import math

import jax
import jax.numpy as jnp
from jax import lax
from jax.experimental import pallas as pl
from jax.experimental.pallas import tpu as pltpu
from jax.sharding import PartitionSpec as P

C = 16
PQ = 4
PV = 8
LANES = 128
SUBLANES = 8
ROWS16 = 16
LOGIT_SCALE = math.sqrt(1.0 / 3.0)
POINT_SCALE = math.sqrt(2.0 / (9.0 * PQ))
F32 = jnp.float32
B16 = jnp.bfloat16


class Layout:
    def __init__(self, heads):
        self.heads = heads
        self.base = heads * C
        self.kp = heads * PQ
        self.vp = heads * PV
        self.square = self.base + 3 * self.kp
        assert self.square + self.kp <= LANES and self.base + 3 * self.vp <= LANES
        assert 2 * heads + 2 <= SUBLANES and PQ == 4


def nn(a, b, precision=None):
    return lax.dot_general(a, b, (((1,), (0,)), ((), ())), precision=precision, preferred_element_type=F32)


def nt(a, b):
    return lax.dot_general(a, b, (((1,), (1,)), ((), ())), preferred_element_type=F32)


def iota(shape, dim):
    return lax.broadcasted_iota(jnp.int32, shape, dim)


def pick(condition):
    return jnp.where(condition, 1.0, 0.0).astype(B16)


def to_lane(rows, offset):
    j, i = iota((LANES, rows), 0), iota((LANES, rows), 1)
    return pick(j == i + offset)


def to_components(rows, offset, points, seg):
    j, i = iota((LANES, rows), 0), iota((LANES, rows), 1)
    found = j < 0
    for c in range(3):
        m = j - (c * seg + offset)
        found = found | ((m >= 0) & (m < points) & (i == 3 * m + c))
    return pick(found)


def unpack(tile, seg):
    return tile, pltpu.roll(tile, LANES - seg, 1), pltpu.roll(tile, LANES - 2 * seg, 1)


def pack(parts, seg, base):
    lane = iota(parts[0].shape, 1)
    keep = (lane >= base) & (lane < base + seg)
    x, y, z = (jnp.where(keep, v, 0.0) for v in parts)
    return x + pltpu.roll(y, seg, 1) + pltpu.roll(z, 2 * seg, 1)


def head_of(shape, lay):
    lane = iota(shape, 1)
    zero = jnp.full(shape, -1, jnp.int32)
    one = jnp.full(shape, -1, jnp.int32)
    for h in range(lay.heads):
        same = (lane >= h * C) & (lane < (h + 1) * C)
        zero, one = jnp.where(same, h, zero), jnp.where(same, h, one)
        for c in range(3):
            k = lay.base + c * lay.kp + h * PQ
            v = lay.base + c * lay.vp + h * PV
            zero = jnp.where((lane >= k) & (lane < k + PQ), h, zero)
            one = jnp.where((lane >= v) & (lane < v + PV), h, one)
    return zero, one


def turned_by(frames, vectors):
    x, y, z = vectors
    return [frames[3 * c] * x + frames[3 * c + 1] * y + frames[3 * c + 2] * z for c in range(3)]


def turned_back(frames, vectors):
    x, y, z = vectors
    return [frames[d] * x + frames[3 + d] * y + frames[6 + d] * z for d in range(3)]


def key_kernel(lay, ready, key_single, frames, w_key, w_value, w_kp, w_vp, packed):
    heads, kp, vp, base = lay.heads, lay.kp, lay.vp, lay.base
    tall = PQ * SUBLANES

    def rows_of(count, width):
        return iota((count, width), 0), iota((count, width), 1)

    r, i = rows_of(tall, 3 * kp)
    to_kp = [pick((i == 3 * PQ * (r & 7) + 3 * (r >> 3) + c) & ((r & 7) < heads)) for c in range(3)]
    r, i = rows_of(vp, 3 * vp)
    to_vp = [pick(i == 3 * r + c) for c in range(3)]
    width = 2 * LANES
    r, j = rows_of(base, width)
    place = [j == r, j == r + LANES]
    r, j = rows_of(tall, width)
    place += [(j == base + c * kp + PQ * (r & 7) + (r >> 3)) & ((r & 7) < heads) for c in range(3)]
    r, j = rows_of(vp, width)
    place += [j == LANES + base + c * vp + r for c in range(3)]
    r, j = rows_of(SUBLANES, width)
    place += [(j == lay.square + PQ * r + piece) & (r < heads) for piece in range(3)]
    place = jnp.concatenate([jnp.where(found, 1.0, 0.0) for found in place], axis=0).astype(B16)
    to_kp = jnp.concatenate(to_kp, axis=0)
    to_vp = jnp.concatenate(to_vp, axis=0)
    ready()
    single = key_single[...]
    turn = [frames[i : i + 1, :] for i in range(12)]
    features = [nt(w_key[...], single), nt(w_value[...], single)]
    for choose, weight, height in ((to_kp, w_kp, tall), (to_vp, w_vp, vp)):
        rows = nt(nn(choose, weight[...]).astype(B16), single)
        moved = turned_by(turn, [rows[c * height : (c + 1) * height] for c in range(3)])
        moved = [(v + turn[9 + c]).astype(B16).astype(F32) for c, v in enumerate(moved)]
        features += moved
        if height == tall:
            square = moved[0] * moved[0] + moved[1] * moved[1] + moved[2] * moved[2]
            square = sum(square[group(p)] for p in range(PQ))
    first = square.astype(B16).astype(F32)
    second = (square - first).astype(B16).astype(F32)
    features = jnp.concatenate(features + [first, second, square - first - second], axis=0)
    packed[...] = nn(jnp.transpose(features).astype(B16), place).astype(B16)


def group(h):
    return slice(h * SUBLANES, (h + 1) * SUBLANES)


def gain_rows(head_weight, lay):
    row = iota((SUBLANES, LANES), 0)
    raw = jnp.zeros((SUBLANES, LANES), F32)
    for h in range(lay.heads):
        raw = jnp.where(row == h, jnp.broadcast_to(head_weight[:, h : h + 1], raw.shape), raw)
    gain = (jnp.maximum(raw, 0.0) + jnp.log1p(jnp.exp(-jnp.abs(raw)))) * POINT_SCALE
    return jnp.where(row < lay.heads, gain, 0.0)


def gain_lanes(gain, lay):
    zero, _ = head_of(gain.shape, lay)
    return jnp.sum(jnp.where(zero == iota(gain.shape, 0), gain, 0.0), axis=0, keepdims=True)


def early_kernel(
    lay, block, order, frames, query_single, w_query, w_qp, bias_weight, w_out, d_out, pair, head_weight, key_frames,
    w_key, w_value, w_kp, w_vp, packed,
    left, base, d_base, d_row, w_out_rows, w_query_rows, table, pair_rows, gains, parcel, turned, scratch,
):
    kp, vp = lay.kp, lay.vp
    zero = nn(to_lane(lay.base, 0), w_key[...]) + nn(to_components(3 * kp, lay.base, kp, kp), w_kp[...])
    one = nn(to_lane(lay.base, 0), w_value[...]) + nn(to_components(3 * vp, lay.base, vp, vp), w_vp[...])
    parcel[:LANES, :] = zero.astype(B16)
    parcel[LANES : 2 * LANES, :] = one.astype(B16)
    half = block // 2
    parcel[2 * LANES :, :LANES] = packed[:half, :LANES]
    parcel[2 * LANES :, LANES : 2 * LANES] = packed[half:, :LANES]
    parcel[2 * LANES :, 2 * LANES :] = jnp.zeros((half, parcel.shape[1] - 2 * LANES), B16)
    gain = gain_rows(head_weight, lay)
    gains[...] = gain
    pieces = jnp.broadcast_to(gain_lanes(gain, lay), (ROWS16, LANES))
    first = pieces.astype(B16).astype(F32)
    second = (pieces - first).astype(B16).astype(F32)
    row = iota(pieces.shape, 0)
    pieces = jnp.where(
        row == 0, first, jnp.where(row == 1, second, jnp.where(row == 2, pieces - first - second, 0.0))
    )
    parcel[2 * LANES : 2 * LANES + ROWS16, 2 * LANES : 3 * LANES] = pieces.astype(B16)
    turn = jnp.transpose(key_frames[...])
    turned[:, : turn.shape[1]] = turn
    me = lax.axis_index("row")
    for place, offset in enumerate(order):
        j = pl.multiple_of((me ^ offset) * block, block)
        pair_rows[place * block : (place + 1) * block, :] = pair[0, pl.ds(j, block), :]
    turn = [jnp.broadcast_to(frames[:, i : i + 1], (1, LANES)) for i in range(12)]
    for i in range(12):
        table[i : i + 1, :] = turn[i]
    heads, start = lay.heads, lay.base
    width = C + 4 * PV + LANES
    near = C + 4 * PV
    shape = (SUBLANES, LANES)
    row, lane = iota(shape, 0), iota(shape, 1)
    zero_head, _ = head_of(shape, lay)
    w_q = nn(to_lane(start, 0), w_query[...]) + nn(to_components(3 * lay.kp, start, lay.kp, lay.kp), w_qp[...])
    w_q = w_q.astype(B16)
    w_query_rows[...] = w_q
    w_o = jnp.zeros((2 * LANES, w_out.shape[1]), F32)
    for h in range(heads):
        i, j = iota((2 * LANES, near), 0), iota((2 * LANES, near), 1)
        m = i - (LANES + h * C)
        found = (m >= 0) & (m < C) & (j == m)
        m = i - (start + h * PV)
        found = found | ((m >= 0) & (m < PV) & (j == C + 3 * PV + m))
        for c in range(3):
            m = i - (LANES + start + c * lay.vp + h * PV)
            found = found | ((m >= 0) & (m < PV) & (j == C + 3 * m + c))
        w_o = w_o + nn(pick(found), w_out[h * width : h * width + near, :])
    w_o = w_o.astype(B16)
    w_out_rows[: 2 * LANES, :] = w_o
    for h in range(heads):
        w_out_rows[(2 + h) * LANES : (3 + h) * LANES, :] = w_out[h * width + near : (h + 1) * width, :]
    single = jnp.broadcast_to(query_single[...], (SUBLANES, query_single.shape[1]))
    rows = nt(single, w_q)
    moved = turned_by(turn, unpack(rows, lay.kp))
    points = pack([(v + turn[9 + c]).astype(B16).astype(F32) for c, v in enumerate(moved)], lay.kp, start)
    query = jnp.where(lane < start, rows, 0.0).astype(B16).astype(F32)
    left[:SUBLANES, :] = jnp.where(zero_head == row, query, 0.0)
    minus = lane < 0
    for h in range(heads):
        at = lay.square + h * PQ
        minus = minus | ((row == h) & (lane >= at) & (lane < at + 3))
    mine = jnp.where(zero_head == row, points, 0.0)
    left[SUBLANES:, :] = jnp.where(minus, -0.5, mine)
    cotangent = jnp.broadcast_to(d_out[...], (SUBLANES, d_out.shape[1]))
    d_row[...] = nt(cotangent, w_o)
    scratch[...] = jnp.zeros_like(scratch)
    scratch[:heads, :] = bias_weight[...].astype(F32)
    for h in range(heads):
        d_pair = nt(cotangent, w_out[h * width + near : (h + 1) * width, :])
        scratch[SUBLANES + h : SUBLANES + h + 1, :] = d_pair[:1, :]
    both = nt(scratch[...].astype(B16), pair_rows[...])
    square = jnp.sum(mine * mine, axis=1, keepdims=True)
    base[...] = both[:SUBLANES] - 0.5 * gain[:, :1] * square
    d_base[...] = both[SUBLANES:]


def attention_kernel(lay, block, order, *refs):
    *parts, left, base, d_base, d_row, gains, table, message, features, weights, scores = refs
    frames = [table[i : i + 1, :] for i in range(12)]
    me = lax.axis_index("row")
    heads, vp, start = lay.heads, lay.vp, lay.base
    shape = (SUBLANES, LANES)
    row, lane = iota(shape, 0), iota(shape, 1)
    _, one_head = head_of(shape, lay)
    gain = gains[...]
    queries = left[...].astype(B16)
    first = jnp.concatenate([nt(queries, part[:, :LANES]) for part in parts], axis=1)
    logits = LOGIT_SCALE * (first[:SUBLANES] * (1.0 / math.sqrt(C)) + base[...] + gain[:, :1] * first[SUBLANES:])
    weight = jnp.exp(logits - jnp.max(logits, axis=1, keepdims=True))
    weight = jnp.where(iota(weight.shape, 0) < heads, weight, 0.0)
    whole = weight.astype(B16).astype(F32)
    sums = spread(jnp.concatenate([whole, weight - whole], axis=0).astype(B16), [part.at[:, LANES:] for part in parts])
    total = jnp.sum(weight, axis=1, keepdims=True)
    total = jnp.where(row[:, :1] < heads, total, 1.0)
    attention = weight / total
    attention_b = attention.astype(B16)
    sums = jnp.where(one_head == row, (sums[:SUBLANES] + sums[SUBLANES:]) / total, 0.0)
    sums = jnp.broadcast_to(jnp.sum(sums, axis=0, keepdims=True), shape)
    local = turned_back(frames, [v - frames[9 + c] for c, v in enumerate(unpack(sums, vp))])
    lengths = jnp.sqrt(1.0 + (local[0] * local[0] + local[1] * local[1] + local[2] * local[2]))
    d_one = d_row[:, LANES:]
    share = d_row[:, :LANES] / lengths
    d_points = turned_by(frames, [v + share * u for v, u in zip(unpack(d_one, vp), local)])
    d_side = jnp.where(lane < start, d_one, 0.0) + pack(d_points, vp, start)
    right = jnp.where(one_head == row, d_side, 0.0).astype(B16)
    d_attention = jnp.concatenate([nt(right, part[:, LANES:]) for part in parts], axis=1) + d_base[...]
    total = jnp.sum(attention * d_attention, axis=1, keepdims=True)
    score_b = (LOGIT_SCALE * attention * (d_attention - total)).astype(B16)
    query = jnp.sum(jnp.where(lane < lay.square, left[:SUBLANES, :] + left[SUBLANES:, :], 0.0), axis=0, keepdims=True)
    side = jnp.where(row == 2 * heads, jnp.broadcast_to(query, shape), 0.0)
    side = side + jnp.where(row == 2 * heads + 1, d_side, 0.0)
    both = attention_b.astype(F32) + pltpu.roll(score_b.astype(F32), heads, 0)
    for at in range(0, both.shape[1], LANES):
        for place in range(at // block, (at + LANES) // block):
            tile = both[:, at : at + LANES]
            if place * block != at:
                tile = pltpu.roll(tile, LANES - (place * block - at), 1)
            tile = jnp.where(row < 2 * heads, tile, side).astype(B16)
            for core in range(2):
                message[(me ^ order[place]) * 2 + core, :, :] = tile
    weights[...] = attention_b
    scores[...] = score_b
    features[:, :LANES] = jnp.where((lane >= start) & (lane < start + vp), lengths, 0.0)
    features[:, LANES:] = jnp.where(lane < start, sums, 0.0) + pack(local, vp, start)


def spread(weights, parts):
    total, at = 0.0, 0
    for part in parts:
        total = total + nn(weights[:, at : at + part.shape[0]], part[...])
        at += part.shape[0]
    return total


def rows_kernel(lay, *refs):
    *parts, pair, left, scores, features, weights, w_out_rows, w_query_rows, gains, table, sums = refs
    frames = [table[i : i + 1, :] for i in range(12)]
    shape = (SUBLANES, LANES)
    row, lane = iota(shape, 0), iota(shape, 1)
    zero_head, _ = head_of(shape, lay)
    pair_sum = nn(weights[...], pair[...])
    pairs = [jnp.broadcast_to(pair_sum[h : h + 1, :], shape) for h in range(lay.heads)]
    result = nn(jnp.concatenate([features[...]] + pairs, axis=1).astype(B16), w_out_rows[...])
    score = scores[...].astype(F32)
    d_rows = spread(scores[...], [part.at[:, :LANES] for part in parts])
    score_sum = jnp.sum(score, axis=1, keepdims=True)
    points = left[SUBLANES:, :]
    d_rows = jnp.where(lane < lay.base, d_rows * (1.0 / math.sqrt(C)), gains[...] * (d_rows - score_sum * points))
    d_rows = jnp.broadcast_to(
        jnp.sum(jnp.where(zero_head == row, d_rows, 0.0), axis=0, keepdims=True), shape
    )
    local = pack(turned_back(frames, unpack(d_rows, lay.kp)), lay.kp, lay.base)
    both = (jnp.where(lane < lay.base, d_rows, 0.0) + local).astype(B16)
    sums[...] = jnp.concatenate([result, nn(both, w_query_rows[...])], axis=1)


def owner_kernel(lay, arrived, turned, parcel, other, result):
    heads, base = lay.heads, lay.base
    count = arrived.shape[0] // 2
    block = turned.shape[0]
    shape = (SUBLANES, LANES)
    whole = (count, SUBLANES, LANES)
    row = iota(shape, 0)
    zero_head, one_head = head_of(shape, lay)
    lane = iota(shape, 1)
    keep0 = (zero_head >= 0) & (zero_head + heads == row)
    keep1 = one_head == row
    ones = jnp.broadcast_to(jnp.where(keep0 & (lane >= base), 1.0, 0.0)[None], whole)
    columns = [turned[:, i : i + 1] for i in range(9)]
    lane = iota((block, LANES), 1)
    me = lax.axis_index("head")
    total = None
    for core, held in ((me, parcel), (1 - me, other)):
        took = jnp.concatenate([arrived[pl.ds(q * 2 + core, 1)] for q in range(count)], axis=0).astype(F32)
        side0 = jnp.where(keep0[None], jnp.broadcast_to(took[:, 2 * heads : 2 * heads + 1, :], whole), 0.0)
        side1 = jnp.where(keep1[None], jnp.broadcast_to(took[:, 2 * heads + 1 : 2 * heads + 2, :], whole), 0.0)
        right = jnp.concatenate([side0, side1, ones], axis=2).reshape(count * SUBLANES, 3 * LANES).astype(B16)
        moved = jnp.transpose(took.reshape(count * SUBLANES, LANES)).astype(B16)
        both = nn(moved, right)[:block]
        pieces = held[2 * LANES : 2 * LANES + ROWS16, 2 * LANES : 3 * LANES].astype(F32)
        gain = pieces[0:1] + pieces[1:2] + pieces[2:3]
        own = [held[2 * LANES :, at : at + LANES].astype(F32) for at in (0, LANES)]
        own = jnp.concatenate(own, axis=0)
        tile0, tile1 = both[:, :LANES], both[:, LANES : 2 * LANES]
        points = gain * (tile0 - both[:, 2 * LANES :] * own)
        points = pack(turned_back(columns, unpack(points, lay.kp)), lay.kp, base)
        tile0 = jnp.where(lane < base, tile0 * (1.0 / math.sqrt(C)), points)
        points = pack(turned_back(columns, unpack(tile1, lay.vp)), lay.vp, base)
        tile1 = jnp.where(lane < base, tile1, points)
        rows = jnp.concatenate([tile0, tile1], axis=1).astype(B16)
        part = nn(rows, held[: 2 * LANES, :])
        total = part if total is None else total + part
    result[...] = total


def finish_kernel(own, other, output, grad_query):
    width = output.shape[1]
    total = own[...] + other[...]
    output[...] = total[:1, :width].astype(output.dtype)
    grad_query[...] = total[:1, width:]


VMEM = pl.BlockSpec(memory_space=pltpu.VMEM)
HBM = pl.BlockSpec(memory_space=pltpu.HBM)


def call(body, outs, args, fresh=0, scratch=(), flops=1000000, last=False, waits=False):
    size = sum(math.prod(v.shape) * v.dtype.itemsize for v in list(args) + list(outs))

    def kernel(*refs):
        if fresh:
            *refs, sems = refs
            held = refs[len(refs) - fresh :]
            copies = [pltpu.make_async_copy(refs[i], held[i], sems.at[i]) for i in range(fresh)]
            for copy in copies:
                copy.start()

            def ready():
                for copy in copies:
                    copy.wait()

            if not waits:
                ready()
            refs = list(held) + list(refs[fresh : len(refs) - fresh])
        body(*([ready] if waits else []), *refs)

    own = [pltpu.VMEM(v.shape, v.dtype) for v in args[:fresh]]
    return pl.pallas_call(
        kernel,
        out_shape=tuple(outs),
        in_specs=[HBM] * fresh + [VMEM] * (len(args) - fresh),
        out_specs=tuple([pl.BlockSpec() if last else VMEM] * len(outs)),
        scratch_shapes=list(scratch) + own + ([pltpu.SemaphoreType.DMA((fresh,))] if fresh else []),
        compiler_params=pltpu.CompilerParams(vmem_limit_bytes=(16 << 20) + 6 * size),
        cost_estimate=pl.CostEstimate(flops=flops, bytes_accessed=size, transcendentals=0),
    )(*[pltpu.with_memory_space_constraint(v, pltpu.HBM) for v in args[:fresh]], *args[fresh:])


def shape_of(*dims, dtype=F32):
    return jax.ShapeDtypeStruct(dims, dtype)


def shards(
    query_single, key_single, pair, query_frames, key_frames, w_query, w_key, w_value, w_query_points, w_key_points,
    w_value_points, head_weight, bias_weight, w_out, d_out,
):
    lay = Layout(head_weight.shape[0])
    count = lax.axis_size("row")
    block, width = key_single.shape
    total = count * block
    near = 1
    while 4 * near * near <= count:
        near *= 2
    assert count & (count - 1) == 0

    def exchange(value, mask):
        return lax.ppermute(value, "row", [(i, i ^ mask) for i in range(count)])

    (packed,) = call(
        functools.partial(key_kernel, lay),
        [shape_of(block, 2 * LANES, dtype=B16)],
        [
            key_single, key_frames, w_key.T, w_value.T, w_key_points.T, w_value_points.T,
        ],
        6,
        waits=True,
    )
    offsets = list(range(0, count, near))
    line = jnp.concatenate([packed] + [exchange(packed, mask) for mask in offsets[1:]], axis=0)
    planes = [0, 2, 1] + list(range(3, near))
    parts = [line] + [exchange(line, m) for m in planes[1:]]
    order = [m ^ o for m in planes for o in offsets]

    left, base, d_base, d_row, w_out_rows, w_query_rows, table, pair_rows, gains, parcel, turned = call(
        functools.partial(early_kernel, lay, block, order),
        [
            shape_of(ROWS16, LANES), shape_of(SUBLANES, total), shape_of(SUBLANES, total),
            shape_of(SUBLANES, 2 * LANES), shape_of((2 + lay.heads) * LANES, width, dtype=B16),
            shape_of(LANES, width, dtype=B16), shape_of(ROWS16, LANES),
            shape_of(total, LANES, dtype=B16), shape_of(SUBLANES, LANES),
            shape_of(2 * LANES + block // 2, width, dtype=B16), shape_of(block, LANES),
        ],
        [
            query_frames.T, query_single, w_query.T, w_query_points.T, bias_weight, w_out, d_out, pair,
            head_weight.reshape(1, -1), key_frames, w_key.T, w_value.T, w_key_points.T, w_value_points.T, packed,
        ],
        14,
        [pltpu.VMEM((ROWS16, LANES), F32)],
    )
    swap = [(i, (i + 1) % 2) for i in range(2)]
    other = lax.ppermute(parcel, "head", swap)
    message, features, weight_rows, scores = call(
        functools.partial(attention_kernel, lay, block, order),
        [
            shape_of(2 * count, SUBLANES, LANES, dtype=B16), shape_of(SUBLANES, 2 * LANES),
            shape_of(SUBLANES, total, dtype=B16), shape_of(SUBLANES, total, dtype=B16),
        ],
        parts + [left, base, d_base, d_row, gains, table],
    )
    arrived = lax.all_to_all(message, ("row", "head"), 0, 0, tiled=True)
    (sums,) = call(
        functools.partial(rows_kernel, lay),
        [shape_of(SUBLANES, 2 * width)],
        parts + [pair_rows, left, scores, features, weight_rows, w_out_rows, w_query_rows, gains, table],
    )
    output, grad_query = call(
        finish_kernel,
        [shape_of(1, width, dtype=B16), shape_of(1, width)],
        [sums, lax.ppermute(sums, "head", swap)],
        last=True,
    )
    (grad_keys,) = call(
        functools.partial(owner_kernel, lay),
        [shape_of(block, width)],
        [arrived, turned, parcel, other],
        last=True,
    )
    return (output, grad_query, grad_keys)


def solution(mesh):
    return jax.shard_map(
        shards,
        mesh=mesh,
        in_specs=(
            P("row", None),
            P("row", None),
            P("row", None, None),
            P(None, "row"),
            P(None, "row"),
            P(None, "head"),
            P(None, "head"),
            P(None, "head"),
            P(None, "head"),
            P(None, "head"),
            P(None, "head"),
            P("head"),
            P("head", None),
            P("head", None),
            P("row", None),
        ),
        out_specs=(P("row", None), P("row", None), P("row", None)),
        check_vma=False,
    )
```

```python
import functools
import math

import jax
import jax.numpy as jnp
from jax import lax
from jax.experimental import pallas as pl
from jax.experimental.pallas import tpu as pltpu
from jax.sharding import PartitionSpec as P

C = 16
PQ = 4
PV = 8
LANES = 128
SUBLANES = 8
ROWS16 = 16
LOGIT_SCALE = math.sqrt(1.0 / 3.0)
POINT_SCALE = math.sqrt(2.0 / (9.0 * PQ))
F32 = jnp.float32
B16 = jnp.bfloat16


class Layout:
    def __init__(self, heads):
        self.heads = heads
        self.base = heads * C
        self.kp = heads * PQ
        self.vp = heads * PV
        self.square = self.base + 3 * self.kp
        assert self.square + self.kp <= LANES and self.base + 3 * self.vp <= LANES
        assert 2 * heads + 2 <= SUBLANES and PQ == 4


def nn(a, b, precision=None):
    return lax.dot_general(a, b, (((1,), (0,)), ((), ())), precision=precision, preferred_element_type=F32)


def nt(a, b):
    return lax.dot_general(a, b, (((1,), (1,)), ((), ())), preferred_element_type=F32)


def iota(shape, dim):
    return lax.broadcasted_iota(jnp.int32, shape, dim)


def pick(condition):
    return jnp.where(condition, 1.0, 0.0).astype(B16)


def to_lane(rows, offset):
    j, i = iota((LANES, rows), 0), iota((LANES, rows), 1)
    return pick(j == i + offset)


def to_components(rows, offset, points, seg):
    j, i = iota((LANES, rows), 0), iota((LANES, rows), 1)
    found = j < 0
    for c in range(3):
        m = j - (c * seg + offset)
        found = found | ((m >= 0) & (m < points) & (i == 3 * m + c))
    return pick(found)


def unpack(tile, seg):
    return tile, pltpu.roll(tile, LANES - seg, 1), pltpu.roll(tile, LANES - 2 * seg, 1)


def pack(parts, seg, base):
    lane = iota(parts[0].shape, 1)
    keep = (lane >= base) & (lane < base + seg)
    x, y, z = (jnp.where(keep, v, 0.0) for v in parts)
    return x + pltpu.roll(y, seg, 1) + pltpu.roll(z, 2 * seg, 1)


def head_of(shape, lay):
    lane = iota(shape, 1)
    zero = jnp.full(shape, -1, jnp.int32)
    one = jnp.full(shape, -1, jnp.int32)
    for h in range(lay.heads):
        same = (lane >= h * C) & (lane < (h + 1) * C)
        zero, one = jnp.where(same, h, zero), jnp.where(same, h, one)
        for c in range(3):
            k = lay.base + c * lay.kp + h * PQ
            v = lay.base + c * lay.vp + h * PV
            zero = jnp.where((lane >= k) & (lane < k + PQ), h, zero)
            one = jnp.where((lane >= v) & (lane < v + PV), h, one)
    return zero, one


def turned_by(frames, vectors):
    x, y, z = vectors
    return [frames[3 * c] * x + frames[3 * c + 1] * y + frames[3 * c + 2] * z for c in range(3)]


def turned_back(frames, vectors):
    x, y, z = vectors
    return [frames[d] * x + frames[3 + d] * y + frames[6 + d] * z for d in range(3)]


def key_kernel(lay, ready, key_single, frames, w_key, w_value, w_kp, w_vp, packed):
    heads, kp, vp, base = lay.heads, lay.kp, lay.vp, lay.base
    tall = PQ * SUBLANES

    def rows_of(count, width):
        return iota((count, width), 0), iota((count, width), 1)

    r, i = rows_of(tall, 3 * kp)
    to_kp = [pick((i == 3 * PQ * (r & 7) + 3 * (r >> 3) + c) & ((r & 7) < heads)) for c in range(3)]
    r, i = rows_of(vp, 3 * vp)
    to_vp = [pick(i == 3 * r + c) for c in range(3)]
    width = 2 * LANES
    r, j = rows_of(base, width)
    place = [j == r, j == r + LANES]
    r, j = rows_of(tall, width)
    place += [(j == base + c * kp + PQ * (r & 7) + (r >> 3)) & ((r & 7) < heads) for c in range(3)]
    r, j = rows_of(vp, width)
    place += [j == LANES + base + c * vp + r for c in range(3)]
    r, j = rows_of(SUBLANES, width)
    place += [(j == lay.square + PQ * r + piece) & (r < heads) for piece in range(3)]
    place = jnp.concatenate([jnp.where(found, 1.0, 0.0) for found in place], axis=0).astype(B16)
    to_kp = jnp.concatenate(to_kp, axis=0)
    to_vp = jnp.concatenate(to_vp, axis=0)
    ready()
    single = key_single[...]
    turn = [frames[i : i + 1, :] for i in range(12)]
    features = [nt(w_key[...], single), nt(w_value[...], single)]
    for choose, weight, height in ((to_kp, w_kp, tall), (to_vp, w_vp, vp)):
        rows = nt(nn(choose, weight[...]).astype(B16), single)
        moved = turned_by(turn, [rows[c * height : (c + 1) * height] for c in range(3)])
        moved = [(v + turn[9 + c]).astype(B16).astype(F32) for c, v in enumerate(moved)]
        features += moved
        if height == tall:
            square = moved[0] * moved[0] + moved[1] * moved[1] + moved[2] * moved[2]
            square = sum(square[group(p)] for p in range(PQ))
    first = square.astype(B16).astype(F32)
    second = (square - first).astype(B16).astype(F32)
    features = jnp.concatenate(features + [first, second, square - first - second], axis=0)
    packed[...] = nn(jnp.transpose(features).astype(B16), place).astype(B16)


def group(h):
    return slice(h * SUBLANES, (h + 1) * SUBLANES)


def gain_rows(head_weight, lay):
    row = iota((SUBLANES, LANES), 0)
    raw = jnp.zeros((SUBLANES, LANES), F32)
    for h in range(lay.heads):
        raw = jnp.where(row == h, jnp.broadcast_to(head_weight[:, h : h + 1], raw.shape), raw)
    gain = (jnp.maximum(raw, 0.0) + jnp.log1p(jnp.exp(-jnp.abs(raw)))) * POINT_SCALE
    return jnp.where(row < lay.heads, gain, 0.0)


def gain_lanes(gain, lay):
    zero, _ = head_of(gain.shape, lay)
    return jnp.sum(jnp.where(zero == iota(gain.shape, 0), gain, 0.0), axis=0, keepdims=True)


def early_kernel(
    lay, block, order, frames, query_single, w_query, w_qp, bias_weight, w_out, d_out, pair, head_weight, key_frames,
    w_key, w_value, w_kp, w_vp, packed,
    left, base, d_base, d_row, w_out_rows, w_query_rows, table, pair_rows, gains, parcel, turned, scratch,
):
    kp, vp = lay.kp, lay.vp
    zero = nn(to_lane(lay.base, 0), w_key[...]) + nn(to_components(3 * kp, lay.base, kp, kp), w_kp[...])
    one = nn(to_lane(lay.base, 0), w_value[...]) + nn(to_components(3 * vp, lay.base, vp, vp), w_vp[...])
    parcel[:LANES, :] = zero.astype(B16)
    parcel[LANES : 2 * LANES, :] = one.astype(B16)
    half = block // 2
    parcel[2 * LANES :, :LANES] = packed[:half, :LANES]
    parcel[2 * LANES :, LANES : 2 * LANES] = packed[half:, :LANES]
    parcel[2 * LANES :, 2 * LANES :] = jnp.zeros((half, parcel.shape[1] - 2 * LANES), B16)
    gain = gain_rows(head_weight, lay)
    gains[...] = gain
    pieces = jnp.broadcast_to(gain_lanes(gain, lay), (ROWS16, LANES))
    first = pieces.astype(B16).astype(F32)
    second = (pieces - first).astype(B16).astype(F32)
    row = iota(pieces.shape, 0)
    pieces = jnp.where(
        row == 0, first, jnp.where(row == 1, second, jnp.where(row == 2, pieces - first - second, 0.0))
    )
    parcel[2 * LANES : 2 * LANES + ROWS16, 2 * LANES : 3 * LANES] = pieces.astype(B16)
    turn = jnp.transpose(key_frames[...])
    turned[:, : turn.shape[1]] = turn
    me = lax.axis_index("row")
    for place, offset in enumerate(order):
        j = pl.multiple_of((me ^ offset) * block, block)
        pair_rows[place * block : (place + 1) * block, :] = pair[0, pl.ds(j, block), :]
    turn = [jnp.broadcast_to(frames[:, i : i + 1], (1, LANES)) for i in range(12)]
    for i in range(12):
        table[i : i + 1, :] = turn[i]
    heads, start = lay.heads, lay.base
    width = C + 4 * PV + LANES
    near = C + 4 * PV
    shape = (SUBLANES, LANES)
    row, lane = iota(shape, 0), iota(shape, 1)
    zero_head, _ = head_of(shape, lay)
    w_q = nn(to_lane(start, 0), w_query[...]) + nn(to_components(3 * lay.kp, start, lay.kp, lay.kp), w_qp[...])
    w_q = w_q.astype(B16)
    w_query_rows[...] = w_q
    w_o = jnp.zeros((2 * LANES, w_out.shape[1]), F32)
    for h in range(heads):
        i, j = iota((2 * LANES, near), 0), iota((2 * LANES, near), 1)
        m = i - (LANES + h * C)
        found = (m >= 0) & (m < C) & (j == m)
        m = i - (start + h * PV)
        found = found | ((m >= 0) & (m < PV) & (j == C + 3 * PV + m))
        for c in range(3):
            m = i - (LANES + start + c * lay.vp + h * PV)
            found = found | ((m >= 0) & (m < PV) & (j == C + 3 * m + c))
        w_o = w_o + nn(pick(found), w_out[h * width : h * width + near, :])
    w_o = w_o.astype(B16)
    w_out_rows[: 2 * LANES, :] = w_o
    for h in range(heads):
        w_out_rows[(2 + h) * LANES : (3 + h) * LANES, :] = w_out[h * width + near : (h + 1) * width, :]
    single = jnp.broadcast_to(query_single[...], (SUBLANES, query_single.shape[1]))
    rows = nt(single, w_q)
    moved = turned_by(turn, unpack(rows, lay.kp))
    points = pack([(v + turn[9 + c]).astype(B16).astype(F32) for c, v in enumerate(moved)], lay.kp, start)
    query = jnp.where(lane < start, rows, 0.0).astype(B16).astype(F32)
    left[:SUBLANES, :] = jnp.where(zero_head == row, query, 0.0)
    minus = lane < 0
    for h in range(heads):
        at = lay.square + h * PQ
        minus = minus | ((row == h) & (lane >= at) & (lane < at + 3))
    mine = jnp.where(zero_head == row, points, 0.0)
    left[SUBLANES:, :] = jnp.where(minus, -0.5, mine)
    cotangent = jnp.broadcast_to(d_out[...], (SUBLANES, d_out.shape[1]))
    d_row[...] = nt(cotangent, w_o)
    scratch[...] = jnp.zeros_like(scratch)
    scratch[:heads, :] = bias_weight[...].astype(F32)
    for h in range(heads):
        d_pair = nt(cotangent, w_out[h * width + near : (h + 1) * width, :])
        scratch[SUBLANES + h : SUBLANES + h + 1, :] = d_pair[:1, :]
    both = nt(scratch[...].astype(B16), pair_rows[...])
    square = jnp.sum(mine * mine, axis=1, keepdims=True)
    base[...] = both[:SUBLANES] - 0.5 * gain[:, :1] * square
    d_base[...] = both[SUBLANES:]


def attention_kernel(lay, block, order, *refs):
    *parts, left, base, d_base, d_row, gains, table, message, features, weights, scores = refs
    frames = [table[i : i + 1, :] for i in range(12)]
    me = lax.axis_index("row")
    heads, vp, start = lay.heads, lay.vp, lay.base
    shape = (SUBLANES, LANES)
    row, lane = iota(shape, 0), iota(shape, 1)
    _, one_head = head_of(shape, lay)
    gain = gains[...]
    queries = left[...].astype(B16)
    first = jnp.concatenate([nt(queries, part[:, :LANES]) for part in parts], axis=1)
    logits = LOGIT_SCALE * (first[:SUBLANES] * (1.0 / math.sqrt(C)) + base[...] + gain[:, :1] * first[SUBLANES:])
    weight = jnp.exp(logits - jnp.max(logits, axis=1, keepdims=True))
    attention = weight * (1.0 / jnp.sum(weight, axis=1, keepdims=True))
    attention = jnp.where(iota(attention.shape, 0) < heads, attention, 0.0)
    attention_b = attention.astype(B16)
    sums = spread(attention_b, [part.at[:, LANES:] for part in parts])
    sums = jnp.sum(jnp.where(one_head == row, sums, 0.0), axis=0, keepdims=True)
    sums = jnp.broadcast_to(sums, shape)
    local = turned_back(frames, [v - frames[9 + c] for c, v in enumerate(unpack(sums, vp))])
    lengths = jnp.sqrt(1.0 + (local[0] * local[0] + local[1] * local[1] + local[2] * local[2]))
    d_one = d_row[:, LANES:]
    share = d_row[:, :LANES] / lengths
    d_points = turned_by(frames, [v + share * u for v, u in zip(unpack(d_one, vp), local)])
    d_side = jnp.where(lane < start, d_one, 0.0) + pack(d_points, vp, start)
    right = jnp.where(one_head == row, d_side, 0.0).astype(B16)
    d_attention = jnp.concatenate([nt(right, part[:, LANES:]) for part in parts], axis=1) + d_base[...]
    total = jnp.sum(attention * d_attention, axis=1, keepdims=True)
    score_b = (LOGIT_SCALE * attention * (d_attention - total)).astype(B16)
    query = jnp.sum(jnp.where(lane < lay.square, left[:SUBLANES, :] + left[SUBLANES:, :], 0.0), axis=0, keepdims=True)
    side = jnp.where(row == 2 * heads, jnp.broadcast_to(query, shape), 0.0)
    side = side + jnp.where(row == 2 * heads + 1, d_side, 0.0)
    both = attention_b.astype(F32) + pltpu.roll(score_b.astype(F32), heads, 0)
    for at in range(0, both.shape[1], LANES):
        for place in range(at // block, (at + LANES) // block):
            tile = both[:, at : at + LANES]
            if place * block != at:
                tile = pltpu.roll(tile, LANES - (place * block - at), 1)
            tile = jnp.where(row < 2 * heads, tile, side).astype(B16)
            for core in range(2):
                message[(me ^ order[place]) * 2 + core, :, :] = tile
    weights[...] = attention_b
    scores[...] = score_b
    features[:, :LANES] = jnp.where((lane >= start) & (lane < start + vp), lengths, 0.0)
    features[:, LANES:] = jnp.where(lane < start, sums, 0.0) + pack(local, vp, start)


def spread(weights, parts):
    total, at = 0.0, 0
    for part in parts:
        total = total + nn(weights[:, at : at + part.shape[0]], part[...])
        at += part.shape[0]
    return total


def rows_kernel(lay, *refs):
    *parts, pair, left, scores, features, weights, w_out_rows, w_query_rows, gains, table, sums = refs
    frames = [table[i : i + 1, :] for i in range(12)]
    shape = (SUBLANES, LANES)
    row, lane = iota(shape, 0), iota(shape, 1)
    zero_head, _ = head_of(shape, lay)
    pair_sum = nn(weights[...], pair[...])
    pairs = [jnp.broadcast_to(pair_sum[h : h + 1, :], shape) for h in range(lay.heads)]
    result = nn(jnp.concatenate([features[...]] + pairs, axis=1).astype(B16), w_out_rows[...])
    score = scores[...].astype(F32)
    d_rows = spread(scores[...], [part.at[:, :LANES] for part in parts])
    score_sum = jnp.sum(score, axis=1, keepdims=True)
    points = left[SUBLANES:, :]
    d_rows = jnp.where(lane < lay.base, d_rows * (1.0 / math.sqrt(C)), gains[...] * (d_rows - score_sum * points))
    d_rows = jnp.broadcast_to(
        jnp.sum(jnp.where(zero_head == row, d_rows, 0.0), axis=0, keepdims=True), shape
    )
    local = pack(turned_back(frames, unpack(d_rows, lay.kp)), lay.kp, lay.base)
    both = (jnp.where(lane < lay.base, d_rows, 0.0) + local).astype(B16)
    sums[...] = jnp.concatenate([result, nn(both, w_query_rows[...])], axis=1)


def owner_kernel(lay, arrived, turned, parcel, other, result):
    heads, base = lay.heads, lay.base
    count = arrived.shape[0] // 2
    block = turned.shape[0]
    shape = (SUBLANES, LANES)
    whole = (count, SUBLANES, LANES)
    row = iota(shape, 0)
    zero_head, one_head = head_of(shape, lay)
    lane = iota(shape, 1)
    keep0 = (zero_head >= 0) & (zero_head + heads == row)
    keep1 = one_head == row
    ones = jnp.broadcast_to(jnp.where(keep0 & (lane >= base), 1.0, 0.0)[None], whole)
    columns = [turned[:, i : i + 1] for i in range(9)]
    lane = iota((block, LANES), 1)
    me = lax.axis_index("head")
    total = None
    for core, held in ((me, parcel), (1 - me, other)):
        took = jnp.concatenate([arrived[pl.ds(q * 2 + core, 1)] for q in range(count)], axis=0).astype(F32)
        side0 = jnp.where(keep0[None], jnp.broadcast_to(took[:, 2 * heads : 2 * heads + 1, :], whole), 0.0)
        side1 = jnp.where(keep1[None], jnp.broadcast_to(took[:, 2 * heads + 1 : 2 * heads + 2, :], whole), 0.0)
        right = jnp.concatenate([side0, side1, ones], axis=2).reshape(count * SUBLANES, 3 * LANES).astype(B16)
        moved = jnp.transpose(took.reshape(count * SUBLANES, LANES)).astype(B16)
        both = nn(moved, right)[:block]
        pieces = held[2 * LANES : 2 * LANES + ROWS16, 2 * LANES : 3 * LANES].astype(F32)
        gain = pieces[0:1] + pieces[1:2] + pieces[2:3]
        own = [held[2 * LANES :, at : at + LANES].astype(F32) for at in (0, LANES)]
        own = jnp.concatenate(own, axis=0)
        tile0, tile1 = both[:, :LANES], both[:, LANES : 2 * LANES]
        points = gain * (tile0 - both[:, 2 * LANES :] * own)
        points = pack(turned_back(columns, unpack(points, lay.kp)), lay.kp, base)
        tile0 = jnp.where(lane < base, tile0 * (1.0 / math.sqrt(C)), points)
        points = pack(turned_back(columns, unpack(tile1, lay.vp)), lay.vp, base)
        tile1 = jnp.where(lane < base, tile1, points)
        rows = jnp.concatenate([tile0, tile1], axis=1).astype(B16)
        part = nn(rows, held[: 2 * LANES, :])
        total = part if total is None else total + part
    result[...] = total


def finish_kernel(own, other, output, grad_query):
    width = output.shape[1]
    total = own[...] + other[...]
    output[...] = total[:1, :width].astype(output.dtype)
    grad_query[...] = total[:1, width:]


VMEM = pl.BlockSpec(memory_space=pltpu.VMEM)
HBM = pl.BlockSpec(memory_space=pltpu.HBM)


def call(body, outs, args, fresh=0, scratch=(), flops=1000000, last=False, waits=False):
    size = sum(math.prod(v.shape) * v.dtype.itemsize for v in list(args) + list(outs))

    def kernel(*refs):
        if fresh:
            *refs, sems = refs
            held = refs[len(refs) - fresh :]
            copies = [pltpu.make_async_copy(refs[i], held[i], sems.at[i]) for i in range(fresh)]
            for copy in copies:
                copy.start()

            def ready():
                for copy in copies:
                    copy.wait()

            if not waits:
                ready()
            refs = list(held) + list(refs[fresh : len(refs) - fresh])
        body(*([ready] if waits else []), *refs)

    own = [pltpu.VMEM(v.shape, v.dtype) for v in args[:fresh]]
    return pl.pallas_call(
        kernel,
        out_shape=tuple(outs),
        in_specs=[HBM] * fresh + [VMEM] * (len(args) - fresh),
        out_specs=tuple([pl.BlockSpec() if last else VMEM] * len(outs)),
        scratch_shapes=list(scratch) + own + ([pltpu.SemaphoreType.DMA((fresh,))] if fresh else []),
        compiler_params=pltpu.CompilerParams(vmem_limit_bytes=(16 << 20) + 6 * size),
        cost_estimate=pl.CostEstimate(flops=flops, bytes_accessed=size, transcendentals=0),
    )(*[pltpu.with_memory_space_constraint(v, pltpu.HBM) for v in args[:fresh]], *args[fresh:])


def shape_of(*dims, dtype=F32):
    return jax.ShapeDtypeStruct(dims, dtype)


def shards(
    query_single, key_single, pair, query_frames, key_frames, w_query, w_key, w_value, w_query_points, w_key_points,
    w_value_points, head_weight, bias_weight, w_out, d_out,
):
    lay = Layout(head_weight.shape[0])
    count = lax.axis_size("row")
    block, width = key_single.shape
    total = count * block
    near = 1
    while 4 * near * near <= count:
        near *= 2
    assert count & (count - 1) == 0

    def exchange(value, mask):
        return lax.ppermute(value, "row", [(i, i ^ mask) for i in range(count)])

    (packed,) = call(
        functools.partial(key_kernel, lay),
        [shape_of(block, 2 * LANES, dtype=B16)],
        [
            key_single, key_frames, w_key.T, w_value.T, w_key_points.T, w_value_points.T,
        ],
        6,
        waits=True,
    )
    offsets = list(range(0, count, near))
    line = jnp.concatenate([packed] + [exchange(packed, mask) for mask in offsets[1:]], axis=0)
    planes = list(range(near))
    parts = [line] + [exchange(line, m) for m in planes[1:]]
    order = [m ^ o for m in planes for o in offsets]

    left, base, d_base, d_row, w_out_rows, w_query_rows, table, pair_rows, gains, parcel, turned = call(
        functools.partial(early_kernel, lay, block, order),
        [
            shape_of(ROWS16, LANES), shape_of(SUBLANES, total), shape_of(SUBLANES, total),
            shape_of(SUBLANES, 2 * LANES), shape_of((2 + lay.heads) * LANES, width, dtype=B16),
            shape_of(LANES, width, dtype=B16), shape_of(ROWS16, LANES),
            shape_of(total, LANES, dtype=B16), shape_of(SUBLANES, LANES),
            shape_of(2 * LANES + block // 2, width, dtype=B16), shape_of(block, LANES),
        ],
        [
            query_frames.T, query_single, w_query.T, w_query_points.T, bias_weight, w_out, d_out, pair,
            head_weight.reshape(1, -1), key_frames, w_key.T, w_value.T, w_key_points.T, w_value_points.T, packed,
        ],
        14,
        [pltpu.VMEM((ROWS16, LANES), F32)],
    )
    swap = [(i, (i + 1) % 2) for i in range(2)]
    other = lax.ppermute(parcel, "head", swap)
    message, features, weight_rows, scores = call(
        functools.partial(attention_kernel, lay, block, order),
        [
            shape_of(2 * count, SUBLANES, LANES, dtype=B16), shape_of(SUBLANES, 2 * LANES),
            shape_of(SUBLANES, total, dtype=B16), shape_of(SUBLANES, total, dtype=B16),
        ],
        parts + [left, base, d_base, d_row, gains, table],
    )
    arrived = lax.all_to_all(message, ("row", "head"), 0, 0, tiled=True)
    (sums,) = call(
        functools.partial(rows_kernel, lay),
        [shape_of(SUBLANES, 2 * width)],
        parts + [pair_rows, left, scores, features, weight_rows, w_out_rows, w_query_rows, gains, table],
    )
    output, grad_query = call(
        finish_kernel,
        [shape_of(1, width, dtype=B16), shape_of(1, width)],
        [sums, lax.ppermute(sums, "head", swap)],
        last=True,
    )
    (grad_keys,) = call(
        functools.partial(owner_kernel, lay),
        [shape_of(block, width)],
        [arrived, turned, parcel, other],
        last=True,
    )
    return (output, grad_query, grad_keys)


def solution(mesh):
    return jax.shard_map(
        shards,
        mesh=mesh,
        in_specs=(
            P("row", None),
            P("row", None),
            P("row", None, None),
            P(None, "row"),
            P(None, "row"),
            P(None, "head"),
            P(None, "head"),
            P(None, "head"),
            P(None, "head"),
            P(None, "head"),
            P(None, "head"),
            P("head"),
            P("head", None),
            P("head", None),
            P("row", None),
        ),
        out_specs=(P("row", None), P("row", None), P("row", None)),
        check_vma=False,
    )
```
